32 devices in a mesh: seg: 8 (over z, x), term: 4 (over y, core).
Axes of the slice: x: 2, y: 2, z: 4, core: 2. Of those that a mesh axis runs over, the one named last changes fastest.
Arguments:
- wave_guess: float32 [8, 256, 16, 256], P('seg', 'term'), may hold values from -6 to 6
- left_env: bfloat16 [8, 12, 256, 256], P('seg', 'term'), may hold values from -0.44194174 to 2.6419417, as said below
- right_env: bfloat16 [8, 12, 256, 256], P('seg', 'term'), may hold values from -0.44194174 to 1.2419417, as said below
- site_ops: bfloat16 [8, 12, 16, 16], P('seg', 'term'), may hold values from -0.51031036 to 0.7686437, as said below
- bond_rank: int32 [8], P('seg'), may hold values from 128 to 256, as said below
Outputs:
- ritz_vector: float32 [8, 256, 16, 256], P('seg', 'term')
- energy: float32 [8], P('seg')
The draws below stay inside these ranges and needn't reach their ends.
Inputs may be any that keep to these rules, and one draw needn't show every extreme that they name: `bond_rank`: the largest rank is 256 in every draw. Every block left_env[s, k] is symmetric. Every block right_env[s, k] is symmetric. Every block site_ops[s, k] is symmetric.
All inputs are finite; a program needn't handle non-finite values.
Results may differ from the reference program's by a relative error of at most 0.005.
Values may be sent and summed in bfloat16 or wider, within the bound.
No kernel may reach another device: no remote copies, remote signals or barrier semaphores. Data moves between devices by JAX's collectives and lax.ppermute only.
A program may use at most 64 MiB of HBM per device.

```python
import jax
import jax.numpy as jnp
from jax import lax

M = 256
PHYS = 16
TERMS = 12
SEGS = 8
N_TERM = 4


def symmetric_part(key, shape, width, spread_low, spread_high):
    first_key, second_key = jax.random.split(key)
    bell_raw = jnp.clip(jax.random.normal(first_key, shape, jnp.float32), -5.0, 5.0)
    raw = bell_raw
    blocks = (raw + jnp.swapaxes(raw, 2, 3)) / jnp.sqrt(2.0 * width)
    scales = jnp.exp(jax.random.uniform(second_key, shape[:3], jnp.float32, jnp.log(spread_low), jnp.log(spread_high)))
    return blocks * scales[:, :, :, None] * scales[:, :, None, :]


def draw_left_env(key, part):
    key = jax.random.fold_in(key, 11)
    shape = (SEGS, TERMS, M, M)
    block_key, parity_key, level_key = jax.random.split(key, 3)
    parity = jax.random.randint(parity_key, (SEGS,), 0, 2)
    row_index = jnp.arange(M, dtype=jnp.int32)
    upper_rows = row_index[None, :] % 2 == parity[:, None]
    jitter = jax.random.uniform(level_key, (SEGS, TERMS, M), jnp.float32, 0.0, 1.0)
    blocks = symmetric_part(block_key, shape, M, 1.0, 1.0)
    high_level = 1.6 + 0.6 * jitter
    low_level = 0.3 + 0.4 * jitter
    levels = jnp.where(upper_rows[:, None, :], high_level, low_level)
    diagonal = jnp.eye(M, dtype=jnp.float32)[None, None] * levels[:, :, :, None]
    return (blocks + diagonal).astype(jnp.bfloat16)


def draw_right_env(key, part):
    key = jax.random.fold_in(key, 23)
    shape = (SEGS, TERMS, M, M)
    first_key, second_key = jax.random.split(key)
    blocks = symmetric_part(first_key, shape, M, 1.0, 1.0)
    levels = jax.random.uniform(second_key, (SEGS, TERMS), jnp.float32, 0.25, 0.75)
    diagonal = jnp.eye(M, dtype=jnp.float32)[None, None] * levels[:, :, None, None]
    return (blocks + diagonal).astype(jnp.bfloat16)


def draw_site_ops(key, part):
    key = jax.random.fold_in(key, 37)
    shape = (SEGS, TERMS, PHYS, PHYS)
    blocks = symmetric_part(key, shape, PHYS * TERMS, 1.0, 1.0)
    rising = (1.0 + 2.0 * jnp.arange(TERMS, dtype=jnp.float32) / max(TERMS - 1, 1)) / TERMS
    diagonal = jnp.eye(PHYS, dtype=jnp.float32)[None, None] * rising[None, :, None, None]
    return (blocks + diagonal).astype(jnp.bfloat16)


def draw_bond_rank(key, part):
    key = jax.random.fold_in(key, 53)
    first_key, second_key = jax.random.split(key)
    ranks = jax.random.randint(first_key, (SEGS,), M // 2, M + 1)
    chosen = jax.random.randint(second_key, (), 0, SEGS)
    positions = jnp.arange(SEGS)
    return jnp.where(positions == chosen, M, ranks).astype(jnp.int32)


def level_of(key, extent, cuts, low, high):
    def one(dim, blocks):
        heights = jax.random.uniform(jax.random.fold_in(jax.random.fold_in(key, 6), dim), (blocks,), jnp.float32, low / len(cuts), high / len(cuts))
        return jnp.repeat(jnp.exp(heights), extent[dim] // blocks).reshape((-1,) + (1,) * (len(extent) - dim - 1))

    gain = one(*cuts[0])
    for cut in cuts[1:]:
        gain = gain * one(*cut)
    return gain


def gaussian(stream_key, shape, deviation, reach, cuts=(), kind=jnp.bfloat16):
    array = jax.random.normal(stream_key, shape, jnp.float32) * deviation
    if len(cuts) > 0:
        array = level_of(stream_key, shape, cuts, -0.22, 0.18) * array
    return jnp.clip(array, min=-reach, max=reach).astype(kind)


def setup_inputs(seed: int = 0) -> dict:
    key_list = jax.random.split(jax.random.key(seed), 6)
    wave_guess = gaussian(key_list[0], (SEGS, M, PHYS, M), 1.0, 6.0, ((0, 8), (1, 4)), jnp.float32)
    left_env = draw_left_env(jax.random.fold_in(key_list[5], 71), 0)
    right_env = draw_right_env(jax.random.fold_in(key_list[5], 71), 0)
    site_ops = draw_site_ops(jax.random.fold_in(key_list[5], 71), 0)
    bond_rank = draw_bond_rank(jax.random.fold_in(key_list[5], 71), 0)
    return dict(wave_guess=wave_guess, left_env=left_env, right_env=right_env, site_ops=site_ops, bond_rank=bond_rank)


epsilon = 1e-06

def round_trip(values):
    return lax.optimization_barrier(values.astype(jnp.bfloat16)).astype(jnp.float32)

def apply_segment(left_blocks, right_blocks, site_blocks, keep_mask, vector_bf):
    per_group = TERMS // N_TERM
    flat_vector = vector_bf.reshape(M, PHYS * M)
    left_groups = left_blocks.reshape(N_TERM, per_group, M, M)
    right_groups = right_blocks.reshape(N_TERM, per_group, M, M)
    site_groups = site_blocks.reshape(N_TERM, per_group, PHYS, PHYS)

    def add_group(running, members):
        left_part, right_part, site_part = members
        partial_value = jnp.zeros((M, PHYS, M), jnp.float32)
        for term_slot in range(per_group):
            left_mixed = jnp.dot(left_part[term_slot], flat_vector, preferred_element_type=jnp.float32).astype(jnp.bfloat16)
            both_mixed = jnp.dot(left_mixed.reshape(M * PHYS, M), right_part[term_slot].T, preferred_element_type=jnp.float32).astype(jnp.bfloat16)
            partial_value = partial_value + jnp.einsum('pq,aqb->apb', site_part[term_slot].astype(jnp.float32), both_mixed.reshape(M, PHYS, M).astype(jnp.float32))
        return (running + round_trip(partial_value), None)
    total_sum, unused_out = lax.scan(add_group, jnp.zeros((M, PHYS, M), jnp.float32), (left_groups, right_groups, site_groups))
    return total_sum * keep_mask

def one_segment(items):
    guess, left_blocks, right_blocks, site_blocks, rank_value = items
    entry_count = M * PHYS * M
    keep_mask = (lax.iota(jnp.int32, M) < rank_value).astype(jnp.float32)[None, None, :]
    masked = guess * keep_mask
    norm_sq = jnp.sum(masked * masked) / entry_count
    vector_now = masked / jnp.sqrt(norm_sq + epsilon)
    vector_bf = vector_now.astype(jnp.bfloat16)
    sigma = apply_segment(left_blocks, right_blocks, site_blocks, keep_mask, vector_bf)
    rayleigh = jnp.sum(vector_now * sigma) / entry_count
    residual = sigma - rayleigh * vector_now
    res_sq = jnp.sum(residual * residual) / entry_count
    res_scale = jnp.sqrt(res_sq + epsilon)
    direction = residual / res_scale
    direction_bf = direction.astype(jnp.bfloat16)
    image_all = apply_segment(left_blocks, right_blocks, site_blocks, keep_mask, direction_bf)
    curvature = jnp.sum(direction_bf.astype(jnp.float32) * image_all) / entry_count
    coupling = res_sq / res_scale
    half_gap = 0.5 * (rayleigh - curvature)
    energy = 0.5 * (rayleigh + curvature) - jnp.sqrt(half_gap * half_gap + coupling * coupling)
    coeff_new = energy - rayleigh
    coeff_norm = jnp.sqrt(coupling * coupling + coeff_new * coeff_new + epsilon)
    ritz = (coupling * vector_now + coeff_new * direction) / coeff_norm
    return (ritz, energy)

def reference(wave_guess, left_env, right_env, site_ops, bond_rank):
    right_used = jnp.concatenate([right_env[1:], right_env[-1:]], axis=0)
    ritz_vector, energy = lax.map(one_segment, (wave_guess, left_env, right_used, site_ops, bond_rank))
    return (ritz_vector, energy)
```

```python
import functools

import jax
import jax.numpy as jnp
from jax import lax
from jax.experimental import pallas as pl
from jax.experimental.pallas import tpu as pltpu
from jax.sharding import PartitionSpec as P

epsilon = 1e-06
CORES = 2
TILE = 16
VMEM_LIMIT = 56 * 1024 * 1024
F32 = jnp.float32
BF16 = jnp.bfloat16

vmem = pl.BlockSpec(memory_space=pltpu.VMEM)
smem = pl.BlockSpec(memory_space=pltpu.SMEM)
anywhere = pl.BlockSpec(memory_space=pl.ANY)


def params():
    return pltpu.CompilerParams(vmem_limit_bytes=VMEM_LIMIT)


def cost(flops, moved):
    return pl.CostEstimate(flops=int(flops), bytes_accessed=int(moved), transcendentals=0)


def keep_row(rank, width):
    return (lax.broadcasted_iota(jnp.int32, (1, width), 1) < rank).astype(F32)


def prepare_kernel(rank_ref, guess_ref, x_ref, norm_ref):
    rows, states, width = guess_ref.shape
    masked = guess_ref[...] * keep_row(rank_ref[0], width)[None]
    norm_ref[...] = jnp.full(norm_ref.shape, jnp.sum(masked * masked), F32)
    x_ref[...] = jnp.swapaxes(masked, 0, 1).astype(BF16)


def spread_site(site_ref, kron_ref):
    terms, states, _ = site_ref.shape
    size = states * TILE
    row_state = lax.broadcasted_iota(jnp.int32, (size, states), 0) // TILE
    pick = (row_state == lax.broadcasted_iota(jnp.int32, (size, states), 1)).astype(BF16)
    col_state = lax.broadcasted_iota(jnp.int32, (states, size), 1) // TILE
    pick_t = (col_state == lax.broadcasted_iota(jnp.int32, (states, size), 0)).astype(BF16)
    same = (
        lax.broadcasted_iota(jnp.int32, (size, size), 0) % TILE
        == lax.broadcasted_iota(jnp.int32, (size, size), 1) % TILE
    )
    for k in range(terms):
        tall = jnp.dot(pick, site_ref[k], preferred_element_type=F32).astype(BF16)
        full = jnp.dot(tall, pick_t, preferred_element_type=F32)
        kron_ref[:, k * size : (k + 1) * size] = jnp.where(same, full, 0.0).astype(BF16)


def mix_bonds(block, left_ref, right_ref, both_ref, p):
    terms, width, _ = left_ref.shape
    mixed = jnp.dot(
        left_ref[...].reshape(terms * width, width), block, preferred_element_type=F32
    ).astype(BF16)
    for k in range(terms):
        both_ref[k, p] = jnp.dot(
            mixed[k * width : (k + 1) * width], right_ref[k], preferred_element_type=F32
        ).astype(BF16)


def mix_sites(both_ref, kron_ref, i):
    terms, states, _, width = both_ref.shape
    at = pl.multiple_of(i * TILE, TILE)
    stack = both_ref[:, :, pl.ds(at, TILE), :].reshape(terms * states * TILE, width)
    return jnp.dot(kron_ref[...], stack, preferred_element_type=F32).reshape(states, TILE, width)


def place_pieces(pieces, hops, whole_ref, sems):
    chips = len(hops)
    me = lax.axis_index("term")
    core = me % CORES
    chip = me // CORES
    copies = []
    for n, piece in enumerate(pieces):
        hop = hops[n // 2]
        owner = ((chip - hop + chips) % chips) * CORES + (core if n % 2 == 0 else 1 - core)
        rows = piece.shape[1]
        at = pl.multiple_of(owner * rows, TILE)
        copies.append(pltpu.make_async_copy(piece, whole_ref.at[:, pl.ds(at, rows), :], sems.at[n]))
    for copy in copies:
        copy.start()
    return copies


def apply_kernel(piece_count, hops, *refs):
    pieces = refs[:piece_count]
    left_ref, right_ref, site_ref, partial_ref, stat_ref, whole_ref, both_ref, kron_ref, sems = refs[piece_count:]
    states, width, _ = whole_ref.shape
    copies = place_pieces(pieces, hops, whole_ref, sems)
    spread_site(site_ref, kron_ref)
    for copy in copies:
        copy.wait()

    def bonds(p, carry):
        mix_bonds(whole_ref[p], left_ref, right_ref, both_ref, p)
        return carry

    lax.fori_loop(0, states, bonds, 0, unroll=2)

    def sites(i, total):
        part = mix_sites(both_ref, kron_ref, i).astype(BF16)
        at = pl.multiple_of(i * TILE, TILE)
        partial_ref[:, pl.ds(at, TILE), :] = part
        held = whole_ref[:, pl.ds(at, TILE), :].astype(F32)
        return total + jnp.sum((held * part.astype(F32)).reshape(states * TILE // 8, 8, width), axis=0)

    total = lax.fori_loop(0, width // TILE, sites, jnp.zeros((8, width), F32), unroll=2)
    stat_ref[...] = jnp.full(stat_ref.shape, jnp.sum(total), F32)


def second_kernel(group_count, hops, scale, *refs):
    groups = refs[:group_count]
    stats = refs[group_count : 2 * group_count]
    pieces = refs[2 * group_count : 3 * group_count]
    rest = refs[3 * group_count :]
    (rank_ref, norm_ref, left_ref, right_ref, site_ref, sigma_ref, out_ref) = rest[:7]
    (whole_ref, group_buf, res_ref, both_ref, kron_ref, sems, group_sems) = rest[7:]
    states, width, _ = whole_ref.shape
    rows = sigma_ref.shape[1]
    copies = place_pieces(pieces, hops, whole_ref, sems)
    for p in range(states):
        for g in range(group_count):
            pltpu.make_async_copy(groups[g].at[p], group_buf.at[g, p], group_sems.at[g, p]).start()
    spread_site(site_ref, kron_ref)
    keep = keep_row(rank_ref[0], width)
    inverse = lax.rsqrt(norm_ref[0:1, :] * scale + epsilon)

    def summed(values):
        evens = functools.reduce(jnp.add, values[0::2])
        odds = functools.reduce(jnp.add, values[1::2])
        return evens + odds

    rayleigh = summed([s[0:1, :] for s in stats]) * (inverse * inverse * scale)
    row_scale = keep * inverse
    me = lax.axis_index("term")
    own = pl.multiple_of(me * rows, TILE)
    for copy in copies:
        copy.wait()

    def bonds(p, total):
        for g in range(group_count):
            pltpu.make_async_copy(groups[g].at[p], group_buf.at[g, p], group_sems.at[g, p]).wait()
        sigma = summed([group_buf[g, p].astype(F32) for g in range(group_count)]) * row_scale
        residual = sigma - (rayleigh * inverse) * whole_ref[p].astype(F32)
        rounded = residual.astype(BF16)
        res_ref[p] = rounded
        mine = summed([group_buf[g, p, pl.ds(own, rows), :].astype(F32) for g in range(group_count)])
        sigma_ref[p] = mine * row_scale
        mix_bonds(rounded, left_ref, right_ref, both_ref, p)
        return total + jnp.sum((residual * residual).reshape(width // 8, 8, width), axis=0)

    square = lax.fori_loop(0, states, bonds, jnp.zeros((8, width), F32))

    def sites(i, total):
        image = mix_sites(both_ref, kron_ref, i)
        at = pl.multiple_of(i * TILE, TILE)
        held = res_ref[:, pl.ds(at, TILE), :].astype(F32)
        return total + jnp.sum((held * image).reshape(states * TILE // 8, 8, width), axis=0)

    cross = lax.fori_loop(0, width // TILE, sites, jnp.zeros((8, width), F32), unroll=2)
    share = 1.0 / group_count
    out_ref[0:1, :] = rayleigh * share
    out_ref[1:2, :] = jnp.full((1, width), jnp.sum(square) * (scale * share), F32)
    out_ref[2:3, :] = jnp.full((1, width), jnp.sum(cross) * scale, F32)
    out_ref[3:8, :] = jnp.zeros((5, width), F32)


def finish_kernel(scale, rank_ref, guess_ref, sigma_ref, stat_ref, norm_ref, ritz_ref, energy_ref):
    rows, states, width = guess_ref.shape
    inverse = lax.rsqrt(norm_ref[0:1, :] * scale + epsilon)
    rayleigh = stat_ref[0:1, :]
    res_sq = stat_ref[1:2, :]
    res_var = res_sq + epsilon
    curvature = stat_ref[2:3, :] / res_var
    res_scale = jnp.sqrt(res_var)
    coupling = res_sq / res_scale
    half_gap = 0.5 * (rayleigh - curvature)
    energy = 0.5 * (rayleigh + curvature) - jnp.sqrt(half_gap * half_gap + coupling * coupling)
    coeff_new = energy - rayleigh
    coeff_norm = jnp.sqrt(coupling * coupling + coeff_new * coeff_new + epsilon)
    old = coupling / coeff_norm
    new = coeff_new / (coeff_norm * res_scale)
    vector = guess_ref[...] * (keep_row(rank_ref[0], width) * inverse)[None]
    sigma = jnp.swapaxes(sigma_ref[...], 0, 1)
    ritz_ref[...] = old[None] * vector + new[None] * (sigma - rayleigh[None] * vector)
    energy_ref[0] = energy[0, 0]


def shards(wave_guess, left_env, right_env, site_ops, bond_rank):
    guess = wave_guess[0]
    left = left_env[0]
    site = site_ops[0]
    rows, states, width = guess.shape
    terms = left.shape[0]
    members = lax.axis_size("term")
    chips = members // CORES
    segments = lax.axis_size("seg")
    scale = 1.0 / float(rows * members * states * width)
    hops = tuple(range(chips))

    def to_sibling(block):
        return lax.ppermute(block, "term", [(i, i ^ 1) for i in range(members)])

    def to_next_chip(block):
        return lax.ppermute(block, "term", [(i, (i + CORES) % members) for i in range(members)])

    def around(block):
        found = [block]
        for _ in range(chips - 1):
            found.append(to_next_chip(found[-1]))
        return found

    def total(block):
        bit = 1
        while bit < members:
            block = block + lax.ppermute(block, "term", [(i, i ^ bit) for i in range(members)])
            bit *= 2
        return block

    tile = jax.ShapeDtypeStruct((8, width), F32)
    x_own, norm_part = pl.pallas_call(
        prepare_kernel,
        out_shape=(jax.ShapeDtypeStruct((states, rows, width), BF16), tile),
        in_specs=[smem, vmem],
        out_specs=(vmem, vmem),
        compiler_params=params(),
        cost_estimate=cost(4 * guess.size, 6 * guess.size),
        name="prepare",
    )(bond_rank, guess)

    shift = [(i + 1, i) for i in range(segments - 1)]
    received = lax.ppermute(right_env, "seg", shift)
    right = jnp.where(lax.axis_index("seg") == segments - 1, right_env, received)[0]

    x_hops = around(x_own)
    pieces = []
    for block in x_hops:
        pieces += [block, to_sibling(block)]
    norm = total(norm_part)

    left_hops = around(left)
    right_hops = around(right)
    site_hops = around(site)

    whole = (states, width, width)
    both = (terms, states, width, width)
    kron = (states * TILE, terms * states * TILE)
    apply_flops = 2 * terms * states * width * width * (2 * width + states * TILE)
    apply_call = pl.pallas_call(
        functools.partial(apply_kernel, members, hops),
        out_shape=(jax.ShapeDtypeStruct(whole, BF16), tile),
        in_specs=[anywhere] * members + [vmem] * 3,
        out_specs=(vmem, vmem),
        scratch_shapes=[
            pltpu.VMEM(whole, BF16),
            pltpu.VMEM(both, BF16),
            pltpu.VMEM(kron, BF16),
            pltpu.SemaphoreType.DMA((members,)),
        ],
        compiler_params=params(),
        cost_estimate=cost(apply_flops, 4 * states * width * width),
        name="apply_terms",
    )

    groups = []
    stats = []
    for hop in hops:
        partial, stat = apply_call(*pieces, left_hops[hop], right_hops[hop], site_hops[hop])
        groups += [partial, to_sibling(partial)]
        stats += [stat, to_sibling(stat)]

    sigma_own, share = pl.pallas_call(
        functools.partial(second_kernel, members, hops, scale),
        out_shape=(jax.ShapeDtypeStruct((states, rows, width), F32), tile),
        in_specs=[anywhere] * members + [vmem] * members + [anywhere] * members + [smem] + [vmem] * 4,
        out_specs=(vmem, vmem),
        scratch_shapes=[
            pltpu.VMEM(whole, BF16),
            pltpu.VMEM((members,) + whole, BF16),
            pltpu.VMEM(whole, BF16),
            pltpu.VMEM(both, BF16),
            pltpu.VMEM(kron, BF16),
            pltpu.SemaphoreType.DMA((members,)),
            pltpu.SemaphoreType.DMA((members, states)),
        ],
        compiler_params=params(),
        cost_estimate=cost(apply_flops, 2 * members * states * width * width),
        name="apply_residual",
    )(*groups, *stats, *pieces, bond_rank, norm, left, right, site)

    ritz, energy = pl.pallas_call(
        functools.partial(finish_kernel, scale),
        out_shape=(jax.ShapeDtypeStruct((rows, states, width), F32), jax.ShapeDtypeStruct((1,), F32)),
        in_specs=[smem] + [vmem] * 4,
        out_specs=(vmem, smem),
        compiler_params=params(),
        cost_estimate=cost(4 * guess.size, 12 * guess.size),
        name="finish",
    )(bond_rank, guess, sigma_own, total(share), norm)
    return (ritz[None], energy)


def solution(mesh):
    in_specs = (
        P("seg", "term", None, None),
        P("seg", "term", None, None),
        P("seg", "term", None, None),
        P("seg", "term", None, None),
        P("seg"),
    )
    out_specs = (P("seg", "term", None, None), P("seg"))
    return jax.shard_map(shards, mesh=mesh, in_specs=in_specs, out_specs=out_specs, check_vma=False)
```

```python
import functools

import jax
import jax.numpy as jnp
from jax import lax
from jax.experimental import pallas as pl
from jax.experimental.pallas import tpu as pltpu
from jax.sharding import PartitionSpec as P

epsilon = 1e-06
CORES = 2
TILE = 16
VMEM_LIMIT = 28 * 1024 * 1024
F32 = jnp.float32
BF16 = jnp.bfloat16

vmem = pl.BlockSpec(memory_space=pltpu.VMEM)
smem = pl.BlockSpec(memory_space=pltpu.SMEM)
anywhere = pl.BlockSpec(memory_space=pl.ANY)


def params():
    return pltpu.CompilerParams(vmem_limit_bytes=VMEM_LIMIT)


def cost(flops, moved):
    return pl.CostEstimate(flops=int(flops), bytes_accessed=int(moved), transcendentals=0)


def keep_row(rank, width):
    return (lax.broadcasted_iota(jnp.int32, (1, width), 1) < rank).astype(F32)


def prepare_kernel(rank_ref, guess_ref, x_ref, norm_ref):
    rows, states, width = guess_ref.shape
    masked = guess_ref[...] * keep_row(rank_ref[0], width)[None]
    norm_ref[...] = jnp.full(norm_ref.shape, jnp.sum(masked * masked), F32)
    x_ref[...] = jnp.swapaxes(masked, 0, 1).astype(BF16)


def spread_site(site_ref, kron_ref):
    terms, states, _ = site_ref.shape
    size = states * TILE
    row_state = lax.broadcasted_iota(jnp.int32, (size, states), 0) // TILE
    pick = (row_state == lax.broadcasted_iota(jnp.int32, (size, states), 1)).astype(BF16)
    col_state = lax.broadcasted_iota(jnp.int32, (states, size), 1) // TILE
    pick_t = (col_state == lax.broadcasted_iota(jnp.int32, (states, size), 0)).astype(BF16)
    same = (
        lax.broadcasted_iota(jnp.int32, (size, size), 0) % TILE
        == lax.broadcasted_iota(jnp.int32, (size, size), 1) % TILE
    )
    for k in range(terms):
        tall = jnp.dot(pick, site_ref[k], preferred_element_type=F32).astype(BF16)
        full = jnp.dot(tall, pick_t, preferred_element_type=F32)
        kron_ref[k * size : (k + 1) * size, :] = jnp.where(same, full, 0.0).astype(BF16)


def mix_sites(source_ref, kron_ref, rotated_ref):
    terms, states, width, _ = rotated_ref.shape

    def step(i, carry):
        at = pl.multiple_of(i * TILE, TILE)
        stack = source_ref[:, pl.ds(at, TILE), :].reshape(states * TILE, width)
        turned = jnp.dot(kron_ref[...], stack, preferred_element_type=F32).astype(BF16)
        rotated_ref[:, :, pl.ds(at, TILE), :] = turned.reshape(terms, states, TILE, width)
        return carry

    lax.fori_loop(0, width // TILE, step, 0, unroll=4)


def fold(values, width):
    return jnp.sum(values.reshape(values.size // (8 * width), 8, width), axis=0)


def summed(values):
    while len(values) > 1:
        values = [values[n] + values[n + 1] for n in range(0, len(values), 2)]
    return values[0]


def place_pieces(pieces, hops, whole_ref, sems):
    chips = len(hops)
    me = lax.axis_index("term")
    core = me % CORES
    chip = me // CORES
    copies = []
    for n, piece in enumerate(pieces):
        hop = hops[n // 2]
        owner = ((chip - hop + chips) % chips) * CORES + (core if n % 2 == 0 else 1 - core)
        rows = piece.shape[1]
        at = pl.multiple_of(owner * rows, TILE)
        copies.append(pltpu.make_async_copy(piece, whole_ref.at[:, pl.ds(at, rows), :], sems.at[n]))
    for copy in copies:
        copy.start()
    return copies


def apply_terms(left_ref, right_ref, site_ref, whole_ref, partial_ref, rotated_ref, mixed_ref, kron_ref):
    terms, states, width, _ = rotated_ref.shape
    mix_sites(whole_ref, kron_ref, rotated_ref)

    def lefts(p, carry):
        for k in range(terms):
            mixed = jnp.dot(left_ref[k], rotated_ref[k, p], preferred_element_type=F32)
            mixed_ref[p, :, k * width : (k + 1) * width] = mixed.astype(BF16)
        return carry

    lax.fori_loop(0, states, lefts, 0, unroll=4)
    group = 4

    def rights(n, total):
        at = n * group
        rows = mixed_ref[pl.ds(at, group)].reshape(group * width, terms * width)
        stacked = right_ref[...].reshape(terms * width, width)
        part = jnp.dot(rows, stacked, preferred_element_type=F32).astype(BF16)
        part = part.reshape(group, width, width)
        partial_ref[pl.ds(at, group)] = part
        held = whole_ref[pl.ds(at, group)].astype(F32)
        return total + fold(held * part.astype(F32), width)

    total = lax.fori_loop(0, states // group, rights, jnp.zeros((8, width), F32))
    return jnp.sum(total)


def first_kernel(piece_count, hops, *refs):
    pieces = refs[:piece_count]
    norms = refs[piece_count : 2 * piece_count]
    rest = refs[2 * piece_count :]
    left_ref, right_ref, site_ref, whole_ref, partial_ref, stat_ref = rest[:6]
    rotated_ref, mixed_ref, kron_ref, sems = rest[6:]
    width = whole_ref.shape[1]
    copies = place_pieces(pieces, hops, whole_ref, sems)
    spread_site(site_ref, kron_ref)
    for copy in copies:
        copy.wait()
    total = apply_terms(
        left_ref, right_ref, site_ref, whole_ref, partial_ref, rotated_ref, mixed_ref, kron_ref
    )
    stat_ref[0:1, :] = jnp.full((1, width), total, F32)
    stat_ref[1:2, :] = summed([norm[0:1, :] for norm in norms])
    stat_ref[2:8, :] = jnp.zeros((6, width), F32)


def next_kernel(
    whole_ref, before_ref, left_ref, right_ref, site_ref, partial_ref, stat_ref, rotated_ref, mixed_ref, kron_ref
):
    spread_site(site_ref, kron_ref)
    total = apply_terms(
        left_ref, right_ref, site_ref, whole_ref, partial_ref, rotated_ref, mixed_ref, kron_ref
    )
    stat_ref[...] = before_ref[...]
    stat_ref[0:1, :] = before_ref[0:1, :] + total


def second_kernel(group_count, scale, *refs):
    groups = refs[:group_count]
    (rank_ref, mine_ref, theirs_ref, whole_ref, left_ref, right_ref, site_ref) = refs[group_count : group_count + 7]
    (sigma_ref, out_ref, res_ref, rotated_ref, mixed_ref, kron_ref) = refs[group_count + 7 :]
    terms, states, width, _ = rotated_ref.shape
    rows = sigma_ref.shape[1]
    spread_site(site_ref, kron_ref)
    keep = keep_row(rank_ref[0], width)
    inverse = lax.rsqrt(mine_ref[1:2, :] * scale + epsilon)
    rayleigh = (mine_ref[0:1, :] + theirs_ref[0:1, :]) * (inverse * inverse * scale)
    row_scale = keep * inverse
    me = lax.axis_index("term")
    own = pl.multiple_of(me * rows, TILE)

    def group_sum(p, rows_at):
        evens = [group[p, rows_at, :].astype(F32) for group in groups[0::2]]
        odds = [group[p, rows_at, :].astype(F32) for group in groups[1::2]]
        return functools.reduce(jnp.add, evens) + functools.reduce(jnp.add, odds)

    def lefts(p, total):
        sigma = group_sum(p, slice(None)) * row_scale
        residual = sigma - (rayleigh * inverse) * whole_ref[p].astype(F32)
        rounded = residual.astype(BF16)
        res_ref[p] = rounded
        sigma_ref[p] = group_sum(p, pl.ds(own, rows)) * row_scale
        mixed = jnp.dot(
            left_ref[...].reshape(terms * width, width), rounded, preferred_element_type=F32
        ).astype(BF16)
        for k in range(terms):
            mixed_ref[k, p] = mixed[k * width : (k + 1) * width]
        return total + fold(residual * residual, width)

    square = lax.fori_loop(0, states, lefts, jnp.zeros((8, width), F32), unroll=2)
    mix_sites(res_ref, kron_ref, rotated_ref)
    group = 4
    cross = jnp.zeros((8, width), F32)
    for k in range(terms):

        def rights(n, total):
            at = n * group
            turned = rotated_ref[k, pl.ds(at, group)].reshape(group * width, width)
            image = jnp.dot(turned, right_ref[k], preferred_element_type=F32)
            held = mixed_ref[k, pl.ds(at, group)].reshape(group * width, width).astype(F32)
            return total + fold(held * image, width)

        cross = lax.fori_loop(0, states // group, rights, cross)
    share = 1.0 / group_count
    out_ref[0:1, :] = rayleigh * share
    out_ref[1:2, :] = jnp.full((1, width), jnp.sum(square) * (scale * share), F32)
    out_ref[2:3, :] = jnp.full((1, width), jnp.sum(cross) * scale, F32)
    out_ref[3:8, :] = jnp.zeros((5, width), F32)


def finish_kernel(scale, rank_ref, guess_ref, sigma_ref, norm_ref, *refs):
    shares = refs[:-2]
    ritz_ref, energy_ref = refs[-2:]
    rows, states, width = guess_ref.shape
    inverse = lax.rsqrt(norm_ref[1:2, :] * scale + epsilon)
    stat = summed([share[...] for share in shares])
    rayleigh = stat[0:1, :]
    res_sq = stat[1:2, :]
    res_var = res_sq + epsilon
    curvature = stat[2:3, :] / res_var
    res_scale = jnp.sqrt(res_var)
    coupling = res_sq / res_scale
    half_gap = 0.5 * (rayleigh - curvature)
    energy = 0.5 * (rayleigh + curvature) - jnp.sqrt(half_gap * half_gap + coupling * coupling)
    coeff_new = energy - rayleigh
    coeff_norm = jnp.sqrt(coupling * coupling + coeff_new * coeff_new + epsilon)
    old = coupling / coeff_norm
    new = coeff_new / (coeff_norm * res_scale)
    vector = guess_ref[...] * (keep_row(rank_ref[0], width) * inverse)[None]
    sigma = jnp.swapaxes(sigma_ref[...], 0, 1)
    ritz_ref[...] = old[None] * vector + new[None] * (sigma - rayleigh[None] * vector)
    energy_ref[0] = energy[0, 0]


def shards(wave_guess, left_env, right_env, site_ops, bond_rank):
    guess = wave_guess[0]
    left = left_env[0]
    site = site_ops[0]
    rows, states, width = guess.shape
    terms = left.shape[0]
    members = lax.axis_size("term")
    chips = members // CORES
    segments = lax.axis_size("seg")
    scale = 1.0 / float(rows * members * states * width)
    hops = tuple(range(chips))

    def to_sibling(block):
        return lax.ppermute(block, "term", [(i, i ^ 1) for i in range(members)])

    def to_next_chip(block):
        return lax.ppermute(block, "term", [(i, (i + CORES) % members) for i in range(members)])

    def around(block):
        found = [block]
        for _ in range(chips - 1):
            found.append(to_next_chip(found[-1]))
        return found

    def everyone(block):
        others = [
            lax.ppermute(block, "term", [(i, i ^ bits) for i in range(members)]) for bits in range(1, members)
        ]
        return [block] + others

    tile = jax.ShapeDtypeStruct((8, width), F32)
    x_own, norm_part = pl.pallas_call(
        prepare_kernel,
        out_shape=(jax.ShapeDtypeStruct((states, rows, width), BF16), tile),
        in_specs=[smem, vmem],
        out_specs=(vmem, vmem),
        compiler_params=params(),
        cost_estimate=cost(4 * guess.size, 6 * guess.size),
        name="prepare",
    )(bond_rank, guess)

    shift = [(i + 1, i) for i in range(segments - 1)]
    received = lax.ppermute(right_env, "seg", shift)
    right = jnp.where(lax.axis_index("seg") == segments - 1, right_env, received)[0]

    x_hops = around(x_own)
    pieces = []
    for block in x_hops:
        pieces += [block, to_sibling(block)]
    norms = everyone(norm_part)

    left_hops = around(left)
    right_hops = around(right)
    site_hops = around(site)

    whole = (states, width, width)
    rotated = (terms, states, width, width)
    scratch = [
        pltpu.VMEM(rotated, BF16),
        pltpu.VMEM((states, width, terms * width), BF16),
        pltpu.VMEM((terms * states * TILE, states * TILE), BF16),
    ]
    apply_flops = 2 * terms * states * width * width * (2 * width + states * TILE)
    apply_cost = cost(apply_flops, 4 * states * width * width)
    vector, partial, stat = pl.pallas_call(
        functools.partial(first_kernel, members, hops),
        out_shape=(jax.ShapeDtypeStruct(whole, BF16), jax.ShapeDtypeStruct(whole, BF16), tile),
        in_specs=[anywhere] * members + [vmem] * (members + 3),
        out_specs=(vmem, vmem, vmem),
        scratch_shapes=scratch + [pltpu.SemaphoreType.DMA((members,))],
        compiler_params=params(),
        cost_estimate=apply_cost,
        name="apply_own_terms",
    )(*pieces, *norms, left, right, site)
    groups = [partial, to_sibling(partial)]
    for hop in hops[1:]:
        partial, stat = pl.pallas_call(
            next_kernel,
            out_shape=(jax.ShapeDtypeStruct(whole, BF16), tile),
            in_specs=[vmem] * 5,
            out_specs=(vmem, vmem),
            scratch_shapes=scratch,
            compiler_params=params(),
            cost_estimate=apply_cost,
            name="apply_received_terms",
        )(vector, stat, left_hops[hop], right_hops[hop], site_hops[hop])
        groups += [partial, to_sibling(partial)]

    sigma_own, share = pl.pallas_call(
        functools.partial(second_kernel, members, scale),
        out_shape=(jax.ShapeDtypeStruct((states, rows, width), F32), tile),
        in_specs=[vmem] * members + [smem] + [vmem] * 6,
        out_specs=(vmem, vmem),
        scratch_shapes=[
            pltpu.VMEM(whole, BF16),
            pltpu.VMEM(rotated, BF16),
            pltpu.VMEM(rotated, BF16),
            pltpu.VMEM((terms * states * TILE, states * TILE), BF16),
        ],
        compiler_params=params(),
        cost_estimate=cost(apply_flops, 2 * members * states * width * width),
        name="apply_residual",
    )(*groups, bond_rank, stat, to_sibling(stat), vector, left, right, site)

    ritz, energy = pl.pallas_call(
        functools.partial(finish_kernel, scale),
        out_shape=(jax.ShapeDtypeStruct((rows, states, width), F32), jax.ShapeDtypeStruct((1,), F32)),
        in_specs=[smem] + [vmem] * (3 + members),
        out_specs=(vmem, smem),
        compiler_params=params(),
        cost_estimate=cost(4 * guess.size, 12 * guess.size),
        name="finish",
    )(bond_rank, guess, sigma_own, stat, *everyone(share))
    return (ritz[None], energy)


def solution(mesh):
    in_specs = (
        P("seg", "term", None, None),
        P("seg", "term", None, None),
        P("seg", "term", None, None),
        P("seg", "term", None, None),
        P("seg"),
    )
    out_specs = (P("seg", "term", None, None), P("seg"))
    return jax.shard_map(shards, mesh=mesh, in_specs=in_specs, out_specs=out_specs, check_vma=False)
```

```python
import functools

import jax
import jax.numpy as jnp
from jax import lax
from jax.experimental import pallas as pl
from jax.experimental.pallas import tpu as pltpu
from jax.sharding import PartitionSpec as P

epsilon = 1e-06
CORES = 2
TILE = 16
UNROLL = 4
GROUP = 4
VMEM_LIMIT = 28 * 1024 * 1024
F32 = jnp.float32
BF16 = jnp.bfloat16

vmem = pl.BlockSpec(memory_space=pltpu.VMEM)
smem = pl.BlockSpec(memory_space=pltpu.SMEM)
anywhere = pl.BlockSpec(memory_space=pl.ANY)


def params():
    return pltpu.CompilerParams(vmem_limit_bytes=VMEM_LIMIT)


def cost(flops, moved):
    return pl.CostEstimate(flops=int(flops), bytes_accessed=int(moved), transcendentals=0)


def keep_row(rank, width):
    return (lax.broadcasted_iota(jnp.int32, (1, width), 1) < rank).astype(F32)


def prepare_kernel(rank_ref, guess_ref, x_ref, norm_ref):
    rows, states, width = guess_ref.shape
    masked = guess_ref[...] * keep_row(rank_ref[0], width)[None]
    norm_ref[...] = jnp.full(norm_ref.shape, jnp.sum(masked * masked), F32)
    x_ref[...] = jnp.swapaxes(masked, 0, 1).astype(BF16)


def triangle(half):
    row = lax.broadcasted_iota(jnp.int32, (half, half), 0)
    col = lax.broadcasted_iota(jnp.int32, (half, half), 1)
    return row, col


def pack_kernel(left_ref, right_ref, site_ref, norm_ref, bundle_ref):
    terms, width, _ = left_ref.shape
    states = site_ref.shape[1]
    half = width // 2
    row, col = triangle(half)
    widen = (
        lax.broadcasted_iota(jnp.int32, (states, half), 0) == lax.broadcasted_iota(jnp.int32, (states, half), 1)
    ).astype(BF16)
    norm = norm_ref[0:1, 0:half]
    parts = []
    for _ in range(3):
        parts.append(norm.astype(BF16).astype(F32))
        norm = norm - parts[-1]
    lines = lax.broadcasted_iota(jnp.int32, (TILE, half), 0)
    lines = functools.reduce(jnp.add, [jnp.where(lines == n, parts[n], 0.0) for n in range(3)]).astype(BF16)
    for k in range(terms):
        for m, ref in enumerate((left_ref, right_ref)):
            base = m * (2 * half + TILE)
            upper = ref[k, 0:half, 0:half].astype(F32)
            lower = ref[k, half:width, half:width].astype(F32)
            diagonal = jnp.sum(jnp.where(row == col, lower, 0.0), axis=0, keepdims=True)
            bundle_ref[k, base : base + half, :] = ref[k, 0:half, half:width]
            bundle_ref[k, base + half : base + 2 * half, :] = jnp.where(row <= col, upper, lower).astype(BF16)
            bundle_ref[k, base + 2 * half : base + 2 * half + TILE, :] = jnp.broadcast_to(
                diagonal, (TILE, half)
            ).astype(BF16)
        base = 2 * (2 * half + TILE)
        bundle_ref[k, base : base + states, :] = jnp.dot(
            site_ref[k], widen, preferred_element_type=F32
        ).astype(BF16)
        bundle_ref[k, base + states : base + states + TILE, :] = lines


def unpack(bundle_ref, left_ref, right_ref):
    terms, width, _ = left_ref.shape
    half = width // 2
    row, col = triangle(half)
    for k in range(terms):
        for m, ref in enumerate((left_ref, right_ref)):
            base = m * (2 * half + TILE)
            corner = bundle_ref[k, base : base + half, :]
            mixed = bundle_ref[k, base + half : base + 2 * half, :].astype(F32)
            diagonal = bundle_ref[k, base + 2 * half : base + 2 * half + TILE, :].astype(F32)[0:1]
            turned = mixed.T
            ref[k, 0:half, 0:half] = jnp.where(row <= col, mixed, turned).astype(BF16)
            ref[k, 0:half, half:width] = corner
            ref[k, half:width, 0:half] = corner.astype(F32).T.astype(BF16)
            ref[k, half:width, half:width] = jnp.where(
                row > col, mixed, jnp.where(row == col, diagonal, turned)
            ).astype(BF16)


def spread_site(sites, states, kron_ref):
    size = states * TILE
    lanes = sites[0].shape[1]
    row_state = lax.broadcasted_iota(jnp.int32, (size, states), 0) // TILE
    pick = (row_state == lax.broadcasted_iota(jnp.int32, (size, states), 1)).astype(BF16)
    col_state = lax.broadcasted_iota(jnp.int32, (lanes, size), 1) // TILE
    pick_t = (col_state == lax.broadcasted_iota(jnp.int32, (lanes, size), 0)).astype(BF16)
    same = (
        lax.broadcasted_iota(jnp.int32, (size, size), 0) % TILE
        == lax.broadcasted_iota(jnp.int32, (size, size), 1) % TILE
    )
    for k, site in enumerate(sites):
        tall = jnp.dot(pick, site, preferred_element_type=F32).astype(BF16)
        full = jnp.dot(tall, pick_t, preferred_element_type=F32)
        kron_ref[k * size : (k + 1) * size, :] = jnp.where(same, full, 0.0).astype(BF16)


def mix_sites(source_ref, kron_ref, rotated_ref):
    terms, states, width, _ = rotated_ref.shape

    def step(i, carry):
        at = pl.multiple_of(i * TILE, TILE)
        stack = source_ref[:, pl.ds(at, TILE), :].reshape(states * TILE, width)
        turned = jnp.dot(kron_ref[...], stack, preferred_element_type=F32).astype(BF16)
        rotated_ref[:, :, pl.ds(at, TILE), :] = turned.reshape(terms, states, TILE, width)
        return carry

    lax.fori_loop(0, width // TILE, step, 0, unroll=2 * UNROLL)


def fold(values, width):
    return jnp.sum(values.reshape(values.size // (8 * width), 8, width), axis=0)


def summed(values):
    while len(values) > 1:
        values = [values[n] + values[n + 1] for n in range(0, len(values), 2)]
    return values[0]


def place_pieces(pieces, hops, whole_ref, sems):
    chips = len(hops)
    me = lax.axis_index("term")
    core = me % CORES
    chip = me // CORES
    copies = []
    for n, piece in enumerate(pieces):
        hop = hops[n // 2]
        owner = ((chip - hop + chips) % chips) * CORES + (core if n % 2 == 0 else 1 - core)
        rows = piece.shape[1]
        at = pl.multiple_of(owner * rows, TILE)
        copies.append(pltpu.make_async_copy(piece, whole_ref.at[:, pl.ds(at, rows), :], sems.at[n]))
    for copy in copies:
        copy.start()
    return copies


def rotate_and_mix(left_ref, whole_ref, rotated_ref, mixed_ref, kron_ref):
    terms, states, width, _ = rotated_ref.shape
    mix_sites(whole_ref, kron_ref, rotated_ref)

    def lefts(p, carry):
        for k in range(terms):
            mixed = jnp.dot(left_ref[k], rotated_ref[k, p], preferred_element_type=F32)
            mixed_ref[p, :, k * width : (k + 1) * width] = mixed.astype(BF16)
        return carry

    lax.fori_loop(0, states, lefts, 0, unroll=UNROLL)


def right_rows(right_ref, mixed_ref, at):
    terms, width, _ = right_ref.shape
    rows = mixed_ref[pl.ds(at, GROUP)].reshape(GROUP * width, terms * width)
    stacked = right_ref[...].reshape(terms * width, width)
    return jnp.dot(rows, stacked, preferred_element_type=F32).reshape(GROUP, width, width)


def first_kernel(piece_count, hops, *refs):
    pieces = refs[:piece_count]
    left_ref, right_ref, site_ref, whole_ref, partial_ref = refs[piece_count : piece_count + 5]
    rotated_ref, mixed_ref, kron_ref, sems = refs[piece_count + 5 :]
    terms, states, _, _ = rotated_ref.shape
    copies = place_pieces(pieces, hops, whole_ref, sems)
    spread_site([site_ref[k] for k in range(terms)], states, kron_ref)
    for copy in copies:
        copy.wait()
    rotate_and_mix(left_ref, whole_ref, rotated_ref, mixed_ref, kron_ref)

    def rights(n, carry):
        at = n * GROUP
        partial_ref[pl.ds(at, GROUP)] = right_rows(right_ref, mixed_ref, at).astype(BF16)
        return carry

    lax.fori_loop(0, states // GROUP, rights, 0)


def next_kernel(
    whole_ref,
    before_ref,
    stat_before_ref,
    bundle_ref,
    partial_ref,
    stat_ref,
    rotated_ref,
    mixed_ref,
    kron_ref,
    left_ref,
    right_ref,
):
    terms, states, width, _ = rotated_ref.shape
    base = 2 * (width + TILE)
    spread_site([bundle_ref[k, base : base + states, :] for k in range(terms)], states, kron_ref)
    unpack(bundle_ref, left_ref, right_ref)
    rotate_and_mix(left_ref, whole_ref, rotated_ref, mixed_ref, kron_ref)

    def rights(n, total):
        at = n * GROUP
        before = before_ref[pl.ds(at, GROUP)].astype(F32)
        part = (before + right_rows(right_ref, mixed_ref, at)).astype(BF16)
        partial_ref[pl.ds(at, GROUP)] = part
        held = whole_ref[pl.ds(at, GROUP)].astype(F32)
        return total + fold(held * part.astype(F32), width)

    total = lax.fori_loop(0, states // GROUP, rights, jnp.zeros((8, width), F32))
    lines = bundle_ref[0, base + states : base + states + TILE, :].astype(F32)
    norm = lines[0:1] + lines[1:2] + lines[2:3]
    stat_ref[0:1, :] = jnp.full((1, width), jnp.sum(total), F32)
    stat_ref[1:2, :] = stat_before_ref[1:2, :] + jnp.concatenate([norm, norm], axis=1)
    stat_ref[2:8, :] = jnp.zeros((6, width), F32)


def scales(rank_ref, mine_ref, theirs_ref, scale, width):
    inverse = lax.rsqrt((mine_ref[1:2, :] + theirs_ref[1:2, :]) * scale + epsilon)
    rayleigh = (mine_ref[0:1, :] + theirs_ref[0:1, :]) * (inverse * inverse * scale)
    return inverse, rayleigh, keep_row(rank_ref[0], width) * inverse


def second_kernel(
    scale,
    members,
    rank_ref,
    mine_ref,
    theirs_ref,
    partial_ref,
    other_ref,
    whole_ref,
    left_ref,
    right_ref,
    site_ref,
    out_ref,
    res_ref,
    rotated_ref,
    mixed_ref,
    kron_ref,
):
    terms, states, width, _ = rotated_ref.shape
    spread_site([site_ref[k] for k in range(terms)], states, kron_ref)
    inverse, rayleigh, row_scale = scales(rank_ref, mine_ref, theirs_ref, scale, width)
    back = rayleigh * inverse

    def lefts(p, total):
        sigma = (partial_ref[p].astype(F32) + other_ref[p].astype(F32)) * row_scale
        residual = sigma - back * whole_ref[p].astype(F32)
        rounded = residual.astype(BF16)
        res_ref[p] = rounded
        mixed = jnp.dot(
            left_ref[...].reshape(terms * width, width), rounded, preferred_element_type=F32
        ).astype(BF16)
        for k in range(terms):
            mixed_ref[k, p] = mixed[k * width : (k + 1) * width]
        return total + fold(residual * residual, width)

    square = lax.fori_loop(0, states, lefts, jnp.zeros((8, width), F32), unroll=UNROLL)
    mix_sites(res_ref, kron_ref, rotated_ref)

    def rights(n, total):
        at = n * GROUP
        for k in range(terms):
            turned = rotated_ref[k, pl.ds(at, GROUP)].reshape(GROUP * width, width)
            image = jnp.dot(turned, right_ref[k], preferred_element_type=F32)
            held = mixed_ref[k, pl.ds(at, GROUP)].reshape(GROUP * width, width).astype(F32)
            total = total + fold(held * image, width)
        return total

    cross = lax.fori_loop(0, states // GROUP, rights, jnp.zeros((8, width), F32))
    share = 1.0 / members
    out_ref[0:1, :] = rayleigh * share
    out_ref[1:2, :] = jnp.full((1, width), jnp.sum(square) * (scale * share), F32)
    out_ref[2:3, :] = jnp.full((1, width), jnp.sum(cross) * scale, F32)
    out_ref[3:8, :] = jnp.zeros((5, width), F32)


def own_rows_kernel(
    scale, rank_ref, guess_ref, mine_ref, theirs_ref, partial_ref, other_ref, vector_ref, residual_ref
):
    rows, states, width = guess_ref.shape
    inverse, rayleigh, row_scale = scales(rank_ref, mine_ref, theirs_ref, scale, width)
    own = pl.ds(pl.multiple_of(lax.axis_index("term") * rows, TILE), rows)
    sigma = (partial_ref[:, own, :].astype(F32) + other_ref[:, own, :].astype(F32)) * row_scale[None]
    vector = guess_ref[...] * row_scale[None]
    vector_ref[...] = vector
    residual_ref[...] = jnp.swapaxes(sigma, 0, 1) - rayleigh[None] * vector


def finish_kernel(vector_ref, residual_ref, *refs):
    shares = refs[:-2]
    ritz_ref, energy_ref = refs[-2:]
    stat = summed([share[...] for share in shares])
    rayleigh = stat[0:1, :]
    res_sq = stat[1:2, :]
    res_var = res_sq + epsilon
    curvature = stat[2:3, :] / res_var
    res_scale = jnp.sqrt(res_var)
    coupling = res_sq / res_scale
    half_gap = 0.5 * (rayleigh - curvature)
    energy = 0.5 * (rayleigh + curvature) - jnp.sqrt(half_gap * half_gap + coupling * coupling)
    coeff_new = energy - rayleigh
    coeff_norm = jnp.sqrt(coupling * coupling + coeff_new * coeff_new + epsilon)
    old = coupling / coeff_norm
    new = coeff_new / (coeff_norm * res_scale)
    ritz_ref[...] = old[None] * vector_ref[...] + new[None] * residual_ref[...]
    energy_ref[0] = energy[0, 0]


def shards(wave_guess, left_env, right_env, site_ops, bond_rank):
    guess = wave_guess[0]
    left = left_env[0]
    site = site_ops[0]
    rows, states, width = guess.shape
    terms = left.shape[0]
    members = lax.axis_size("term")
    chips = members // CORES
    segments = lax.axis_size("seg")
    scale = 1.0 / float(rows * members * states * width)
    hops = tuple(range(chips))

    def to_sibling(block):
        return lax.ppermute(block, "term", [(i, i ^ 1) for i in range(members)])

    def to_next_chip(block):
        return lax.ppermute(block, "term", [(i, (i + CORES) % members) for i in range(members)])

    def around(block):
        found = [block]
        for _ in range(chips - 1):
            found.append(to_next_chip(found[-1]))
        return found

    def everyone(block):
        others = [
            lax.ppermute(block, "term", [(i, i ^ bits) for i in range(members)]) for bits in range(1, members)
        ]
        return [block] + others

    tile = jax.ShapeDtypeStruct((8, width), F32)
    x_own, norm_part = pl.pallas_call(
        prepare_kernel,
        out_shape=(jax.ShapeDtypeStruct((states, rows, width), BF16), tile),
        in_specs=[smem, vmem],
        out_specs=(vmem, vmem),
        compiler_params=params(),
        cost_estimate=cost(4 * guess.size, 6 * guess.size),
        name="prepare",
    )(bond_rank, guess)

    shift = [(i + 1, i) for i in range(segments - 1)]
    received = lax.ppermute(right_env, "seg", shift)
    right = jnp.where(lax.axis_index("seg") == segments - 1, right_env, received)[0]

    x_hops = around(x_own)
    pieces = []
    for block in x_hops:
        pieces += [block, to_sibling(block)]
    bundle_rows = 2 * (width + TILE) + states + TILE
    bundle = pl.pallas_call(
        pack_kernel,
        out_shape=jax.ShapeDtypeStruct((terms, bundle_rows, width // 2), BF16),
        in_specs=[vmem] * 4,
        out_specs=vmem,
        compiler_params=params(),
        cost_estimate=cost(8 * left.size, 6 * left.size),
        name="pack",
    )(left, right, site, norm_part)
    bundles = around(bundle)

    whole = (states, width, width)
    rotated = (terms, states, width, width)
    scratch = [
        pltpu.VMEM(rotated, BF16),
        pltpu.VMEM((states, width, terms * width), BF16),
        pltpu.VMEM((terms * states * TILE, states * TILE), BF16),
    ]
    square = pltpu.VMEM((terms, width, width), BF16)
    apply_flops = 2 * terms * states * width * width * (2 * width + states * TILE)
    apply_cost = cost(apply_flops, 4 * states * width * width)
    whole_bf = jax.ShapeDtypeStruct(whole, BF16)
    vector, partial = pl.pallas_call(
        functools.partial(first_kernel, members, hops),
        out_shape=(whole_bf, whole_bf),
        in_specs=[anywhere] * members + [vmem] * 3,
        out_specs=(vmem, vmem),
        scratch_shapes=scratch + [pltpu.SemaphoreType.DMA((members,))],
        compiler_params=params(),
        cost_estimate=apply_cost,
        name="apply_own_terms",
    )(*pieces, left, right, site)
    stat = norm_part
    for hop in hops[1:]:
        partial, stat = pl.pallas_call(
            next_kernel,
            out_shape=(whole_bf, tile),
            in_specs=[vmem] * 4,
            out_specs=(vmem, vmem),
            scratch_shapes=scratch + [square, square],
            compiler_params=params(),
            cost_estimate=apply_cost,
            name="apply_received_terms",
        )(vector, partial, stat, bundles[hop])
    other = to_sibling(partial)
    stat_other = to_sibling(stat)

    share = pl.pallas_call(
        functools.partial(second_kernel, scale, members),
        out_shape=tile,
        in_specs=[smem] + [vmem] * 8,
        out_specs=vmem,
        scratch_shapes=[
            pltpu.VMEM(whole, BF16),
            pltpu.VMEM(rotated, BF16),
            pltpu.VMEM(rotated, BF16),
            pltpu.VMEM((terms * states * TILE, states * TILE), BF16),
        ],
        compiler_params=params(),
        cost_estimate=cost(apply_flops, 6 * states * width * width),
        name="apply_residual",
    )(bond_rank, stat, stat_other, partial, other, vector, left, right, site)
    shares = everyone(share)

    local = jax.ShapeDtypeStruct((rows, states, width), F32)
    vector_own, residual_own = pl.pallas_call(
        functools.partial(own_rows_kernel, scale),
        out_shape=(local, local),
        in_specs=[smem] + [vmem] * 5,
        out_specs=(vmem, vmem),
        compiler_params=params(),
        cost_estimate=cost(8 * guess.size, 16 * guess.size),
        name="own_rows",
    )(bond_rank, guess, stat, stat_other, partial, other)

    ritz, energy = pl.pallas_call(
        finish_kernel,
        out_shape=(local, jax.ShapeDtypeStruct((1,), F32)),
        in_specs=[vmem] * (2 + members),
        out_specs=(vmem, smem),
        compiler_params=params(),
        cost_estimate=cost(3 * guess.size, 12 * guess.size),
        name="finish",
    )(vector_own, residual_own, *shares)
    return (ritz[None], energy)


def solution(mesh):
    in_specs = (
        P("seg", "term", None, None),
        P("seg", "term", None, None),
        P("seg", "term", None, None),
        P("seg", "term", None, None),
        P("seg"),
    )
    out_specs = (P("seg", "term", None, None), P("seg"))
    return jax.shard_map(shards, mesh=mesh, in_specs=in_specs, out_specs=out_specs, check_vma=False)
```

```python
import functools

import jax
import jax.numpy as jnp
from jax import lax
from jax.experimental import pallas as pl
from jax.experimental.pallas import tpu as pltpu
from jax.sharding import PartitionSpec as P

epsilon = 1e-06
CORES = 2
TILE = 16
UNROLL = 4
GROUP = 4
VMEM_LIMIT = 28 * 1024 * 1024
F32 = jnp.float32
BF16 = jnp.bfloat16

vmem = pl.BlockSpec(memory_space=pltpu.VMEM)
smem = pl.BlockSpec(memory_space=pltpu.SMEM)
anywhere = pl.BlockSpec(memory_space=pl.ANY)


def params():
    return pltpu.CompilerParams(vmem_limit_bytes=VMEM_LIMIT)


def cost(flops, moved):
    return pl.CostEstimate(flops=int(flops) // 100, bytes_accessed=int(moved) // 100, transcendentals=0)


def keep_row(rank, width):
    return (lax.broadcasted_iota(jnp.int32, (1, width), 1) < rank).astype(F32)


def prepare_kernel(rank_ref, guess_ref, x_ref, norm_ref):
    rows, states, width = guess_ref.shape
    masked = guess_ref[...] * keep_row(rank_ref[0], width)[None]
    norm_ref[...] = jnp.full(norm_ref.shape, jnp.sum(masked * masked), F32)
    x_ref[...] = jnp.swapaxes(masked, 0, 1).astype(BF16)


def triangle(half):
    row = lax.broadcasted_iota(jnp.int32, (half, half), 0)
    col = lax.broadcasted_iota(jnp.int32, (half, half), 1)
    return row, col


def pack_symmetric(block_ref, k, out_ref, base):
    width = block_ref.shape[1]
    half = width // 2
    row, col = triangle(half)
    upper = block_ref[k, 0:half, 0:half].astype(F32)
    lower = block_ref[k, half:width, half:width].astype(F32)
    out_ref[k, base : base + half, :] = block_ref[k, 0:half, half:width]
    out_ref[k, base + half : base + width, :] = jnp.where(row <= col, upper, lower).astype(BF16)
    return jnp.sum(jnp.where(row == col, lower, 0.0), axis=0, keepdims=True)


def pack_kernel(block_ref, packed_ref):
    terms, width, _ = block_ref.shape
    for k in range(terms):
        diagonal = pack_symmetric(block_ref, k, packed_ref, 0)
        packed_ref[k, width : width + TILE, :] = jnp.broadcast_to(diagonal, (TILE, width // 2)).astype(BF16)


def unpack_symmetric(packed_ref, k, base, diagonal, full_ref):
    width = full_ref.shape[1]
    half = width // 2
    row, col = triangle(half)
    corner = packed_ref[k, base : base + half, :]
    mixed = packed_ref[k, base + half : base + width, :].astype(F32)
    turned = mixed.T
    full_ref[k, 0:half, 0:half] = jnp.where(row <= col, mixed, turned).astype(BF16)
    full_ref[k, 0:half, half:width] = corner
    full_ref[k, half:width, 0:half] = corner.astype(F32).T.astype(BF16)
    full_ref[k, half:width, half:width] = jnp.where(
        row > col, mixed, jnp.where(row == col, diagonal, turned)
    ).astype(BF16)


def header_kernel(site_ref, norm_ref, header_ref):
    terms, states, _ = site_ref.shape
    half = header_ref.shape[2]
    widen = (
        lax.broadcasted_iota(jnp.int32, (states, half), 0) == lax.broadcasted_iota(jnp.int32, (states, half), 1)
    ).astype(BF16)
    norm = norm_ref[0:1, 0:half]
    parts = []
    for _ in range(3):
        parts.append(norm.astype(BF16).astype(F32))
        norm = norm - parts[-1]
    lines = lax.broadcasted_iota(jnp.int32, (TILE, half), 0)
    lines = functools.reduce(jnp.add, [jnp.where(lines == n, parts[n], 0.0) for n in range(3)]).astype(BF16)
    for k in range(terms):
        header_ref[k, 0:states, :] = jnp.dot(site_ref[k], widen, preferred_element_type=F32).astype(BF16)
        header_ref[k, states : states + TILE, :] = lines


def spread_kernel(header_ref, kron_ref):
    terms = header_ref.shape[0]
    lanes = header_ref.shape[2]
    size = kron_ref.shape[1]
    states = size // TILE
    row_state = lax.broadcasted_iota(jnp.int32, (size, states), 0) // TILE
    pick = (row_state == lax.broadcasted_iota(jnp.int32, (size, states), 1)).astype(BF16)
    col_state = lax.broadcasted_iota(jnp.int32, (lanes, size), 1) // TILE
    pick_t = (col_state == lax.broadcasted_iota(jnp.int32, (lanes, size), 0)).astype(BF16)
    same = (
        lax.broadcasted_iota(jnp.int32, (size, size), 0) % TILE
        == lax.broadcasted_iota(jnp.int32, (size, size), 1) % TILE
    )
    for k in range(terms):
        tall = jnp.dot(pick, header_ref[k, 0:states, :], preferred_element_type=F32).astype(BF16)
        full = jnp.dot(tall, pick_t, preferred_element_type=F32)
        kron_ref[k * size : (k + 1) * size, :] = jnp.where(same, full, 0.0).astype(BF16)


def mix_sites(source_ref, kron_ref, rotated_ref, base, unroll):
    terms, states, _, width = rotated_ref.shape
    rows = source_ref.shape[1]

    def step(i, carry):
        at = pl.multiple_of(i * TILE, TILE)
        to = pl.multiple_of(base + i * TILE, TILE)
        stack = source_ref[:, pl.ds(at, TILE), :].reshape(states * TILE, width)
        turned = jnp.dot(kron_ref[...], stack, preferred_element_type=F32).astype(BF16)
        rotated_ref[:, :, pl.ds(to, TILE), :] = turned.reshape(terms, states, TILE, width)
        return carry

    lax.fori_loop(0, rows // TILE, step, 0, unroll=min(unroll, rows // TILE))


def fold(values, width):
    return jnp.sum(values.reshape(values.size // (8 * width), 8, width), axis=0)


def summed(values):
    while len(values) > 1:
        values = [values[n] + values[n + 1] for n in range(0, len(values), 2)]
    return values[0]


def chip_kernel(hop, chips, *refs):
    own_ref, sib_ref, left_ref, packed_ref, kron_ref = refs[:5]
    if hop == 0:
        before_ref = None
        out_ref, bundle_ref = refs[5:7]
        rest = refs[7:]
    else:
        before_ref, out_ref = refs[5:7]
        rest = refs[7:]
    rotated_ref, turned_ref, columns_ref, right_ref = rest
    terms, states, chip_rows, width = rotated_ref.shape
    rows = own_ref.shape[1]
    me = lax.axis_index("term")
    core = me % CORES
    chip = (me // CORES - hop + chips) % chips
    mix_sites(own_ref, kron_ref, rotated_ref, core * rows, UNROLL)
    mix_sites(sib_ref, kron_ref, rotated_ref, (1 - core) * rows, UNROLL)
    at = pl.multiple_of(chip * chip_rows, TILE)
    for k in range(terms):
        diagonal = packed_ref[k, width : width + TILE, :].astype(F32)[0:1]
        unpack_symmetric(packed_ref, k, 0, diagonal, right_ref)
    columns = jnp.concatenate([left_ref[k, pl.ds(at, chip_rows), :] for k in range(terms)], axis=0)
    columns_ref[...] = columns.astype(F32).T.astype(BF16)
    if hop == 0:
        line = lax.broadcasted_iota(jnp.int32, (TILE, width // 2), 0)
        for k in range(terms):
            first = packed_ref[k, width : width + TILE, :].astype(F32)
            second = pack_symmetric(left_ref, k, bundle_ref, width + TILE)
            bundle_ref[k, 0:width, :] = packed_ref[k, 0:width, :]
            bundle_ref[k, width : width + TILE, :] = jnp.where(line == 0, first, second).astype(BF16)
    for k in range(terms):
        for n in range(0, states, 8):
            source = rotated_ref[k, n : n + 8].reshape(8 * chip_rows, width)
            turned = jnp.dot(source, right_ref[k], preferred_element_type=F32).astype(BF16)
            turned_ref[n : n + 8, k * chip_rows : (k + 1) * chip_rows, :] = turned.reshape(8, chip_rows, width)

    def lefts(p, carry):
        image = jnp.dot(columns_ref[...], turned_ref[p], preferred_element_type=F32)
        if before_ref is not None:
            image = before_ref[p] + image
        out_ref[p] = image
        return carry

    lax.fori_loop(0, states, lefts, 0, unroll=UNROLL)


def rotate_kernel(piece_count, hops, *refs):
    pieces = refs[:piece_count]
    kron_ref, rotated_ref, whole_ref, sems = refs[piece_count:]
    chips = len(hops)
    me = lax.axis_index("term")
    core = me % CORES
    chip = me // CORES
    copies = []
    for n, piece in enumerate(pieces):
        rows = piece.shape[1]
        owner = ((chip - hops[n // 2] + chips) % chips) * CORES + (core if n % 2 == 0 else 1 - core)
        at = pl.multiple_of(owner * rows, TILE)
        copies.append(pltpu.make_async_copy(piece, whole_ref.at[:, pl.ds(at, rows), :], sems.at[n]))
        copies[-1].start()
    for n, piece in enumerate(pieces):
        rows = piece.shape[1]
        owner = ((chip - hops[n // 2] + chips) % chips) * CORES + (core if n % 2 == 0 else 1 - core)
        mix_sites(piece, kron_ref, rotated_ref, owner * rows, UNROLL)
    for copy in copies:
        copy.wait()


def next_kernel(
    whole_ref,
    rotated_ref,
    before_ref,
    stat_before_ref,
    header_ref,
    bundle_ref,
    partial_ref,
    stat_ref,
    mixed_ref,
    left_ref,
    right_ref,
):
    terms, states, width, _ = rotated_ref.shape
    for k in range(terms):
        diagonals = bundle_ref[k, width : width + TILE, :].astype(F32)
        unpack_symmetric(bundle_ref, k, width + TILE, diagonals[1:2], left_ref)
        unpack_symmetric(bundle_ref, k, 0, diagonals[0:1], right_ref)

    def lefts(p, carry):
        for k in range(terms):
            mixed = jnp.dot(left_ref[k], rotated_ref[k, p], preferred_element_type=F32)
            mixed_ref[p, :, k * width : (k + 1) * width] = mixed.astype(BF16)
        return carry

    lax.fori_loop(0, states, lefts, 0, unroll=UNROLL)

    def rights(n, total):
        at = n * GROUP
        rows = mixed_ref[pl.ds(at, GROUP)].reshape(GROUP * width, terms * width)
        stacked = right_ref[...].reshape(terms * width, width)
        image = jnp.dot(rows, stacked, preferred_element_type=F32).reshape(GROUP, width, width)
        part = (before_ref[pl.ds(at, GROUP)].astype(F32) + image).astype(partial_ref.dtype)
        partial_ref[pl.ds(at, GROUP)] = part
        held = whole_ref[pl.ds(at, GROUP)].astype(F32)
        return total + fold(held * part.astype(F32), width)

    total = lax.fori_loop(0, states // GROUP, rights, jnp.zeros((8, width), F32))
    lines = header_ref[0, states : states + TILE, :].astype(F32)
    norm = lines[0:1] + lines[1:2] + lines[2:3]
    stat_ref[0:1, :] = jnp.full((1, width), jnp.sum(total), F32)
    stat_ref[1:2, :] = stat_before_ref[1:2, :] + jnp.concatenate([norm, norm], axis=1)
    stat_ref[2:8, :] = jnp.zeros((6, width), F32)


def scales(rank_ref, mine_ref, theirs_ref, scale, width):
    inverse = lax.rsqrt((mine_ref[1:2, :] + theirs_ref[1:2, :]) * scale + epsilon)
    rayleigh = (mine_ref[0:1, :] + theirs_ref[0:1, :]) * (inverse * inverse * scale)
    return inverse, rayleigh, keep_row(rank_ref[0], width) * inverse


def second_kernel(
    scale,
    members,
    rank_ref,
    mine_ref,
    theirs_ref,
    partial_ref,
    other_ref,
    whole_ref,
    left_ref,
    packed_ref,
    kron_ref,
    out_ref,
    res_ref,
    rotated_ref,
    mixed_ref,
    right_ref,
):
    terms, states, width, _ = rotated_ref.shape
    for k in range(terms):
        diagonal = packed_ref[k, width : width + TILE, :].astype(F32)[0:1]
        unpack_symmetric(packed_ref, k, 0, diagonal, right_ref)
    inverse, rayleigh, row_scale = scales(rank_ref, mine_ref, theirs_ref, scale, width)
    back = rayleigh * inverse

    def lefts(p, total):
        sigma = (partial_ref[p].astype(F32) + other_ref[p].astype(F32)) * row_scale
        residual = sigma - back * whole_ref[p].astype(F32)
        rounded = residual.astype(BF16)
        res_ref[p] = rounded
        mixed = jnp.dot(
            left_ref[...].reshape(terms * width, width), rounded, preferred_element_type=F32
        ).astype(BF16)
        for k in range(terms):
            mixed_ref[k, p] = mixed[k * width : (k + 1) * width]
        return total + fold(residual * residual, width)

    square = lax.fori_loop(0, states, lefts, jnp.zeros((8, width), F32), unroll=UNROLL)
    mix_sites(res_ref, kron_ref, rotated_ref, 0, 2 * UNROLL)

    def rights(n, total):
        at = n * GROUP
        for k in range(terms):
            turned = rotated_ref[k, pl.ds(at, GROUP)].reshape(GROUP * width, width)
            image = jnp.dot(turned, right_ref[k], preferred_element_type=F32)
            held = mixed_ref[k, pl.ds(at, GROUP)].reshape(GROUP * width, width).astype(F32)
            total = total + fold(held * image, width)
        return total

    cross = lax.fori_loop(0, states // GROUP, rights, jnp.zeros((8, width), F32))
    share = 1.0 / members
    out_ref[0:1, :] = rayleigh * share
    out_ref[1:2, :] = jnp.full((1, width), jnp.sum(square) * (scale * share), F32)
    out_ref[2:3, :] = jnp.full((1, width), jnp.sum(cross) * scale, F32)
    out_ref[3:8, :] = jnp.zeros((5, width), F32)


def own_rows_kernel(
    scale, rank_ref, guess_ref, mine_ref, theirs_ref, partial_ref, other_ref, vector_ref, residual_ref
):
    rows, states, width = guess_ref.shape
    inverse, rayleigh, row_scale = scales(rank_ref, mine_ref, theirs_ref, scale, width)
    own = pl.ds(pl.multiple_of(lax.axis_index("term") * rows, TILE), rows)
    sigma = (partial_ref[:, own, :].astype(F32) + other_ref[:, own, :].astype(F32)) * row_scale[None]
    vector = guess_ref[...] * row_scale[None]
    vector_ref[...] = vector
    residual_ref[...] = jnp.swapaxes(sigma, 0, 1) - rayleigh[None] * vector


def finish_kernel(vector_ref, residual_ref, *refs):
    shares = refs[:-2]
    ritz_ref, energy_ref = refs[-2:]
    stat = summed([share[...] for share in shares])
    rayleigh = stat[0:1, :]
    res_sq = stat[1:2, :]
    res_var = res_sq + epsilon
    curvature = stat[2:3, :] / res_var
    res_scale = jnp.sqrt(res_var)
    coupling = res_sq / res_scale
    half_gap = 0.5 * (rayleigh - curvature)
    energy = 0.5 * (rayleigh + curvature) - jnp.sqrt(half_gap * half_gap + coupling * coupling)
    coeff_new = energy - rayleigh
    coeff_norm = jnp.sqrt(coupling * coupling + coeff_new * coeff_new + epsilon)
    old = coupling / coeff_norm
    new = coeff_new / (coeff_norm * res_scale)
    ritz_ref[...] = old[None] * vector_ref[...] + new[None] * residual_ref[...]
    energy_ref[0] = energy[0, 0]


def shards(wave_guess, left_env, right_env, site_ops, bond_rank):
    guess = wave_guess[0]
    left = left_env[0]
    site = site_ops[0]
    rows, states, width = guess.shape
    terms = left.shape[0]
    members = lax.axis_size("term")
    chips = members // CORES
    segments = lax.axis_size("seg")
    scale = 1.0 / float(rows * members * states * width)
    hops = tuple(range(chips))

    def to_sibling(block):
        return lax.ppermute(block, "term", [(i, i ^ 1) for i in range(members)])

    def to_next_chip(block):
        return lax.ppermute(block, "term", [(i, (i + CORES) % members) for i in range(members)])

    def around(block):
        found = [block]
        for _ in range(chips - 1):
            found.append(to_next_chip(found[-1]))
        return found

    def everyone(block):
        others = [
            lax.ppermute(block, "term", [(i, i ^ bits) for i in range(members)]) for bits in range(1, members)
        ]
        return [block] + others

    tile = jax.ShapeDtypeStruct((8, width), F32)
    x_own, norm_part = pl.pallas_call(
        prepare_kernel,
        out_shape=(jax.ShapeDtypeStruct((states, rows, width), BF16), tile),
        in_specs=[smem, vmem],
        out_specs=(vmem, vmem),
        compiler_params=params(),
        cost_estimate=cost(4 * guess.size, 6 * guess.size),
        name="prepare",
    )(bond_rank, guess)

    packed_own = pl.pallas_call(
        pack_kernel,
        out_shape=jax.ShapeDtypeStruct((terms, width + TILE, width // 2), BF16),
        in_specs=[vmem],
        out_specs=vmem,
        compiler_params=params(),
        cost_estimate=cost(4 * left.size, 3 * left.size),
        name="pack_right",
    )(right_env[0])
    shift = [(i + 1, i) for i in range(segments - 1)]
    received = lax.ppermute(packed_own, "seg", shift)
    packed = jnp.where(lax.axis_index("seg") == segments - 1, packed_own, received)

    x_hops = around(x_own)
    pieces = [x_own, to_sibling(x_own)]

    headers = around(
        pl.pallas_call(
            header_kernel,
            out_shape=jax.ShapeDtypeStruct((terms, states + TILE, width // 2), BF16),
            in_specs=[vmem] * 2,
            out_specs=vmem,
            compiler_params=params(),
            cost_estimate=cost(2 * site.size * width, 4 * site.size),
            name="header",
        )(site, norm_part)
    )
    size = states * TILE
    krons = [
        pl.pallas_call(
            spread_kernel,
            out_shape=jax.ShapeDtypeStruct((terms * size, size), BF16),
            in_specs=[vmem],
            out_specs=vmem,
            compiler_params=params(),
            cost_estimate=cost(2 * terms * size * size * width, 2 * terms * size * size),
            name="spread_site",
        )(header)
        for header in headers
    ]

    left, krons = lax.optimization_barrier((left, krons))

    whole = (states, width, width)
    whole_bf = jax.ShapeDtypeStruct(whole, BF16)
    whole_f32 = jax.ShapeDtypeStruct(whole, F32)
    rotated = (terms, states, width, width)
    square = pltpu.VMEM((terms, width, width), BF16)
    chip_rows = CORES * rows
    stage_flops = 2 * terms * states * width * width * width
    partial = None
    for hop in hops:
        outs = [whole_f32]
        if hop == 0:
            outs.append(jax.ShapeDtypeStruct((terms, 2 * width + TILE, width // 2), BF16))
        result = pl.pallas_call(
            functools.partial(chip_kernel, hop, chips),
            out_shape=tuple(outs),
            in_specs=[vmem] * (5 if hop == 0 else 6),
            out_specs=tuple([vmem] * len(outs)),
            scratch_shapes=[
                pltpu.VMEM((terms, states, chip_rows, width), BF16),
                pltpu.VMEM((states, terms * chip_rows, width), BF16),
                pltpu.VMEM((width, terms * chip_rows), BF16),
                square,
            ],
            compiler_params=params(),
            cost_estimate=cost(3 * stage_flops * chip_rows / width, 8 * states * width * width),
            name="apply_rows_here" if hop == 0 else "apply_rows_there",
        )(*pieces[2 * hop : 2 * hop + 2], left, packed, krons[0], *([] if hop == 0 else [partial]))
        partial = result[0]
        if hop == 0:
            bundles = around(result[1])
            for block in x_hops[1:]:
                block = lax.optimization_barrier((block, result[1]))[0]
                pieces += [block, to_sibling(block)]
    stat = norm_part
    for hop in hops[1:]:
        turned, vector = pl.pallas_call(
            functools.partial(rotate_kernel, members, hops),
            out_shape=(jax.ShapeDtypeStruct(rotated, BF16), whole_bf),
            in_specs=[vmem] * (members + 1),
            out_specs=(vmem, vmem),
            scratch_shapes=[pltpu.SemaphoreType.DMA((members,))],
            compiler_params=params(),
            cost_estimate=cost(stage_flops, 8 * states * width * width),
            name="rotate_received",
        )(*pieces, krons[hop])
        partial, stat = pl.pallas_call(
            next_kernel,
            out_shape=(whole_bf if hop == hops[-1] else whole_f32, tile),
            in_specs=[vmem] * 6,
            out_specs=(vmem, vmem),
            scratch_shapes=[pltpu.VMEM((states, width, terms * width), BF16), square, square],
            compiler_params=params(),
            cost_estimate=cost(2 * stage_flops, 12 * states * width * width),
            name="apply_received_terms",
        )(vector, turned, partial, stat, headers[hop], bundles[hop])
    other = to_sibling(partial)
    stat_other = to_sibling(stat)

    share = pl.pallas_call(
        functools.partial(second_kernel, scale, members),
        out_shape=tile,
        in_specs=[smem] + [vmem] * 8,
        out_specs=vmem,
        scratch_shapes=[
            pltpu.VMEM(whole, BF16),
            pltpu.VMEM(rotated, BF16),
            pltpu.VMEM(rotated, BF16),
            square,
        ],
        compiler_params=params(),
        cost_estimate=cost(3 * stage_flops, 6 * states * width * width),
        name="apply_residual",
    )(bond_rank, stat, stat_other, partial, other, vector, left, packed, krons[0])
    shares = everyone(share)

    local = jax.ShapeDtypeStruct((rows, states, width), F32)
    vector_own, residual_own = pl.pallas_call(
        functools.partial(own_rows_kernel, scale),
        out_shape=(local, local),
        in_specs=[smem] + [vmem] * 5,
        out_specs=(vmem, vmem),
        compiler_params=params(),
        cost_estimate=cost(8 * guess.size, 16 * guess.size),
        name="own_rows",
    )(bond_rank, guess, stat, stat_other, partial, other)

    ritz, energy = pl.pallas_call(
        finish_kernel,
        out_shape=(local, jax.ShapeDtypeStruct((1,), F32)),
        in_specs=[vmem] * (2 + members),
        out_specs=(vmem, smem),
        compiler_params=params(),
        cost_estimate=cost(3 * guess.size, 12 * guess.size),
        name="finish",
    )(vector_own, residual_own, *shares)
    return (ritz[None], energy)


def solution(mesh):
    in_specs = (
        P("seg", "term", None, None),
        P("seg", "term", None, None),
        P("seg", "term", None, None),
        P("seg", "term", None, None),
        P("seg"),
    )
    out_specs = (P("seg", "term", None, None), P("seg"))
    return jax.shard_map(shards, mesh=mesh, in_specs=in_specs, out_specs=out_specs, check_vma=False)
```

```python
import functools

import jax
import jax.numpy as jnp
from jax import lax
from jax.experimental import pallas as pl
from jax.experimental.pallas import tpu as pltpu
from jax.sharding import PartitionSpec as P

epsilon = 1e-06
CORES = 2
TILE = 16
UNROLL = 4
GROUP = 4
VMEM_LIMIT = 20 * 1024 * 1024
F32 = jnp.float32
BF16 = jnp.bfloat16

vmem = pl.BlockSpec(memory_space=pltpu.VMEM)
smem = pl.BlockSpec(memory_space=pltpu.SMEM)
anywhere = pl.BlockSpec(memory_space=pl.ANY)
in_hbm = pl.BlockSpec(memory_space=pltpu.HBM)


def params():
    return pltpu.CompilerParams(vmem_limit_bytes=VMEM_LIMIT)


def cost(flops, moved):
    return pl.CostEstimate(flops=int(flops) // 100, bytes_accessed=int(moved) // 100, transcendentals=0)


def keep_row(rank, width):
    return (lax.broadcasted_iota(jnp.int32, (1, width), 1) < rank).astype(F32)


def prepare_kernel(
    rank_ref,
    guess_in,
    left_in,
    right_in,
    site_in,
    x_ref,
    norm_ref,
    left_packed_ref,
    right_packed_ref,
    left_ref,
    guess_ref,
    right_ref,
    site_ref,
    sems,
):
    rows, states, width = guess_ref.shape
    terms = left_ref.shape[0]
    half = width // 2
    sources = (guess_in, site_in, right_in, left_in)
    targets = (guess_ref, site_ref, right_ref, left_ref)
    copies = [pltpu.make_async_copy(sources[n], targets[n], sems.at[n]) for n in range(4)]
    for copy in copies:
        copy.start()
    copies[0].wait()
    masked = guess_ref[...] * keep_row(rank_ref[0], width)[None]
    total = jnp.sum(masked * masked)
    norm_ref[...] = jnp.full(norm_ref.shape, total, F32)
    x_ref[0:states] = jnp.swapaxes(masked, 0, 1).astype(BF16)
    copies[1].wait()
    widen = (
        lax.broadcasted_iota(jnp.int32, (states, width), 0) == lax.broadcasted_iota(jnp.int32, (states, width), 1)
    ).astype(BF16)
    norm = jnp.full((1, width), total, F32)
    parts = []
    for _ in range(3):
        parts.append(norm.astype(BF16).astype(F32))
        norm = norm - parts[-1]
    lines = lax.broadcasted_iota(jnp.int32, (TILE, width), 0)
    lines = functools.reduce(jnp.add, [jnp.where(lines == n, parts[n], 0.0) for n in range(3)]).astype(BF16)
    for k in range(terms + 1):
        slab, row = divmod(k * TILE, rows)
        sites = lines if k == terms else jnp.dot(site_ref[k], widen, preferred_element_type=F32).astype(BF16)
        x_ref[states + slab, row : row + TILE, :] = sites
    for copy, block_ref, packed_ref in zip(copies[2:], (right_ref, left_ref), (right_packed_ref, left_packed_ref)):
        copy.wait()
        for k in range(terms):
            diagonal = pack_symmetric(block_ref, k, packed_ref)
            packed_ref[k, width : width + TILE, :] = jnp.broadcast_to(diagonal, (TILE, half)).astype(BF16)


def triangle(half):
    row = lax.broadcasted_iota(jnp.int32, (half, half), 0)
    col = lax.broadcasted_iota(jnp.int32, (half, half), 1)
    return row, col


def pack_symmetric(block_ref, k, out_ref):
    width = block_ref.shape[1]
    half = width // 2
    row, col = triangle(half)
    upper = block_ref[k, 0:half, 0:half].astype(F32)
    lower = block_ref[k, half:width, half:width].astype(F32)
    out_ref[k, 0:half, :] = block_ref[k, 0:half, half:width]
    out_ref[k, half:width, :] = jnp.where(row <= col, upper, lower).astype(BF16)
    return jnp.sum(jnp.where(row == col, lower, 0.0), axis=0, keepdims=True)


def unpack_symmetric(packed_ref, full_ref):
    terms, width, _ = full_ref.shape
    half = width // 2
    row, col = triangle(half)
    for k in range(terms):
        corner = packed_ref[k, 0:half, :]
        mixed = packed_ref[k, half:width, :].astype(F32)
        diagonal = packed_ref[k, width : width + TILE, :].astype(F32)[0:1]
        turned = mixed.T
        full_ref[k, 0:half, 0:half] = jnp.where(row <= col, mixed, turned).astype(BF16)
        full_ref[k, 0:half, half:width] = corner
        full_ref[k, half:width, 0:half] = corner.astype(F32).T.astype(BF16)
        full_ref[k, half:width, half:width] = jnp.where(
            row > col, mixed, jnp.where(row == col, diagonal, turned)
        ).astype(BF16)


def spread_kernel(x_ref, kron_ref, norm_ref):
    rows, lanes = x_ref.shape[1:]
    size = kron_ref.shape[1]
    terms = kron_ref.shape[0] // size
    states = size // TILE
    row_state = lax.broadcasted_iota(jnp.int32, (size, states), 0) // TILE
    pick = (row_state == lax.broadcasted_iota(jnp.int32, (size, states), 1)).astype(BF16)
    col_state = lax.broadcasted_iota(jnp.int32, (lanes, size), 1) // TILE
    pick_t = (col_state == lax.broadcasted_iota(jnp.int32, (lanes, size), 0)).astype(BF16)
    same = (
        lax.broadcasted_iota(jnp.int32, (size, size), 0) % TILE
        == lax.broadcasted_iota(jnp.int32, (size, size), 1) % TILE
    )
    for k in range(terms + 1):
        slab, row = divmod(k * TILE, rows)
        sites = x_ref[states + slab, row : row + TILE, :]
        if k == terms:
            lines = sites.astype(F32)
            norm_ref[...] = jnp.broadcast_to(lines[0:1] + lines[1:2] + lines[2:3], norm_ref.shape)
            break
        tall = jnp.dot(pick, sites, preferred_element_type=F32).astype(BF16)
        full = jnp.dot(tall, pick_t, preferred_element_type=F32)
        kron_ref[k * size : (k + 1) * size, :] = jnp.where(same, full, 0.0).astype(BF16)


def mix_sites(source_ref, kron_ref, rotated_ref, base, unroll):
    terms, states, _, width = rotated_ref.shape
    rows = source_ref.shape[1]

    def step(i, carry):
        at = pl.multiple_of(i * TILE, TILE)
        to = pl.multiple_of(base + i * TILE, TILE)
        stack = source_ref[0:states, pl.ds(at, TILE), :].reshape(states * TILE, width)
        turned = jnp.dot(kron_ref[...], stack, preferred_element_type=F32).astype(BF16)
        rotated_ref[:, :, pl.ds(to, TILE), :] = turned.reshape(terms, states, TILE, width)
        return carry

    lax.fori_loop(0, rows // TILE, step, 0, unroll=min(unroll, rows // TILE))


def fold(values, width):
    return jnp.sum(values.reshape(values.size // (8 * width), 8, width), axis=0)


def summed(values):
    while len(values) > 1:
        values = [values[n] + values[n + 1] for n in range(0, len(values), 2)]
    return values[0]


def place(hop, chips):
    me = lax.axis_index("term")
    chip = (me // CORES - hop + chips) % chips
    return chip, me % CORES


def chip_kernel(hop, chips, own_ref, sib_ref, left_ref, packed_ref, kron_ref, *refs):
    before_ref = None if hop == 0 else refs[0]
    out_ref, rotated_ref, turned_ref, columns_ref, right_ref = refs[-5:]
    terms, states, chip_rows, width = rotated_ref.shape
    rows = own_ref.shape[1]
    chip, core = place(hop, chips)
    mix_sites(own_ref, kron_ref, rotated_ref, core * rows, UNROLL)
    mix_sites(sib_ref, kron_ref, rotated_ref, (1 - core) * rows, UNROLL)
    at = pl.multiple_of(chip * chip_rows, TILE)
    unpack_symmetric(packed_ref, right_ref)
    columns = jnp.concatenate([left_ref[k, pl.ds(at, chip_rows), :] for k in range(terms)], axis=0)
    columns_ref[...] = columns.astype(F32).T.astype(BF16)
    for k in range(terms):
        for n in range(0, states, 8):
            source = rotated_ref[k, n : n + 8].reshape(8 * chip_rows, width)
            turned = jnp.dot(source, right_ref[k], preferred_element_type=F32).astype(BF16)
            turned_ref[n : n + 8, k * chip_rows : (k + 1) * chip_rows, :] = turned.reshape(8, chip_rows, width)

    def lefts(p, carry):
        image = jnp.dot(columns_ref[...], turned_ref[p], preferred_element_type=F32)
        if before_ref is not None:
            image = before_ref[p] + image
        out_ref[p] = image
        return carry

    lax.fori_loop(0, states, lefts, 0, unroll=UNROLL)


def rotate_kernel(hops, chips, *refs):
    pieces = refs[: CORES * len(hops)]
    kron_ref = refs[len(pieces)]
    rotated_ref, whole_ref, sems = refs[-3:]
    rows = pieces[0].shape[1]
    copies = []
    for n, piece in enumerate(pieces):
        chip, core = place(hops[n // 2], chips)
        at = (chip * CORES + (core if n % 2 == 0 else 1 - core)) * rows
        copies.append(
            pltpu.make_async_copy(
                piece.at[0 : whole_ref.shape[0]],
                whole_ref.at[:, pl.ds(pl.multiple_of(at, TILE), rows), :],
                sems.at[n],
            )
        )
        copies[-1].start()
    for n, piece in enumerate(pieces):
        chip, core = place(hops[n // 2], chips)
        at = (chip * CORES + (core if n % 2 == 0 else 1 - core)) * rows
        mix_sites(piece, kron_ref, rotated_ref, at, UNROLL)
    for copy in copies:
        copy.wait()


def lefts_kernel(rotated_ref, packed_ref, mixed_ref, left_ref):
    terms, states, width, _ = rotated_ref.shape
    unpack_symmetric(packed_ref, left_ref)

    def lefts(p, carry):
        for k in range(terms):
            mixed = jnp.dot(left_ref[k], rotated_ref[k, p], preferred_element_type=F32)
            mixed_ref[p, :, k * width : (k + 1) * width] = mixed.astype(BF16)
        return carry

    lax.fori_loop(0, states, lefts, 0, unroll=UNROLL)


def rights_kernel(
    mixed_ref, packed_ref, whole_ref, before_ref, stat_before_ref, norm_ref, partial_ref, stat_ref, right_ref
):
    states, width, _ = whole_ref.shape
    terms = right_ref.shape[0]
    unpack_symmetric(packed_ref, right_ref)

    def rights(n, total):
        at = n * GROUP
        rows = mixed_ref[pl.ds(at, GROUP)].reshape(GROUP * width, terms * width)
        stacked = right_ref[...].reshape(terms * width, width)
        image = jnp.dot(rows, stacked, preferred_element_type=F32).reshape(GROUP, width, width)
        part = (before_ref[pl.ds(at, GROUP)].astype(F32) + image).astype(partial_ref.dtype)
        partial_ref[pl.ds(at, GROUP)] = part
        held = whole_ref[pl.ds(at, GROUP)].astype(F32)
        return total + fold(held * part.astype(F32), width)

    total = lax.fori_loop(0, states // GROUP, rights, jnp.zeros((8, width), F32))
    stat_ref[0:1, :] = jnp.full((1, width), jnp.sum(total), F32)
    stat_ref[1:2, :] = stat_before_ref[1:2, :] + norm_ref[1:2, :]
    stat_ref[2:8, :] = jnp.zeros((6, width), F32)


def scales(rank_ref, mine_ref, theirs_ref, scale, width):
    inverse = lax.rsqrt((mine_ref[1:2, :] + theirs_ref[1:2, :]) * scale + epsilon)
    rayleigh = (mine_ref[0:1, :] + theirs_ref[0:1, :]) * (inverse * inverse * scale)
    return inverse, rayleigh, keep_row(rank_ref[0], width) * inverse


def second_kernel(
    scale,
    members,
    rank_ref,
    mine_ref,
    theirs_ref,
    partial_ref,
    other_ref,
    whole_ref,
    left_ref,
    packed_ref,
    kron_ref,
    out_ref,
    res_ref,
    rotated_ref,
    mixed_ref,
    right_ref,
):
    terms, states, width, _ = rotated_ref.shape
    unpack_symmetric(packed_ref, right_ref)
    inverse, rayleigh, row_scale = scales(rank_ref, mine_ref, theirs_ref, scale, width)
    back = rayleigh * inverse

    def lefts(p, total):
        sigma = (partial_ref[p].astype(F32) + other_ref[p].astype(F32)) * row_scale
        residual = sigma - back * whole_ref[p].astype(F32)
        rounded = residual.astype(BF16)
        res_ref[p] = rounded
        mixed = jnp.dot(
            left_ref[...].reshape(terms * width, width), rounded, preferred_element_type=F32
        ).astype(BF16)
        for k in range(terms):
            mixed_ref[k, p] = mixed[k * width : (k + 1) * width]
        return total + fold(residual * residual, width)

    square = lax.fori_loop(0, states, lefts, jnp.zeros((8, width), F32), unroll=UNROLL)
    mix_sites(res_ref, kron_ref, rotated_ref, 0, 2 * UNROLL)

    def rights(n, total):
        at = n * GROUP
        for k in range(terms):
            turned = rotated_ref[k, pl.ds(at, GROUP)].reshape(GROUP * width, width)
            image = jnp.dot(turned, right_ref[k], preferred_element_type=F32)
            held = mixed_ref[k, pl.ds(at, GROUP)].reshape(GROUP * width, width).astype(F32)
            total = total + fold(held * image, width)
        return total

    cross = lax.fori_loop(0, states // GROUP, rights, jnp.zeros((8, width), F32))
    share = 1.0 / members
    out_ref[0:1, :] = rayleigh * share
    out_ref[1:2, :] = jnp.full((1, width), jnp.sum(square) * (scale * share), F32)
    out_ref[2:3, :] = jnp.full((1, width), jnp.sum(cross) * scale, F32)
    out_ref[3:8, :] = jnp.zeros((5, width), F32)


def own_rows_kernel(
    scale, rank_ref, guess_ref, mine_ref, theirs_ref, partial_ref, other_ref, vector_ref, residual_ref
):
    rows, states, width = guess_ref.shape
    inverse, rayleigh, row_scale = scales(rank_ref, mine_ref, theirs_ref, scale, width)
    own = pl.ds(pl.multiple_of(lax.axis_index("term") * rows, TILE), rows)
    sigma = (partial_ref[:, own, :].astype(F32) + other_ref[:, own, :].astype(F32)) * row_scale[None]
    vector = guess_ref[...] * row_scale[None]
    vector_ref[...] = vector
    residual_ref[...] = jnp.swapaxes(sigma, 0, 1) - rayleigh[None] * vector


def finish_kernel(vector_ref, residual_ref, *refs):
    shares = refs[:-2]
    ritz_ref, energy_ref = refs[-2:]
    stat = summed([share[...] for share in shares])
    rayleigh = stat[0:1, :]
    res_sq = stat[1:2, :]
    res_var = res_sq + epsilon
    curvature = stat[2:3, :] / res_var
    res_scale = jnp.sqrt(res_var)
    coupling = res_sq / res_scale
    half_gap = 0.5 * (rayleigh - curvature)
    energy = 0.5 * (rayleigh + curvature) - jnp.sqrt(half_gap * half_gap + coupling * coupling)
    coeff_new = energy - rayleigh
    coeff_norm = jnp.sqrt(coupling * coupling + coeff_new * coeff_new + epsilon)
    old = coupling / coeff_norm
    new = coeff_new / (coeff_norm * res_scale)
    ritz_ref[...] = old[None] * vector_ref[...] + new[None] * residual_ref[...]
    energy_ref[0] = energy[0, 0]


def shards(wave_guess, left_env, right_env, site_ops, bond_rank):
    guess = wave_guess[0]
    left = left_env[0]
    site = site_ops[0]
    rows, states, width = guess.shape
    terms = left.shape[0]
    members = lax.axis_size("term")
    chips = members // CORES
    segments = lax.axis_size("seg")
    scale = 1.0 / float(rows * members * states * width)
    hops = tuple(range(chips))

    def to_sibling(block):
        return lax.ppermute(block, "term", [(i, i ^ 1) for i in range(members)])

    def to_next_chip(block):
        return lax.ppermute(block, "term", [(i, (i + CORES) % members) for i in range(members)])

    def around(block):
        found = [block]
        for _ in range(chips - 1):
            found.append(to_next_chip(found[-1]))
        return found

    def everyone(block):
        others = [
            lax.ppermute(block, "term", [(i, i ^ bits) for i in range(members)]) for bits in range(1, members)
        ]
        return [block] + others

    tile = jax.ShapeDtypeStruct((8, width), F32)
    half = width // 2
    packed_shape = jax.ShapeDtypeStruct((terms, width + TILE, half), BF16)
    slabs = -(-(terms + 1) * TILE // rows)
    x_own, norm_part, left_packed, right_packed, left = pl.pallas_call(
        prepare_kernel,
        out_shape=(
            jax.ShapeDtypeStruct((states + slabs, rows, width), BF16),
            tile,
            packed_shape,
            packed_shape,
            jax.ShapeDtypeStruct(left.shape, BF16),
        ),
        in_specs=[smem] + [in_hbm] * 4,
        out_specs=(vmem,) * 5,
        scratch_shapes=[
            pltpu.VMEM(guess.shape, F32),
            pltpu.VMEM(left.shape, BF16),
            pltpu.VMEM(site.shape, BF16),
            pltpu.SemaphoreType.DMA((4,)),
        ],
        compiler_params=params(),
        cost_estimate=cost(4 * guess.size, 6 * guess.size),
        name="prepare",
    )(bond_rank, *[pltpu.with_memory_space_constraint(a, pltpu.HBM) for a in (guess, left, right_env[0], site)])

    x_hops = around(x_own)
    pieces = [x_own, to_sibling(x_own)]
    lefts = around(left_packed)
    shift = [(i + 1, i) for i in range(segments - 1)]
    received = lax.ppermute(right_packed, "seg", shift)
    packed = jnp.where(lax.axis_index("seg") == segments - 1, right_packed, received)
    rights = around(packed)

    size = states * TILE

    def spread(block):
        return pl.pallas_call(
            spread_kernel,
            out_shape=(jax.ShapeDtypeStruct((terms * size, size), BF16), tile),
            in_specs=[vmem],
            out_specs=(vmem, vmem),
            compiler_params=params(),
            cost_estimate=cost(2 * terms * size * size * width, 2 * terms * size * size),
            name="spread_site",
        )(block)

    kron_own, _ = spread(x_own)

    whole = (states, width, width)
    whole_bf = jax.ShapeDtypeStruct(whole, BF16)
    whole_f32 = jax.ShapeDtypeStruct(whole, F32)
    rotated = (terms, states, width, width)
    rotated_bf = jax.ShapeDtypeStruct(rotated, BF16)
    square = pltpu.VMEM((terms, width, width), BF16)
    chip_rows = CORES * rows
    stage_flops = 2 * terms * states * width * width * width

    def chip_part(hop, before):
        return pl.pallas_call(
            functools.partial(chip_kernel, hop, chips),
            out_shape=whole_f32,
            in_specs=[vmem] * (5 if hop == 0 else 6),
            out_specs=vmem,
            scratch_shapes=[
                pltpu.VMEM((terms, states, chip_rows, width), BF16),
                pltpu.VMEM((states, terms * chip_rows, width), BF16),
                pltpu.VMEM((width, terms * chip_rows), BF16),
                square,
            ],
            compiler_params=params(),
            cost_estimate=cost(3 * stage_flops * chip_rows / width, 8 * states * width * width),
            name="apply_rows_here" if hop == 0 else "apply_rows_there",
        )(*pieces[2 * hop : 2 * hop + 2], left, packed, kron_own, *before)

    def rotate(part, kron, before):
        inputs = pieces[CORES * part[0] : CORES * (part[-1] + 1)]
        return pl.pallas_call(
            functools.partial(rotate_kernel, part, chips),
            out_shape=(rotated_bf, whole_bf),
            in_specs=[vmem] * (len(inputs) + 1) + [anywhere] * len(before),
            out_specs=(vmem, vmem),
            scratch_shapes=[pltpu.SemaphoreType.DMA((len(inputs),))],
            input_output_aliases={len(inputs) + 1 + n: n for n in range(len(before))},
            compiler_params=params(),
            cost_estimate=cost(stage_flops / 2, 8 * states * width * width),
            name="rotate_here" if part[0] == 0 else "rotate_there",
        )(*inputs, kron, *before)

    partial = chip_part(0, ())
    crossed, partial = lax.optimization_barrier((x_hops[1:], partial))
    for block in crossed:
        pieces += [block, to_sibling(block)]
    kron, norm_far = spread(crossed[0])
    turned_here = rotate(hops[:1], kron, ())
    for hop in hops[1:]:
        partial = chip_part(hop, (partial,))
    stat = norm_part
    for hop in hops[1:]:
        if hop > 1:
            block, partial = lax.optimization_barrier((crossed[hop - 1], partial))
            kron, norm_far = spread(block)
            turned_here = rotate(hops[:1], kron, ())
        turned, vector = rotate(hops[1:], kron, turned_here)
        left_far, partial = lax.optimization_barrier((lefts[hop], partial))
        mixed = pl.pallas_call(
            lefts_kernel,
            out_shape=jax.ShapeDtypeStruct((states, width, terms * width), BF16),
            in_specs=[vmem] * 2,
            out_specs=vmem,
            scratch_shapes=[square],
            compiler_params=params(),
            cost_estimate=cost(stage_flops, 12 * states * width * width),
            name="received_lefts",
        )(turned, left_far)
        partial, stat = pl.pallas_call(
            rights_kernel,
            out_shape=(whole_bf if hop == hops[-1] else whole_f32, tile),
            in_specs=[vmem] * 6,
            out_specs=(vmem, vmem),
            scratch_shapes=[square],
            compiler_params=params(),
            cost_estimate=cost(stage_flops, 12 * states * width * width),
            name="received_rights",
        )(mixed, rights[hop], vector, partial, stat, norm_far)
    other = to_sibling(partial)
    stat_other = to_sibling(stat)

    share = pl.pallas_call(
        functools.partial(second_kernel, scale, members),
        out_shape=tile,
        in_specs=[smem] + [vmem] * 8,
        out_specs=vmem,
        scratch_shapes=[
            pltpu.VMEM(whole, BF16),
            pltpu.VMEM(rotated, BF16),
            pltpu.VMEM(rotated, BF16),
            square,
        ],
        compiler_params=params(),
        cost_estimate=cost(3 * stage_flops, 6 * states * width * width),
        name="apply_residual",
    )(bond_rank, stat, stat_other, partial, other, vector, left, packed, kron_own)
    shares = everyone(share)

    local = jax.ShapeDtypeStruct((rows, states, width), F32)
    vector_own, residual_own = pl.pallas_call(
        functools.partial(own_rows_kernel, scale),
        out_shape=(local, local),
        in_specs=[smem] + [vmem] * 5,
        out_specs=(vmem, vmem),
        compiler_params=params(),
        cost_estimate=cost(8 * guess.size, 16 * guess.size),
        name="own_rows",
    )(bond_rank, guess, stat, stat_other, partial, other)

    ritz, energy = pl.pallas_call(
        finish_kernel,
        out_shape=(local, jax.ShapeDtypeStruct((1,), F32)),
        in_specs=[vmem] * (2 + members),
        out_specs=(vmem, smem),
        compiler_params=params(),
        cost_estimate=cost(3 * guess.size, 12 * guess.size),
        name="finish",
    )(vector_own, residual_own, *shares)
    return (ritz[None], energy)


def solution(mesh):
    in_specs = (
        P("seg", "term", None, None),
        P("seg", "term", None, None),
        P("seg", "term", None, None),
        P("seg", "term", None, None),
        P("seg"),
    )
    out_specs = (P("seg", "term", None, None), P("seg"))
    return jax.shard_map(shards, mesh=mesh, in_specs=in_specs, out_specs=out_specs, check_vma=False)
```

```python
import functools

import jax
import jax.numpy as jnp
from jax import lax
from jax.experimental import pallas as pl
from jax.experimental.pallas import tpu as pltpu
from jax.sharding import PartitionSpec as P

epsilon = 1e-06
CORES = 2
TILE = 16
UNROLL = 8
GROUP = 4
VMEM_LIMIT = 20 * 1024 * 1024
F32 = jnp.float32
BF16 = jnp.bfloat16

vmem = pl.BlockSpec(memory_space=pltpu.VMEM)
smem = pl.BlockSpec(memory_space=pltpu.SMEM)
anywhere = pl.BlockSpec(memory_space=pl.ANY)
in_hbm = pl.BlockSpec(memory_space=pltpu.HBM)


def params():
    return pltpu.CompilerParams(vmem_limit_bytes=VMEM_LIMIT)


def cost(flops, moved):
    return pl.CostEstimate(flops=int(flops) // 100, bytes_accessed=int(moved) // 100, transcendentals=0)


def keep_row(rank, width):
    return (lax.broadcasted_iota(jnp.int32, (1, width), 1) < rank).astype(F32)


def fold(values, width):
    return jnp.sum(values.reshape(values.size // (8 * width), 8, width), axis=0)


def prepare_kernel(
    rank_ref,
    guess_in,
    left_in,
    right_in,
    site_in,
    x_ref,
    norm_ref,
    left_packed_ref,
    right_packed_ref,
    left_ref,
    guess_ref,
    right_ref,
    site_ref,
    sems,
):
    rows, states, width = guess_ref.shape
    terms = left_ref.shape[0]
    half = width // 2
    parts = [pl.ds(n, TILE) for n in range(0, rows, TILE)]
    sources = [guess_in.at[part] for part in parts] + [site_in, right_in, left_in]
    targets = [guess_ref.at[part] for part in parts] + [site_ref, right_ref, left_ref]
    copies = [
        pltpu.make_async_copy(source, target, sems.at[n])
        for n, (source, target) in enumerate(zip(sources, targets))
    ]
    for copy in copies:
        copy.start()
    keep = keep_row(rank_ref[0], width)[None]
    squares = jnp.zeros((8, width), F32)
    for n, part in enumerate(parts):
        copies[n].wait()
        masked = guess_ref[part] * keep
        squares = squares + fold(masked * masked, width)
        x_ref[0:states, part, :] = jnp.swapaxes(masked, 0, 1).astype(BF16)
    total = jnp.sum(squares)
    norm_ref[...] = jnp.full(norm_ref.shape, total, F32)
    copies[-3].wait()
    widen = (
        lax.broadcasted_iota(jnp.int32, (states, width), 0) == lax.broadcasted_iota(jnp.int32, (states, width), 1)
    ).astype(BF16)
    norm = jnp.full((1, width), total, F32)
    parts = []
    for _ in range(3):
        parts.append(norm.astype(BF16).astype(F32))
        norm = norm - parts[-1]
    lines = lax.broadcasted_iota(jnp.int32, (TILE, width), 0)
    lines = functools.reduce(jnp.add, [jnp.where(lines == n, parts[n], 0.0) for n in range(3)]).astype(BF16)
    for k in range(terms + 1):
        slab, row = divmod(k * TILE, rows)
        sites = lines if k == terms else jnp.dot(site_ref[k], widen, preferred_element_type=F32).astype(BF16)
        x_ref[states + slab, row : row + TILE, :] = sites
    for copy, block_ref, packed_ref in zip(copies[-2:], (right_ref, left_ref), (right_packed_ref, left_packed_ref)):
        copy.wait()
        for k in range(terms):
            diagonal = pack_symmetric(block_ref, k, packed_ref)
            packed_ref[k, width : width + TILE, :] = jnp.broadcast_to(diagonal, (TILE, half)).astype(BF16)


def triangle(half):
    row = lax.broadcasted_iota(jnp.int32, (half, half), 0)
    col = lax.broadcasted_iota(jnp.int32, (half, half), 1)
    return row, col


def pack_symmetric(block_ref, k, out_ref):
    width = block_ref.shape[1]
    half = width // 2
    row, col = triangle(half)
    upper = block_ref[k, 0:half, 0:half].astype(F32)
    lower = block_ref[k, half:width, half:width].astype(F32)
    out_ref[k, 0:half, :] = block_ref[k, 0:half, half:width]
    out_ref[k, half:width, :] = jnp.where(row <= col, upper, lower).astype(BF16)
    return jnp.sum(jnp.where(row == col, lower, 0.0), axis=0, keepdims=True)


def unpack_symmetric(packed_ref, full_ref):
    terms, width, _ = full_ref.shape
    half = width // 2
    row, col = triangle(half)
    for k in range(terms):
        corner = packed_ref[k, 0:half, :]
        mixed = packed_ref[k, half:width, :].astype(F32)
        diagonal = packed_ref[k, width : width + TILE, :].astype(F32)[0:1]
        turned = mixed.T
        full_ref[k, 0:half, 0:half] = jnp.where(row <= col, mixed, turned).astype(BF16)
        full_ref[k, 0:half, half:width] = corner
        full_ref[k, half:width, 0:half] = corner.astype(F32).T.astype(BF16)
        full_ref[k, half:width, half:width] = jnp.where(
            row > col, mixed, jnp.where(row == col, diagonal, turned)
        ).astype(BF16)


def spread_kernel(x_ref, kron_ref, norm_ref):
    rows, lanes = x_ref.shape[1:]
    size = kron_ref.shape[1]
    terms = kron_ref.shape[0] // size
    states = size // TILE
    row_state = lax.broadcasted_iota(jnp.int32, (size, states), 0) // TILE
    pick = (row_state == lax.broadcasted_iota(jnp.int32, (size, states), 1)).astype(BF16)
    col_state = lax.broadcasted_iota(jnp.int32, (lanes, size), 1) // TILE
    pick_t = (col_state == lax.broadcasted_iota(jnp.int32, (lanes, size), 0)).astype(BF16)
    same = (
        lax.broadcasted_iota(jnp.int32, (size, size), 0) % TILE
        == lax.broadcasted_iota(jnp.int32, (size, size), 1) % TILE
    )
    for k in range(terms + 1):
        slab, row = divmod(k * TILE, rows)
        sites = x_ref[states + slab, row : row + TILE, :]
        if k == terms:
            lines = sites.astype(F32)
            norm_ref[...] = jnp.broadcast_to(lines[0:1] + lines[1:2] + lines[2:3], norm_ref.shape)
            break
        tall = jnp.dot(pick, sites, preferred_element_type=F32).astype(BF16)
        full = jnp.dot(tall, pick_t, preferred_element_type=F32)
        kron_ref[k * size : (k + 1) * size, :] = jnp.where(same, full, 0.0).astype(BF16)


def mix_sites(source_ref, kron_ref, rotated_ref, base, unroll):
    terms, states, _, width = rotated_ref.shape
    rows = source_ref.shape[1]

    def step(i, carry):
        at = pl.multiple_of(i * TILE, TILE)
        to = pl.multiple_of(base + i * TILE, TILE)
        stack = source_ref[0:states, pl.ds(at, TILE), :].reshape(states * TILE, width)
        turned = jnp.dot(kron_ref[...], stack, preferred_element_type=F32).astype(BF16)
        rotated_ref[:, :, pl.ds(to, TILE), :] = turned.reshape(terms, states, TILE, width)
        return carry

    lax.fori_loop(0, rows // TILE, step, 0, unroll=min(unroll, rows // TILE))


def summed(values):
    while len(values) > 1:
        values = [values[n] + values[n + 1] for n in range(0, len(values), 2)]
    return values[0]


def place(hop, chips):
    me = lax.axis_index("term")
    chip = (me // CORES - hop + chips) % chips
    return chip, me % CORES


def rotate_own_kernel(own_ref, sib_ref, kron_ref, rotated_ref):
    rows = own_ref.shape[1]
    _, core = place(0, 1)
    mix_sites(own_ref, kron_ref, rotated_ref, core * rows, UNROLL)
    mix_sites(sib_ref, kron_ref, rotated_ref, (1 - core) * rows, UNROLL)


def turn_and_mix(chip, left_ref, right_ref, rotated_ref, before_ref, out_ref, turned_ref, columns_ref):
    terms, states, chip_rows, width = rotated_ref.shape
    at = pl.multiple_of(chip * chip_rows, TILE)
    columns = jnp.concatenate([left_ref[k, pl.ds(at, chip_rows), :] for k in range(terms)], axis=0)
    columns_ref[...] = columns.astype(F32).T.astype(BF16)
    for k in range(terms):
        for n in range(0, states, 8):
            source = rotated_ref[k, n : n + 8].reshape(8 * chip_rows, width)
            turned = jnp.dot(source, right_ref[k], preferred_element_type=F32).astype(BF16)
            turned_ref[n : n + 8, k * chip_rows : (k + 1) * chip_rows, :] = turned.reshape(8, chip_rows, width)

    def lefts(p, carry):
        image = jnp.dot(columns_ref[...], turned_ref[p], preferred_element_type=F32)
        if before_ref is not None:
            image = before_ref[p] + image
        out_ref[p] = image
        return carry

    lax.fori_loop(0, states, lefts, 0, unroll=UNROLL)


def here_kernel(chips, rotated_ref, left_ref, packed_ref, out_ref, right_ref, turned_ref, columns_ref):
    chip, _ = place(0, chips)
    unpack_symmetric(packed_ref, right_ref)
    turn_and_mix(chip, left_ref, right_ref, rotated_ref, None, out_ref, turned_ref, columns_ref)


def there_kernel(hop, chips, own_ref, sib_ref, left_ref, right_ref, kron_ref, before_ref, out_ref, *scratch):
    rotated_ref, turned_ref, columns_ref = scratch
    chip, _ = place(hop, chips)
    rotate_own_kernel(own_ref, sib_ref, kron_ref, rotated_ref)
    turn_and_mix(chip, left_ref, right_ref, rotated_ref, before_ref, out_ref, turned_ref, columns_ref)


def rotate_kernel(hops, chips, *refs):
    pieces = refs[: CORES * len(hops)]
    kron_ref = refs[len(pieces)]
    rotated_ref, whole_ref, sems = refs[-3:]
    rows = pieces[0].shape[1]
    copies = []
    for n, piece in enumerate(pieces):
        chip, core = place(hops[n // 2], chips)
        at = (chip * CORES + (core if n % 2 == 0 else 1 - core)) * rows
        copies.append(
            pltpu.make_async_copy(
                piece.at[0 : whole_ref.shape[0]],
                whole_ref.at[:, pl.ds(pl.multiple_of(at, TILE), rows), :],
                sems.at[n],
            )
        )
        copies[-1].start()
    for n, piece in enumerate(pieces):
        chip, core = place(hops[n // 2], chips)
        at = (chip * CORES + (core if n % 2 == 0 else 1 - core)) * rows
        mix_sites(piece, kron_ref, rotated_ref, at, UNROLL)
    for copy in copies:
        copy.wait()


def lefts_kernel(hops, chips, *refs):
    count = CORES * len(hops)
    packed_ref = refs[count + 3]
    mixed_ref, rotated_ref, whole_ref, left_ref, sems = refs[-5:]
    terms, states, width, _ = rotated_ref.shape
    unpack_symmetric(packed_ref, left_ref)
    rotate_kernel(hops, chips, *refs[: count + 1], rotated_ref, whole_ref, sems)

    def lefts(p, carry):
        for k in range(terms):
            mixed = jnp.dot(left_ref[k], rotated_ref[k, p], preferred_element_type=F32)
            mixed_ref[p, :, k * width : (k + 1) * width] = mixed.astype(BF16)
        return carry

    lax.fori_loop(0, states, lefts, 0, unroll=UNROLL)


def rights_kernel(start, stop, packed_ref, mixed_ref, whole_ref, before_ref, *refs):
    if start == 0:
        stats = refs[:-3]
        partial_ref, stat_ref, right_ref = refs[-3:]
        unpack_symmetric(packed_ref, right_ref)
    else:
        stats = refs[:-2]
        partial_ref, stat_ref = refs[-2:]
        right_ref = packed_ref
    states, width, _ = whole_ref.shape
    terms = right_ref.shape[0]

    def rights(n, total):
        at = n * GROUP
        rows = mixed_ref[pl.ds(start + at, GROUP)].reshape(GROUP * width, terms * width)
        stacked = right_ref[...].reshape(terms * width, width)
        image = jnp.dot(rows, stacked, preferred_element_type=F32).reshape(GROUP, width, width)
        part = (before_ref[pl.ds(start + at, GROUP)].astype(F32) + image).astype(partial_ref.dtype)
        partial_ref[pl.ds(at, GROUP)] = part
        held = whole_ref[pl.ds(start + at, GROUP)].astype(F32)
        return total + fold(held * part.astype(F32), width)

    total = lax.fori_loop(0, (stop - start) // GROUP, rights, jnp.zeros((8, width), F32))
    stat_ref[...] = functools.reduce(jnp.add, [stat[...] for stat in stats])
    product = jnp.full((1, width), jnp.sum(total), F32)
    stat_ref[0:1, :] = product if start == 0 else stats[0][0:1, :] + product


def scales(rank_ref, mine_ref, theirs_ref, scale, width):
    inverse = lax.rsqrt((mine_ref[1:2, :] + theirs_ref[1:2, :]) * scale + epsilon)
    rayleigh = (mine_ref[0:1, :] + theirs_ref[0:1, :]) * (inverse * inverse * scale)
    return inverse, rayleigh, keep_row(rank_ref[0], width) * inverse


def add_kernel(mine_ref, other_ref, sum_ref):
    sum_ref[...] = mine_ref[...].astype(F32) + other_ref[...].astype(F32)


def second_kernel(
    scale,
    members,
    rank_ref,
    mine_ref,
    theirs_ref,
    low_ref,
    high_ref,
    high_other_ref,
    whole_ref,
    left_ref,
    right_ref,
    kron_ref,
    out_ref,
    res_ref,
    rotated_ref,
    mixed_ref,
):
    terms, states, width, _ = rotated_ref.shape
    inverse, rayleigh, row_scale = scales(rank_ref, mine_ref, theirs_ref, scale, width)
    back = rayleigh * inverse

    square = jnp.zeros((8, width), F32)
    for start, halves in ((0, (low_ref,)), (states // 2, (high_ref, high_other_ref))):

        def lefts(n, total):
            p = start + n
            sigma = functools.reduce(jnp.add, [half[n].astype(F32) for half in halves]) * row_scale
            residual = sigma - back * whole_ref[p].astype(F32)
            rounded = residual.astype(BF16)
            res_ref[p] = rounded
            mixed = jnp.dot(
                left_ref[...].reshape(terms * width, width), rounded, preferred_element_type=F32
            ).astype(BF16)
            for k in range(terms):
                mixed_ref[k, p] = mixed[k * width : (k + 1) * width]
            return total + fold(residual * residual, width)

        square = lax.fori_loop(0, states // 2, lefts, square, unroll=UNROLL)
    mix_sites(res_ref, kron_ref, rotated_ref, 0, 2 * UNROLL)

    def rights(n, total):
        at = n * GROUP
        for k in range(terms):
            turned = rotated_ref[k, pl.ds(at, GROUP)].reshape(GROUP * width, width)
            image = jnp.dot(turned, right_ref[k], preferred_element_type=F32)
            held = mixed_ref[k, pl.ds(at, GROUP)].reshape(GROUP * width, width).astype(F32)
            total = total + fold(held * image, width)
        return total

    cross = lax.fori_loop(0, states // GROUP, rights, jnp.zeros((8, width), F32))
    share = 1.0 / members
    out_ref[0:1, :] = rayleigh * share
    out_ref[1:2, :] = jnp.full((1, width), jnp.sum(square) * (scale * share), F32)
    out_ref[2:3, :] = jnp.full((1, width), jnp.sum(cross) * scale, F32)
    out_ref[3:8, :] = jnp.zeros((5, width), F32)


def own_rows_kernel(scale, rank_ref, guess_ref, mine_ref, theirs_ref, *refs):
    low_ref, high_ref, high_other_ref, vector_ref, residual_ref = refs
    rows, states, width = guess_ref.shape
    inverse, rayleigh, row_scale = scales(rank_ref, mine_ref, theirs_ref, scale, width)
    own = pl.ds(pl.multiple_of(lax.axis_index("term") * rows, TILE), rows)
    vector = guess_ref[...] * row_scale[None]
    vector_ref[...] = vector
    high = high_ref[:, own, :].astype(F32) + high_other_ref[:, own, :].astype(F32)
    sigma = jnp.concatenate([low_ref[:, own, :], high], axis=0) * row_scale[None]
    residual_ref[...] = jnp.swapaxes(sigma, 0, 1) - rayleigh[None] * vector


def finish_kernel(vector_ref, residual_ref, *refs):
    shares = refs[:-4]
    ritz_hbm, energy_ref, ritz_ref, sems = refs[-4:]
    stat = summed([share[...] for share in shares])
    rayleigh = stat[0:1, :]
    res_sq = stat[1:2, :]
    res_var = res_sq + epsilon
    curvature = stat[2:3, :] / res_var
    res_scale = jnp.sqrt(res_var)
    coupling = res_sq / res_scale
    half_gap = 0.5 * (rayleigh - curvature)
    energy = 0.5 * (rayleigh + curvature) - jnp.sqrt(half_gap * half_gap + coupling * coupling)
    coeff_new = energy - rayleigh
    coeff_norm = jnp.sqrt(coupling * coupling + coeff_new * coeff_new + epsilon)
    old = coupling / coeff_norm
    new = coeff_new / (coeff_norm * res_scale)
    rows = vector_ref.shape[0]
    copies = []
    for n in range(0, rows, TILE):
        part = pl.ds(n, TILE)
        ritz_ref[part] = old[None] * vector_ref[part] + new[None] * residual_ref[part]
        copies.append(pltpu.make_async_copy(ritz_ref.at[part], ritz_hbm.at[part], sems.at[n // TILE]))
        copies[-1].start()
    energy_ref[0] = energy[0, 0]
    for copy in copies:
        copy.wait()


def shards(wave_guess, left_env, right_env, site_ops, bond_rank):
    guess = wave_guess[0]
    left = left_env[0]
    site = site_ops[0]
    rows, states, width = guess.shape
    terms = left.shape[0]
    members = lax.axis_size("term")
    chips = members // CORES
    segments = lax.axis_size("seg")
    scale = 1.0 / float(rows * members * states * width)
    hops = tuple(range(chips))

    def to_sibling(block):
        return lax.ppermute(block, "term", [(i, i ^ 1) for i in range(members)])

    def to_next_chip(block):
        return lax.ppermute(block, "term", [(i, (i + CORES) % members) for i in range(members)])

    def around(block):
        found = [block]
        for _ in range(chips - 1):
            found.append(to_next_chip(found[-1]))
        return found

    def everyone(block):
        others = [
            lax.ppermute(block, "term", [(i, i ^ bits) for i in range(members)]) for bits in range(1, members)
        ]
        return [block] + others

    tile = jax.ShapeDtypeStruct((8, width), F32)
    half = width // 2
    packed_shape = jax.ShapeDtypeStruct((terms, width + TILE, half), BF16)
    slabs = -(-(terms + 1) * TILE // rows)
    x_own, norm_part, left_packed, right_packed, left = pl.pallas_call(
        prepare_kernel,
        out_shape=(
            jax.ShapeDtypeStruct((states + slabs, rows, width), BF16),
            tile,
            packed_shape,
            packed_shape,
            jax.ShapeDtypeStruct(left.shape, BF16),
        ),
        in_specs=[smem] + [in_hbm] * 4,
        out_specs=(vmem,) * 5,
        scratch_shapes=[
            pltpu.VMEM(guess.shape, F32),
            pltpu.VMEM(left.shape, BF16),
            pltpu.VMEM(site.shape, BF16),
            pltpu.SemaphoreType.DMA((rows // TILE + 3,)),
        ],
        compiler_params=params(),
        cost_estimate=cost(4 * guess.size, 6 * guess.size),
        name="prepare",
    )(bond_rank, *[pltpu.with_memory_space_constraint(a, pltpu.HBM) for a in (guess, left, right_env[0], site)])

    x_hops = around(x_own)
    pieces = [x_own, to_sibling(x_own)]
    lefts = around(left_packed)
    shift = [(i + 1, i) for i in range(segments - 1)]
    received = lax.ppermute(right_packed, "seg", shift)

    size = states * TILE

    def spread(block):
        return pl.pallas_call(
            spread_kernel,
            out_shape=(jax.ShapeDtypeStruct((terms * size, size), BF16), tile),
            in_specs=[vmem],
            out_specs=(vmem, vmem),
            compiler_params=params(),
            cost_estimate=cost(2 * terms * size * size * width, 2 * terms * size * size),
            name="spread_site",
        )(block)

    kron_own, _ = spread(x_own)

    whole = (states, width, width)
    whole_bf = jax.ShapeDtypeStruct(whole, BF16)
    whole_f32 = jax.ShapeDtypeStruct(whole, F32)
    rotated = (terms, states, width, width)
    rotated_bf = jax.ShapeDtypeStruct(rotated, BF16)
    square = pltpu.VMEM((terms, width, width), BF16)
    chip_rows = CORES * rows
    stage_flops = 2 * terms * states * width * width * width

    mix_scratch = [
        pltpu.VMEM((states, terms * chip_rows, width), BF16),
        pltpu.VMEM((width, terms * chip_rows), BF16),
    ]
    chip_rotated = (terms, states, chip_rows, width)
    chip_cost = cost(3 * stage_flops * chip_rows / width, 8 * states * width * width)
    rotated_own = pl.pallas_call(
        rotate_own_kernel,
        out_shape=jax.ShapeDtypeStruct(chip_rotated, BF16),
        in_specs=[vmem] * 3,
        out_specs=vmem,
        compiler_params=params(),
        cost_estimate=chip_cost,
        name="rotate_own",
    )(*pieces, kron_own)
    received, rotated_own = lax.optimization_barrier((received, rotated_own))
    packed = jnp.where(lax.axis_index("seg") == segments - 1, right_packed, received)
    rights = around(packed)
    partial, right = pl.pallas_call(
        functools.partial(here_kernel, chips),
        out_shape=(whole_f32, jax.ShapeDtypeStruct(left.shape, BF16)),
        in_specs=[vmem] * 3,
        out_specs=(vmem, vmem),
        scratch_shapes=mix_scratch,
        compiler_params=params(),
        cost_estimate=chip_cost,
        name="apply_rows_here",
    )(rotated_own, left, packed)

    def there(hop, before):
        return pl.pallas_call(
            functools.partial(there_kernel, hop, chips),
            out_shape=whole_f32,
            in_specs=[vmem] * 6,
            out_specs=vmem,
            scratch_shapes=[pltpu.VMEM(chip_rotated, BF16)] + mix_scratch,
            compiler_params=params(),
            cost_estimate=chip_cost,
            name="apply_rows_there",
        )(*pieces[2 * hop : 2 * hop + 2], left, right, kron_own, before)

    def rotate(kron):
        return pl.pallas_call(
            functools.partial(rotate_kernel, hops[:1], chips),
            out_shape=(rotated_bf, whole_bf),
            in_specs=[vmem] * 3,
            out_specs=(vmem, vmem),
            scratch_shapes=[pltpu.SemaphoreType.DMA((CORES,))],
            compiler_params=params(),
            cost_estimate=chip_cost,
            name="rotate_here",
        )(*pieces[:CORES], kron)

    crossed, partial = lax.optimization_barrier((x_hops[1:], partial))
    for block in crossed:
        pieces += [block, to_sibling(block)]
    kron, norm_far = spread(crossed[0])
    turned = rotate(kron)
    for hop in hops[1:]:
        partial = there(hop, partial)
    far = pieces[CORES:]
    norms = [norm_part]
    for hop in hops[1:]:
        if hop > 1:
            block, partial = lax.optimization_barrier((crossed[hop - 1], partial))
            kron, norm_far = spread(block)
            turned = rotate(kron)
        norms.append(norm_far)
        left_far, partial = lax.optimization_barrier((lefts[hop], partial))
        mixed, _, vector = pl.pallas_call(
            functools.partial(lefts_kernel, hops[1:], chips),
            out_shape=(jax.ShapeDtypeStruct((states, width, terms * width), BF16), rotated_bf, whole_bf),
            in_specs=[vmem] * (len(far) + 1) + [anywhere] * 2 + [vmem],
            out_specs=(vmem,) * 3,
            scratch_shapes=[square, pltpu.SemaphoreType.DMA((len(far),))],
            input_output_aliases={len(far) + 1: 1, len(far) + 2: 2},
            compiler_params=params(),
            cost_estimate=cost(stage_flops, 12 * states * width * width),
            name="received_lefts",
        )(*far, kron, *turned, left_far)
        last = hop == hops[-1]
        stats = norms if last else norms[:1]
        right_far = rights[hop]
        parts = []
        bounds = (0, states // 2, states) if last else (0, states)
        for start, stop in zip(bounds[:-1], bounds[1:]):
            outs = [jax.ShapeDtypeStruct((stop - start, width, width), BF16 if last else F32), tile]
            part, stat, *unpacked = pl.pallas_call(
                functools.partial(rights_kernel, start, stop),
                out_shape=tuple(outs + ([jax.ShapeDtypeStruct(left.shape, BF16)] if start == 0 else [])),
                in_specs=[vmem] * (4 + len(stats)),
                out_specs=(vmem,) * (3 if start == 0 else 2),
                compiler_params=params(),
                cost_estimate=cost(stage_flops / 2, 12 * states * width * width),
                name="received_rights",
            )(right_far, mixed, vector, partial, *stats)
            stats = [stat]
            if unpacked:
                right_far = unpacked[0]
            parts.append(part)
        if not last:
            partial = parts[0]
    low = pl.pallas_call(
        add_kernel,
        out_shape=jax.ShapeDtypeStruct(parts[0].shape, F32),
        in_specs=[vmem] * 2,
        out_specs=vmem,
        compiler_params=params(),
        cost_estimate=cost(parts[0].size, 8 * parts[0].size),
        name="add_low_half",
    )(parts[0], to_sibling(parts[0]))
    halves = [low, parts[1], to_sibling(parts[1])]
    stat_other = to_sibling(stat)

    share = pl.pallas_call(
        functools.partial(second_kernel, scale, members),
        out_shape=tile,
        in_specs=[smem] + [vmem] * 9,
        out_specs=vmem,
        scratch_shapes=[
            pltpu.VMEM(whole, BF16),
            pltpu.VMEM(rotated, BF16),
            pltpu.VMEM(rotated, BF16),
        ],
        compiler_params=params(),
        cost_estimate=cost(3 * stage_flops, 6 * states * width * width),
        name="apply_residual",
    )(bond_rank, stat, stat_other, *halves, vector, left, right, kron_own)
    shares = everyone(share)

    local = jax.ShapeDtypeStruct((rows, states, width), F32)
    vector_own, residual_own = pl.pallas_call(
        functools.partial(own_rows_kernel, scale),
        out_shape=(local, local),
        in_specs=[smem] + [vmem] * 6,
        out_specs=(vmem, vmem),
        compiler_params=params(),
        cost_estimate=cost(8 * guess.size, 16 * guess.size),
        name="own_rows",
    )(bond_rank, guess, stat, stat_other, *halves)

    ritz, energy = pl.pallas_call(
        finish_kernel,
        out_shape=(local, jax.ShapeDtypeStruct((1,), F32)),
        in_specs=[vmem] * (2 + members),
        out_specs=(anywhere, smem),
        scratch_shapes=[pltpu.VMEM(guess.shape, F32), pltpu.SemaphoreType.DMA((rows // TILE,))],
        compiler_params=params(),
        cost_estimate=cost(3 * guess.size, 12 * guess.size),
        name="finish",
    )(vector_own, residual_own, *shares)
    return (ritz[None], energy)


def solution(mesh):
    in_specs = (
        P("seg", "term", None, None),
        P("seg", "term", None, None),
        P("seg", "term", None, None),
        P("seg", "term", None, None),
        P("seg"),
    )
    out_specs = (P("seg", "term", None, None), P("seg"))
    return jax.shard_map(shards, mesh=mesh, in_specs=in_specs, out_specs=out_specs, check_vma=False)
```

```python
import functools

import jax
import jax.numpy as jnp
from jax import lax
from jax.experimental import pallas as pl
from jax.experimental.pallas import tpu as pltpu
from jax.sharding import PartitionSpec as P

epsilon = 1e-06
CORES = 2
TILE = 16
UNROLL = 8
GROUP = 4
VMEM_LIMIT = 20 * 1024 * 1024
F32 = jnp.float32
BF16 = jnp.bfloat16

vmem = pl.BlockSpec(memory_space=pltpu.VMEM)
smem = pl.BlockSpec(memory_space=pltpu.SMEM)
anywhere = pl.BlockSpec(memory_space=pl.ANY)
in_hbm = pl.BlockSpec(memory_space=pltpu.HBM)


def params():
    return pltpu.CompilerParams(vmem_limit_bytes=VMEM_LIMIT)


def cost(flops, moved):
    return pl.CostEstimate(flops=int(flops) // 100, bytes_accessed=int(moved) // 100, transcendentals=0)


def keep_row(rank, width):
    return (lax.broadcasted_iota(jnp.int32, (1, width), 1) < rank).astype(F32)


def fold(values, width):
    return jnp.sum(values.reshape(values.size // (8 * width), 8, width), axis=0)


def prepare_kernel(
    starts,
    rank_ref,
    guess_in,
    left_in,
    right_in,
    site_in,
    x_ref,
    norm_ref,
    left_packed_ref,
    right_packed_ref,
    left_ref,
    *refs,
):
    chunk_refs = refs[: len(starts)]
    guess_ref, right_ref, site_ref, sems = refs[len(starts) :]
    rows, states, width = guess_ref.shape
    terms = left_ref.shape[0]
    half = width // 2
    parts = [pl.ds(n, TILE) for n in range(0, rows, TILE)]
    sources = [guess_in.at[part] for part in parts] + [site_in, right_in, left_in]
    targets = [guess_ref.at[part] for part in parts] + [site_ref, right_ref, left_ref]
    copies = [
        pltpu.make_async_copy(source, target, sems.at[n])
        for n, (source, target) in enumerate(zip(sources, targets))
    ]
    for copy in copies:
        copy.start()
    keep = keep_row(rank_ref[0], width)[None]
    squares = jnp.zeros((8, width), F32)
    for n, part in enumerate(parts):
        copies[n].wait()
        masked = guess_ref[part] * keep
        squares = squares + fold(masked * masked, width)
        turned = jnp.swapaxes(masked, 0, 1).astype(BF16)
        x_ref[:, part, :] = turned
        chunk = max(c for c, start in enumerate(starts) if start <= n * TILE)
        at = n * TILE - starts[chunk]
        chunk_refs[chunk][0:states, at : at + TILE, :] = turned
    total = jnp.sum(squares)
    norm_ref[...] = jnp.full(norm_ref.shape, total, F32)
    copies[-3].wait()
    line = lax.broadcasted_iota(jnp.int32, (TILE, width), 0)
    lane = lax.broadcasted_iota(jnp.int32, (TILE, width), 1)
    norm = jnp.full((TILE, width), total, F32)
    extra = jnp.zeros((TILE, width), F32)
    for n in range(3):
        part = norm.astype(BF16).astype(F32)
        norm = norm - part
        extra = jnp.where((line == n) & (lane >= half), part, extra)
    for k in range(terms):
        place_at = (lane == line + k * TILE).astype(BF16)
        extra = extra + jnp.dot(site_ref[k], place_at, preferred_element_type=F32)
    chunk_refs[0][states, 0:TILE, :] = extra.astype(BF16)
    for copy, block_ref, packed_ref in zip(copies[-2:], (right_ref, left_ref), (right_packed_ref, left_packed_ref)):
        copy.wait()
        for k in range(terms):
            diagonal = pack_symmetric(block_ref, k, packed_ref)
            packed_ref[k, width : width + TILE, :] = jnp.broadcast_to(diagonal, (TILE, half)).astype(BF16)


def triangle(half):
    row = lax.broadcasted_iota(jnp.int32, (half, half), 0)
    col = lax.broadcasted_iota(jnp.int32, (half, half), 1)
    return row, col


def pack_symmetric(block_ref, k, out_ref):
    width = block_ref.shape[1]
    half = width // 2
    row, col = triangle(half)
    upper = block_ref[k, 0:half, 0:half].astype(F32)
    lower = block_ref[k, half:width, half:width].astype(F32)
    out_ref[k, 0:half, :] = block_ref[k, 0:half, half:width]
    out_ref[k, half:width, :] = jnp.where(row <= col, upper, lower).astype(BF16)
    return jnp.sum(jnp.where(row == col, lower, 0.0), axis=0, keepdims=True)


def unpack_symmetric(packed_ref, full_ref):
    terms, width, _ = full_ref.shape
    half = width // 2
    row, col = triangle(half)
    for k in range(terms):
        corner = packed_ref[k, 0:half, :]
        mixed = packed_ref[k, half:width, :].astype(F32)
        diagonal = packed_ref[k, width : width + TILE, :].astype(F32)[0:1]
        turned = mixed.T
        full_ref[k, 0:half, 0:half] = jnp.where(row <= col, mixed, turned).astype(BF16)
        full_ref[k, 0:half, half:width] = corner
        full_ref[k, half:width, 0:half] = corner.astype(F32).T.astype(BF16)
        full_ref[k, half:width, half:width] = jnp.where(
            row > col, mixed, jnp.where(row == col, diagonal, turned)
        ).astype(BF16)


def spread_kernel(chunk_ref, kron_ref, norm_ref):
    width = chunk_ref.shape[2]
    half = width // 2
    size = kron_ref.shape[1]
    terms = kron_ref.shape[0] // size
    states = size // TILE
    tile = chunk_ref[states, 0:TILE, :]
    lines = tile.astype(F32)
    norm = lines[0:1, half:width] + lines[1:2, half:width] + lines[2:3, half:width]
    norm_ref[...] = jnp.broadcast_to(jnp.concatenate([norm, norm], axis=1), norm_ref.shape)
    row_state = lax.broadcasted_iota(jnp.int32, (size, states), 0) // TILE
    pick = (row_state == lax.broadcasted_iota(jnp.int32, (size, states), 1)).astype(BF16)
    tall = jnp.dot(pick, tile, preferred_element_type=F32).astype(BF16)
    lane = lax.broadcasted_iota(jnp.int32, (width, size), 0)
    col_state = lax.broadcasted_iota(jnp.int32, (width, size), 1) // TILE
    same = (
        lax.broadcasted_iota(jnp.int32, (size, size), 0) % TILE
        == lax.broadcasted_iota(jnp.int32, (size, size), 1) % TILE
    )
    for k in range(terms):
        pick_t = (lane == col_state + k * TILE).astype(BF16)
        full = jnp.dot(tall, pick_t, preferred_element_type=F32)
        kron_ref[k * size : (k + 1) * size, :] = jnp.where(same, full, 0.0).astype(BF16)


def mix_sites(source_ref, kron_ref, rotated_ref, base, unroll):
    terms, states, _, width = rotated_ref.shape
    rows = source_ref.shape[1]

    def step(i, carry):
        at = pl.multiple_of(i * TILE, TILE)
        to = pl.multiple_of(base + i * TILE, TILE)
        stack = source_ref[0:states, pl.ds(at, TILE), :].reshape(states * TILE, width)
        turned = jnp.dot(kron_ref[...], stack, preferred_element_type=F32).astype(BF16)
        rotated_ref[:, :, pl.ds(to, TILE), :] = turned.reshape(terms, states, TILE, width)
        return carry

    lax.fori_loop(0, rows // TILE, step, 0, unroll=min(unroll, rows // TILE))


def summed(values):
    while len(values) > 1:
        values = [values[n] + values[n + 1] for n in range(0, len(values), 2)]
    return values[0]


def place(hop, chips):
    me = lax.axis_index("term")
    chip = (me // CORES - hop + chips) % chips
    return chip, me % CORES


def rotate_own_kernel(spots, rows, *refs):
    pieces = refs[: len(spots)]
    kron_ref, rotated_ref = refs[len(spots) :]
    _, core = place(0, 1)
    for (_, flip, offset), piece in zip(spots, pieces):
        at = (core if flip == 0 else 1 - core) * rows + offset
        mix_sites(piece, kron_ref, rotated_ref, at, UNROLL)


def turn_and_mix(chip, left_ref, right_ref, rotated_ref, before_ref, out_ref, turned_ref, columns_ref):
    terms, states, chip_rows, width = rotated_ref.shape
    at = pl.multiple_of(chip * chip_rows, TILE)
    columns = jnp.concatenate([left_ref[k, pl.ds(at, chip_rows), :] for k in range(terms)], axis=0)
    columns_ref[...] = columns.astype(F32).T.astype(BF16)
    for k in range(terms):
        for n in range(0, states, 8):
            source = rotated_ref[k, n : n + 8].reshape(8 * chip_rows, width)
            turned = jnp.dot(source, right_ref[k], preferred_element_type=F32).astype(BF16)
            turned_ref[n : n + 8, k * chip_rows : (k + 1) * chip_rows, :] = turned.reshape(8, chip_rows, width)

    def lefts(p, carry):
        image = jnp.dot(columns_ref[...], turned_ref[p], preferred_element_type=F32)
        if before_ref is not None:
            image = before_ref[p] + image
        out_ref[p] = image
        return carry

    lax.fori_loop(0, states, lefts, 0, unroll=UNROLL)


def here_kernel(chips, rotated_ref, left_ref, packed_ref, out_ref, right_ref, turned_ref, columns_ref):
    chip, _ = place(0, chips)
    unpack_symmetric(packed_ref, right_ref)
    turn_and_mix(chip, left_ref, right_ref, rotated_ref, None, out_ref, turned_ref, columns_ref)


def there_kernel(spots, rows, chips, *refs):
    count = len(spots)
    left_ref, right_ref, kron_ref, before_ref, out_ref = refs[count : count + 5]
    rotated_ref, turned_ref, columns_ref = refs[count + 5 :]
    chip, _ = place(spots[0][0], chips)
    rotate_own_kernel(spots, rows, *refs[:count], kron_ref, rotated_ref)
    turn_and_mix(chip, left_ref, right_ref, rotated_ref, before_ref, out_ref, turned_ref, columns_ref)


def rotate_kernel(spots, rows, chips, *refs):
    pieces = refs[: len(spots)]
    kron_ref = refs[len(spots)]
    rotated_ref, whole_ref, sems = refs[-3:]
    states = whole_ref.shape[0]
    copies = []
    bases = []
    for n, ((hop, flip, offset), piece) in enumerate(zip(spots, pieces)):
        chip, core = place(hop, chips)
        at = pl.multiple_of((chip * CORES + (core if flip == 0 else 1 - core)) * rows + offset, TILE)
        bases.append(at)
        target = whole_ref.at[:, pl.ds(at, piece.shape[1]), :]
        copies.append(pltpu.make_async_copy(piece.at[0:states], target, sems.at[n]))
        copies[-1].start()
    for at, piece in zip(bases, pieces):
        mix_sites(piece, kron_ref, rotated_ref, at, UNROLL)
    for copy in copies:
        copy.wait()


def lefts_kernel(spots, rows, chips, *refs):
    count = len(spots)
    packed_ref = refs[count + 3]
    mixed_ref, rotated_ref, whole_ref, left_ref, sems = refs[-5:]
    terms, states, width, _ = rotated_ref.shape
    unpack_symmetric(packed_ref, left_ref)
    rotate_kernel(spots, rows, chips, *refs[: count + 1], rotated_ref, whole_ref, sems)

    def lefts(p, carry):
        for k in range(terms):
            mixed = jnp.dot(left_ref[k], rotated_ref[k, p], preferred_element_type=F32)
            mixed_ref[p, :, k * width : (k + 1) * width] = mixed.astype(BF16)
        return carry

    lax.fori_loop(0, states, lefts, 0, unroll=UNROLL)


def rights_kernel(start, stop, packed_ref, mixed_ref, whole_ref, before_ref, *refs):
    if start == 0:
        stats = refs[:-3]
        partial_ref, stat_ref, right_ref = refs[-3:]
        unpack_symmetric(packed_ref, right_ref)
    else:
        stats = refs[:-2]
        partial_ref, stat_ref = refs[-2:]
        right_ref = packed_ref
    states, width, _ = whole_ref.shape
    terms = right_ref.shape[0]

    def rights(n, total):
        at = n * GROUP
        rows = mixed_ref[pl.ds(start + at, GROUP)].reshape(GROUP * width, terms * width)
        stacked = right_ref[...].reshape(terms * width, width)
        image = jnp.dot(rows, stacked, preferred_element_type=F32).reshape(GROUP, width, width)
        part = (before_ref[pl.ds(start + at, GROUP)].astype(F32) + image).astype(partial_ref.dtype)
        partial_ref[pl.ds(at, GROUP)] = part
        held = whole_ref[pl.ds(start + at, GROUP)].astype(F32)
        return total + fold(held * part.astype(F32), width)

    total = lax.fori_loop(0, (stop - start) // GROUP, rights, jnp.zeros((8, width), F32))
    stat_ref[...] = functools.reduce(jnp.add, [stat[...] for stat in stats])
    product = jnp.full((1, width), jnp.sum(total), F32)
    stat_ref[0:1, :] = product if start == 0 else stats[0][0:1, :] + product


def scales(rank_ref, mine_ref, theirs_ref, scale, width):
    inverse = lax.rsqrt((mine_ref[1:2, :] + theirs_ref[1:2, :]) * scale + epsilon)
    rayleigh = (mine_ref[0:1, :] + theirs_ref[0:1, :]) * (inverse * inverse * scale)
    return inverse, rayleigh, keep_row(rank_ref[0], width) * inverse


def add_kernel(mine_ref, other_ref, sum_ref):
    sum_ref[...] = mine_ref[...].astype(F32) + other_ref[...].astype(F32)


def second_kernel(
    scale,
    members,
    rank_ref,
    mine_ref,
    theirs_ref,
    low_ref,
    high_ref,
    high_other_ref,
    whole_ref,
    left_ref,
    right_ref,
    kron_ref,
    out_ref,
    res_ref,
    rotated_ref,
    mixed_ref,
):
    terms, states, width, _ = rotated_ref.shape
    inverse, rayleigh, row_scale = scales(rank_ref, mine_ref, theirs_ref, scale, width)
    back = rayleigh * inverse

    square = jnp.zeros((8, width), F32)
    for start, halves in ((0, (low_ref,)), (states // 2, (high_ref, high_other_ref))):

        def lefts(n, total):
            p = start + n
            sigma = functools.reduce(jnp.add, [half[n].astype(F32) for half in halves]) * row_scale
            residual = sigma - back * whole_ref[p].astype(F32)
            rounded = residual.astype(BF16)
            res_ref[p] = rounded
            mixed = jnp.dot(
                left_ref[...].reshape(terms * width, width), rounded, preferred_element_type=F32
            ).astype(BF16)
            for k in range(terms):
                mixed_ref[k, p] = mixed[k * width : (k + 1) * width]
            return total + fold(residual * residual, width)

        square = lax.fori_loop(0, states // 2, lefts, square, unroll=UNROLL)
    mix_sites(res_ref, kron_ref, rotated_ref, 0, 2 * UNROLL)

    def rights(n, total):
        at = n * GROUP
        for k in range(terms):
            turned = rotated_ref[k, pl.ds(at, GROUP)].reshape(GROUP * width, width)
            image = jnp.dot(turned, right_ref[k], preferred_element_type=F32)
            held = mixed_ref[k, pl.ds(at, GROUP)].reshape(GROUP * width, width).astype(F32)
            total = total + fold(held * image, width)
        return total

    cross = lax.fori_loop(0, states // GROUP, rights, jnp.zeros((8, width), F32))
    share = 1.0 / members
    out_ref[0:1, :] = rayleigh * share
    out_ref[1:2, :] = jnp.full((1, width), jnp.sum(square) * (scale * share), F32)
    out_ref[2:3, :] = jnp.full((1, width), jnp.sum(cross) * scale, F32)
    out_ref[3:8, :] = jnp.zeros((5, width), F32)


def own_rows_kernel(scale, rank_ref, guess_ref, mine_ref, theirs_ref, *refs):
    low_ref, high_ref, high_other_ref, vector_ref, residual_ref = refs
    rows, states, width = guess_ref.shape
    inverse, rayleigh, row_scale = scales(rank_ref, mine_ref, theirs_ref, scale, width)
    own = pl.ds(pl.multiple_of(lax.axis_index("term") * rows, TILE), rows)
    vector = guess_ref[...] * row_scale[None]
    vector_ref[...] = vector
    high = high_ref[:, own, :].astype(F32) + high_other_ref[:, own, :].astype(F32)
    sigma = jnp.concatenate([low_ref[:, own, :], high], axis=0) * row_scale[None]
    residual_ref[...] = jnp.swapaxes(sigma, 0, 1) - rayleigh[None] * vector


def finish_kernel(vector_ref, residual_ref, *refs):
    shares = refs[:-2]
    ritz_ref, energy_ref = refs[-2:]
    stat = summed([share[...] for share in shares])
    rayleigh = stat[0:1, :]
    res_sq = stat[1:2, :]
    res_var = res_sq + epsilon
    curvature = stat[2:3, :] / res_var
    res_scale = jnp.sqrt(res_var)
    coupling = res_sq / res_scale
    half_gap = 0.5 * (rayleigh - curvature)
    energy = 0.5 * (rayleigh + curvature) - jnp.sqrt(half_gap * half_gap + coupling * coupling)
    coeff_new = energy - rayleigh
    coeff_norm = jnp.sqrt(coupling * coupling + coeff_new * coeff_new + epsilon)
    old = coupling / coeff_norm
    new = coeff_new / (coeff_norm * res_scale)
    ritz_ref[...] = old[None] * vector_ref[...] + new[None] * residual_ref[...]
    energy_ref[0] = energy[0, 0]


def shards(wave_guess, left_env, right_env, site_ops, bond_rank):
    guess = wave_guess[0]
    left = left_env[0]
    site = site_ops[0]
    rows, states, width = guess.shape
    terms = left.shape[0]
    members = lax.axis_size("term")
    chips = members // CORES
    segments = lax.axis_size("seg")
    scale = 1.0 / float(rows * members * states * width)
    hops = tuple(range(chips))

    def to_sibling(block):
        return lax.ppermute(block, "term", [(i, i ^ 1) for i in range(members)])

    def to_next_chip(block):
        return lax.ppermute(block, "term", [(i, (i + CORES) % members) for i in range(members)])

    def around(block):
        found = [block]
        for _ in range(chips - 1):
            found.append(to_next_chip(found[-1]))
        return found

    def everyone(block):
        others = [
            lax.ppermute(block, "term", [(i, i ^ bits) for i in range(members)]) for bits in range(1, members)
        ]
        return [block] + others

    tile = jax.ShapeDtypeStruct((8, width), F32)
    half = width // 2
    packed_shape = jax.ShapeDtypeStruct((terms, width + TILE, half), BF16)
    starts = (0, rows - 2 * TILE, rows - TILE) if rows >= 4 * TILE else (0,)
    lengths = [stop - start for start, stop in zip(starts, starts[1:] + (rows,))]
    x_own, norm_part, left_packed, right_packed, left, *chunks = pl.pallas_call(
        functools.partial(prepare_kernel, starts),
        out_shape=(
            jax.ShapeDtypeStruct((states, rows, width), BF16),
            tile,
            packed_shape,
            packed_shape,
            jax.ShapeDtypeStruct(left.shape, BF16),
            *[
                jax.ShapeDtypeStruct((states + (n == 0), length, width), BF16)
                for n, length in enumerate(lengths)
            ],
        ),
        in_specs=[smem] + [in_hbm] * 4,
        out_specs=(vmem,) * (5 + len(lengths)),
        scratch_shapes=[
            pltpu.VMEM(guess.shape, F32),
            pltpu.VMEM(left.shape, BF16),
            pltpu.VMEM(site.shape, BF16),
            pltpu.SemaphoreType.DMA((rows // TILE + 3,)),
        ],
        compiler_params=params(),
        cost_estimate=cost(4 * guess.size, 6 * guess.size),
        name="prepare",
    )(bond_rank, *[pltpu.with_memory_space_constraint(a, pltpu.HBM) for a in (guess, left, right_env[0], site)])

    chunk_hops = [around(chunk) for chunk in chunks]
    here_pieces = [x_own, to_sibling(x_own)]
    here_spots = ((0, 0, 0), (0, 1, 0))
    lefts = around(left_packed)
    shift = [(i + 1, i) for i in range(segments - 1)]
    received = lax.ppermute(right_packed, "seg", shift)

    size = states * TILE

    def spread(block):
        return pl.pallas_call(
            spread_kernel,
            out_shape=(jax.ShapeDtypeStruct((terms * size, size), BF16), tile),
            in_specs=[vmem],
            out_specs=(vmem, vmem),
            compiler_params=params(),
            cost_estimate=cost(2 * terms * size * size * width, 2 * terms * size * size),
            name="spread_site",
        )(block)

    kron_own, _ = spread(chunks[0])

    whole = (states, width, width)
    whole_bf = jax.ShapeDtypeStruct(whole, BF16)
    whole_f32 = jax.ShapeDtypeStruct(whole, F32)
    rotated = (terms, states, width, width)
    rotated_bf = jax.ShapeDtypeStruct(rotated, BF16)
    square = pltpu.VMEM((terms, width, width), BF16)
    chip_rows = CORES * rows
    stage_flops = 2 * terms * states * width * width * width

    mix_scratch = [
        pltpu.VMEM((states, terms * chip_rows, width), BF16),
        pltpu.VMEM((width, terms * chip_rows), BF16),
    ]
    chip_rotated = (terms, states, chip_rows, width)
    chip_cost = cost(3 * stage_flops * chip_rows / width, 8 * states * width * width)
    rotated_own = pl.pallas_call(
        functools.partial(rotate_own_kernel, here_spots, rows),
        out_shape=jax.ShapeDtypeStruct(chip_rotated, BF16),
        in_specs=[vmem] * 3,
        out_specs=vmem,
        compiler_params=params(),
        cost_estimate=chip_cost,
        name="rotate_own",
    )(*here_pieces, kron_own)
    def there(hop, before):
        spots = tuple(spot for spot in far_spots if spot[0] == hop)
        pieces = [piece for spot, piece in zip(far_spots, far_pieces) if spot[0] == hop]
        return pl.pallas_call(
            functools.partial(there_kernel, spots, rows, chips),
            out_shape=whole_f32,
            in_specs=[vmem] * (len(pieces) + 4),
            out_specs=vmem,
            scratch_shapes=[pltpu.VMEM(chip_rotated, BF16)] + mix_scratch,
            compiler_params=params(),
            cost_estimate=chip_cost,
            name="apply_rows_there",
        )(*pieces, left, right, kron_own, before)

    def rotate(kron):
        return pl.pallas_call(
            functools.partial(rotate_kernel, here_spots, rows, chips),
            out_shape=(rotated_bf, whole_bf),
            in_specs=[vmem] * 3,
            out_specs=(vmem, vmem),
            scratch_shapes=[pltpu.SemaphoreType.DMA((CORES,))],
            compiler_params=params(),
            cost_estimate=chip_cost,
            name="rotate_here",
        )(*here_pieces, kron)

    firsts, rotated_own = lax.optimization_barrier((chunk_hops[0][1:], rotated_own))
    kron, norm_far = spread(firsts[0])
    turned = rotate(kron)
    received, turned = lax.optimization_barrier((received, turned))
    packed = jnp.where(lax.axis_index("seg") == segments - 1, right_packed, received)
    rights = around(packed)
    partial, right = pl.pallas_call(
        functools.partial(here_kernel, chips),
        out_shape=(whole_f32, jax.ShapeDtypeStruct(left.shape, BF16)),
        in_specs=[vmem] * 3,
        out_specs=(vmem, vmem),
        scratch_shapes=mix_scratch,
        compiler_params=params(),
        cost_estimate=chip_cost,
        name="apply_rows_here",
    )(rotated_own, left, packed)

    far_pieces = []
    far_spots = ()
    for n, start in enumerate(starts):
        if n == 0:
            crossed = firsts
        elif n + 1 < len(starts):
            crossed, turned = lax.optimization_barrier((chunk_hops[n][1:], turned))
        else:
            crossed, partial = lax.optimization_barrier((chunk_hops[n][1:], partial))
        for hop, block in zip(hops[1:], crossed):
            far_pieces += [block, to_sibling(block)]
            far_spots += ((hop, 0, start), (hop, 1, start))
    for hop in hops[1:]:
        partial = there(hop, partial)
    norms = [norm_part]
    for hop in hops[1:]:
        if hop > 1:
            block, partial = lax.optimization_barrier((firsts[hop - 1], partial))
            kron, norm_far = spread(block)
            turned = rotate(kron)
        norms.append(norm_far)
        left_far, partial = lax.optimization_barrier((lefts[hop], partial))
        mixed, _, vector = pl.pallas_call(
            functools.partial(lefts_kernel, far_spots, rows, chips),
            out_shape=(jax.ShapeDtypeStruct((states, width, terms * width), BF16), rotated_bf, whole_bf),
            in_specs=[vmem] * (len(far_pieces) + 1) + [anywhere] * 2 + [vmem],
            out_specs=(vmem,) * 3,
            scratch_shapes=[square, pltpu.SemaphoreType.DMA((len(far_pieces),))],
            input_output_aliases={len(far_pieces) + 1: 1, len(far_pieces) + 2: 2},
            compiler_params=params(),
            cost_estimate=cost(stage_flops, 12 * states * width * width),
            name="received_lefts",
        )(*far_pieces, kron, *turned, left_far)
        last = hop == hops[-1]
        stats = norms if last else norms[:1]
        right_far = rights[hop]
        parts = []
        bounds = (0, states // 2, states) if last else (0, states)
        for start, stop in zip(bounds[:-1], bounds[1:]):
            outs = [jax.ShapeDtypeStruct((stop - start, width, width), BF16 if last else F32), tile]
            part, stat, *unpacked = pl.pallas_call(
                functools.partial(rights_kernel, start, stop),
                out_shape=tuple(outs + ([jax.ShapeDtypeStruct(left.shape, BF16)] if start == 0 else [])),
                in_specs=[vmem] * (4 + len(stats)),
                out_specs=(vmem,) * (3 if start == 0 else 2),
                compiler_params=params(),
                cost_estimate=cost(stage_flops / 2, 12 * states * width * width),
                name="received_rights",
            )(right_far, mixed, vector, partial, *stats)
            stats = [stat]
            if unpacked:
                right_far = unpacked[0]
            parts.append(part)
        if not last:
            partial = parts[0]
    low = pl.pallas_call(
        add_kernel,
        out_shape=jax.ShapeDtypeStruct(parts[0].shape, F32),
        in_specs=[vmem] * 2,
        out_specs=vmem,
        compiler_params=params(),
        cost_estimate=cost(parts[0].size, 8 * parts[0].size),
        name="add_low_half",
    )(parts[0], to_sibling(parts[0]))
    halves = [low, parts[1], to_sibling(parts[1])]
    stat_other = to_sibling(stat)

    share = pl.pallas_call(
        functools.partial(second_kernel, scale, members),
        out_shape=tile,
        in_specs=[smem] + [vmem] * 9,
        out_specs=vmem,
        scratch_shapes=[
            pltpu.VMEM(whole, BF16),
            pltpu.VMEM(rotated, BF16),
            pltpu.VMEM(rotated, BF16),
        ],
        compiler_params=params(),
        cost_estimate=cost(3 * stage_flops, 6 * states * width * width),
        name="apply_residual",
    )(bond_rank, stat, stat_other, *halves, vector, left, right, kron_own)
    shares = everyone(share)

    local = jax.ShapeDtypeStruct((rows, states, width), F32)
    vector_own, residual_own = pl.pallas_call(
        functools.partial(own_rows_kernel, scale),
        out_shape=(local, local),
        in_specs=[smem] + [vmem] * 6,
        out_specs=(vmem, vmem),
        compiler_params=params(),
        cost_estimate=cost(8 * guess.size, 16 * guess.size),
        name="own_rows",
    )(bond_rank, guess, stat, stat_other, *halves)

    ritz, energy = pl.pallas_call(
        finish_kernel,
        out_shape=(local, jax.ShapeDtypeStruct((1,), F32)),
        in_specs=[vmem] * (2 + members),
        out_specs=(vmem, smem),
        compiler_params=params(),
        cost_estimate=cost(3 * guess.size, 12 * guess.size),
        name="finish",
    )(vector_own, residual_own, *shares)
    return (ritz[None], energy)


def solution(mesh):
    in_specs = (
        P("seg", "term", None, None),
        P("seg", "term", None, None),
        P("seg", "term", None, None),
        P("seg", "term", None, None),
        P("seg"),
    )
    out_specs = (P("seg", "term", None, None), P("seg"))
    return jax.shard_map(shards, mesh=mesh, in_specs=in_specs, out_specs=out_specs, check_vma=False)
```

```python
import functools

import jax
import jax.numpy as jnp
from jax import lax
from jax.experimental import pallas as pl
from jax.experimental.pallas import tpu as pltpu
from jax.sharding import PartitionSpec as P

epsilon = 1e-06
CORES = 2
TILE = 16
UNROLL = 8
GROUP = 8
VMEM_LIMIT = 20 * 1024 * 1024
F32 = jnp.float32
BF16 = jnp.bfloat16

vmem = pl.BlockSpec(memory_space=pltpu.VMEM)
smem = pl.BlockSpec(memory_space=pltpu.SMEM)
anywhere = pl.BlockSpec(memory_space=pl.ANY)
in_hbm = pl.BlockSpec(memory_space=pltpu.HBM)


def params():
    return pltpu.CompilerParams(vmem_limit_bytes=VMEM_LIMIT)


def cost(flops, moved):
    return pl.CostEstimate(flops=int(flops) // 100, bytes_accessed=int(moved) // 100, transcendentals=0)


def fold(values, width):
    return jnp.sum(values.reshape(values.size // (8 * width), 8, width), axis=0)


def prepare_kernel(
    starts,
    rank_ref,
    guess_in,
    left_in,
    right_in,
    site_in,
    x_ref,
    norm_ref,
    keep_ref,
    left_packed_ref,
    right_packed_ref,
    left_ref,
    *refs,
):
    chunk_refs = refs[: len(starts)]
    guess_ref, right_ref, site_ref, sems = refs[len(starts) :]
    rows, states, width = guess_ref.shape
    terms = left_ref.shape[0]
    half = width // 2
    parts = [pl.ds(n, TILE) for n in range(0, rows, TILE)]
    sources = [guess_in.at[part] for part in parts] + [site_in, right_in, left_in]
    targets = [guess_ref.at[part] for part in parts] + [site_ref, right_ref, left_ref]
    copies = [
        pltpu.make_async_copy(source, target, sems.at[n])
        for n, (source, target) in enumerate(zip(sources, targets))
    ]
    for copy in copies:
        copy.start()
    column = lax.broadcasted_iota(jnp.int32, (1, width), 1)
    keep = (column < rank_ref[...]).astype(F32)
    keep_ref[...] = jnp.broadcast_to(keep, keep_ref.shape)
    keep = keep[None]
    squares = jnp.zeros((8, width), F32)
    for n, part in enumerate(parts):
        copies[n].wait()
        masked = guess_ref[part] * keep
        squares = squares + fold(masked * masked, width)
        turned = jnp.swapaxes(masked, 0, 1).astype(BF16)
        x_ref[:, part, :] = turned
        chunk = max(c for c, start in enumerate(starts) if start <= n * TILE)
        at = n * TILE - starts[chunk]
        chunk_refs[chunk][0:states, at : at + TILE, :] = turned
    total = jnp.sum(squares)
    norm_ref[...] = jnp.full(norm_ref.shape, total, F32)
    copies[-3].wait()
    line = lax.broadcasted_iota(jnp.int32, (TILE, width), 0)
    lane = lax.broadcasted_iota(jnp.int32, (TILE, width), 1)
    norm = jnp.full((TILE, width), total, F32)
    extra = jnp.zeros((TILE, width), F32)
    for n in range(3):
        part = norm.astype(BF16).astype(F32)
        norm = norm - part
        extra = jnp.where((line == n) & (lane >= half), part, extra)
    for k in range(terms):
        place_at = (lane == line + k * TILE).astype(BF16)
        extra = extra + jnp.dot(site_ref[k], place_at, preferred_element_type=F32)
    chunk_refs[0][states, 0:TILE, :] = extra.astype(BF16)
    for copy, block_ref, packed_ref in zip(copies[-2:], (right_ref, left_ref), (right_packed_ref, left_packed_ref)):
        copy.wait()
        for k in range(terms):
            diagonal = pack_symmetric(block_ref, k, packed_ref)
            packed_ref[k, width : width + TILE, :] = jnp.broadcast_to(diagonal, (TILE, half)).astype(BF16)


def triangle(half):
    row = lax.broadcasted_iota(jnp.int32, (half, half), 0)
    col = lax.broadcasted_iota(jnp.int32, (half, half), 1)
    return row, col


def pack_symmetric(block_ref, k, out_ref):
    width = block_ref.shape[1]
    half = width // 2
    row, col = triangle(half)
    upper = block_ref[k, 0:half, 0:half].astype(F32)
    lower = block_ref[k, half:width, half:width].astype(F32)
    out_ref[k, 0:half, :] = block_ref[k, 0:half, half:width]
    out_ref[k, half:width, :] = jnp.where(row <= col, upper, lower).astype(BF16)
    return jnp.sum(jnp.where(row == col, lower, 0.0), axis=0, keepdims=True)


def unpack_symmetric(packed_ref, full_ref):
    terms, width, _ = full_ref.shape
    half = width // 2
    row, col = triangle(half)
    for k in range(terms):
        corner = packed_ref[k, 0:half, :]
        mixed = packed_ref[k, half:width, :].astype(F32)
        diagonal = packed_ref[k, width : width + TILE, :].astype(F32)[0:1]
        turned = mixed.T
        full_ref[k, 0:half, 0:half] = jnp.where(row <= col, mixed, turned).astype(BF16)
        full_ref[k, 0:half, half:width] = corner
        full_ref[k, half:width, 0:half] = corner.astype(F32).T.astype(BF16)
        full_ref[k, half:width, half:width] = jnp.where(
            row > col, mixed, jnp.where(row == col, diagonal, turned)
        ).astype(BF16)


def spread_kernel(chunk_ref, kron_ref, norm_ref):
    width = chunk_ref.shape[2]
    half = width // 2
    size = kron_ref.shape[1]
    terms = kron_ref.shape[0] // size
    states = size // TILE
    tile = chunk_ref[states, 0:TILE, :]
    lines = tile.astype(F32)
    norm = lines[0:1, half:width] + lines[1:2, half:width] + lines[2:3, half:width]
    norm_ref[...] = jnp.broadcast_to(jnp.concatenate([norm, norm], axis=1), norm_ref.shape)
    row_state = lax.broadcasted_iota(jnp.int32, (size, states), 0) // TILE
    pick = (row_state == lax.broadcasted_iota(jnp.int32, (size, states), 1)).astype(BF16)
    tall = jnp.dot(pick, tile, preferred_element_type=F32).astype(BF16)
    lane = lax.broadcasted_iota(jnp.int32, (width, size), 0)
    col_state = lax.broadcasted_iota(jnp.int32, (width, size), 1) // TILE
    same = (
        lax.broadcasted_iota(jnp.int32, (size, size), 0) % TILE
        == lax.broadcasted_iota(jnp.int32, (size, size), 1) % TILE
    )
    for k in range(terms):
        pick_t = (lane == col_state + k * TILE).astype(BF16)
        full = jnp.dot(tall, pick_t, preferred_element_type=F32)
        kron_ref[k * size : (k + 1) * size, :] = jnp.where(same, full, 0.0).astype(BF16)


def mix_sites(source_ref, kron_ref, rotated_ref, base, unroll):
    terms, states, _, width = rotated_ref.shape
    rows = source_ref.shape[1]

    def step(i, carry):
        at = pl.multiple_of(i * TILE, TILE)
        to = pl.multiple_of(base + i * TILE, TILE)
        stack = source_ref[0:states, pl.ds(at, TILE), :].reshape(states * TILE, width)
        turned = jnp.dot(kron_ref[...], stack, preferred_element_type=F32).astype(BF16)
        rotated_ref[:, :, pl.ds(to, TILE), :] = turned.reshape(terms, states, TILE, width)
        return carry

    lax.fori_loop(0, rows // TILE, step, 0, unroll=min(unroll, rows // TILE))


def summed(values):
    while len(values) > 1:
        values = [values[n] + values[n + 1] for n in range(0, len(values), 2)]
    return values[0]


def place(hop, chips):
    me = lax.axis_index("term")
    chip = (me // CORES - hop + chips) % chips
    return chip, me % CORES


def mix_pieces(spots, rows, pieces, kron_ref, rotated_ref):
    _, core = place(0, 1)
    for (_, flip, offset), piece in zip(spots, pieces):
        at = (core if flip == 0 else 1 - core) * rows + offset
        mix_sites(piece, kron_ref, rotated_ref, at, UNROLL)


def rotate_own_kernel(spots, rows, chips, *refs):
    pieces = refs[: len(spots)]
    kron_ref, left_ref, rotated_ref, columns_ref = refs[len(spots) :]
    terms, states, chip_rows, width = rotated_ref.shape
    mix_pieces(spots, rows, pieces, kron_ref, rotated_ref)
    blocks = []
    for hop in range(chips):
        chip, _ = place(hop, chips)
        at = pl.multiple_of(chip * chip_rows, TILE)
        blocks += [left_ref[k, pl.ds(at, chip_rows), :] for k in range(terms)]
    columns_ref[...] = jnp.concatenate(blocks, axis=0).astype(F32).T.astype(BF16)


def turn(right_ref, rotated_ref, turned_ref):
    terms, states, chip_rows, width = rotated_ref.shape
    for k in range(terms):
        for n in range(0, states, 8):
            source = rotated_ref[k, n : n + 8].reshape(8 * chip_rows, width)
            turned = jnp.dot(source, right_ref[k], preferred_element_type=F32).astype(BF16)
            turned_ref[n : n + 8, k * chip_rows : (k + 1) * chip_rows, :] = turned.reshape(8, chip_rows, width)


def here_kernel(rotated_ref, packed_ref, turned_ref, right_ref):
    unpack_symmetric(packed_ref, right_ref)
    turn(right_ref, rotated_ref, turned_ref)


def there_kernel(spots, rows, *refs):
    count = len(spots)
    right_ref, kron_ref, turned_ref, rotated_ref = refs[count:]
    mix_pieces(spots, rows, refs[:count], kron_ref, rotated_ref)
    turn(right_ref, rotated_ref, turned_ref)


def last_kernel(spots, rows, *refs):
    count = len(spots)
    right_ref, kron_ref, columns_ref = refs[count : count + 3]
    out_ref, rotated_ref, turned_ref = refs[-3:]
    there_kernel(spots, rows, *refs[:count], right_ref, kron_ref, turned_ref, rotated_ref)
    blocks = list(refs[count + 3 : -3]) + [turned_ref]

    def lefts(p, carry):
        stack = jnp.concatenate([block[p] for block in blocks], axis=0)
        out_ref[p] = jnp.dot(columns_ref[...], stack, preferred_element_type=F32)
        return carry

    lax.fori_loop(0, out_ref.shape[0], lefts, 0, unroll=UNROLL)


def rotate_kernel(spots, rows, chips, *refs):
    pieces = refs[: len(spots)]
    kron_ref = refs[len(spots)]
    rotated_ref, whole_ref, sems = refs[-3:]
    states = whole_ref.shape[0]
    copies = []
    bases = []
    for n, ((hop, flip, offset), piece) in enumerate(zip(spots, pieces)):
        chip, core = place(hop, chips)
        at = pl.multiple_of((chip * CORES + (core if flip == 0 else 1 - core)) * rows + offset, TILE)
        bases.append(at)
        target = whole_ref.at[:, pl.ds(at, piece.shape[1]), :]
        copies.append(pltpu.make_async_copy(piece.at[0:states], target, sems.at[n]))
        copies[-1].start()
    for at, piece in zip(bases, pieces):
        mix_sites(piece, kron_ref, rotated_ref, at, UNROLL)
    for copy in copies:
        copy.wait()


def lefts_kernel(spots, rows, chips, *refs):
    count = len(spots)
    packed_ref = refs[count + 3]
    mixed_ref, rotated_ref, whole_ref, left_ref, sems = refs[-5:]
    terms, states, width, _ = rotated_ref.shape
    unpack_symmetric(packed_ref, left_ref)
    rotate_kernel(spots, rows, chips, *refs[: count + 1], rotated_ref, whole_ref, sems)

    def lefts(p, carry):
        for k in range(terms):
            mixed = jnp.dot(left_ref[k], rotated_ref[k, p], preferred_element_type=F32)
            mixed_ref[p, :, k * width : (k + 1) * width] = mixed.astype(BF16)
        return carry

    lax.fori_loop(0, states, lefts, 0, unroll=UNROLL)


def rights_kernel(start, stop, packed_ref, mixed_ref, whole_ref, before_ref, *refs):
    if start == 0:
        stats = refs[:-3]
        partial_ref, stat_ref, right_ref = refs[-3:]
        unpack_symmetric(packed_ref, right_ref)
    else:
        stats = refs[:-2]
        partial_ref, stat_ref = refs[-2:]
        right_ref = packed_ref
    states, width, _ = whole_ref.shape
    terms = right_ref.shape[0]

    def rights(n, total):
        at = n * GROUP
        rows = mixed_ref[pl.ds(start + at, GROUP)].reshape(GROUP * width, terms * width)
        stacked = right_ref[...].reshape(terms * width, width)
        image = jnp.dot(rows, stacked, preferred_element_type=F32).reshape(GROUP, width, width)
        part = (before_ref[pl.ds(start + at, GROUP)].astype(F32) + image).astype(partial_ref.dtype)
        partial_ref[pl.ds(at, GROUP)] = part
        held = whole_ref[pl.ds(start + at, GROUP)].astype(F32)
        return total + fold(held * part.astype(F32), width)

    total = lax.fori_loop(0, (stop - start) // GROUP, rights, jnp.zeros((8, width), F32))
    stat_ref[...] = functools.reduce(jnp.add, [stat[...] for stat in stats])
    product = jnp.full((1, width), jnp.sum(total), F32)
    stat_ref[0:1, :] = product if start == 0 else stats[0][0:1, :] + product


def scales(keep_ref, mine_ref, theirs_ref, scale, width):
    inverse = lax.rsqrt((mine_ref[1:2, :] + theirs_ref[1:2, :]) * scale + epsilon)
    rayleigh = (mine_ref[0:1, :] + theirs_ref[0:1, :]) * (inverse * inverse * scale)
    return inverse, rayleigh, keep_ref[0:1, :] * inverse


def add_kernel(mine_ref, other_ref, sum_ref):
    sum_ref[...] = mine_ref[...].astype(F32) + other_ref[...].astype(F32)


def second_kernel(
    scale,
    members,
    keep_ref,
    mine_ref,
    theirs_ref,
    low_ref,
    high_ref,
    high_other_ref,
    whole_ref,
    left_ref,
    right_ref,
    kron_ref,
    out_ref,
    res_ref,
    rotated_ref,
    mixed_ref,
):
    terms, states, width, _ = rotated_ref.shape
    inverse, rayleigh, row_scale = scales(keep_ref, mine_ref, theirs_ref, scale, width)
    back = rayleigh * inverse

    square = jnp.zeros((8, width), F32)
    for start, halves in ((0, (low_ref,)), (states // 2, (high_ref, high_other_ref))):

        def lefts(n, total):
            p = start + n
            sigma = functools.reduce(jnp.add, [half[n].astype(F32) for half in halves]) * row_scale
            residual = sigma - back * whole_ref[p].astype(F32)
            rounded = residual.astype(BF16)
            res_ref[p] = rounded
            mixed = jnp.dot(
                left_ref[...].reshape(terms * width, width), rounded, preferred_element_type=F32
            ).astype(BF16)
            for k in range(terms):
                mixed_ref[k, p] = mixed[k * width : (k + 1) * width]
            return total + fold(residual * residual, width)

        square = lax.fori_loop(0, states // 2, lefts, square, unroll=UNROLL)
    mix_sites(res_ref, kron_ref, rotated_ref, 0, 2 * UNROLL)

    def rights(n, total):
        at = n * GROUP
        for k in range(terms):
            turned = rotated_ref[k, pl.ds(at, GROUP)].reshape(GROUP * width, width)
            image = jnp.dot(turned, right_ref[k], preferred_element_type=F32)
            held = mixed_ref[k, pl.ds(at, GROUP)].reshape(GROUP * width, width).astype(F32)
            total = total + fold(held * image, width)
        return total

    cross = lax.fori_loop(0, states // GROUP, rights, jnp.zeros((8, width), F32))
    share = 1.0 / members
    out_ref[0:1, :] = rayleigh * share
    out_ref[1:2, :] = jnp.full((1, width), jnp.sum(square) * (scale * share), F32)
    out_ref[2:3, :] = jnp.full((1, width), jnp.sum(cross) * scale, F32)
    out_ref[3:8, :] = jnp.zeros((5, width), F32)


def own_rows_kernel(scale, keep_ref, guess_ref, mine_ref, theirs_ref, *refs):
    low_ref, high_ref, high_other_ref, vector_ref, residual_ref = refs
    rows, states, width = guess_ref.shape
    inverse, rayleigh, row_scale = scales(keep_ref, mine_ref, theirs_ref, scale, width)
    own = pl.ds(pl.multiple_of(lax.axis_index("term") * rows, TILE), rows)
    vector = guess_ref[...] * row_scale[None]
    vector_ref[...] = vector
    high = high_ref[:, own, :].astype(F32) + high_other_ref[:, own, :].astype(F32)
    sigma = jnp.concatenate([low_ref[:, own, :], high], axis=0) * row_scale[None]
    residual_ref[...] = jnp.swapaxes(sigma, 0, 1) - rayleigh[None] * vector


def finish_kernel(vector_ref, residual_ref, *refs):
    shares = refs[:-2]
    ritz_ref, energy_ref = refs[-2:]
    stat = summed([share[...] for share in shares])
    rayleigh = stat[0:1, :]
    res_sq = stat[1:2, :]
    res_var = res_sq + epsilon
    curvature = stat[2:3, :] / res_var
    res_scale = jnp.sqrt(res_var)
    coupling = res_sq / res_scale
    half_gap = 0.5 * (rayleigh - curvature)
    energy = 0.5 * (rayleigh + curvature) - jnp.sqrt(half_gap * half_gap + coupling * coupling)
    coeff_new = energy - rayleigh
    coeff_norm = jnp.sqrt(coupling * coupling + coeff_new * coeff_new + epsilon)
    old = coupling / coeff_norm
    new = coeff_new / (coeff_norm * res_scale)
    ritz_ref[...] = old[None] * vector_ref[...] + new[None] * residual_ref[...]
    energy_ref[0] = energy[0, 0]


def shards(wave_guess, left_env, right_env, site_ops, bond_rank):
    guess = wave_guess[0]
    left = left_env[0]
    site = site_ops[0]
    rows, states, width = guess.shape
    terms = left.shape[0]
    members = lax.axis_size("term")
    chips = members // CORES
    segments = lax.axis_size("seg")
    scale = 1.0 / float(rows * members * states * width)
    hops = tuple(range(chips))

    def to_sibling(block):
        return lax.ppermute(block, "term", [(i, i ^ 1) for i in range(members)])

    def to_next_chip(block):
        return lax.ppermute(block, "term", [(i, (i + CORES) % members) for i in range(members)])

    def around(block):
        found = [block]
        for _ in range(chips - 1):
            found.append(to_next_chip(found[-1]))
        return found

    def everyone(block):
        others = [
            lax.ppermute(block, "term", [(i, i ^ bits) for i in range(members)]) for bits in range(1, members)
        ]
        return [block] + others

    tile = jax.ShapeDtypeStruct((8, width), F32)
    half = width // 2
    packed_shape = jax.ShapeDtypeStruct((terms, width + TILE, half), BF16)
    starts = (0, rows - 2 * TILE, rows - TILE) if rows >= 4 * TILE else (0,)
    lengths = [stop - start for start, stop in zip(starts, starts[1:] + (rows,))]
    x_own, norm_part, keep, left_packed, right_packed, left, *chunks = pl.pallas_call(
        functools.partial(prepare_kernel, starts),
        out_shape=(
            jax.ShapeDtypeStruct((states, rows, width), BF16),
            tile,
            tile,
            packed_shape,
            packed_shape,
            jax.ShapeDtypeStruct(left.shape, BF16),
            *[
                jax.ShapeDtypeStruct((states + (n == 0), length, width), BF16)
                for n, length in enumerate(lengths)
            ],
        ),
        in_specs=[vmem] + [in_hbm] * 4,
        out_specs=(vmem,) * (6 + len(lengths)),
        scratch_shapes=[
            pltpu.VMEM(guess.shape, F32),
            pltpu.VMEM(left.shape, BF16),
            pltpu.VMEM(site.shape, BF16),
            pltpu.SemaphoreType.DMA((rows // TILE + 3,)),
        ],
        compiler_params=params(),
        cost_estimate=cost(4 * guess.size, 6 * guess.size),
        name="prepare",
    )(bond_rank.reshape(1, 1), *[pltpu.with_memory_space_constraint(a, pltpu.HBM) for a in (guess, left, right_env[0], site)])

    chunk_hops = [around(chunk) for chunk in chunks]
    here_pieces = [x_own, to_sibling(x_own)]
    here_spots = ((0, 0, 0), (0, 1, 0))
    lefts = around(left_packed)
    shift = [(i + 1, i) for i in range(segments - 1)]
    received = lax.ppermute(right_packed, "seg", shift)

    size = states * TILE

    def spread(block):
        return pl.pallas_call(
            spread_kernel,
            out_shape=(jax.ShapeDtypeStruct((terms * size, size), BF16), tile),
            in_specs=[vmem],
            out_specs=(vmem, vmem),
            compiler_params=params(),
            cost_estimate=cost(2 * terms * size * size * width, 2 * terms * size * size),
            name="spread_site",
        )(block)

    kron_own, _ = spread(chunks[0])

    whole = (states, width, width)
    whole_bf = jax.ShapeDtypeStruct(whole, BF16)
    whole_f32 = jax.ShapeDtypeStruct(whole, F32)
    rotated = (terms, states, width, width)
    rotated_bf = jax.ShapeDtypeStruct(rotated, BF16)
    square = pltpu.VMEM((terms, width, width), BF16)
    chip_rows = CORES * rows
    stage_flops = 2 * terms * states * width * width * width

    chip_rotated = (terms, states, chip_rows, width)
    chip_turned = jax.ShapeDtypeStruct((states, terms * chip_rows, width), BF16)
    chip_cost = cost(3 * stage_flops * chip_rows / width, 8 * states * width * width)
    rotated_own, columns = pl.pallas_call(
        functools.partial(rotate_own_kernel, here_spots, rows, chips),
        out_shape=(
            jax.ShapeDtypeStruct(chip_rotated, BF16),
            jax.ShapeDtypeStruct((width, terms * width), BF16),
        ),
        in_specs=[vmem] * 4,
        out_specs=(vmem, vmem),
        compiler_params=params(),
        cost_estimate=chip_cost,
        name="rotate_own",
    )(*here_pieces, kron_own, left)

    def there(hop, before):
        spots = tuple(spot for spot in far_spots if spot[0] == hop)
        pieces = [piece for spot, piece in zip(far_spots, far_pieces) if spot[0] == hop]
        last = hop == hops[-1]
        return pl.pallas_call(
            functools.partial(last_kernel if last else there_kernel, spots, rows),
            out_shape=whole_f32 if last else chip_turned,
            in_specs=[vmem] * (len(pieces) + 2 + (1 + len(before) if last else 0)),
            out_specs=vmem,
            scratch_shapes=[pltpu.VMEM(chip_rotated, BF16)]
            + ([pltpu.VMEM(chip_turned.shape, BF16)] if last else []),
            compiler_params=params(),
            cost_estimate=chip_cost,
            name="apply_rows_there",
        )(*pieces, right, kron_own, *([columns] + before if last else []))

    def rotate(kron):
        return pl.pallas_call(
            functools.partial(rotate_kernel, here_spots, rows, chips),
            out_shape=(rotated_bf, whole_bf),
            in_specs=[vmem] * 3,
            out_specs=(vmem, vmem),
            scratch_shapes=[pltpu.SemaphoreType.DMA((CORES,))],
            compiler_params=params(),
            cost_estimate=chip_cost,
            name="rotate_here",
        )(*here_pieces, kron)

    firsts, rotated_own = lax.optimization_barrier((chunk_hops[0][1:], rotated_own))
    kron, norm_far = spread(firsts[0])
    turned = rotate(kron)
    received, turned = lax.optimization_barrier((received, turned))
    packed = jnp.where(lax.axis_index("seg") == segments - 1, right_packed, received)
    rights = around(packed)
    turned_own, right = pl.pallas_call(
        here_kernel,
        out_shape=(chip_turned, jax.ShapeDtypeStruct(left.shape, BF16)),
        in_specs=[vmem] * 2,
        out_specs=(vmem, vmem),
        compiler_params=params(),
        cost_estimate=chip_cost,
        name="apply_rows_here",
    )(rotated_own, packed)
    far_pieces = []
    far_spots = ()
    for n, start in enumerate(starts):
        if n == 0:
            crossed = firsts
        elif n + 1 < len(starts):
            crossed, turned = lax.optimization_barrier((chunk_hops[n][1:], turned))
        else:
            crossed, turned_own = lax.optimization_barrier((chunk_hops[n][1:], turned_own))
        for hop, block in zip(hops[1:], crossed):
            far_pieces += [block, to_sibling(block)]
            far_spots += ((hop, 0, start), (hop, 1, start))
    parts = [turned_own]
    for hop in hops[1:]:
        parts.append(there(hop, parts))
    partial = parts[-1]
    norms = [norm_part]
    for hop in hops[1:]:
        if hop > 1:
            block, partial = lax.optimization_barrier((firsts[hop - 1], partial))
            kron, norm_far = spread(block)
            turned = rotate(kron)
        norms.append(norm_far)
        left_far, partial = lax.optimization_barrier((lefts[hop], partial))
        mixed, _, vector = pl.pallas_call(
            functools.partial(lefts_kernel, far_spots, rows, chips),
            out_shape=(jax.ShapeDtypeStruct((states, width, terms * width), BF16), rotated_bf, whole_bf),
            in_specs=[vmem] * (len(far_pieces) + 1) + [anywhere] * 2 + [vmem],
            out_specs=(vmem,) * 3,
            scratch_shapes=[square, pltpu.SemaphoreType.DMA((len(far_pieces),))],
            input_output_aliases={len(far_pieces) + 1: 1, len(far_pieces) + 2: 2},
            compiler_params=params(),
            cost_estimate=cost(stage_flops, 12 * states * width * width),
            name="received_lefts",
        )(*far_pieces, kron, *turned, left_far)
        last = hop == hops[-1]
        stats = norms if last else norms[:1]
        right_far = rights[hop]
        parts = []
        bounds = (0, states // 2, states) if last else (0, states)
        for start, stop in zip(bounds[:-1], bounds[1:]):
            outs = [jax.ShapeDtypeStruct((stop - start, width, width), BF16 if last else F32), tile]
            part, stat, *unpacked = pl.pallas_call(
                functools.partial(rights_kernel, start, stop),
                out_shape=tuple(outs + ([jax.ShapeDtypeStruct(left.shape, BF16)] if start == 0 else [])),
                in_specs=[vmem] * (4 + len(stats)),
                out_specs=(vmem,) * (3 if start == 0 else 2),
                compiler_params=params(),
                cost_estimate=cost(stage_flops / 2, 12 * states * width * width),
                name="received_rights",
            )(right_far, mixed, vector, partial, *stats)
            stats = [stat]
            if unpacked:
                right_far = unpacked[0]
            parts.append(part)
        if not last:
            partial = parts[0]
    low = pl.pallas_call(
        add_kernel,
        out_shape=jax.ShapeDtypeStruct(parts[0].shape, F32),
        in_specs=[vmem] * 2,
        out_specs=vmem,
        compiler_params=params(),
        cost_estimate=cost(parts[0].size, 8 * parts[0].size),
        name="add_low_half",
    )(parts[0], to_sibling(parts[0]))
    halves = [low, parts[1], to_sibling(parts[1])]
    stat_other = to_sibling(stat)

    share = pl.pallas_call(
        functools.partial(second_kernel, scale, members),
        out_shape=tile,
        in_specs=[vmem] * 10,
        out_specs=vmem,
        scratch_shapes=[
            pltpu.VMEM(whole, BF16),
            pltpu.VMEM(rotated, BF16),
            pltpu.VMEM(rotated, BF16),
        ],
        compiler_params=params(),
        cost_estimate=cost(3 * stage_flops, 6 * states * width * width),
        name="apply_residual",
    )(keep, stat, stat_other, *halves, vector, left, right, kron_own)
    shares = everyone(share)

    local = jax.ShapeDtypeStruct((rows, states, width), F32)
    vector_own, residual_own = pl.pallas_call(
        functools.partial(own_rows_kernel, scale),
        out_shape=(local, local),
        in_specs=[vmem] * 7,
        out_specs=(vmem, vmem),
        compiler_params=params(),
        cost_estimate=cost(8 * guess.size, 16 * guess.size),
        name="own_rows",
    )(keep, guess, stat, stat_other, *halves)

    ritz, energy = pl.pallas_call(
        finish_kernel,
        out_shape=(local, jax.ShapeDtypeStruct((1,), F32)),
        in_specs=[vmem] * (2 + members),
        out_specs=(vmem, smem),
        compiler_params=params(),
        cost_estimate=cost(3 * guess.size, 12 * guess.size),
        name="finish",
    )(vector_own, residual_own, *shares)
    return (ritz[None], energy)


def solution(mesh):
    in_specs = (
        P("seg", "term", None, None),
        P("seg", "term", None, None),
        P("seg", "term", None, None),
        P("seg", "term", None, None),
        P("seg"),
    )
    out_specs = (P("seg", "term", None, None), P("seg"))
    return jax.shard_map(shards, mesh=mesh, in_specs=in_specs, out_specs=out_specs, check_vma=False)
```

```python
import functools

import jax
import jax.numpy as jnp
from jax import lax
from jax.experimental import pallas as pl
from jax.experimental.pallas import tpu as pltpu
from jax.sharding import PartitionSpec as P

epsilon = 1e-06
CORES = 2
TILE = 16
UNROLL = 8
GROUP = 8
VMEM_LIMIT = 20 * 1024 * 1024
F32 = jnp.float32
BF16 = jnp.bfloat16

vmem = pl.BlockSpec(memory_space=pltpu.VMEM)
smem = pl.BlockSpec(memory_space=pltpu.SMEM)
anywhere = pl.BlockSpec(memory_space=pl.ANY)
in_hbm = pl.BlockSpec(memory_space=pltpu.HBM)


def params():
    return pltpu.CompilerParams(vmem_limit_bytes=VMEM_LIMIT)


def cost(flops, moved):
    return pl.CostEstimate(flops=int(flops) // 100, bytes_accessed=int(moved) // 100, transcendentals=0)


def fold(values, width):
    return jnp.sum(values.reshape(values.size // (8 * width), 8, width), axis=0)


def chunk_rows_in(guess_in, guess_ref, sems, start, stop):
    copies = []
    for n in range(start, stop, TILE):
        part = pl.ds(n, TILE)
        copies.append(pltpu.make_async_copy(guess_in.at[part], guess_ref.at[pl.ds(n - start, TILE)], sems.at[n // TILE]))
        copies[-1].start()
    return copies


def first_chunk_kernel(rank_ref, guess_in, site_ref, x_ref, keep_ref, squares_ref, guess_ref, sems):
    rows, states, width = guess_ref.shape
    terms = site_ref.shape[0]
    copies = chunk_rows_in(guess_in, guess_ref, sems, 0, rows)
    column = lax.broadcasted_iota(jnp.int32, (1, width), 1)
    keep = (column < rank_ref[...]).astype(F32)
    keep_ref[...] = jnp.broadcast_to(keep, keep_ref.shape)
    line = lax.broadcasted_iota(jnp.int32, (TILE, width), 0)
    lane = lax.broadcasted_iota(jnp.int32, (TILE, width), 1)
    extra = jnp.zeros((TILE, width), F32)
    for k in range(terms):
        place_at = (lane == line + k * TILE).astype(BF16)
        extra = extra + jnp.dot(site_ref[k], place_at, preferred_element_type=F32)
    x_ref[states, 0:TILE, :] = extra.astype(BF16)
    squares = jnp.zeros((8, width), F32)
    for n, copy in enumerate(copies):
        copy.wait()
        part = pl.ds(n * TILE, TILE)
        masked = guess_ref[part] * keep[None]
        squares = squares + fold(masked * masked, width)
        x_ref[0:states, part, :] = jnp.swapaxes(masked, 0, 1).astype(BF16)
    squares_ref[...] = squares


def prepare_kernel(
    starts,
    keep_ref,
    squares_ref,
    guess_in,
    left_in,
    right_in,
    norm_ref,
    left_packed_ref,
    right_packed_ref,
    left_ref,
    *refs,
):
    x_refs = refs[: len(starts)]
    guess_ref, right_ref, sems = refs[len(starts) :]
    rows, states, width = guess_in.shape
    terms = left_ref.shape[0]
    half = width // 2
    done = starts[1] if len(starts) > 1 else rows
    copies = chunk_rows_in(guess_in, guess_ref, sems, done, rows)
    for source, target in ((right_in, right_ref), (left_in, left_ref)):
        copies.append(pltpu.make_async_copy(source, target, sems.at[rows // TILE + len(copies) - (rows - done) // TILE]))
        copies[-1].start()
    keep = keep_ref[0:1, :][None]
    squares = squares_ref[...]
    for n in range((rows - done) // TILE):
        copies[n].wait()
        masked = guess_ref[pl.ds(n * TILE, TILE)] * keep
        squares = squares + fold(masked * masked, width)
        turned = jnp.swapaxes(masked, 0, 1).astype(BF16)
        x_refs[0][:, n * TILE : (n + 1) * TILE, :] = turned
        chunk = max(c for c, start in enumerate(starts) if start <= done + n * TILE)
        at = done + n * TILE - starts[chunk]
        x_refs[chunk][:, at : at + TILE, :] = turned
    total = jnp.sum(squares)
    norm_ref[...] = jnp.full(norm_ref.shape, total, F32)
    line = lax.broadcasted_iota(jnp.int32, (TILE, half), 0)
    norm = jnp.full((TILE, half), total, F32)
    extra = jnp.zeros((TILE, half), F32)
    for n in range(1, 4):
        part = norm.astype(BF16).astype(F32)
        norm = norm - part
        extra = jnp.where(line == n, part, extra)
    for copy, block_ref, packed_ref in zip(copies[-2:], (right_ref, left_ref), (right_packed_ref, left_packed_ref)):
        copy.wait()
        for k in range(terms):
            diagonal = pack_symmetric(block_ref, k, packed_ref)
            packed_ref[k, width : width + TILE, :] = jnp.where(line == 0, diagonal, extra).astype(BF16)


def triangle(half):
    row = lax.broadcasted_iota(jnp.int32, (half, half), 0)
    col = lax.broadcasted_iota(jnp.int32, (half, half), 1)
    return row, col


def pack_symmetric(block_ref, k, out_ref):
    width = block_ref.shape[1]
    half = width // 2
    row, col = triangle(half)
    upper = block_ref[k, 0:half, 0:half].astype(F32)
    lower = block_ref[k, half:width, half:width].astype(F32)
    out_ref[k, 0:half, :] = block_ref[k, 0:half, half:width]
    out_ref[k, half:width, :] = jnp.where(row <= col, upper, lower).astype(BF16)
    return jnp.sum(jnp.where(row == col, lower, 0.0), axis=0, keepdims=True)


def unpack_symmetric(packed_ref, full_ref):
    terms, width, _ = full_ref.shape
    half = width // 2
    row, col = triangle(half)
    for k in range(terms):
        corner = packed_ref[k, 0:half, :]
        mixed = packed_ref[k, half:width, :].astype(F32)
        diagonal = packed_ref[k, width : width + TILE, :].astype(F32)[0:1]
        turned = mixed.T
        full_ref[k, 0:half, 0:half] = jnp.where(row <= col, mixed, turned).astype(BF16)
        full_ref[k, 0:half, half:width] = corner
        full_ref[k, half:width, 0:half] = corner.astype(F32).T.astype(BF16)
        full_ref[k, half:width, half:width] = jnp.where(
            row > col, mixed, jnp.where(row == col, diagonal, turned)
        ).astype(BF16)


def spread_kernel(chunk_ref, kron_ref):
    width = chunk_ref.shape[2]
    size = kron_ref.shape[1]
    terms = kron_ref.shape[0] // size
    states = size // TILE
    tile = chunk_ref[states, 0:TILE, :]
    row_state = lax.broadcasted_iota(jnp.int32, (size, states), 0) // TILE
    pick = (row_state == lax.broadcasted_iota(jnp.int32, (size, states), 1)).astype(BF16)
    tall = jnp.dot(pick, tile, preferred_element_type=F32).astype(BF16)
    lane = lax.broadcasted_iota(jnp.int32, (width, size), 0)
    col_state = lax.broadcasted_iota(jnp.int32, (width, size), 1) // TILE
    same = (
        lax.broadcasted_iota(jnp.int32, (size, size), 0) % TILE
        == lax.broadcasted_iota(jnp.int32, (size, size), 1) % TILE
    )
    for k in range(terms):
        pick_t = (lane == col_state + k * TILE).astype(BF16)
        full = jnp.dot(tall, pick_t, preferred_element_type=F32)
        kron_ref[k * size : (k + 1) * size, :] = jnp.where(same, full, 0.0).astype(BF16)


def mix_sites(source_ref, kron_ref, rotated_ref, base, unroll):
    terms, states, _, width = rotated_ref.shape
    rows = source_ref.shape[1]

    def step(i, carry):
        at = pl.multiple_of(i * TILE, TILE)
        to = pl.multiple_of(base + i * TILE, TILE)
        stack = source_ref[0:states, pl.ds(at, TILE), :].reshape(states * TILE, width)
        turned = jnp.dot(kron_ref[...], stack, preferred_element_type=F32).astype(BF16)
        rotated_ref[:, :, pl.ds(to, TILE), :] = turned.reshape(terms, states, TILE, width)
        return carry

    lax.fori_loop(0, rows // TILE, step, 0, unroll=min(unroll, rows // TILE))


def summed(values):
    while len(values) > 1:
        values = [values[n] + values[n + 1] for n in range(0, len(values), 2)]
    return values[0]


def place(hop, chips):
    me = lax.axis_index("term")
    chip = (me // CORES - hop + chips) % chips
    return chip, me % CORES


def row_of(spot, rows, chips):
    chip, core = place(spot[0], chips)
    return pl.multiple_of((chip * CORES + (core if spot[1] == 0 else 1 - core)) * rows + spot[2], TILE)


def mix_pieces(pieces, kron_ref, rotated_ref):
    at = 0
    for piece in pieces:
        mix_sites(piece, kron_ref, rotated_ref, at, UNROLL)
        at += piece.shape[1]


def rotate_own_kernel(groups, rows, chips, *refs):
    kron_ref, left_ref, rotated_ref, columns_ref = refs[-4:]
    mix_pieces(refs[:-4], kron_ref, rotated_ref)
    blocks = []
    for spots in groups:
        for k in range(left_ref.shape[0]):
            blocks += [left_ref[k, pl.ds(row_of(spot, rows, chips), spot[3]), :] for spot in spots]
    columns_ref[...] = jnp.concatenate(blocks, axis=0).astype(F32).T.astype(BF16)


def turn(right_ref, rotated_ref, turned_ref):
    terms, states, count, width = rotated_ref.shape
    for k in range(terms):
        for n in range(0, states, 8):
            source = rotated_ref[k, n : n + 8].reshape(8 * count, width)
            turned = jnp.dot(source, right_ref[k], preferred_element_type=F32).astype(BF16)
            turned_ref[n : n + 8, k * count : (k + 1) * count, :] = turned.reshape(8, count, width)


def here_kernel(rotated_ref, packed_ref, turned_ref, right_ref):
    unpack_symmetric(packed_ref, right_ref)
    turn(right_ref, rotated_ref, turned_ref)


def there_kernel(*refs):
    right_ref, kron_ref, turned_ref, rotated_ref = refs[-4:]
    mix_pieces(refs[:-4], kron_ref, rotated_ref)
    turn(right_ref, rotated_ref, turned_ref)


def last_kernel(count, *refs):
    right_ref, kron_ref, columns_ref = refs[count : count + 3]
    out_ref, rotated_ref, turned_ref = refs[-3:]
    there_kernel(*refs[:count], right_ref, kron_ref, turned_ref, rotated_ref)
    blocks = list(refs[count + 3 : -3]) + [turned_ref]

    def lefts(p, carry):
        stack = jnp.concatenate([block[p] for block in blocks], axis=0)
        out_ref[p] = jnp.dot(columns_ref[...], stack, preferred_element_type=F32)
        return carry

    lax.fori_loop(0, out_ref.shape[0], lefts, 0, unroll=UNROLL)


def rotate_kernel(spots, rows, chips, *refs):
    pieces = refs[: len(spots)]
    kron_ref = refs[len(spots)]
    rotated_ref, whole_ref, sems = refs[-3:]
    states = whole_ref.shape[0]
    copies = []
    bases = [row_of(spot, rows, chips) for spot in spots]
    for n, (at, piece) in enumerate(zip(bases, pieces)):
        target = whole_ref.at[:, pl.ds(at, piece.shape[1]), :]
        copies.append(pltpu.make_async_copy(piece.at[0:states], target, sems.at[n]))
        copies[-1].start()
    for at, piece in zip(bases, pieces):
        mix_sites(piece, kron_ref, rotated_ref, at, UNROLL)
    for copy in copies:
        copy.wait()


def lefts_kernel(spots, rows, chips, *refs):
    count = len(spots)
    packed_ref = refs[count + 3]
    mixed_ref, norm_ref, rotated_ref, whole_ref, left_ref, sems = refs[-6:]
    terms, states, width, _ = rotated_ref.shape
    lines = packed_ref[0, width : width + TILE, :].astype(F32)
    norm = lines[1:2] + lines[2:3] + lines[3:4]
    norm_ref[...] = jnp.broadcast_to(jnp.concatenate([norm, norm], axis=1), norm_ref.shape)
    unpack_symmetric(packed_ref, left_ref)
    rotate_kernel(spots, rows, chips, *refs[: count + 1], rotated_ref, whole_ref, sems)

    def lefts(p, carry):
        for k in range(terms):
            mixed = jnp.dot(left_ref[k], rotated_ref[k, p], preferred_element_type=F32)
            mixed_ref[p, :, k * width : (k + 1) * width] = mixed.astype(BF16)
        return carry

    lax.fori_loop(0, states, lefts, 0, unroll=UNROLL)


def rights_kernel(start, stop, packed_ref, mixed_ref, whole_ref, before_ref, *refs):
    if start == 0:
        stats = refs[:-3]
        partial_ref, stat_ref, right_ref = refs[-3:]
        unpack_symmetric(packed_ref, right_ref)
    else:
        stats = refs[:-2]
        partial_ref, stat_ref = refs[-2:]
        right_ref = packed_ref
    states, width, _ = whole_ref.shape
    terms = right_ref.shape[0]

    def rights(n, total):
        at = n * GROUP
        rows = mixed_ref[pl.ds(start + at, GROUP)].reshape(GROUP * width, terms * width)
        stacked = right_ref[...].reshape(terms * width, width)
        image = jnp.dot(rows, stacked, preferred_element_type=F32).reshape(GROUP, width, width)
        part = (before_ref[pl.ds(start + at, GROUP)].astype(F32) + image).astype(partial_ref.dtype)
        partial_ref[pl.ds(at, GROUP)] = part
        held = whole_ref[pl.ds(start + at, GROUP)].astype(F32)
        return total + fold(held * part.astype(F32), width)

    total = lax.fori_loop(0, (stop - start) // GROUP, rights, jnp.zeros((8, width), F32))
    stat_ref[...] = functools.reduce(jnp.add, [stat[...] for stat in stats])
    product = jnp.full((1, width), jnp.sum(total), F32)
    stat_ref[0:1, :] = product if start == 0 else stats[0][0:1, :] + product


def scales(keep_ref, mine_ref, theirs_ref, scale, width):
    inverse = lax.rsqrt((mine_ref[1:2, :] + theirs_ref[1:2, :]) * scale + epsilon)
    rayleigh = (mine_ref[0:1, :] + theirs_ref[0:1, :]) * (inverse * inverse * scale)
    return inverse, rayleigh, keep_ref[0:1, :] * inverse


def add_kernel(mine_ref, other_ref, sum_ref):
    sum_ref[...] = mine_ref[...].astype(F32) + other_ref[...].astype(F32)


def second_kernel(
    scale,
    members,
    keep_ref,
    mine_ref,
    theirs_ref,
    low_ref,
    high_ref,
    high_other_ref,
    whole_ref,
    left_ref,
    right_ref,
    kron_ref,
    out_ref,
    res_ref,
    rotated_ref,
    mixed_ref,
):
    terms, states, width, _ = rotated_ref.shape
    inverse, rayleigh, row_scale = scales(keep_ref, mine_ref, theirs_ref, scale, width)
    back = rayleigh * inverse

    square = jnp.zeros((8, width), F32)
    for start, halves in ((0, (low_ref,)), (states // 2, (high_ref, high_other_ref))):

        def lefts(n, total):
            p = start + n
            sigma = functools.reduce(jnp.add, [half[n].astype(F32) for half in halves]) * row_scale
            residual = sigma - back * whole_ref[p].astype(F32)
            rounded = residual.astype(BF16)
            res_ref[p] = rounded
            mixed = jnp.dot(
                left_ref[...].reshape(terms * width, width), rounded, preferred_element_type=F32
            ).astype(BF16)
            for k in range(terms):
                mixed_ref[k, p] = mixed[k * width : (k + 1) * width]
            return total + fold(residual * residual, width)

        square = lax.fori_loop(0, states // 2, lefts, square, unroll=UNROLL)
    mix_sites(res_ref, kron_ref, rotated_ref, 0, 2 * UNROLL)

    def rights(n, total):
        at = n * GROUP
        for k in range(terms):
            turned = rotated_ref[k, pl.ds(at, GROUP)].reshape(GROUP * width, width)
            image = jnp.dot(turned, right_ref[k], preferred_element_type=F32)
            held = mixed_ref[k, pl.ds(at, GROUP)].reshape(GROUP * width, width).astype(F32)
            total = total + fold(held * image, width)
        return total

    cross = lax.fori_loop(0, states // GROUP, rights, jnp.zeros((8, width), F32))
    share = 1.0 / members
    out_ref[0:1, :] = rayleigh * share
    out_ref[1:2, :] = jnp.full((1, width), jnp.sum(square) * (scale * share), F32)
    out_ref[2:3, :] = jnp.full((1, width), jnp.sum(cross) * scale, F32)
    out_ref[3:8, :] = jnp.zeros((5, width), F32)


def own_rows_kernel(scale, keep_ref, guess_ref, mine_ref, theirs_ref, *refs):
    low_ref, high_ref, high_other_ref, vector_ref, residual_ref = refs
    rows, states, width = guess_ref.shape
    inverse, rayleigh, row_scale = scales(keep_ref, mine_ref, theirs_ref, scale, width)
    own = pl.ds(pl.multiple_of(lax.axis_index("term") * rows, TILE), rows)
    vector = guess_ref[...] * row_scale[None]
    vector_ref[...] = vector
    high = high_ref[:, own, :].astype(F32) + high_other_ref[:, own, :].astype(F32)
    sigma = jnp.concatenate([low_ref[:, own, :], high], axis=0) * row_scale[None]
    residual_ref[...] = jnp.swapaxes(sigma, 0, 1) - rayleigh[None] * vector


def finish_kernel(vector_ref, residual_ref, *refs):
    shares = refs[:-2]
    ritz_ref, energy_ref = refs[-2:]
    stat = summed([share[...] for share in shares])
    rayleigh = stat[0:1, :]
    res_sq = stat[1:2, :]
    res_var = res_sq + epsilon
    curvature = stat[2:3, :] / res_var
    res_scale = jnp.sqrt(res_var)
    coupling = res_sq / res_scale
    half_gap = 0.5 * (rayleigh - curvature)
    energy = 0.5 * (rayleigh + curvature) - jnp.sqrt(half_gap * half_gap + coupling * coupling)
    coeff_new = energy - rayleigh
    coeff_norm = jnp.sqrt(coupling * coupling + coeff_new * coeff_new + epsilon)
    old = coupling / coeff_norm
    new = coeff_new / (coeff_norm * res_scale)
    ritz_ref[...] = old[None] * vector_ref[...] + new[None] * residual_ref[...]
    energy_ref[0] = energy[0, 0]


def shards(wave_guess, left_env, right_env, site_ops, bond_rank):
    guess = wave_guess[0]
    left = left_env[0]
    site = site_ops[0]
    rows, states, width = guess.shape
    terms = left.shape[0]
    members = lax.axis_size("term")
    chips = members // CORES
    segments = lax.axis_size("seg")
    scale = 1.0 / float(rows * members * states * width)
    hops = tuple(range(chips))

    def to_sibling(block):
        return lax.ppermute(block, "term", [(i, i ^ 1) for i in range(members)])

    def to_next_chip(block):
        return lax.ppermute(block, "term", [(i, (i + CORES) % members) for i in range(members)])

    def around(block):
        found = [block]
        for _ in range(chips - 1):
            found.append(to_next_chip(found[-1]))
        return found

    def everyone(block):
        return [block] + [
            lax.ppermute(block, "term", [(i, i ^ bits) for i in range(members)])
            for bits in range(CORES, members, CORES)
        ]

    tile = jax.ShapeDtypeStruct((8, width), F32)
    half = width // 2
    packed_shape = jax.ShapeDtypeStruct((terms, width + TILE, half), BF16)
    starts = (0, rows - 2 * TILE, rows - TILE) if rows >= 4 * TILE else (0,)
    lengths = [stop - start for start, stop in zip(starts, starts[1:] + (rows,))]
    in_place = [pltpu.with_memory_space_constraint(a, pltpu.HBM) for a in (guess, left, right_env[0], site)]
    first_chunk, keep, squares = pl.pallas_call(
        first_chunk_kernel,
        out_shape=(jax.ShapeDtypeStruct((states + 1, lengths[0], width), BF16), tile, tile),
        in_specs=[vmem, in_hbm, vmem],
        out_specs=(vmem,) * 3,
        scratch_shapes=[
            pltpu.VMEM((lengths[0], states, width), F32),
            pltpu.SemaphoreType.DMA((lengths[0] // TILE,)),
        ],
        compiler_params=params(),
        cost_estimate=cost(2 * guess.size, 3 * guess.size),
        name="first_chunk",
    )(bond_rank.reshape(1, 1), in_place[0], in_place[3])
    rest = rows - lengths[0]
    norm_part, left_packed, right_packed, left, *chunks = pl.pallas_call(
        functools.partial(prepare_kernel, starts),
        out_shape=(
            tile,
            packed_shape,
            packed_shape,
            jax.ShapeDtypeStruct(left.shape, BF16),
            *[
                jax.ShapeDtypeStruct((states, length, width), BF16)
                for length in ([rest] + lengths[1:] if rest else [TILE])
            ],
        ),
        in_specs=[vmem] * 2 + [in_hbm] * 3,
        out_specs=(vmem,) * (4 + len(lengths)),
        scratch_shapes=[
            pltpu.VMEM((max(rest, TILE), states, width), F32),
            pltpu.VMEM(left.shape, BF16),
            pltpu.SemaphoreType.DMA((rows // TILE + 2,)),
        ],
        compiler_params=params(),
        cost_estimate=cost(4 * guess.size, 6 * guess.size),
        name="prepare",
    )(keep, squares, *in_place[:3])
    own_pieces = [first_chunk] + (chunks[:1] if rest else [])
    chunks = [first_chunk] + chunks[1:]

    chunk_hops = [around(chunk) for chunk in chunks]
    here_pieces = own_pieces + [to_sibling(piece) for piece in own_pieces]
    bounds = (0, lengths[0], rows) if rest else (0, rows)
    here_spots = tuple(
        (0, flip, start, stop - start) for flip in range(CORES) for start, stop in zip(bounds[:-1], bounds[1:])
    )
    far_spots = [
        tuple((hop, flip, start, length) for hop in hops[1:] for flip in range(CORES))
        for start, length in zip(starts, lengths)
    ]
    mid_spots = sum(far_spots[:-1], ())
    groups = [group for group in (here_spots, mid_spots, far_spots[-1]) if group]
    lefts = around(left_packed)
    shift = [(i + 1, i) for i in range(segments - 1)]
    received = lax.ppermute(right_packed, "seg", shift)

    size = states * TILE

    def spread(block):
        return pl.pallas_call(
            spread_kernel,
            out_shape=jax.ShapeDtypeStruct((terms * size, size), BF16),
            in_specs=[vmem],
            out_specs=vmem,
            compiler_params=params(),
            cost_estimate=cost(2 * terms * size * size * width, 2 * terms * size * size),
            name="spread_site",
        )(block)

    kron_own = spread(chunks[0])

    whole = (states, width, width)
    whole_bf = jax.ShapeDtypeStruct(whole, BF16)
    whole_f32 = jax.ShapeDtypeStruct(whole, F32)
    rotated = (terms, states, width, width)
    rotated_bf = jax.ShapeDtypeStruct(rotated, BF16)
    square = pltpu.VMEM((terms, width, width), BF16)
    chip_rows = CORES * rows
    stage_flops = 2 * terms * states * width * width * width

    def buffers(spots):
        count = sum(spot[3] for spot in spots)
        return (terms, states, count, width), (states, terms * count, width)

    here_rotated, here_turned = buffers(here_spots)
    part_cost = cost(stage_flops, 8 * states * width * width)
    rotated_own, columns = pl.pallas_call(
        functools.partial(rotate_own_kernel, groups, rows, chips),
        out_shape=(
            jax.ShapeDtypeStruct(here_rotated, BF16),
            jax.ShapeDtypeStruct((width, terms * width), BF16),
        ),
        in_specs=[vmem] * (len(here_pieces) + 2),
        out_specs=(vmem, vmem),
        compiler_params=params(),
        cost_estimate=part_cost,
        name="rotate_own",
    )(*here_pieces, kron_own, left)

    def rotate(spots, pieces, kron, before):
        return pl.pallas_call(
            functools.partial(rotate_kernel, spots, rows, chips),
            out_shape=(rotated_bf, whole_bf),
            in_specs=[vmem] * (len(pieces) + 1) + [anywhere] * len(before),
            out_specs=(vmem, vmem),
            scratch_shapes=[pltpu.SemaphoreType.DMA((len(pieces),))],
            input_output_aliases={len(pieces) + 1 + n: n for n in range(len(before))},
            compiler_params=params(),
            cost_estimate=part_cost,
            name="rotate_crossed" if before else "rotate_here",
        )(*pieces, kron, *before)

    def relayed(blocks):
        return [piece for block in blocks for piece in (block, to_sibling(block))]

    firsts, rotated_own = lax.optimization_barrier((chunk_hops[0][1:], rotated_own))
    kron = spread(firsts[0])
    turned = rotate(here_spots, here_pieces, kron, ())
    received, turned = lax.optimization_barrier((received, turned))
    packed = jnp.where(lax.axis_index("seg") == segments - 1, right_packed, received)
    rights = around(packed)
    turned_own, right = pl.pallas_call(
        here_kernel,
        out_shape=(jax.ShapeDtypeStruct(here_turned, BF16), jax.ShapeDtypeStruct(left.shape, BF16)),
        in_specs=[vmem] * 2,
        out_specs=(vmem, vmem),
        compiler_params=params(),
        cost_estimate=part_cost,
        name="apply_rows_here",
    )(rotated_own, packed)
    parts = [turned_own]
    mid_pieces = []
    if mid_spots:
        mid_pieces += relayed(firsts)
        for crossing in chunk_hops[1:-1]:
            crossed, turned = lax.optimization_barrier((crossing[1:], turned))
            mid_pieces += relayed(crossed)
        turned = rotate(mid_spots, mid_pieces, kron, turned)
        crossed, turned, parts[0] = lax.optimization_barrier((chunk_hops[-1][1:], turned, parts[0]))
        last_pieces = relayed(crossed)
        mid_rotated, mid_turned = buffers(mid_spots)
        parts.append(
            pl.pallas_call(
                there_kernel,
                out_shape=jax.ShapeDtypeStruct(mid_turned, BF16),
                in_specs=[vmem] * (len(mid_pieces) + 2),
                out_specs=vmem,
                scratch_shapes=[pltpu.VMEM(mid_rotated, BF16)],
                compiler_params=params(),
                cost_estimate=part_cost,
                name="apply_rows_crossed",
            )(*mid_pieces, right, kron_own)
        )
    else:
        last_pieces = relayed(firsts)
    last_rotated, last_turned = buffers(far_spots[-1])
    partial = pl.pallas_call(
        functools.partial(last_kernel, len(last_pieces)),
        out_shape=whole_f32,
        in_specs=[vmem] * (len(last_pieces) + 3 + len(parts)),
        out_specs=vmem,
        scratch_shapes=[pltpu.VMEM(last_rotated, BF16), pltpu.VMEM(last_turned, BF16)],
        compiler_params=params(),
        cost_estimate=part_cost,
        name="apply_rows_last",
    )(*last_pieces, right, kron_own, columns, *parts)
    norms = [norm_part]
    for hop in hops[1:]:
        if hop > 1:
            block, partial = lax.optimization_barrier((firsts[hop - 1], partial))
            kron = spread(block)
            turned = rotate(here_spots, here_pieces, kron, ())
            if mid_spots:
                turned = rotate(mid_spots, mid_pieces, kron, turned)
        left_far, partial = lax.optimization_barrier((lefts[hop], partial))
        mixed, norm_far, _, vector = pl.pallas_call(
            functools.partial(lefts_kernel, far_spots[-1], rows, chips),
            out_shape=(jax.ShapeDtypeStruct((states, width, terms * width), BF16), tile, rotated_bf, whole_bf),
            in_specs=[vmem] * (len(last_pieces) + 1) + [anywhere] * 2 + [vmem],
            out_specs=(vmem,) * 4,
            scratch_shapes=[square, pltpu.SemaphoreType.DMA((len(last_pieces),))],
            input_output_aliases={len(last_pieces) + 1: 2, len(last_pieces) + 2: 3},
            compiler_params=params(),
            cost_estimate=cost(stage_flops, 12 * states * width * width),
            name="received_lefts",
        )(*last_pieces, kron, *turned, left_far)
        norms.append(norm_far)
        last = hop == hops[-1]
        stats = norms if last else norms[:1]
        right_far = rights[hop]
        parts = []
        bounds = (0, states // 2, states) if last else (0, states)
        for start, stop in zip(bounds[:-1], bounds[1:]):
            outs = [jax.ShapeDtypeStruct((stop - start, width, width), BF16 if last else F32), tile]
            part, stat, *unpacked = pl.pallas_call(
                functools.partial(rights_kernel, start, stop),
                out_shape=tuple(outs + ([jax.ShapeDtypeStruct(left.shape, BF16)] if start == 0 else [])),
                in_specs=[vmem] * (4 + len(stats)),
                out_specs=(vmem,) * (3 if start == 0 else 2),
                compiler_params=params(),
                cost_estimate=cost(stage_flops / 2, 12 * states * width * width),
                name="received_rights",
            )(right_far, mixed, vector, partial, *stats)
            stats = [stat]
            if unpacked:
                right_far = unpacked[0]
            parts.append(part)
        if not last:
            partial = parts[0]
    low = pl.pallas_call(
        add_kernel,
        out_shape=jax.ShapeDtypeStruct(parts[0].shape, F32),
        in_specs=[vmem] * 2,
        out_specs=vmem,
        compiler_params=params(),
        cost_estimate=cost(parts[0].size, 8 * parts[0].size),
        name="add_low_half",
    )(parts[0], to_sibling(parts[0]))
    halves = [low, parts[1], to_sibling(parts[1])]
    stat_other = to_sibling(stat)

    share = pl.pallas_call(
        functools.partial(second_kernel, scale, members),
        out_shape=tile,
        in_specs=[vmem] * 10,
        out_specs=vmem,
        scratch_shapes=[
            pltpu.VMEM(whole, BF16),
            pltpu.VMEM(rotated, BF16),
            pltpu.VMEM(rotated, BF16),
        ],
        compiler_params=params(),
        cost_estimate=cost(3 * stage_flops, 6 * states * width * width),
        name="apply_residual",
    )(keep, stat, stat_other, *halves, vector, left, right, kron_own)
    crossed = everyone(share)

    local = jax.ShapeDtypeStruct((rows, states, width), F32)
    vector_own, residual_own = pl.pallas_call(
        functools.partial(own_rows_kernel, scale),
        out_shape=(local, local),
        in_specs=[vmem] * 7,
        out_specs=(vmem, vmem),
        compiler_params=params(),
        cost_estimate=cost(8 * guess.size, 16 * guess.size),
        name="own_rows",
    )(keep, guess, stat, stat_other, *halves)

    shares = [share, to_sibling(share)]
    gated, residual_own = lax.optimization_barrier((crossed[1:], residual_own))
    shares += relayed(gated)
    ritz, energy = pl.pallas_call(
        finish_kernel,
        out_shape=(local, jax.ShapeDtypeStruct((1,), F32)),
        in_specs=[vmem] * (2 + members),
        out_specs=(vmem, smem),
        compiler_params=params(),
        cost_estimate=cost(3 * guess.size, 12 * guess.size),
        name="finish",
    )(vector_own, residual_own, *shares)
    return (ritz[None], energy)


def solution(mesh):
    in_specs = (
        P("seg", "term", None, None),
        P("seg", "term", None, None),
        P("seg", "term", None, None),
        P("seg", "term", None, None),
        P("seg"),
    )
    out_specs = (P("seg", "term", None, None), P("seg"))
    return jax.shard_map(shards, mesh=mesh, in_specs=in_specs, out_specs=out_specs, check_vma=False)
```

```python
import functools

import jax
import jax.numpy as jnp
from jax import lax
from jax.experimental import pallas as pl
from jax.experimental.pallas import tpu as pltpu
from jax.sharding import PartitionSpec as P

epsilon = 1e-06
CORES = 2
TILE = 16
UNROLL = 8
GROUP = 8
VMEM_LIMIT = 20 * 1024 * 1024
F32 = jnp.float32
BF16 = jnp.bfloat16

vmem = pl.BlockSpec(memory_space=pltpu.VMEM)
smem = pl.BlockSpec(memory_space=pltpu.SMEM)
anywhere = pl.BlockSpec(memory_space=pl.ANY)
in_hbm = pl.BlockSpec(memory_space=pltpu.HBM)


def params():
    return pltpu.CompilerParams(vmem_limit_bytes=VMEM_LIMIT)


def cost(flops, moved):
    return pl.CostEstimate(flops=int(flops) // 100, bytes_accessed=int(moved) // 100, transcendentals=0)


def fold(values, width):
    return jnp.sum(values.reshape(values.size // (8 * width), 8, width), axis=0)


def chunk_rows_in(guess_in, guess_ref, sems, start, stop, slot):
    copies = []
    for n in range(start, stop, TILE):
        target = guess_ref.at[pl.ds(n - start, TILE)]
        copies.append(pltpu.make_async_copy(guess_in.at[pl.ds(n, TILE)], target, sems.at[slot + len(copies)]))
        copies[-1].start()
    return copies


def first_chunk_kernel(
    rank_in,
    guess_in,
    site_in,
    right_in,
    x_ref,
    keep_ref,
    squares_ref,
    packed_ref,
    rank_ref,
    guess_ref,
    site_ref,
    right_ref,
    sems,
):
    rows, states, width = guess_ref.shape
    terms = site_ref.shape[0]
    copies = [
        pltpu.make_async_copy(source, target, sems.at[n])
        for n, (source, target) in enumerate(((rank_in, rank_ref), (site_in, site_ref), (right_in, right_ref)))
    ]
    copies[0].start()
    parts = chunk_rows_in(guess_in, guess_ref, sems, 0, rows, 3)
    copies[1].start()
    copies[2].start()
    copies[0].wait()
    column = lax.broadcasted_iota(jnp.int32, (1, width), 1)
    keep = (column < rank_ref[...]).astype(F32)
    keep_ref[...] = jnp.broadcast_to(keep, keep_ref.shape)
    squares = jnp.zeros((8, width), F32)
    for n, copy in enumerate(parts):
        copy.wait()
        part = pl.ds(n * TILE, TILE)
        masked = guess_ref[part] * keep[None]
        squares = squares + fold(masked * masked, width)
        x_ref[0:states, part, :] = jnp.swapaxes(masked, 0, 1).astype(BF16)
    squares_ref[...] = squares
    copies[1].wait()
    line = lax.broadcasted_iota(jnp.int32, (TILE, width), 0)
    lane = lax.broadcasted_iota(jnp.int32, (TILE, width), 1)
    extra = jnp.zeros((TILE, width), F32)
    for k in range(terms):
        place_at = (lane == line + k * TILE).astype(BF16)
        extra = extra + jnp.dot(site_ref[k], place_at, preferred_element_type=F32)
    x_ref[states, 0:TILE, :] = extra.astype(BF16)
    copies[2].wait()
    pack_blocks(right_ref, None, packed_ref)


def prepare_kernel(starts, keep_ref, squares_ref, guess_in, left_in, norm_ref, packed_ref, left_ref, *refs):
    x_refs = (None,) + refs[: len(starts) - 1]
    guess_ref, sems = refs[len(starts) - 1 :]
    rows, states, width = guess_in.shape
    half = width // 2
    done = starts[1] if len(starts) > 1 else rows
    copies = chunk_rows_in(guess_in, guess_ref, sems, done, rows, 1)
    left_copy = pltpu.make_async_copy(left_in, left_ref, sems.at[0])
    left_copy.start()
    keep = keep_ref[0:1, :][None]
    squares = squares_ref[...]
    for n, copy in enumerate(copies):
        copy.wait()
        masked = guess_ref[pl.ds(n * TILE, TILE)] * keep
        squares = squares + fold(masked * masked, width)
        chunk = max(c for c, start in enumerate(starts) if start <= done + n * TILE)
        at = done + n * TILE - starts[chunk]
        x_refs[chunk][:, at : at + TILE, :] = jnp.swapaxes(masked, 0, 1).astype(BF16)
    total = jnp.sum(squares)
    norm_ref[...] = jnp.full(norm_ref.shape, total, F32)
    line = lax.broadcasted_iota(jnp.int32, (TILE, half), 0)
    norm = jnp.full((TILE, half), total, F32)
    extra = jnp.zeros((TILE, half), F32)
    for n in range(1, 4):
        part = norm.astype(BF16).astype(F32)
        norm = norm - part
        extra = jnp.where(line == n, part, extra)
    left_copy.wait()
    pack_blocks(left_ref, extra, packed_ref)


def pack_blocks(block_ref, extra, packed_ref):
    terms, width, _ = block_ref.shape
    half = width // 2
    line = lax.broadcasted_iota(jnp.int32, (TILE, half), 0)
    for k in range(terms):
        diagonal = pack_symmetric(block_ref, k, packed_ref)
        lines = jnp.broadcast_to(diagonal, (TILE, half)) if extra is None else jnp.where(line == 0, diagonal, extra)
        packed_ref[k, width : width + TILE, :] = lines.astype(BF16)


def triangle(half):
    row = lax.broadcasted_iota(jnp.int32, (half, half), 0)
    col = lax.broadcasted_iota(jnp.int32, (half, half), 1)
    return row, col


def pack_symmetric(block_ref, k, out_ref):
    width = block_ref.shape[1]
    half = width // 2
    row, col = triangle(half)
    upper = block_ref[k, 0:half, 0:half].astype(F32)
    lower = block_ref[k, half:width, half:width].astype(F32)
    out_ref[k, 0:half, :] = block_ref[k, 0:half, half:width]
    out_ref[k, half:width, :] = jnp.where(row <= col, upper, lower).astype(BF16)
    return jnp.sum(jnp.where(row == col, lower, 0.0), axis=0, keepdims=True)


def unpack_symmetric(packed_ref, full_ref):
    terms, width, _ = full_ref.shape
    half = width // 2
    row, col = triangle(half)
    for k in range(terms):
        corner = packed_ref[k, 0:half, :]
        mixed = packed_ref[k, half:width, :].astype(F32)
        diagonal = packed_ref[k, width : width + TILE, :].astype(F32)[0:1]
        turned = mixed.T
        full_ref[k, 0:half, 0:half] = jnp.where(row <= col, mixed, turned).astype(BF16)
        full_ref[k, 0:half, half:width] = corner
        full_ref[k, half:width, 0:half] = corner.astype(F32).T.astype(BF16)
        full_ref[k, half:width, half:width] = jnp.where(
            row > col, mixed, jnp.where(row == col, diagonal, turned)
        ).astype(BF16)


def spread_kernel(chunk_ref, kron_ref):
    width = chunk_ref.shape[2]
    size = kron_ref.shape[1]
    terms = kron_ref.shape[0] // size
    states = size // TILE
    tile = chunk_ref[states, 0:TILE, :]
    row_state = lax.broadcasted_iota(jnp.int32, (size, states), 0) // TILE
    pick = (row_state == lax.broadcasted_iota(jnp.int32, (size, states), 1)).astype(BF16)
    tall = jnp.dot(pick, tile, preferred_element_type=F32).astype(BF16)
    lane = lax.broadcasted_iota(jnp.int32, (width, size), 0)
    col_state = lax.broadcasted_iota(jnp.int32, (width, size), 1) // TILE
    same = (
        lax.broadcasted_iota(jnp.int32, (size, size), 0) % TILE
        == lax.broadcasted_iota(jnp.int32, (size, size), 1) % TILE
    )
    for k in range(terms):
        pick_t = (lane == col_state + k * TILE).astype(BF16)
        full = jnp.dot(tall, pick_t, preferred_element_type=F32)
        kron_ref[k * size : (k + 1) * size, :] = jnp.where(same, full, 0.0).astype(BF16)


def mix_sites(source_ref, kron_ref, rotated_ref, base, unroll):
    terms, states, _, width = rotated_ref.shape
    rows = source_ref.shape[1]

    def step(i, carry):
        at = pl.multiple_of(i * TILE, TILE)
        to = pl.multiple_of(base + i * TILE, TILE)
        stack = source_ref[0:states, pl.ds(at, TILE), :].reshape(states * TILE, width)
        turned = jnp.dot(kron_ref[...], stack, preferred_element_type=F32).astype(BF16)
        rotated_ref[:, :, pl.ds(to, TILE), :] = turned.reshape(terms, states, TILE, width)
        return carry

    lax.fori_loop(0, rows // TILE, step, 0, unroll=min(unroll, rows // TILE))


def summed(values):
    while len(values) > 1:
        values = [values[n] + values[n + 1] for n in range(0, len(values), 2)]
    return values[0]


def place(hop, chips):
    me = lax.axis_index("term")
    chip = (me // CORES - hop + chips) % chips
    return chip, me % CORES


def row_of(spot, rows, chips):
    chip, core = place(spot[0], chips)
    return pl.multiple_of((chip * CORES + (core if spot[1] == 0 else 1 - core)) * rows + spot[2], TILE)


def mix_pieces(pieces, kron_ref, rotated_ref):
    at = 0
    for piece in pieces:
        mix_sites(piece, kron_ref, rotated_ref, at, UNROLL)
        at += piece.shape[1]


def rotate_own_kernel(groups, rows, chips, *refs):
    kron_ref, left_ref, rotated_ref, columns_ref = refs[-4:]
    mix_pieces(refs[:-4], kron_ref, rotated_ref)
    blocks = []
    for spots in groups:
        for k in range(left_ref.shape[0]):
            blocks += [left_ref[k, pl.ds(row_of(spot, rows, chips), spot[3]), :] for spot in spots]
    columns_ref[...] = jnp.concatenate(blocks, axis=0).astype(F32).T.astype(BF16)


def turn(right_ref, rotated_ref, turned_ref):
    terms, states, count, width = rotated_ref.shape
    for k in range(terms):
        for n in range(0, states, 8):
            source = rotated_ref[k, n : n + 8].reshape(8 * count, width)
            turned = jnp.dot(source, right_ref[k], preferred_element_type=F32).astype(BF16)
            turned_ref[n : n + 8, k * count : (k + 1) * count, :] = turned.reshape(8, count, width)


def here_kernel(rotated_ref, packed_ref, turned_ref, right_ref):
    unpack_symmetric(packed_ref, right_ref)
    turn(right_ref, rotated_ref, turned_ref)


def there_kernel(*refs):
    right_ref, kron_ref, turned_ref, rotated_ref = refs[-4:]
    mix_pieces(refs[:-4], kron_ref, rotated_ref)
    turn(right_ref, rotated_ref, turned_ref)


def last_kernel(count, *refs):
    right_ref, kron_ref, columns_ref = refs[count : count + 3]
    out_ref, rotated_ref, turned_ref = refs[-3:]
    there_kernel(*refs[:count], right_ref, kron_ref, turned_ref, rotated_ref)
    blocks = list(refs[count + 3 : -3]) + [turned_ref]

    def lefts(p, carry):
        stack = jnp.concatenate([block[p] for block in blocks], axis=0)
        out_ref[p] = jnp.dot(columns_ref[...], stack, preferred_element_type=F32)
        return carry

    lax.fori_loop(0, out_ref.shape[0], lefts, 0, unroll=UNROLL)


def rotate_kernel(spots, rows, chips, *refs):
    pieces = refs[: len(spots)]
    kron_ref = refs[len(spots)]
    rotated_ref, whole_ref, sems = refs[-3:]
    states = whole_ref.shape[0]
    copies = []
    bases = [row_of(spot, rows, chips) for spot in spots]
    for n, (at, piece) in enumerate(zip(bases, pieces)):
        target = whole_ref.at[:, pl.ds(at, piece.shape[1]), :]
        copies.append(pltpu.make_async_copy(piece.at[0:states], target, sems.at[n]))
        copies[-1].start()
    for at, piece in zip(bases, pieces):
        mix_sites(piece, kron_ref, rotated_ref, at, UNROLL)
    for copy in copies:
        copy.wait()


def lefts_kernel(spots, rows, chips, *refs):
    count = len(spots)
    packed_ref = refs[count + 3]
    mixed_ref, norm_ref, rotated_ref, whole_ref, left_ref, sems = refs[-6:]
    terms, states, width, _ = rotated_ref.shape
    lines = packed_ref[0, width : width + TILE, :].astype(F32)
    norm = lines[1:2] + lines[2:3] + lines[3:4]
    norm_ref[...] = jnp.broadcast_to(jnp.concatenate([norm, norm], axis=1), norm_ref.shape)
    unpack_symmetric(packed_ref, left_ref)
    rotate_kernel(spots, rows, chips, *refs[: count + 1], rotated_ref, whole_ref, sems)

    def lefts(p, carry):
        for k in range(terms):
            mixed = jnp.dot(left_ref[k], rotated_ref[k, p], preferred_element_type=F32)
            mixed_ref[p, :, k * width : (k + 1) * width] = mixed.astype(BF16)
        return carry

    lax.fori_loop(0, states, lefts, 0, unroll=UNROLL)


def rights_kernel(start, stop, packed_ref, mixed_ref, whole_ref, before_ref, *refs):
    if start == 0:
        stats = refs[:-3]
        partial_ref, stat_ref, right_ref = refs[-3:]
        unpack_symmetric(packed_ref, right_ref)
    else:
        stats = refs[:-2]
        partial_ref, stat_ref = refs[-2:]
        right_ref = packed_ref
    states, width, _ = whole_ref.shape
    terms = right_ref.shape[0]

    def rights(n, total):
        at = n * GROUP
        rows = mixed_ref[pl.ds(start + at, GROUP)].reshape(GROUP * width, terms * width)
        stacked = right_ref[...].reshape(terms * width, width)
        image = jnp.dot(rows, stacked, preferred_element_type=F32).reshape(GROUP, width, width)
        part = (before_ref[pl.ds(start + at, GROUP)].astype(F32) + image).astype(partial_ref.dtype)
        partial_ref[pl.ds(at, GROUP)] = part
        held = whole_ref[pl.ds(start + at, GROUP)].astype(F32)
        return total + fold(held * part.astype(F32), width)

    total = lax.fori_loop(0, (stop - start) // GROUP, rights, jnp.zeros((8, width), F32))
    stat_ref[...] = functools.reduce(jnp.add, [stat[...] for stat in stats])
    product = jnp.full((1, width), jnp.sum(total), F32)
    stat_ref[0:1, :] = product if start == 0 else stats[0][0:1, :] + product


def scales(keep_ref, mine_ref, theirs_ref, scale, width):
    inverse = lax.rsqrt((mine_ref[1:2, :] + theirs_ref[1:2, :]) * scale + epsilon)
    rayleigh = (mine_ref[0:1, :] + theirs_ref[0:1, :]) * (inverse * inverse * scale)
    return inverse, rayleigh, keep_ref[0:1, :] * inverse


def add_kernel(mine_ref, other_ref, sum_ref):
    sum_ref[...] = mine_ref[...].astype(F32) + other_ref[...].astype(F32)


def second_kernel(
    scale,
    members,
    keep_ref,
    mine_ref,
    theirs_ref,
    low_ref,
    high_ref,
    high_other_ref,
    whole_ref,
    left_ref,
    right_ref,
    kron_ref,
    out_ref,
    res_ref,
    rotated_ref,
    mixed_ref,
):
    terms, states, width, _ = rotated_ref.shape
    inverse, rayleigh, row_scale = scales(keep_ref, mine_ref, theirs_ref, scale, width)
    back = rayleigh * inverse

    square = jnp.zeros((8, width), F32)
    for start, halves in ((0, (low_ref,)), (states // 2, (high_ref, high_other_ref))):

        def lefts(n, total):
            p = start + n
            sigma = functools.reduce(jnp.add, [half[n].astype(F32) for half in halves]) * row_scale
            residual = sigma - back * whole_ref[p].astype(F32)
            rounded = residual.astype(BF16)
            res_ref[p] = rounded
            mixed = jnp.dot(
                left_ref[...].reshape(terms * width, width), rounded, preferred_element_type=F32
            ).astype(BF16)
            for k in range(terms):
                mixed_ref[k, p] = mixed[k * width : (k + 1) * width]
            return total + fold(residual * residual, width)

        square = lax.fori_loop(0, states // 2, lefts, square, unroll=UNROLL)
    mix_sites(res_ref, kron_ref, rotated_ref, 0, 2 * UNROLL)

    def rights(n, total):
        at = n * GROUP
        for k in range(terms):
            turned = rotated_ref[k, pl.ds(at, GROUP)].reshape(GROUP * width, width)
            image = jnp.dot(turned, right_ref[k], preferred_element_type=F32)
            held = mixed_ref[k, pl.ds(at, GROUP)].reshape(GROUP * width, width).astype(F32)
            total = total + fold(held * image, width)
        return total

    cross = lax.fori_loop(0, states // GROUP, rights, jnp.zeros((8, width), F32))
    share = 1.0 / members
    out_ref[0:1, :] = rayleigh * share
    out_ref[1:2, :] = jnp.full((1, width), jnp.sum(square) * (scale * share), F32)
    out_ref[2:3, :] = jnp.full((1, width), jnp.sum(cross) * scale, F32)
    out_ref[3:8, :] = jnp.zeros((5, width), F32)


def own_rows_kernel(scale, keep_ref, guess_ref, mine_ref, theirs_ref, *refs):
    low_ref, high_ref, high_other_ref, vector_ref, residual_ref = refs
    rows, states, width = guess_ref.shape
    inverse, rayleigh, row_scale = scales(keep_ref, mine_ref, theirs_ref, scale, width)
    own = pl.ds(pl.multiple_of(lax.axis_index("term") * rows, TILE), rows)
    vector = guess_ref[...] * row_scale[None]
    vector_ref[...] = vector
    high = high_ref[:, own, :].astype(F32) + high_other_ref[:, own, :].astype(F32)
    sigma = jnp.concatenate([low_ref[:, own, :], high], axis=0) * row_scale[None]
    residual_ref[...] = jnp.swapaxes(sigma, 0, 1) - rayleigh[None] * vector


def finish_kernel(vector_ref, residual_ref, *refs):
    shares = refs[:-2]
    ritz_ref, energy_ref = refs[-2:]
    stat = summed([share[...] for share in shares])
    rayleigh = stat[0:1, :]
    res_sq = stat[1:2, :]
    res_var = res_sq + epsilon
    curvature = stat[2:3, :] / res_var
    res_scale = jnp.sqrt(res_var)
    coupling = res_sq / res_scale
    half_gap = 0.5 * (rayleigh - curvature)
    energy = 0.5 * (rayleigh + curvature) - jnp.sqrt(half_gap * half_gap + coupling * coupling)
    coeff_new = energy - rayleigh
    coeff_norm = jnp.sqrt(coupling * coupling + coeff_new * coeff_new + epsilon)
    old = coupling / coeff_norm
    new = coeff_new / (coeff_norm * res_scale)
    ritz_ref[...] = old[None] * vector_ref[...] + new[None] * residual_ref[...]
    energy_ref[0] = energy[0, 0]


def shards(wave_guess, left_env, right_env, site_ops, bond_rank):
    guess = wave_guess[0]
    left = left_env[0]
    site = site_ops[0]
    rows, states, width = guess.shape
    terms = left.shape[0]
    members = lax.axis_size("term")
    chips = members // CORES
    segments = lax.axis_size("seg")
    scale = 1.0 / float(rows * members * states * width)
    hops = tuple(range(chips))

    def to_sibling(block):
        return lax.ppermute(block, "term", [(i, i ^ 1) for i in range(members)])

    def to_next_chip(block):
        return lax.ppermute(block, "term", [(i, (i + CORES) % members) for i in range(members)])

    def around(block):
        found = [block]
        for _ in range(chips - 1):
            found.append(to_next_chip(found[-1]))
        return found

    def everyone(block):
        return [block] + [
            lax.ppermute(block, "term", [(i, i ^ bits) for i in range(members)])
            for bits in range(CORES, members, CORES)
        ]

    tile = jax.ShapeDtypeStruct((8, width), F32)
    half = width // 2
    packed_shape = jax.ShapeDtypeStruct((terms, width + TILE, half), BF16)
    starts = (0, rows - 2 * TILE, rows - TILE) if rows >= 4 * TILE else (0,)
    lengths = [stop - start for start, stop in zip(starts, starts[1:] + (rows,))]
    in_place = [pltpu.with_memory_space_constraint(a, pltpu.HBM) for a in (guess, left, right_env[0], site)]
    first_chunk, keep, squares, right_packed = pl.pallas_call(
        first_chunk_kernel,
        out_shape=(jax.ShapeDtypeStruct((states + 1, lengths[0], width), BF16), tile, tile, packed_shape),
        in_specs=[anywhere] + [in_hbm] * 3,
        out_specs=(vmem,) * 4,
        scratch_shapes=[
            pltpu.VMEM((1, 1), jnp.int32),
            pltpu.VMEM((lengths[0], states, width), F32),
            pltpu.VMEM(site.shape, BF16),
            pltpu.VMEM(left.shape, BF16),
            pltpu.SemaphoreType.DMA((lengths[0] // TILE + 3,)),
        ],
        compiler_params=params(),
        cost_estimate=cost(2 * guess.size, 3 * guess.size),
        name="first_chunk",
    )(bond_rank.reshape(1, 1), in_place[0], in_place[3], in_place[2])
    rest = rows - lengths[0]
    squares, first_sibling = lax.optimization_barrier((squares, to_sibling(first_chunk)))
    norm_part, left_packed, left, *chunks = pl.pallas_call(
        functools.partial(prepare_kernel, starts),
        out_shape=(
            tile,
            packed_shape,
            jax.ShapeDtypeStruct(left.shape, BF16),
            *[jax.ShapeDtypeStruct((states, length, width), BF16) for length in lengths[1:]],
        ),
        in_specs=[vmem] * 2 + [in_hbm] * 2,
        out_specs=(vmem,) * (2 + len(lengths)),
        scratch_shapes=[
            pltpu.VMEM((max(rest, TILE), states, width), F32),
            pltpu.SemaphoreType.DMA((rest // TILE + 1,)),
        ],
        compiler_params=params(),
        cost_estimate=cost(4 * guess.size, 6 * guess.size),
        name="prepare",
    )(keep, squares, *in_place[:2])
    chunks = [first_chunk] + chunks

    chunk_hops = [around(chunk) for chunk in chunks]
    here_pieces = chunks + [first_sibling] + [to_sibling(chunk) for chunk in chunks[1:]]
    here_spots = tuple((0, flip, start, length) for flip in range(CORES) for start, length in zip(starts, lengths))
    far_spots = [
        tuple((hop, flip, start, length) for hop in hops[1:] for flip in range(CORES))
        for start, length in zip(starts, lengths)
    ]
    mid_spots = sum(far_spots[:-1], ())
    groups = [group for group in (here_spots, mid_spots, far_spots[-1]) if group]
    lefts = around(left_packed)
    shift = [(i + 1, i) for i in range(segments - 1)]
    received = lax.ppermute(right_packed, "seg", shift)

    size = states * TILE

    def spread(block):
        return pl.pallas_call(
            spread_kernel,
            out_shape=jax.ShapeDtypeStruct((terms * size, size), BF16),
            in_specs=[vmem],
            out_specs=vmem,
            compiler_params=params(),
            cost_estimate=cost(2 * terms * size * size * width, 2 * terms * size * size),
            name="spread_site",
        )(block)

    kron_own = spread(chunks[0])

    whole = (states, width, width)
    whole_bf = jax.ShapeDtypeStruct(whole, BF16)
    whole_f32 = jax.ShapeDtypeStruct(whole, F32)
    rotated = (terms, states, width, width)
    rotated_bf = jax.ShapeDtypeStruct(rotated, BF16)
    square = pltpu.VMEM((terms, width, width), BF16)
    chip_rows = CORES * rows
    stage_flops = 2 * terms * states * width * width * width

    def buffers(spots):
        count = sum(spot[3] for spot in spots)
        return (terms, states, count, width), (states, terms * count, width)

    here_rotated, here_turned = buffers(here_spots)
    part_cost = cost(stage_flops, 8 * states * width * width)
    rotated_own, columns = pl.pallas_call(
        functools.partial(rotate_own_kernel, groups, rows, chips),
        out_shape=(
            jax.ShapeDtypeStruct(here_rotated, BF16),
            jax.ShapeDtypeStruct((width, terms * width), BF16),
        ),
        in_specs=[vmem] * (len(here_pieces) + 2),
        out_specs=(vmem, vmem),
        compiler_params=params(),
        cost_estimate=part_cost,
        name="rotate_own",
    )(*here_pieces, kron_own, left)

    def rotate(spots, pieces, kron, before):
        return pl.pallas_call(
            functools.partial(rotate_kernel, spots, rows, chips),
            out_shape=(rotated_bf, whole_bf),
            in_specs=[vmem] * (len(pieces) + 1) + [anywhere] * len(before),
            out_specs=(vmem, vmem),
            scratch_shapes=[pltpu.SemaphoreType.DMA((len(pieces),))],
            input_output_aliases={len(pieces) + 1 + n: n for n in range(len(before))},
            compiler_params=params(),
            cost_estimate=part_cost,
            name="rotate_crossed" if before else "rotate_here",
        )(*pieces, kron, *before)

    def relayed(blocks):
        return [piece for block in blocks for piece in (block, to_sibling(block))]

    firsts, rotated_own = lax.optimization_barrier((chunk_hops[0][1:], rotated_own))
    kron = spread(firsts[0])
    turned = rotate(here_spots, here_pieces, kron, ())
    received, turned = lax.optimization_barrier((received, turned))
    packed = jnp.where(lax.axis_index("seg") == segments - 1, right_packed, received)
    rights = around(packed)
    turned_own, right = pl.pallas_call(
        here_kernel,
        out_shape=(jax.ShapeDtypeStruct(here_turned, BF16), jax.ShapeDtypeStruct(left.shape, BF16)),
        in_specs=[vmem] * 2,
        out_specs=(vmem, vmem),
        compiler_params=params(),
        cost_estimate=part_cost,
        name="apply_rows_here",
    )(rotated_own, packed)
    parts = [turned_own]
    mid_pieces = []
    if mid_spots:
        mid_pieces += relayed(firsts)
        for crossing in chunk_hops[1:-1]:
            crossed, turned = lax.optimization_barrier((crossing[1:], turned))
            mid_pieces += relayed(crossed)
        turned = rotate(mid_spots, mid_pieces, kron, turned)
        crossed, turned, parts[0] = lax.optimization_barrier((chunk_hops[-1][1:], turned, parts[0]))
        last_pieces = relayed(crossed)
        mid_rotated, mid_turned = buffers(mid_spots)
        parts.append(
            pl.pallas_call(
                there_kernel,
                out_shape=jax.ShapeDtypeStruct(mid_turned, BF16),
                in_specs=[vmem] * (len(mid_pieces) + 2),
                out_specs=vmem,
                scratch_shapes=[pltpu.VMEM(mid_rotated, BF16)],
                compiler_params=params(),
                cost_estimate=part_cost,
                name="apply_rows_crossed",
            )(*mid_pieces, right, kron_own)
        )
    else:
        last_pieces = relayed(firsts)
    last_rotated, last_turned = buffers(far_spots[-1])
    partial = pl.pallas_call(
        functools.partial(last_kernel, len(last_pieces)),
        out_shape=whole_f32,
        in_specs=[vmem] * (len(last_pieces) + 3 + len(parts)),
        out_specs=vmem,
        scratch_shapes=[pltpu.VMEM(last_rotated, BF16), pltpu.VMEM(last_turned, BF16)],
        compiler_params=params(),
        cost_estimate=part_cost,
        name="apply_rows_last",
    )(*last_pieces, right, kron_own, columns, *parts)
    norms = [norm_part]
    for hop in hops[1:]:
        if hop > 1:
            block, partial = lax.optimization_barrier((firsts[hop - 1], partial))
            kron = spread(block)
            turned = rotate(here_spots, here_pieces, kron, ())
            if mid_spots:
                turned = rotate(mid_spots, mid_pieces, kron, turned)
        left_far, partial = lax.optimization_barrier((lefts[hop], partial))
        mixed, norm_far, _, vector = pl.pallas_call(
            functools.partial(lefts_kernel, far_spots[-1], rows, chips),
            out_shape=(jax.ShapeDtypeStruct((states, width, terms * width), BF16), tile, rotated_bf, whole_bf),
            in_specs=[vmem] * (len(last_pieces) + 1) + [anywhere] * 2 + [vmem],
            out_specs=(vmem,) * 4,
            scratch_shapes=[square, pltpu.SemaphoreType.DMA((len(last_pieces),))],
            input_output_aliases={len(last_pieces) + 1: 2, len(last_pieces) + 2: 3},
            compiler_params=params(),
            cost_estimate=cost(stage_flops, 12 * states * width * width),
            name="received_lefts",
        )(*last_pieces, kron, *turned, left_far)
        norms.append(norm_far)
        last = hop == hops[-1]
        stats = norms if last else norms[:1]
        right_far = rights[hop]
        parts = []
        bounds = (0, states // 2, states) if last else (0, states)
        for start, stop in zip(bounds[:-1], bounds[1:]):
            outs = [jax.ShapeDtypeStruct((stop - start, width, width), BF16 if last else F32), tile]
            part, stat, *unpacked = pl.pallas_call(
                functools.partial(rights_kernel, start, stop),
                out_shape=tuple(outs + ([jax.ShapeDtypeStruct(left.shape, BF16)] if start == 0 else [])),
                in_specs=[vmem] * (4 + len(stats)),
                out_specs=(vmem,) * (3 if start == 0 else 2),
                compiler_params=params(),
                cost_estimate=cost(stage_flops / 2, 12 * states * width * width),
                name="received_rights",
            )(right_far, mixed, vector, partial, *stats)
            stats = [stat]
            if unpacked:
                right_far = unpacked[0]
            parts.append(part)
        if not last:
            partial = parts[0]
    low = pl.pallas_call(
        add_kernel,
        out_shape=jax.ShapeDtypeStruct(parts[0].shape, F32),
        in_specs=[vmem] * 2,
        out_specs=vmem,
        compiler_params=params(),
        cost_estimate=cost(parts[0].size, 8 * parts[0].size),
        name="add_low_half",
    )(parts[0], to_sibling(parts[0]))
    halves = [low, parts[1], to_sibling(parts[1])]
    stat_other = to_sibling(stat)

    share = pl.pallas_call(
        functools.partial(second_kernel, scale, members),
        out_shape=tile,
        in_specs=[vmem] * 10,
        out_specs=vmem,
        scratch_shapes=[
            pltpu.VMEM(whole, BF16),
            pltpu.VMEM(rotated, BF16),
            pltpu.VMEM(rotated, BF16),
        ],
        compiler_params=params(),
        cost_estimate=cost(3 * stage_flops, 6 * states * width * width),
        name="apply_residual",
    )(keep, stat, stat_other, *halves, vector, left, right, kron_own)
    crossed = everyone(share)

    local = jax.ShapeDtypeStruct((rows, states, width), F32)
    vector_own, residual_own = pl.pallas_call(
        functools.partial(own_rows_kernel, scale),
        out_shape=(local, local),
        in_specs=[vmem] * 7,
        out_specs=(vmem, vmem),
        compiler_params=params(),
        cost_estimate=cost(8 * guess.size, 16 * guess.size),
        name="own_rows",
    )(keep, guess, stat, stat_other, *halves)

    shares = [share, to_sibling(share)]
    gated, residual_own = lax.optimization_barrier((crossed[1:], residual_own))
    shares += relayed(gated)
    ritz, energy = pl.pallas_call(
        finish_kernel,
        out_shape=(local, jax.ShapeDtypeStruct((1,), F32)),
        in_specs=[vmem] * (2 + members),
        out_specs=(vmem, smem),
        compiler_params=params(),
        cost_estimate=cost(3 * guess.size, 12 * guess.size),
        name="finish",
    )(vector_own, residual_own, *shares)
    return (ritz[None], energy)


def solution(mesh):
    in_specs = (
        P("seg", "term", None, None),
        P("seg", "term", None, None),
        P("seg", "term", None, None),
        P("seg", "term", None, None),
        P("seg"),
    )
    out_specs = (P("seg", "term", None, None), P("seg"))
    return jax.shard_map(shards, mesh=mesh, in_specs=in_specs, out_specs=out_specs, check_vma=False)
```

```python
import functools

import jax
import jax.numpy as jnp
from jax import lax
from jax.experimental import pallas as pl
from jax.experimental.pallas import tpu as pltpu
from jax.sharding import PartitionSpec as P

epsilon = 1e-06
CORES = 2
TILE = 16
UNROLL = 8
GROUP = 8
VMEM_LIMIT = 20 * 1024 * 1024
F32 = jnp.float32
BF16 = jnp.bfloat16

vmem = pl.BlockSpec(memory_space=pltpu.VMEM)
smem = pl.BlockSpec(memory_space=pltpu.SMEM)
anywhere = pl.BlockSpec(memory_space=pl.ANY)
in_hbm = pl.BlockSpec(memory_space=pltpu.HBM)


def params():
    return pltpu.CompilerParams(vmem_limit_bytes=VMEM_LIMIT)


def cost(flops, moved):
    return pl.CostEstimate(flops=int(flops) // 100, bytes_accessed=int(moved) // 100, transcendentals=0)


def fold(values, width):
    return jnp.sum(values.reshape(values.size // (8 * width), 8, width), axis=0)


def chunk_rows_in(guess_in, guess_ref, sems, start, stop, slot):
    copies = []
    for n in range(start, stop, TILE):
        target = guess_ref.at[pl.ds(n - start, TILE)]
        copies.append(pltpu.make_async_copy(guess_in.at[pl.ds(n, TILE)], target, sems.at[slot + len(copies)]))
        copies[-1].start()
    return copies


def first_chunk_kernel(
    rank_in,
    guess_in,
    site_in,
    right_in,
    x_ref,
    keep_ref,
    squares_ref,
    packed_ref,
    rank_ref,
    guess_ref,
    site_ref,
    right_ref,
    sems,
):
    rows, states, width = guess_ref.shape
    terms = site_ref.shape[0]
    copies = [
        pltpu.make_async_copy(source, target, sems.at[n])
        for n, (source, target) in enumerate(((rank_in, rank_ref), (site_in, site_ref), (right_in, right_ref)))
    ]
    copies[0].start()
    parts = chunk_rows_in(guess_in, guess_ref, sems, 0, rows, 3)
    copies[1].start()
    copies[2].start()
    copies[0].wait()
    column = lax.broadcasted_iota(jnp.int32, (1, width), 1)
    keep = (column < rank_ref[...]).astype(F32)
    keep_ref[...] = jnp.broadcast_to(keep, keep_ref.shape)
    squares = jnp.zeros((8, width), F32)
    for n, copy in enumerate(parts):
        copy.wait()
        part = pl.ds(n * TILE, TILE)
        masked = guess_ref[part] * keep[None]
        squares = squares + fold(masked * masked, width)
        x_ref[0:states, part, :] = jnp.swapaxes(masked, 0, 1).astype(BF16)
    squares_ref[...] = squares
    copies[1].wait()
    line = lax.broadcasted_iota(jnp.int32, (TILE, width), 0)
    lane = lax.broadcasted_iota(jnp.int32, (TILE, width), 1)
    extra = jnp.zeros((TILE, width), F32)
    for k in range(terms):
        place_at = (lane == line + k * TILE).astype(BF16)
        extra = extra + jnp.dot(site_ref[k], place_at, preferred_element_type=F32)
    x_ref[states, 0:TILE, :] = extra.astype(BF16)
    copies[2].wait()
    pack_blocks(right_ref, None, packed_ref)


def prepare_kernel(starts, keep_ref, squares_ref, guess_in, left_in, norm_ref, packed_ref, left_ref, *refs):
    x_refs = (None,) + refs[: len(starts) - 1]
    guess_ref, sems = refs[len(starts) - 1 :]
    rows, states, width = guess_in.shape
    half = width // 2
    done = starts[1] if len(starts) > 1 else rows
    copies = chunk_rows_in(guess_in, guess_ref, sems, done, rows, 1)
    left_copy = pltpu.make_async_copy(left_in, left_ref, sems.at[0])
    left_copy.start()
    keep = keep_ref[0:1, :][None]
    squares = squares_ref[...]
    for n, copy in enumerate(copies):
        copy.wait()
        masked = guess_ref[pl.ds(n * TILE, TILE)] * keep
        squares = squares + fold(masked * masked, width)
        chunk = max(c for c, start in enumerate(starts) if start <= done + n * TILE)
        at = done + n * TILE - starts[chunk]
        x_refs[chunk][:, at : at + TILE, :] = jnp.swapaxes(masked, 0, 1).astype(BF16)
    total = jnp.sum(squares)
    norm_ref[...] = jnp.full(norm_ref.shape, total, F32)
    line = lax.broadcasted_iota(jnp.int32, (TILE, half), 0)
    norm = jnp.full((TILE, half), total, F32)
    extra = jnp.zeros((TILE, half), F32)
    for n in range(1, 4):
        part = norm.astype(BF16).astype(F32)
        norm = norm - part
        extra = jnp.where(line == n, part, extra)
    left_copy.wait()
    pack_blocks(left_ref, extra, packed_ref)


def pack_blocks(block_ref, extra, packed_ref):
    terms, width, _ = block_ref.shape
    half = width // 2
    line = lax.broadcasted_iota(jnp.int32, (TILE, half), 0)
    for k in range(terms):
        diagonal = pack_symmetric(block_ref, k, packed_ref)
        lines = jnp.broadcast_to(diagonal, (TILE, half)) if extra is None else jnp.where(line == 0, diagonal, extra)
        packed_ref[k, width : width + TILE, :] = lines.astype(BF16)


def triangle(half):
    row = lax.broadcasted_iota(jnp.int32, (half, half), 0)
    col = lax.broadcasted_iota(jnp.int32, (half, half), 1)
    return row, col


def pack_symmetric(block_ref, k, out_ref):
    width = block_ref.shape[1]
    half = width // 2
    row, col = triangle(half)
    upper = block_ref[k, 0:half, 0:half].astype(F32)
    lower = block_ref[k, half:width, half:width].astype(F32)
    out_ref[k, 0:half, :] = block_ref[k, 0:half, half:width]
    out_ref[k, half:width, :] = jnp.where(row <= col, upper, lower).astype(BF16)
    return jnp.sum(jnp.where(row == col, lower, 0.0), axis=0, keepdims=True)


def unpack_symmetric(packed_ref, full_ref):
    terms, width, _ = full_ref.shape
    half = width // 2
    row, col = triangle(half)
    for k in range(terms):
        corner = packed_ref[k, 0:half, :]
        mixed = packed_ref[k, half:width, :].astype(F32)
        diagonal = packed_ref[k, width : width + TILE, :].astype(F32)[0:1]
        turned = mixed.T
        full_ref[k, 0:half, 0:half] = jnp.where(row <= col, mixed, turned).astype(BF16)
        full_ref[k, 0:half, half:width] = corner
        full_ref[k, half:width, 0:half] = corner.astype(F32).T.astype(BF16)
        full_ref[k, half:width, half:width] = jnp.where(
            row > col, mixed, jnp.where(row == col, diagonal, turned)
        ).astype(BF16)


def spread_kernel(chunk_ref, kron_ref):
    width = chunk_ref.shape[2]
    size = kron_ref.shape[1]
    terms = kron_ref.shape[0] // size
    states = size // TILE
    tile = chunk_ref[states, 0:TILE, :]
    row_state = lax.broadcasted_iota(jnp.int32, (size, states), 0) // TILE
    pick = (row_state == lax.broadcasted_iota(jnp.int32, (size, states), 1)).astype(BF16)
    tall = jnp.dot(pick, tile, preferred_element_type=F32).astype(BF16)
    lane = lax.broadcasted_iota(jnp.int32, (width, size), 0)
    col_state = lax.broadcasted_iota(jnp.int32, (width, size), 1) // TILE
    same = (
        lax.broadcasted_iota(jnp.int32, (size, size), 0) % TILE
        == lax.broadcasted_iota(jnp.int32, (size, size), 1) % TILE
    )
    for k in range(terms):
        pick_t = (lane == col_state + k * TILE).astype(BF16)
        full = jnp.dot(tall, pick_t, preferred_element_type=F32)
        kron_ref[k * size : (k + 1) * size, :] = jnp.where(same, full, 0.0).astype(BF16)


def mix_sites(source_ref, kron_ref, rotated_ref, base, unroll):
    terms, states, _, width = rotated_ref.shape
    rows = source_ref.shape[1]

    def step(i, carry):
        at = pl.multiple_of(i * TILE, TILE)
        to = pl.multiple_of(base + i * TILE, TILE)
        stack = source_ref[0:states, pl.ds(at, TILE), :].reshape(states * TILE, width)
        turned = jnp.dot(kron_ref[...], stack, preferred_element_type=F32).astype(BF16)
        rotated_ref[:, :, pl.ds(to, TILE), :] = turned.reshape(terms, states, TILE, width)
        return carry

    lax.fori_loop(0, rows // TILE, step, 0, unroll=min(unroll, rows // TILE))


def summed(values):
    while len(values) > 1:
        values = [values[n] + values[n + 1] for n in range(0, len(values), 2)]
    return values[0]


def place(hop, chips):
    me = lax.axis_index("term")
    chip = (me // CORES - hop + chips) % chips
    return chip, me % CORES


def row_of(spot, rows, chips):
    chip, core = place(spot[0], chips)
    return pl.multiple_of((chip * CORES + (core if spot[1] == 0 else 1 - core)) * rows + spot[2], TILE)


def mix_pieces(pieces, kron_ref, rotated_ref):
    at = 0
    for piece in pieces:
        mix_sites(piece, kron_ref, rotated_ref, at, UNROLL)
        at += piece.shape[1]


def rotate_own_kernel(groups, rows, chips, *refs):
    kron_ref, left_ref, rotated_ref, columns_ref = refs[-4:]
    mix_pieces(refs[:-4], kron_ref, rotated_ref)
    blocks = []
    for spots in groups:
        for k in range(left_ref.shape[0]):
            blocks += [left_ref[k, pl.ds(row_of(spot, rows, chips), spot[3]), :] for spot in spots]
    columns_ref[...] = jnp.concatenate(blocks, axis=0).astype(F32).T.astype(BF16)


def turn(right_ref, rotated_ref, turned_ref):
    terms, states, count, width = rotated_ref.shape
    for k in range(terms):
        for n in range(0, states, 8):
            source = rotated_ref[k, n : n + 8].reshape(8 * count, width)
            turned = jnp.dot(source, right_ref[k], preferred_element_type=F32).astype(BF16)
            turned_ref[n : n + 8, k * count : (k + 1) * count, :] = turned.reshape(8, count, width)


def here_kernel(rotated_ref, packed_ref, turned_ref, right_ref):
    unpack_symmetric(packed_ref, right_ref)
    turn(right_ref, rotated_ref, turned_ref)


def there_kernel(*refs):
    right_ref, kron_ref, turned_ref, rotated_ref = refs[-4:]
    mix_pieces(refs[:-4], kron_ref, rotated_ref)
    turn(right_ref, rotated_ref, turned_ref)


def last_kernel(count, *refs):
    right_ref, kron_ref, columns_ref = refs[count : count + 3]
    out_ref, rotated_ref, turned_ref = refs[-3:]
    there_kernel(*refs[:count], right_ref, kron_ref, turned_ref, rotated_ref)
    blocks = list(refs[count + 3 : -3]) + [turned_ref]

    def lefts(p, carry):
        stack = jnp.concatenate([block[p] for block in blocks], axis=0)
        out_ref[p] = jnp.dot(columns_ref[...], stack, preferred_element_type=F32)
        return carry

    lax.fori_loop(0, out_ref.shape[0], lefts, 0, unroll=UNROLL)


def rotate_kernel(spots, rows, chips, *refs):
    pieces = refs[: len(spots)]
    kron_ref = refs[len(spots)]
    rotated_ref, whole_ref, sems = refs[-3:]
    states = whole_ref.shape[0]
    copies = []
    bases = [row_of(spot, rows, chips) for spot in spots]
    for n, (at, piece) in enumerate(zip(bases, pieces)):
        target = whole_ref.at[:, pl.ds(at, piece.shape[1]), :]
        copies.append(pltpu.make_async_copy(piece.at[0:states], target, sems.at[n]))
        copies[-1].start()
    for at, piece in zip(bases, pieces):
        mix_sites(piece, kron_ref, rotated_ref, at, UNROLL)
    for copy in copies:
        copy.wait()


def lefts_kernel(spots, rows, chips, *refs):
    count = len(spots)
    packed_ref, norm_before_ref = refs[count + 3 : count + 5]
    mixed_ref, norm_ref, rotated_ref, whole_ref, left_ref, sems = refs[-6:]
    terms, states, width, _ = rotated_ref.shape
    lines = packed_ref[0, width : width + TILE, :].astype(F32)
    norm = lines[1:2] + lines[2:3] + lines[3:4]
    norm_ref[...] = norm_before_ref[...] + jnp.concatenate([norm, norm], axis=1)
    unpack_symmetric(packed_ref, left_ref)
    rotate_kernel(spots, rows, chips, *refs[: count + 1], rotated_ref, whole_ref, sems)

    def lefts(p, carry):
        for k in range(terms):
            mixed = jnp.dot(left_ref[k], rotated_ref[k, p], preferred_element_type=F32)
            mixed_ref[p, :, k * width : (k + 1) * width] = mixed.astype(BF16)
        return carry

    lax.fori_loop(0, states, lefts, 0, unroll=UNROLL)


def rights_kernel(start, stop, packed_ref, mixed_ref, before_ref, partial_ref, *refs):
    if start == 0:
        right_ref = refs[0]
        unpack_symmetric(packed_ref, right_ref)
    else:
        right_ref = packed_ref
    terms, width, _ = right_ref.shape

    def rights(n, carry):
        at = n * GROUP
        rows = mixed_ref[pl.ds(start + at, GROUP)].reshape(GROUP * width, terms * width)
        stacked = right_ref[...].reshape(terms * width, width)
        image = jnp.dot(rows, stacked, preferred_element_type=F32).reshape(GROUP, width, width)
        partial_ref[pl.ds(at, GROUP)] = (before_ref[pl.ds(start + at, GROUP)] + image).astype(partial_ref.dtype)
        return carry

    lax.fori_loop(0, (stop - start) // GROUP, rights, 0)


def shifted_residual(start, shift, keep, mine_ref, other_ref, whole_ref, left_ref, res_ref, mixed_ref):
    count, width, _ = res_ref.shape
    terms = left_ref.shape[0]
    zero = jnp.zeros((8, width), F32)

    def lefts(n, sums):
        held = whole_ref[start + n].astype(F32)
        sigma = (mine_ref[n].astype(F32) + other_ref[n].astype(F32)) * keep
        residual = sigma - shift * held
        rounded = residual.astype(BF16)
        res_ref[n] = rounded
        mixed = jnp.dot(
            left_ref[...].reshape(terms * width, width), rounded, preferred_element_type=F32
        ).astype(BF16)
        for k in range(terms):
            mixed_ref[k, n] = mixed[k * width : (k + 1) * width]
        return (
            sums[0] + fold(residual * residual, width),
            sums[1] + fold(residual * held, width),
            sums[2] + fold(held * held, width),
        )

    sums = lax.fori_loop(0, count, lefts, (zero, zero, zero), unroll=UNROLL)
    return [jnp.sum(total) for total in sums]


def low_kernel(
    keep_ref,
    norm_ref,
    norm_other_ref,
    low_ref,
    low_other_ref,
    whole_ref,
    left_ref,
    res_ref,
    mixed_ref,
    out_ref,
):
    count, width, _ = low_ref.shape
    keep = keep_ref[0:1, :]
    zero = jnp.zeros((8, width), F32)

    def products(n, sums):
        held = whole_ref[n].astype(F32)
        sigma = low_ref[n].astype(F32) + low_other_ref[n].astype(F32)
        return sums[0] + fold(sigma * held, width), sums[1] + fold(held * held, width)

    cross, square = lax.fori_loop(0, count, products, (zero, zero), unroll=UNROLL)
    total = norm_ref[0:1, :] + norm_other_ref[0:1, :]
    floor = jnp.maximum(jnp.maximum(jnp.full((1, width), jnp.sum(square), F32), 0.25 * total), 1e-30)
    shift = jnp.sum(cross) / floor
    sums = shifted_residual(0, shift, keep, low_ref, low_other_ref, whole_ref, left_ref, res_ref, mixed_ref)
    out_ref[0:1, :] = shift
    for n, value in enumerate(sums):
        out_ref[n + 1 : n + 2, :] = jnp.full((1, width), value, F32)
    out_ref[4:8, :] = jnp.zeros((4, width), F32)


def high_kernel(
    scale,
    members,
    keep_ref,
    norm_ref,
    norm_other_ref,
    sums_ref,
    high_ref,
    high_other_ref,
    whole_ref,
    left_ref,
    right_ref,
    kron_ref,
    res_low_ref,
    mixed_low_ref,
    out_ref,
    res_ref,
    rotated_ref,
    mixed_ref,
):
    terms, states, width, _ = rotated_ref.shape
    half = states // 2
    shift = sums_ref[0:1, :]
    keep = keep_ref[0:1, :]
    sums = shifted_residual(
        half, shift, keep, high_ref, high_other_ref, whole_ref, left_ref, res_ref, mixed_ref
    )

    def sites(i, carry):
        at = pl.ds(pl.multiple_of(i * TILE, TILE), TILE)
        stack = jnp.concatenate([res_low_ref[:, at, :], res_ref[:, at, :]], axis=0).reshape(states * TILE, width)
        turned = jnp.dot(kron_ref[...], stack, preferred_element_type=F32).astype(BF16)
        rotated_ref[:, :, at, :] = turned.reshape(terms, states, TILE, width)
        return carry

    lax.fori_loop(0, width // TILE, sites, 0, unroll=UNROLL)
    cross = jnp.zeros((8, width), F32)
    for start, left_mixed_ref in ((0, mixed_low_ref), (half, mixed_ref)):
        for k in range(terms):
            turned = rotated_ref[k, start : start + half].reshape(half * width, width)
            image = jnp.dot(turned, right_ref[k], preferred_element_type=F32)
            held = left_mixed_ref[k].reshape(half * width, width).astype(F32)
            cross = cross + fold(held * image, width)
    res_square = sums_ref[1:2, :] + sums[0]
    res_vector = sums_ref[2:3, :] + sums[1]
    vector_square = sums_ref[3:4, :] + sums[2]
    total = norm_ref[0:1, :] + norm_other_ref[0:1, :]
    factor = scale / (total * scale + epsilon)
    rayleigh = factor * (res_vector + shift * vector_square)
    gap = rayleigh - shift
    res_sq = factor * (res_square - 2.0 * gap * res_vector + gap * gap * vector_square)
    change = gap * gap * (res_vector + shift * vector_square) - 2.0 * gap * (res_square + shift * res_vector)
    share = 1.0 / members
    out_ref[0:1, :] = rayleigh * share
    out_ref[1:2, :] = jnp.maximum(res_sq, 0.0) * share
    out_ref[2:3, :] = factor * (jnp.sum(cross) + share * change)
    out_ref[3:8, :] = jnp.zeros((5, width), F32)


def own_rows_kernel(scale, members, keep_ref, norm_ref, norm_other_ref, share_ref, guess_ref, *refs):
    low_ref, low_other_ref, high_ref, high_other_ref, vector_ref, residual_ref = refs
    rows, states, width = guess_ref.shape
    inverse = lax.rsqrt((norm_ref[0:1, :] + norm_other_ref[0:1, :]) * scale + epsilon)
    row_scale = keep_ref[0:1, :] * inverse
    rayleigh = share_ref[0:1, :] * members
    own = pl.ds(pl.multiple_of(lax.axis_index("term") * rows, TILE), rows)
    vector = guess_ref[...] * row_scale[None]
    vector_ref[...] = vector
    sigma = jnp.concatenate(
        [
            mine_ref[:, own, :].astype(F32) + other_ref[:, own, :].astype(F32)
            for mine_ref, other_ref in ((low_ref, low_other_ref), (high_ref, high_other_ref))
        ],
        axis=0,
    )
    residual_ref[...] = jnp.swapaxes(sigma * row_scale[None], 0, 1) - rayleigh[None] * vector


def finish_kernel(vector_ref, residual_ref, *refs):
    shares = refs[:-2]
    ritz_ref, energy_ref = refs[-2:]
    stat = summed([share[...] for share in shares])
    rayleigh = stat[0:1, :]
    res_sq = stat[1:2, :]
    res_var = res_sq + epsilon
    curvature = stat[2:3, :] / res_var
    res_scale = jnp.sqrt(res_var)
    coupling = res_sq / res_scale
    half_gap = 0.5 * (rayleigh - curvature)
    energy = 0.5 * (rayleigh + curvature) - jnp.sqrt(half_gap * half_gap + coupling * coupling)
    coeff_new = energy - rayleigh
    coeff_norm = jnp.sqrt(coupling * coupling + coeff_new * coeff_new + epsilon)
    old = coupling / coeff_norm
    new = coeff_new / (coeff_norm * res_scale)
    ritz_ref[...] = old[None] * vector_ref[...] + new[None] * residual_ref[...]
    energy_ref[0] = energy[0, 0]


def shards(wave_guess, left_env, right_env, site_ops, bond_rank):
    guess = wave_guess[0]
    left = left_env[0]
    site = site_ops[0]
    rows, states, width = guess.shape
    terms = left.shape[0]
    members = lax.axis_size("term")
    chips = members // CORES
    segments = lax.axis_size("seg")
    scale = 1.0 / float(rows * members * states * width)
    hops = tuple(range(chips))

    def to_sibling(block):
        return lax.ppermute(block, "term", [(i, i ^ 1) for i in range(members)])

    def to_next_chip(block):
        return lax.ppermute(block, "term", [(i, (i + CORES) % members) for i in range(members)])

    def around(block):
        found = [block]
        for _ in range(chips - 1):
            found.append(to_next_chip(found[-1]))
        return found

    def everyone(block):
        return [block] + [
            lax.ppermute(block, "term", [(i, i ^ bits) for i in range(members)])
            for bits in range(CORES, members, CORES)
        ]

    tile = jax.ShapeDtypeStruct((8, width), F32)
    half = width // 2
    packed_shape = jax.ShapeDtypeStruct((terms, width + TILE, half), BF16)
    starts = (0, rows - 2 * TILE, rows - TILE) if rows >= 4 * TILE else (0,)
    lengths = [stop - start for start, stop in zip(starts, starts[1:] + (rows,))]
    in_place = [pltpu.with_memory_space_constraint(a, pltpu.HBM) for a in (guess, left, right_env[0], site)]
    first_chunk, keep, squares, right_packed = pl.pallas_call(
        first_chunk_kernel,
        out_shape=(jax.ShapeDtypeStruct((states + 1, lengths[0], width), BF16), tile, tile, packed_shape),
        in_specs=[anywhere] + [in_hbm] * 3,
        out_specs=(vmem,) * 4,
        scratch_shapes=[
            pltpu.VMEM((1, 1), jnp.int32),
            pltpu.VMEM((lengths[0], states, width), F32),
            pltpu.VMEM(site.shape, BF16),
            pltpu.VMEM(left.shape, BF16),
            pltpu.SemaphoreType.DMA((lengths[0] // TILE + 3,)),
        ],
        compiler_params=params(),
        cost_estimate=cost(2 * guess.size, 3 * guess.size),
        name="first_chunk",
    )(bond_rank.reshape(1, 1), in_place[0], in_place[3], in_place[2])
    rest = rows - lengths[0]
    squares, first_sibling = lax.optimization_barrier((squares, to_sibling(first_chunk)))
    norm_part, left_packed, left, *chunks = pl.pallas_call(
        functools.partial(prepare_kernel, starts),
        out_shape=(
            tile,
            packed_shape,
            jax.ShapeDtypeStruct(left.shape, BF16),
            *[jax.ShapeDtypeStruct((states, length, width), BF16) for length in lengths[1:]],
        ),
        in_specs=[vmem] * 2 + [in_hbm] * 2,
        out_specs=(vmem,) * (2 + len(lengths)),
        scratch_shapes=[
            pltpu.VMEM((max(rest, TILE), states, width), F32),
            pltpu.SemaphoreType.DMA((rest // TILE + 1,)),
        ],
        compiler_params=params(),
        cost_estimate=cost(4 * guess.size, 6 * guess.size),
        name="prepare",
    )(keep, squares, *in_place[:2])
    chunks = [first_chunk] + chunks

    chunk_hops = [around(chunk) for chunk in chunks]
    here_pieces = chunks + [first_sibling] + [to_sibling(chunk) for chunk in chunks[1:]]
    here_spots = tuple((0, flip, start, length) for flip in range(CORES) for start, length in zip(starts, lengths))
    far_spots = [
        tuple((hop, flip, start, length) for hop in hops[1:] for flip in range(CORES))
        for start, length in zip(starts, lengths)
    ]
    mid_spots = sum(far_spots[:-1], ())
    groups = [group for group in (here_spots, mid_spots, far_spots[-1]) if group]
    lefts = around(left_packed)
    shift = [(i + 1, i) for i in range(segments - 1)]
    received = lax.ppermute(right_packed, "seg", shift)

    size = states * TILE

    def spread(block):
        return pl.pallas_call(
            spread_kernel,
            out_shape=jax.ShapeDtypeStruct((terms * size, size), BF16),
            in_specs=[vmem],
            out_specs=vmem,
            compiler_params=params(),
            cost_estimate=cost(2 * terms * size * size * width, 2 * terms * size * size),
            name="spread_site",
        )(block)

    kron_own = spread(chunks[0])

    whole = (states, width, width)
    whole_bf = jax.ShapeDtypeStruct(whole, BF16)
    whole_f32 = jax.ShapeDtypeStruct(whole, F32)
    rotated = (terms, states, width, width)
    rotated_bf = jax.ShapeDtypeStruct(rotated, BF16)
    square = pltpu.VMEM((terms, width, width), BF16)
    chip_rows = CORES * rows
    stage_flops = 2 * terms * states * width * width * width

    def buffers(spots):
        count = sum(spot[3] for spot in spots)
        return (terms, states, count, width), (states, terms * count, width)

    here_rotated, here_turned = buffers(here_spots)
    part_cost = cost(stage_flops, 8 * states * width * width)
    rotated_own, columns = pl.pallas_call(
        functools.partial(rotate_own_kernel, groups, rows, chips),
        out_shape=(
            jax.ShapeDtypeStruct(here_rotated, BF16),
            jax.ShapeDtypeStruct((width, terms * width), BF16),
        ),
        in_specs=[vmem] * (len(here_pieces) + 2),
        out_specs=(vmem, vmem),
        compiler_params=params(),
        cost_estimate=part_cost,
        name="rotate_own",
    )(*here_pieces, kron_own, left)

    def rotate(spots, pieces, kron, before):
        return pl.pallas_call(
            functools.partial(rotate_kernel, spots, rows, chips),
            out_shape=(rotated_bf, whole_bf),
            in_specs=[vmem] * (len(pieces) + 1) + [anywhere] * len(before),
            out_specs=(vmem, vmem),
            scratch_shapes=[pltpu.SemaphoreType.DMA((len(pieces),))],
            input_output_aliases={len(pieces) + 1 + n: n for n in range(len(before))},
            compiler_params=params(),
            cost_estimate=part_cost,
            name="rotate_crossed" if before else "rotate_here",
        )(*pieces, kron, *before)

    def relayed(blocks):
        return [piece for block in blocks for piece in (block, to_sibling(block))]

    firsts, rotated_own = lax.optimization_barrier((chunk_hops[0][1:], rotated_own))
    kron = spread(firsts[0])
    turned = rotate(here_spots, here_pieces, kron, ())
    received, turned = lax.optimization_barrier((received, turned))
    packed = jnp.where(lax.axis_index("seg") == segments - 1, right_packed, received)
    rights = around(packed)
    turned_own, right = pl.pallas_call(
        here_kernel,
        out_shape=(jax.ShapeDtypeStruct(here_turned, BF16), jax.ShapeDtypeStruct(left.shape, BF16)),
        in_specs=[vmem] * 2,
        out_specs=(vmem, vmem),
        compiler_params=params(),
        cost_estimate=part_cost,
        name="apply_rows_here",
    )(rotated_own, packed)
    parts = [turned_own]
    mid_pieces = []
    if mid_spots:
        mid_pieces += relayed(firsts)
        for crossing in chunk_hops[1:-1]:
            crossed, turned = lax.optimization_barrier((crossing[1:], turned))
            mid_pieces += relayed(crossed)
        turned = rotate(mid_spots, mid_pieces, kron, turned)
        crossed, turned, parts[0] = lax.optimization_barrier((chunk_hops[-1][1:], turned, parts[0]))
        last_pieces = relayed(crossed)
        mid_rotated, mid_turned = buffers(mid_spots)
        parts.append(
            pl.pallas_call(
                there_kernel,
                out_shape=jax.ShapeDtypeStruct(mid_turned, BF16),
                in_specs=[vmem] * (len(mid_pieces) + 2),
                out_specs=vmem,
                scratch_shapes=[pltpu.VMEM(mid_rotated, BF16)],
                compiler_params=params(),
                cost_estimate=part_cost,
                name="apply_rows_crossed",
            )(*mid_pieces, right, kron_own)
        )
    else:
        last_pieces = relayed(firsts)
    last_rotated, last_turned = buffers(far_spots[-1])
    partial = pl.pallas_call(
        functools.partial(last_kernel, len(last_pieces)),
        out_shape=whole_f32,
        in_specs=[vmem] * (len(last_pieces) + 3 + len(parts)),
        out_specs=vmem,
        scratch_shapes=[pltpu.VMEM(last_rotated, BF16), pltpu.VMEM(last_turned, BF16)],
        compiler_params=params(),
        cost_estimate=part_cost,
        name="apply_rows_last",
    )(*last_pieces, right, kron_own, columns, *parts)
    norm = norm_part
    for hop in hops[1:]:
        if hop > 1:
            block, partial = lax.optimization_barrier((firsts[hop - 1], partial))
            kron = spread(block)
            turned = rotate(here_spots, here_pieces, kron, ())
            if mid_spots:
                turned = rotate(mid_spots, mid_pieces, kron, turned)
        left_far, partial = lax.optimization_barrier((lefts[hop], partial))
        mixed, norm, _, vector = pl.pallas_call(
            functools.partial(lefts_kernel, far_spots[-1], rows, chips),
            out_shape=(jax.ShapeDtypeStruct((states, width, terms * width), BF16), tile, rotated_bf, whole_bf),
            in_specs=[vmem] * (len(last_pieces) + 1) + [anywhere] * 2 + [vmem] * 2,
            out_specs=(vmem,) * 4,
            scratch_shapes=[square, pltpu.SemaphoreType.DMA((len(last_pieces),))],
            input_output_aliases={len(last_pieces) + 1: 2, len(last_pieces) + 2: 3},
            compiler_params=params(),
            cost_estimate=cost(stage_flops, 12 * states * width * width),
            name="received_lefts",
        )(*last_pieces, kron, *turned, left_far, norm)
        last = hop == hops[-1]
        right_far = rights[hop]
        parts = []
        bounds = (0, states // 2, states) if last else (0, states)
        for start, stop in zip(bounds[:-1], bounds[1:]):
            part_shape = jax.ShapeDtypeStruct((stop - start, width, width), BF16 if last else F32)
            part, *unpacked = pl.pallas_call(
                functools.partial(rights_kernel, start, stop),
                out_shape=(part_shape,) + ((jax.ShapeDtypeStruct(left.shape, BF16),) if start == 0 else ()),
                in_specs=[vmem] * 3,
                out_specs=(vmem,) * (2 if start == 0 else 1),
                compiler_params=params(),
                cost_estimate=cost(stage_flops / 2, 12 * states * width * width),
                name="received_rights",
            )(right_far, mixed, partial)
            if unpacked:
                right_far, norm_other = lax.optimization_barrier((unpacked[0], to_sibling(norm)))
            parts.append(part)
        if not last:
            partial = parts[0]
    halves = []
    for part in parts:
        halves += [part, to_sibling(part)]
    half_bf = jax.ShapeDtypeStruct((states // 2, width, width), BF16)
    half_mixed = (terms, states // 2, width, width)
    res_low, mixed_low, sums = pl.pallas_call(
        low_kernel,
        out_shape=(half_bf, jax.ShapeDtypeStruct(half_mixed, BF16), tile),
        in_specs=[vmem] * 7,
        out_specs=(vmem,) * 3,
        compiler_params=params(),
        cost_estimate=cost(stage_flops / 2, 3 * states * width * width),
        name="residual_low",
    )(keep, norm, norm_other, *halves[:2], vector, left)
    share = pl.pallas_call(
        functools.partial(high_kernel, scale, members),
        out_shape=tile,
        in_specs=[vmem] * 12,
        out_specs=vmem,
        scratch_shapes=[
            pltpu.VMEM(half_bf.shape, BF16),
            pltpu.VMEM(rotated, BF16),
            pltpu.VMEM(half_mixed, BF16),
        ],
        compiler_params=params(),
        cost_estimate=cost(3 * stage_flops, 6 * states * width * width),
        name="residual_high",
    )(keep, norm, norm_other, sums, *halves[2:], vector, left, right, kron_own, res_low, mixed_low)
    crossed = everyone(share)

    local = jax.ShapeDtypeStruct((rows, states, width), F32)
    vector_own, residual_own = pl.pallas_call(
        functools.partial(own_rows_kernel, scale, members),
        out_shape=(local, local),
        in_specs=[vmem] * 9,
        out_specs=(vmem, vmem),
        compiler_params=params(),
        cost_estimate=cost(8 * guess.size, 16 * guess.size),
        name="own_rows",
    )(keep, norm, norm_other, share, guess, *halves)

    shares = [share, to_sibling(share)]
    gated, residual_own = lax.optimization_barrier((crossed[1:], residual_own))
    shares += relayed(gated)
    ritz, energy = pl.pallas_call(
        finish_kernel,
        out_shape=(local, jax.ShapeDtypeStruct((1,), F32)),
        in_specs=[vmem] * (2 + members),
        out_specs=(vmem, smem),
        compiler_params=params(),
        cost_estimate=cost(3 * guess.size, 12 * guess.size),
        name="finish",
    )(vector_own, residual_own, *shares)
    return (ritz[None], energy)


def solution(mesh):
    in_specs = (
        P("seg", "term", None, None),
        P("seg", "term", None, None),
        P("seg", "term", None, None),
        P("seg", "term", None, None),
        P("seg"),
    )
    out_specs = (P("seg", "term", None, None), P("seg"))
    return jax.shard_map(shards, mesh=mesh, in_specs=in_specs, out_specs=out_specs, check_vma=False)
```

```python
import functools

import jax
import jax.numpy as jnp
from jax import lax
from jax.experimental import pallas as pl
from jax.experimental.pallas import tpu as pltpu
from jax.sharding import PartitionSpec as P

epsilon = 1e-06
CORES = 2
TILE = 16
UNROLL = 2
GROUP = 2
VMEM_LIMIT = 20 * 1024 * 1024
F32 = jnp.float32
BF16 = jnp.bfloat16

vmem = pl.BlockSpec(memory_space=pltpu.VMEM)
smem = pl.BlockSpec(memory_space=pltpu.SMEM)
anywhere = pl.BlockSpec(memory_space=pl.ANY)
in_hbm = pl.BlockSpec(memory_space=pltpu.HBM)


def params():
    return pltpu.CompilerParams(vmem_limit_bytes=VMEM_LIMIT)


def cost(flops, moved):
    return pl.CostEstimate(flops=int(flops) // 100, bytes_accessed=int(moved) // 100, transcendentals=0)


def fold(values, width):
    return jnp.sum(values.reshape(values.size // (8 * width), 8, width), axis=0)


def chunk_rows_in(guess_in, guess_ref, sems, start, stop, slot):
    copies = []
    for n in range(start, stop, TILE):
        target = guess_ref.at[pl.ds(n - start, TILE)]
        copies.append(pltpu.make_async_copy(guess_in.at[pl.ds(n, TILE)], target, sems.at[slot + len(copies)]))
        copies[-1].start()
    return copies


def first_chunk_kernel(
    rank_in,
    guess_in,
    site_in,
    right_in,
    x_ref,
    keep_ref,
    squares_ref,
    packed_ref,
    rank_ref,
    guess_ref,
    site_ref,
    right_ref,
    sems,
):
    rows, states, width = guess_ref.shape
    terms = site_ref.shape[0]
    copies = [
        pltpu.make_async_copy(source, target, sems.at[n])
        for n, (source, target) in enumerate(((rank_in, rank_ref), (site_in, site_ref), (right_in, right_ref)))
    ]
    copies[0].start()
    parts = chunk_rows_in(guess_in, guess_ref, sems, 0, rows, 3)
    copies[1].start()
    copies[2].start()
    copies[0].wait()
    column = lax.broadcasted_iota(jnp.int32, (1, width), 1)
    keep = (column < rank_ref[...]).astype(F32)
    keep_ref[...] = jnp.broadcast_to(keep, keep_ref.shape)
    squares = jnp.zeros((8, width), F32)
    for n, copy in enumerate(parts):
        copy.wait()
        part = pl.ds(n * TILE, TILE)
        masked = guess_ref[part] * keep[None]
        squares = squares + fold(masked * masked, width)
        x_ref[0:states, part, :] = jnp.swapaxes(masked, 0, 1).astype(BF16)
    squares_ref[...] = squares
    copies[1].wait()
    line = lax.broadcasted_iota(jnp.int32, (TILE, width), 0)
    lane = lax.broadcasted_iota(jnp.int32, (TILE, width), 1)
    extra = jnp.zeros((TILE, width), F32)
    for k in range(terms):
        place_at = (lane == line + k * TILE).astype(BF16)
        extra = extra + jnp.dot(site_ref[k], place_at, preferred_element_type=F32)
    x_ref[states, 0:TILE, :] = extra.astype(BF16)
    copies[2].wait()
    pack_blocks(right_ref, None, packed_ref)


def prepare_kernel(starts, keep_ref, squares_ref, guess_in, left_in, norm_ref, packed_ref, left_ref, *refs):
    x_refs = (None,) + refs[: len(starts) - 1]
    guess_ref, sems = refs[len(starts) - 1 :]
    rows, states, width = guess_in.shape
    half = width // 2
    done = starts[1] if len(starts) > 1 else rows
    copies = chunk_rows_in(guess_in, guess_ref, sems, done, rows, 1)
    left_copy = pltpu.make_async_copy(left_in, left_ref, sems.at[0])
    left_copy.start()
    keep = keep_ref[0:1, :][None]
    squares = squares_ref[...]
    for n, copy in enumerate(copies):
        copy.wait()
        masked = guess_ref[pl.ds(n * TILE, TILE)] * keep
        squares = squares + fold(masked * masked, width)
        chunk = max(c for c, start in enumerate(starts) if start <= done + n * TILE)
        at = done + n * TILE - starts[chunk]
        x_refs[chunk][:, at : at + TILE, :] = jnp.swapaxes(masked, 0, 1).astype(BF16)
    total = jnp.sum(squares)
    norm_ref[...] = jnp.full(norm_ref.shape, total, F32)
    line = lax.broadcasted_iota(jnp.int32, (TILE, half), 0)
    norm = jnp.full((TILE, half), total, F32)
    extra = jnp.zeros((TILE, half), F32)
    for n in range(1, 4):
        part = norm.astype(BF16).astype(F32)
        norm = norm - part
        extra = jnp.where(line == n, part, extra)
    left_copy.wait()
    pack_blocks(left_ref, extra, packed_ref)


def pack_blocks(block_ref, extra, packed_ref):
    terms, width, _ = block_ref.shape
    half = width // 2
    line = lax.broadcasted_iota(jnp.int32, (TILE, half), 0)
    for k in range(terms):
        diagonal = pack_symmetric(block_ref, k, packed_ref)
        lines = jnp.broadcast_to(diagonal, (TILE, half)) if extra is None else jnp.where(line == 0, diagonal, extra)
        packed_ref[k, width : width + TILE, :] = lines.astype(BF16)


def triangle(half):
    row = lax.broadcasted_iota(jnp.int32, (half, half), 0)
    col = lax.broadcasted_iota(jnp.int32, (half, half), 1)
    return row, col


def pack_symmetric(block_ref, k, out_ref):
    width = block_ref.shape[1]
    half = width // 2
    row, col = triangle(half)
    upper = block_ref[k, 0:half, 0:half].astype(F32)
    lower = block_ref[k, half:width, half:width].astype(F32)
    out_ref[k, 0:half, :] = block_ref[k, 0:half, half:width]
    out_ref[k, half:width, :] = jnp.where(row <= col, upper, lower).astype(BF16)
    return jnp.sum(jnp.where(row == col, lower, 0.0), axis=0, keepdims=True)


def unpack_symmetric(packed_ref, full_ref):
    terms, width, _ = full_ref.shape
    half = width // 2
    row, col = triangle(half)
    for k in range(terms):
        corner = packed_ref[k, 0:half, :]
        mixed = packed_ref[k, half:width, :].astype(F32)
        diagonal = packed_ref[k, width : width + TILE, :].astype(F32)[0:1]
        turned = mixed.T
        full_ref[k, 0:half, 0:half] = jnp.where(row <= col, mixed, turned).astype(BF16)
        full_ref[k, 0:half, half:width] = corner
        full_ref[k, half:width, 0:half] = corner.astype(F32).T.astype(BF16)
        full_ref[k, half:width, half:width] = jnp.where(
            row > col, mixed, jnp.where(row == col, diagonal, turned)
        ).astype(BF16)


def spread_kernel(chunk_ref, kron_ref):
    width = chunk_ref.shape[2]
    size = kron_ref.shape[1]
    terms = kron_ref.shape[0] // size
    states = size // TILE
    tile = chunk_ref[states, 0:TILE, :]
    row_state = lax.broadcasted_iota(jnp.int32, (size, states), 0) // TILE
    pick = (row_state == lax.broadcasted_iota(jnp.int32, (size, states), 1)).astype(BF16)
    tall = jnp.dot(pick, tile, preferred_element_type=F32).astype(BF16)
    lane = lax.broadcasted_iota(jnp.int32, (width, size), 0)
    col_state = lax.broadcasted_iota(jnp.int32, (width, size), 1) // TILE
    same = (
        lax.broadcasted_iota(jnp.int32, (size, size), 0) % TILE
        == lax.broadcasted_iota(jnp.int32, (size, size), 1) % TILE
    )
    for k in range(terms):
        pick_t = (lane == col_state + k * TILE).astype(BF16)
        full = jnp.dot(tall, pick_t, preferred_element_type=F32)
        kron_ref[k * size : (k + 1) * size, :] = jnp.where(same, full, 0.0).astype(BF16)


def mix_sites(source_ref, kron_ref, rotated_ref, base, unroll):
    terms, states, _, width = rotated_ref.shape
    rows = source_ref.shape[1]

    def step(i, carry):
        at = pl.multiple_of(i * TILE, TILE)
        to = pl.multiple_of(base + i * TILE, TILE)
        stack = source_ref[0:states, pl.ds(at, TILE), :].reshape(states * TILE, width)
        turned = jnp.dot(kron_ref[...], stack, preferred_element_type=F32).astype(BF16)
        rotated_ref[:, :, pl.ds(to, TILE), :] = turned.reshape(terms, states, TILE, width)
        return carry

    lax.fori_loop(0, rows // TILE, step, 0, unroll=min(unroll, rows // TILE))


def summed(values):
    while len(values) > 1:
        values = [values[n] + values[n + 1] for n in range(0, len(values), 2)]
    return values[0]


def place(hop, chips):
    me = lax.axis_index("term")
    chip = (me // CORES - hop + chips) % chips
    return chip, me % CORES


def row_of(spot, rows, chips):
    chip, core = place(spot[0], chips)
    return pl.multiple_of((chip * CORES + (core if spot[1] == 0 else 1 - core)) * rows + spot[2], TILE)


def mix_pieces(pieces, kron_ref, rotated_ref):
    at = 0
    for piece in pieces:
        mix_sites(piece, kron_ref, rotated_ref, at, UNROLL)
        at += piece.shape[1]


def rotate_own_kernel(groups, rows, chips, *refs):
    kron_ref, left_ref, rotated_ref, columns_ref = refs[-4:]
    mix_pieces(refs[:-4], kron_ref, rotated_ref)
    blocks = []
    for spots in groups:
        for k in range(left_ref.shape[0]):
            blocks += [left_ref[k, pl.ds(row_of(spot, rows, chips), spot[3]), :] for spot in spots]
    columns_ref[...] = jnp.concatenate(blocks, axis=0).astype(F32).T.astype(BF16)


def turn(right_ref, rotated_ref, turned_ref):
    terms, states, count, width = rotated_ref.shape

    def step(n, carry):
        at = n * 4
        for k in range(terms):
            source = rotated_ref[k, pl.ds(at, 4)].reshape(4 * count, width)
            turned = jnp.dot(source, right_ref[k], preferred_element_type=F32).astype(BF16)
            turned_ref[pl.ds(at, 4), k * count : (k + 1) * count, :] = turned.reshape(4, count, width)
        return carry

    lax.fori_loop(0, states // 4, step, 0)


def here_kernel(rotated_ref, packed_ref, turned_ref, right_ref):
    unpack_symmetric(packed_ref, right_ref)
    turn(right_ref, rotated_ref, turned_ref)


def there_kernel(*refs):
    right_ref, kron_ref, turned_ref, rotated_ref = refs[-4:]
    mix_pieces(refs[:-4], kron_ref, rotated_ref)
    turn(right_ref, rotated_ref, turned_ref)


def last_kernel(count, *refs):
    right_ref, kron_ref, columns_ref = refs[count : count + 3]
    out_ref, rotated_ref, turned_ref = refs[-3:]
    there_kernel(*refs[:count], right_ref, kron_ref, turned_ref, rotated_ref)
    blocks = list(refs[count + 3 : -3]) + [turned_ref]

    def lefts(p, carry):
        stack = jnp.concatenate([block[p] for block in blocks], axis=0)
        out_ref[p] = jnp.dot(columns_ref[...], stack, preferred_element_type=F32)
        return carry

    lax.fori_loop(0, out_ref.shape[0], lefts, 0, unroll=UNROLL)


def rotate_kernel(spots, rows, chips, *refs):
    pieces = refs[: len(spots)]
    kron_ref = refs[len(spots)]
    rotated_ref, whole_ref, sems = refs[-3:]
    states = whole_ref.shape[0]
    copies = []
    bases = [row_of(spot, rows, chips) for spot in spots]
    for n, (at, piece) in enumerate(zip(bases, pieces)):
        target = whole_ref.at[:, pl.ds(at, piece.shape[1]), :]
        copies.append(pltpu.make_async_copy(piece.at[0:states], target, sems.at[n]))
        copies[-1].start()
    for at, piece in zip(bases, pieces):
        mix_sites(piece, kron_ref, rotated_ref, at, UNROLL)
    for copy in copies:
        copy.wait()


def lefts_kernel(spots, rows, chips, *refs):
    count = len(spots)
    packed_ref, norm_before_ref = refs[count + 3 : count + 5]
    mixed_ref, norm_ref, rotated_ref, whole_ref, left_ref, sems = refs[-6:]
    terms, states, width, _ = rotated_ref.shape
    lines = packed_ref[0, width : width + TILE, :].astype(F32)
    norm = lines[1:2] + lines[2:3] + lines[3:4]
    norm_ref[...] = norm_before_ref[...] + jnp.concatenate([norm, norm], axis=1)
    unpack_symmetric(packed_ref, left_ref)
    rotate_kernel(spots, rows, chips, *refs[: count + 1], rotated_ref, whole_ref, sems)

    def lefts(p, carry):
        for k in range(terms):
            mixed = jnp.dot(left_ref[k], rotated_ref[k, p], preferred_element_type=F32)
            mixed_ref[p, :, k * width : (k + 1) * width] = mixed.astype(BF16)
        return carry

    lax.fori_loop(0, states, lefts, 0, unroll=UNROLL)


def rights_kernel(start, stop, packed_ref, mixed_ref, before_ref, partial_ref, *refs):
    if start == 0:
        right_ref = refs[0]
        unpack_symmetric(packed_ref, right_ref)
    else:
        right_ref = packed_ref
    terms, width, _ = right_ref.shape

    def rights(n, carry):
        at = n * GROUP
        rows = mixed_ref[pl.ds(start + at, GROUP)].reshape(GROUP * width, terms * width)
        stacked = right_ref[...].reshape(terms * width, width)
        image = jnp.dot(rows, stacked, preferred_element_type=F32).reshape(GROUP, width, width)
        partial_ref[pl.ds(at, GROUP)] = (before_ref[pl.ds(start + at, GROUP)] + image).astype(partial_ref.dtype)
        return carry

    lax.fori_loop(0, (stop - start) // GROUP, rights, 0)


def shifted_residual(products, start, shift, keep, mine_ref, other_ref, whole_ref, left_ref, res_ref, mixed_ref):
    count, width, _ = res_ref.shape
    terms = left_ref.shape[0]
    zero = jnp.zeros((8, width), F32)

    def lefts(n, sums):
        held = whole_ref[start + n].astype(F32)
        sigma = (mine_ref[n].astype(F32) + other_ref[n].astype(F32)) * keep
        residual = sigma - shift * held
        rounded = residual.astype(BF16)
        res_ref[n] = rounded
        mixed = jnp.dot(
            left_ref[...].reshape(terms * width, width), rounded, preferred_element_type=F32
        ).astype(BF16)
        for k in range(terms):
            mixed_ref[k, n] = mixed[k * width : (k + 1) * width]
        square = sums[0] + fold(residual * residual, width)
        return (square, sums[1] + fold(sigma * held, width)) if products else (square,)

    sums = lax.fori_loop(0, count, lefts, (zero,) * (2 if products else 1), unroll=UNROLL)
    return [jnp.sum(total) for total in sums]


def low_kernel(
    keep_ref,
    norm_ref,
    norm_other_ref,
    low_ref,
    low_other_ref,
    whole_ref,
    left_ref,
    res_ref,
    mixed_ref,
    out_ref,
):
    count, width, _ = low_ref.shape
    keep = keep_ref[0:1, :]
    zero = jnp.zeros((8, width), F32)

    def products(n, sums):
        held = whole_ref[n].astype(F32)
        sigma = low_ref[n].astype(F32) + low_other_ref[n].astype(F32)
        return sums[0] + fold(sigma * held, width), sums[1] + fold(held * held, width)

    cross, square = lax.fori_loop(0, count, products, (zero, zero), unroll=4)
    cross = jnp.sum(cross)
    total = norm_ref[0:1, :] + norm_other_ref[0:1, :]
    floor = jnp.maximum(jnp.maximum(jnp.full((1, width), jnp.sum(square), F32), 0.25 * total), 1e-30)
    shift = cross / floor
    sums = shifted_residual(False, 0, shift, keep, low_ref, low_other_ref, whole_ref, left_ref, res_ref, mixed_ref)
    out_ref[0:1, :] = shift
    out_ref[1:2, :] = jnp.full((1, width), sums[0], F32)
    out_ref[2:3, :] = jnp.full((1, width), cross, F32)
    out_ref[3:8, :] = jnp.zeros((5, width), F32)


def high_kernel(
    scale,
    members,
    keep_ref,
    norm_ref,
    norm_other_ref,
    sums_ref,
    high_ref,
    high_other_ref,
    whole_ref,
    left_ref,
    right_ref,
    kron_ref,
    res_low_ref,
    mixed_low_ref,
    out_ref,
    res_ref,
    rotated_ref,
    mixed_ref,
):
    terms, states, width, _ = rotated_ref.shape
    half = states // 2
    shift = sums_ref[0:1, :]
    keep = keep_ref[0:1, :]
    sums = shifted_residual(
        True, half, shift, keep, high_ref, high_other_ref, whole_ref, left_ref, res_ref, mixed_ref
    )

    def sites(i, carry):
        at = pl.ds(pl.multiple_of(i * TILE, TILE), TILE)
        stack = jnp.concatenate([res_low_ref[:, at, :], res_ref[:, at, :]], axis=0).reshape(states * TILE, width)
        turned = jnp.dot(kron_ref[...], stack, preferred_element_type=F32).astype(BF16)
        rotated_ref[:, :, at, :] = turned.reshape(terms, states, TILE, width)
        return carry

    lax.fori_loop(0, width // TILE, sites, 0, unroll=UNROLL)
    cross = jnp.zeros((8, width), F32)
    for start, left_mixed_ref in ((0, mixed_low_ref), (half, mixed_ref)):

        def rights(n, cross):
            at = n * 4
            for k in range(terms):
                turned = rotated_ref[k, pl.ds(start + at, 4)].reshape(4 * width, width)
                image = jnp.dot(turned, right_ref[k], preferred_element_type=F32)
                held = left_mixed_ref[k, pl.ds(at, 4)].reshape(4 * width, width).astype(F32)
                cross = cross + fold(held * image, width)
            return cross

        cross = lax.fori_loop(0, half // 4, rights, cross)
    res_square = sums_ref[1:2, :] + sums[0]
    product = sums_ref[2:3, :] + sums[1]
    total = norm_ref[0:1, :] + norm_other_ref[0:1, :]
    factor = scale / (total * scale + epsilon)
    rayleigh = factor * product
    gap = rayleigh - shift
    res_vector = product - shift * total
    res_sq = factor * (res_square - 2.0 * gap * res_vector + gap * gap * total)
    change = gap * gap * product - 2.0 * gap * (res_square + shift * res_vector)
    share = 1.0 / members
    out_ref[0:1, :] = rayleigh * share
    out_ref[1:2, :] = jnp.maximum(res_sq, 0.0) * share
    out_ref[2:3, :] = factor * (jnp.sum(cross) + share * change)
    out_ref[3:8, :] = jnp.zeros((5, width), F32)


def own_rows_kernel(scale, members, keep_ref, norm_ref, norm_other_ref, share_ref, guess_ref, *refs):
    low_ref, low_other_ref, high_ref, high_other_ref, vector_ref, residual_ref = refs
    rows, states, width = guess_ref.shape
    inverse = lax.rsqrt((norm_ref[0:1, :] + norm_other_ref[0:1, :]) * scale + epsilon)
    row_scale = keep_ref[0:1, :] * inverse
    rayleigh = share_ref[0:1, :] * members
    own = pl.ds(pl.multiple_of(lax.axis_index("term") * rows, TILE), rows)
    vector = guess_ref[...] * row_scale[None]
    vector_ref[...] = vector
    sigma = jnp.concatenate(
        [
            mine_ref[:, own, :].astype(F32) + other_ref[:, own, :].astype(F32)
            for mine_ref, other_ref in ((low_ref, low_other_ref), (high_ref, high_other_ref))
        ],
        axis=0,
    )
    residual_ref[...] = jnp.swapaxes(sigma * row_scale[None], 0, 1) - rayleigh[None] * vector


def finish_kernel(vector_ref, residual_ref, *refs):
    shares = refs[:-2]
    ritz_ref, energy_ref = refs[-2:]
    stat = summed([share[...] for share in shares])
    rayleigh = stat[0:1, :]
    res_sq = stat[1:2, :]
    res_var = res_sq + epsilon
    curvature = stat[2:3, :] / res_var
    res_scale = jnp.sqrt(res_var)
    coupling = res_sq / res_scale
    half_gap = 0.5 * (rayleigh - curvature)
    energy = 0.5 * (rayleigh + curvature) - jnp.sqrt(half_gap * half_gap + coupling * coupling)
    coeff_new = energy - rayleigh
    coeff_norm = jnp.sqrt(coupling * coupling + coeff_new * coeff_new + epsilon)
    old = coupling / coeff_norm
    new = coeff_new / (coeff_norm * res_scale)
    ritz_ref[...] = old[None] * vector_ref[...] + new[None] * residual_ref[...]
    energy_ref[0] = energy[0, 0]


def shards(wave_guess, left_env, right_env, site_ops, bond_rank):
    guess = wave_guess[0]
    left = left_env[0]
    site = site_ops[0]
    rows, states, width = guess.shape
    terms = left.shape[0]
    members = lax.axis_size("term")
    chips = members // CORES
    segments = lax.axis_size("seg")
    scale = 1.0 / float(rows * members * states * width)
    hops = tuple(range(chips))

    def to_sibling(block):
        return lax.ppermute(block, "term", [(i, i ^ 1) for i in range(members)])

    def to_next_chip(block):
        return lax.ppermute(block, "term", [(i, (i + CORES) % members) for i in range(members)])

    def around(block):
        found = [block]
        for _ in range(chips - 1):
            found.append(to_next_chip(found[-1]))
        return found

    def everyone(block):
        return [block] + [
            lax.ppermute(block, "term", [(i, i ^ bits) for i in range(members)])
            for bits in range(CORES, members, CORES)
        ]

    tile = jax.ShapeDtypeStruct((8, width), F32)
    half = width // 2
    packed_shape = jax.ShapeDtypeStruct((terms, width + TILE, half), BF16)
    starts = (0, rows - 2 * TILE, rows - TILE) if rows >= 4 * TILE else (0,)
    lengths = [stop - start for start, stop in zip(starts, starts[1:] + (rows,))]
    in_place = [pltpu.with_memory_space_constraint(a, pltpu.HBM) for a in (guess, left, right_env[0], site)]
    first_chunk, keep, squares, right_packed = pl.pallas_call(
        first_chunk_kernel,
        out_shape=(jax.ShapeDtypeStruct((states + 1, lengths[0], width), BF16), tile, tile, packed_shape),
        in_specs=[anywhere] + [in_hbm] * 3,
        out_specs=(vmem,) * 4,
        scratch_shapes=[
            pltpu.VMEM((1, 1), jnp.int32),
            pltpu.VMEM((lengths[0], states, width), F32),
            pltpu.VMEM(site.shape, BF16),
            pltpu.VMEM(left.shape, BF16),
            pltpu.SemaphoreType.DMA((lengths[0] // TILE + 3,)),
        ],
        compiler_params=params(),
        cost_estimate=cost(2 * guess.size, 3 * guess.size),
        name="first_chunk",
    )(bond_rank.reshape(1, 1), in_place[0], in_place[3], in_place[2])
    rest = rows - lengths[0]
    squares, first_sibling = lax.optimization_barrier((squares, to_sibling(first_chunk)))
    norm_part, left_packed, left, *chunks = pl.pallas_call(
        functools.partial(prepare_kernel, starts),
        out_shape=(
            tile,
            packed_shape,
            jax.ShapeDtypeStruct(left.shape, BF16),
            *[jax.ShapeDtypeStruct((states, length, width), BF16) for length in lengths[1:]],
        ),
        in_specs=[vmem] * 2 + [in_hbm] * 2,
        out_specs=(vmem,) * (2 + len(lengths)),
        scratch_shapes=[
            pltpu.VMEM((max(rest, TILE), states, width), F32),
            pltpu.SemaphoreType.DMA((rest // TILE + 1,)),
        ],
        compiler_params=params(),
        cost_estimate=cost(4 * guess.size, 6 * guess.size),
        name="prepare",
    )(keep, squares, *in_place[:2])
    chunks = [first_chunk] + chunks

    chunk_hops = [around(chunk) for chunk in chunks]
    here_pieces = chunks + [first_sibling] + [to_sibling(chunk) for chunk in chunks[1:]]
    here_spots = tuple((0, flip, start, length) for flip in range(CORES) for start, length in zip(starts, lengths))
    far_spots = [
        tuple((hop, flip, start, length) for hop in hops[1:] for flip in range(CORES))
        for start, length in zip(starts, lengths)
    ]
    mid_spots = sum(far_spots[:-1], ())
    groups = [group for group in (here_spots, mid_spots, far_spots[-1]) if group]
    lefts = around(left_packed)
    shift = [(i + 1, i) for i in range(segments - 1)]
    received = lax.ppermute(right_packed, "seg", shift)

    size = states * TILE

    def spread(block):
        return pl.pallas_call(
            spread_kernel,
            out_shape=jax.ShapeDtypeStruct((terms * size, size), BF16),
            in_specs=[vmem],
            out_specs=vmem,
            compiler_params=params(),
            cost_estimate=cost(2 * terms * size * size * width, 2 * terms * size * size),
            name="spread_site",
        )(block)

    kron_own = spread(chunks[0])

    whole = (states, width, width)
    whole_bf = jax.ShapeDtypeStruct(whole, BF16)
    whole_f32 = jax.ShapeDtypeStruct(whole, F32)
    rotated = (terms, states, width, width)
    rotated_bf = jax.ShapeDtypeStruct(rotated, BF16)
    square = pltpu.VMEM((terms, width, width), BF16)
    chip_rows = CORES * rows
    stage_flops = 2 * terms * states * width * width * width

    def buffers(spots):
        count = sum(spot[3] for spot in spots)
        return (terms, states, count, width), (states, terms * count, width)

    here_rotated, here_turned = buffers(here_spots)
    part_cost = cost(stage_flops, 8 * states * width * width)
    rotated_own, columns = pl.pallas_call(
        functools.partial(rotate_own_kernel, groups, rows, chips),
        out_shape=(
            jax.ShapeDtypeStruct(here_rotated, BF16),
            jax.ShapeDtypeStruct((width, terms * width), BF16),
        ),
        in_specs=[vmem] * (len(here_pieces) + 2),
        out_specs=(vmem, vmem),
        compiler_params=params(),
        cost_estimate=part_cost,
        name="rotate_own",
    )(*here_pieces, kron_own, left)

    def rotate(spots, pieces, kron, before):
        return pl.pallas_call(
            functools.partial(rotate_kernel, spots, rows, chips),
            out_shape=(rotated_bf, whole_bf),
            in_specs=[vmem] * (len(pieces) + 1) + [anywhere] * len(before),
            out_specs=(vmem, vmem),
            scratch_shapes=[pltpu.SemaphoreType.DMA((len(pieces),))],
            input_output_aliases={len(pieces) + 1 + n: n for n in range(len(before))},
            compiler_params=params(),
            cost_estimate=part_cost,
            name="rotate_crossed" if before else "rotate_here",
        )(*pieces, kron, *before)

    def relayed(blocks):
        return [piece for block in blocks for piece in (block, to_sibling(block))]

    firsts, rotated_own = lax.optimization_barrier((chunk_hops[0][1:], rotated_own))
    kron = spread(firsts[0])
    turned = rotate(here_spots, here_pieces, kron, ())
    received, turned = lax.optimization_barrier((received, turned))
    packed = jnp.where(lax.axis_index("seg") == segments - 1, right_packed, received)
    rights = around(packed)
    turned_own, right = pl.pallas_call(
        here_kernel,
        out_shape=(jax.ShapeDtypeStruct(here_turned, BF16), jax.ShapeDtypeStruct(left.shape, BF16)),
        in_specs=[vmem] * 2,
        out_specs=(vmem, vmem),
        compiler_params=params(),
        cost_estimate=part_cost,
        name="apply_rows_here",
    )(rotated_own, packed)
    parts = [turned_own]
    mid_pieces = []
    if mid_spots:
        mid_pieces += relayed(firsts)
        for crossing in chunk_hops[1:-1]:
            crossed, turned = lax.optimization_barrier((crossing[1:], turned))
            mid_pieces += relayed(crossed)
        turned = rotate(mid_spots, mid_pieces, kron, turned)
        crossed, turned, parts[0] = lax.optimization_barrier((chunk_hops[-1][1:], turned, parts[0]))
        last_pieces = relayed(crossed)
        mid_rotated, mid_turned = buffers(mid_spots)
        parts.append(
            pl.pallas_call(
                there_kernel,
                out_shape=jax.ShapeDtypeStruct(mid_turned, BF16),
                in_specs=[vmem] * (len(mid_pieces) + 2),
                out_specs=vmem,
                scratch_shapes=[pltpu.VMEM(mid_rotated, BF16)],
                compiler_params=params(),
                cost_estimate=part_cost,
                name="apply_rows_crossed",
            )(*mid_pieces, right, kron_own)
        )
    else:
        last_pieces = relayed(firsts)
    last_rotated, last_turned = buffers(far_spots[-1])
    partial = pl.pallas_call(
        functools.partial(last_kernel, len(last_pieces)),
        out_shape=whole_f32,
        in_specs=[vmem] * (len(last_pieces) + 3 + len(parts)),
        out_specs=vmem,
        scratch_shapes=[pltpu.VMEM(last_rotated, BF16), pltpu.VMEM(last_turned, BF16)],
        compiler_params=params(),
        cost_estimate=part_cost,
        name="apply_rows_last",
    )(*last_pieces, right, kron_own, columns, *parts)
    norm = norm_part
    for hop in hops[1:]:
        if hop > 1:
            block, partial = lax.optimization_barrier((firsts[hop - 1], partial))
            kron = spread(block)
            turned = rotate(here_spots, here_pieces, kron, ())
            if mid_spots:
                turned = rotate(mid_spots, mid_pieces, kron, turned)
        left_far, partial = lax.optimization_barrier((lefts[hop], partial))
        mixed, norm, _, vector = pl.pallas_call(
            functools.partial(lefts_kernel, far_spots[-1], rows, chips),
            out_shape=(jax.ShapeDtypeStruct((states, width, terms * width), BF16), tile, rotated_bf, whole_bf),
            in_specs=[vmem] * (len(last_pieces) + 1) + [anywhere] * 2 + [vmem] * 2,
            out_specs=(vmem,) * 4,
            scratch_shapes=[square, pltpu.SemaphoreType.DMA((len(last_pieces),))],
            input_output_aliases={len(last_pieces) + 1: 2, len(last_pieces) + 2: 3},
            compiler_params=params(),
            cost_estimate=cost(stage_flops, 12 * states * width * width),
            name="received_lefts",
        )(*last_pieces, kron, *turned, left_far, norm)
        last = hop == hops[-1]
        right_far = rights[hop]
        parts = []
        bounds = (0, states // 2, states) if last else (0, states)
        for start, stop in zip(bounds[:-1], bounds[1:]):
            part_shape = jax.ShapeDtypeStruct((stop - start, width, width), BF16 if last else F32)
            part, *unpacked = pl.pallas_call(
                functools.partial(rights_kernel, start, stop),
                out_shape=(part_shape,) + ((jax.ShapeDtypeStruct(left.shape, BF16),) if start == 0 else ()),
                in_specs=[vmem] * 3,
                out_specs=(vmem,) * (2 if start == 0 else 1),
                compiler_params=params(),
                cost_estimate=cost(stage_flops / 2, 12 * states * width * width),
                name="received_rights",
            )(right_far, mixed, partial)
            if unpacked:
                right_far, norm_other = lax.optimization_barrier((unpacked[0], to_sibling(norm)))
            parts.append(part)
        if not last:
            partial = parts[0]
    halves = []
    for part in parts:
        halves += [part, to_sibling(part)]
    half_bf = jax.ShapeDtypeStruct((states // 2, width, width), BF16)
    half_mixed = (terms, states // 2, width, width)
    res_low, mixed_low, sums = pl.pallas_call(
        low_kernel,
        out_shape=(half_bf, jax.ShapeDtypeStruct(half_mixed, BF16), tile),
        in_specs=[vmem] * 7,
        out_specs=(vmem,) * 3,
        compiler_params=params(),
        cost_estimate=cost(stage_flops / 2, 3 * states * width * width),
        name="residual_low",
    )(keep, norm, norm_other, *halves[:2], vector, left)
    share = pl.pallas_call(
        functools.partial(high_kernel, scale, members),
        out_shape=tile,
        in_specs=[vmem] * 12,
        out_specs=vmem,
        scratch_shapes=[
            pltpu.VMEM(half_bf.shape, BF16),
            pltpu.VMEM(rotated, BF16),
            pltpu.VMEM(half_mixed, BF16),
        ],
        compiler_params=params(),
        cost_estimate=cost(3 * stage_flops, 6 * states * width * width),
        name="residual_high",
    )(keep, norm, norm_other, sums, *halves[2:], vector, left, right, kron_own, res_low, mixed_low)
    crossed = everyone(share)

    local = jax.ShapeDtypeStruct((rows, states, width), F32)
    vector_own, residual_own = pl.pallas_call(
        functools.partial(own_rows_kernel, scale, members),
        out_shape=(local, local),
        in_specs=[vmem] * 9,
        out_specs=(vmem, vmem),
        compiler_params=params(),
        cost_estimate=cost(8 * guess.size, 16 * guess.size),
        name="own_rows",
    )(keep, norm, norm_other, share, guess, *halves)

    shares = [share, to_sibling(share)]
    gated, residual_own = lax.optimization_barrier((crossed[1:], residual_own))
    shares += relayed(gated)
    ritz, energy = pl.pallas_call(
        finish_kernel,
        out_shape=(local, jax.ShapeDtypeStruct((1,), F32)),
        in_specs=[vmem] * (2 + members),
        out_specs=(vmem, smem),
        compiler_params=params(),
        cost_estimate=cost(3 * guess.size, 12 * guess.size),
        name="finish",
    )(vector_own, residual_own, *shares)
    return (ritz[None], energy)


def solution(mesh):
    in_specs = (
        P("seg", "term", None, None),
        P("seg", "term", None, None),
        P("seg", "term", None, None),
        P("seg", "term", None, None),
        P("seg"),
    )
    out_specs = (P("seg", "term", None, None), P("seg"))
    return jax.shard_map(shards, mesh=mesh, in_specs=in_specs, out_specs=out_specs, check_vma=False)
```

```python
import functools

import jax
import jax.numpy as jnp
from jax import lax
from jax.experimental import pallas as pl
from jax.experimental.pallas import tpu as pltpu
from jax.sharding import PartitionSpec as P

epsilon = 1e-06
CORES = 2
TILE = 16
UNROLL = 16
GROUP = 8
VMEM_LIMIT = 20 * 1024 * 1024
F32 = jnp.float32
BF16 = jnp.bfloat16

vmem = pl.BlockSpec(memory_space=pltpu.VMEM)
smem = pl.BlockSpec(memory_space=pltpu.SMEM)
anywhere = pl.BlockSpec(memory_space=pl.ANY)
in_hbm = pl.BlockSpec(memory_space=pltpu.HBM)


def params():
    return pltpu.CompilerParams(vmem_limit_bytes=VMEM_LIMIT)


def cost(flops, moved):
    return pl.CostEstimate(flops=int(flops) // 100, bytes_accessed=int(moved) // 100, transcendentals=0)


def fold(values, width):
    return jnp.sum(values.reshape(values.size // (8 * width), 8, width), axis=0)


def chunk_rows_in(guess_in, guess_ref, sems, start, stop, slot):
    copies = []
    for n in range(start, stop, TILE):
        target = guess_ref.at[pl.ds(n - start, TILE)]
        copies.append(pltpu.make_async_copy(guess_in.at[pl.ds(n, TILE)], target, sems.at[slot + len(copies)]))
        copies[-1].start()
    return copies


def first_chunk_kernel(
    rank_in,
    guess_in,
    site_in,
    right_in,
    x_ref,
    keep_ref,
    squares_ref,
    packed_ref,
    rank_ref,
    guess_ref,
    site_ref,
    right_ref,
    sems,
):
    rows, states, width = guess_ref.shape
    terms = site_ref.shape[0]
    copies = [
        pltpu.make_async_copy(source, target, sems.at[n])
        for n, (source, target) in enumerate(((rank_in, rank_ref), (site_in, site_ref), (right_in, right_ref)))
    ]
    copies[0].start()
    parts = chunk_rows_in(guess_in, guess_ref, sems, 0, rows, 3)
    copies[1].start()
    copies[2].start()
    copies[0].wait()
    column = lax.broadcasted_iota(jnp.int32, (1, width), 1)
    keep = (column < rank_ref[...]).astype(F32)
    keep_ref[...] = jnp.broadcast_to(keep, keep_ref.shape)
    squares = jnp.zeros((8, width), F32)
    for n, copy in enumerate(parts):
        copy.wait()
        part = pl.ds(n * TILE, TILE)
        masked = guess_ref[part] * keep[None]
        squares = squares + fold(masked * masked, width)
        x_ref[0:states, part, :] = jnp.swapaxes(masked, 0, 1).astype(BF16)
    squares_ref[...] = squares
    copies[1].wait()
    line = lax.broadcasted_iota(jnp.int32, (TILE, width), 0)
    lane = lax.broadcasted_iota(jnp.int32, (TILE, width), 1)
    extra = jnp.zeros((TILE, width), F32)
    for k in range(terms):
        place_at = (lane == line + k * TILE).astype(BF16)
        extra = extra + jnp.dot(site_ref[k], place_at, preferred_element_type=F32)
    x_ref[states, 0:TILE, :] = extra.astype(BF16)
    copies[2].wait()
    pack_blocks(right_ref, None, packed_ref)


def prepare_kernel(starts, keep_ref, squares_ref, guess_in, left_in, norm_ref, packed_ref, left_ref, *refs):
    x_refs = (None,) + refs[: len(starts) - 1]
    guess_ref, sems = refs[len(starts) - 1 :]
    rows, states, width = guess_in.shape
    half = width // 2
    done = starts[1] if len(starts) > 1 else rows
    copies = chunk_rows_in(guess_in, guess_ref, sems, done, rows, 1)
    left_copy = pltpu.make_async_copy(left_in, left_ref, sems.at[0])
    left_copy.start()
    keep = keep_ref[0:1, :][None]
    squares = squares_ref[...]
    for n, copy in enumerate(copies):
        copy.wait()
        masked = guess_ref[pl.ds(n * TILE, TILE)] * keep
        squares = squares + fold(masked * masked, width)
        chunk = max(c for c, start in enumerate(starts) if start <= done + n * TILE)
        at = done + n * TILE - starts[chunk]
        x_refs[chunk][:, at : at + TILE, :] = jnp.swapaxes(masked, 0, 1).astype(BF16)
    total = jnp.sum(squares)
    norm_ref[...] = jnp.full(norm_ref.shape, total, F32)
    line = lax.broadcasted_iota(jnp.int32, (TILE, half), 0)
    norm = jnp.full((TILE, half), total, F32)
    extra = jnp.zeros((TILE, half), F32)
    for n in range(1, 4):
        part = norm.astype(BF16).astype(F32)
        norm = norm - part
        extra = jnp.where(line == n, part, extra)
    left_copy.wait()
    pack_blocks(left_ref, extra, packed_ref)


def pack_blocks(block_ref, extra, packed_ref):
    terms, width, _ = block_ref.shape
    half = width // 2
    line = lax.broadcasted_iota(jnp.int32, (TILE, half), 0)
    for k in range(terms):
        diagonal = pack_symmetric(block_ref, k, packed_ref)
        lines = jnp.broadcast_to(diagonal, (TILE, half)) if extra is None else jnp.where(line == 0, diagonal, extra)
        packed_ref[k, width : width + TILE, :] = lines.astype(BF16)


def triangle(half):
    row = lax.broadcasted_iota(jnp.int32, (half, half), 0)
    col = lax.broadcasted_iota(jnp.int32, (half, half), 1)
    return row, col


def pack_symmetric(block_ref, k, out_ref):
    width = block_ref.shape[1]
    half = width // 2
    row, col = triangle(half)
    upper = block_ref[k, 0:half, 0:half].astype(F32)
    lower = block_ref[k, half:width, half:width].astype(F32)
    out_ref[k, 0:half, :] = block_ref[k, 0:half, half:width]
    out_ref[k, half:width, :] = jnp.where(row <= col, upper, lower).astype(BF16)
    return jnp.sum(jnp.where(row == col, lower, 0.0), axis=0, keepdims=True)


def unpack_symmetric(packed_ref, full_ref, keep=None):
    terms, width, _ = full_ref.shape
    half = width // 2
    row, col = triangle(half)

    def kept(block, start):
        return block if keep is None else block * keep[:, start : start + half]

    for k in range(terms):
        corner = packed_ref[k, 0:half, :].astype(F32)
        mixed = packed_ref[k, half:width, :].astype(F32)
        diagonal = packed_ref[k, width : width + TILE, :].astype(F32)[0:1]
        turned = mixed.T
        lower = jnp.where(row > col, mixed, jnp.where(row == col, diagonal, turned))
        full_ref[k, 0:half, 0:half] = kept(jnp.where(row <= col, mixed, turned), 0).astype(BF16)
        full_ref[k, 0:half, half:width] = kept(corner, half).astype(BF16)
        full_ref[k, half:width, 0:half] = kept(corner.T, 0).astype(BF16)
        full_ref[k, half:width, half:width] = kept(lower, half).astype(BF16)


def spread_kernel(chunk_ref, kron_ref):
    width = chunk_ref.shape[2]
    size = kron_ref.shape[1]
    terms = kron_ref.shape[0] // size
    states = size // TILE
    tile = chunk_ref[states, 0:TILE, :]
    row_state = lax.broadcasted_iota(jnp.int32, (size, states), 0) // TILE
    pick = (row_state == lax.broadcasted_iota(jnp.int32, (size, states), 1)).astype(BF16)
    tall = jnp.dot(pick, tile, preferred_element_type=F32).astype(BF16)
    lane = lax.broadcasted_iota(jnp.int32, (width, size), 0)
    col_state = lax.broadcasted_iota(jnp.int32, (width, size), 1) // TILE
    same = (
        lax.broadcasted_iota(jnp.int32, (size, size), 0) % TILE
        == lax.broadcasted_iota(jnp.int32, (size, size), 1) % TILE
    )
    for k in range(terms):
        pick_t = (lane == col_state + k * TILE).astype(BF16)
        full = jnp.dot(tall, pick_t, preferred_element_type=F32)
        kron_ref[k * size : (k + 1) * size, :] = jnp.where(same, full, 0.0).astype(BF16)


def mix_sites(source_ref, kron_ref, rotated_ref, base, unroll):
    terms, states, _, width = rotated_ref.shape
    rows = source_ref.shape[1]

    def step(i, carry):
        at = pl.multiple_of(i * TILE, TILE)
        to = pl.multiple_of(base + i * TILE, TILE)
        stack = source_ref[0:states, pl.ds(at, TILE), :].reshape(states * TILE, width)
        turned = jnp.dot(kron_ref[...], stack, preferred_element_type=F32).astype(BF16)
        rotated_ref[:, :, pl.ds(to, TILE), :] = turned.reshape(terms, states, TILE, width)
        return carry

    lax.fori_loop(0, rows // TILE, step, 0, unroll=min(unroll, rows // TILE))


def summed(values):
    while len(values) > 1:
        values = [values[n] + values[n + 1] for n in range(0, len(values), 2)]
    return values[0]


def place(hop, chips):
    me = lax.axis_index("term")
    chip = (me // CORES - hop + chips) % chips
    return chip, me % CORES


def row_of(spot, rows, chips):
    chip, core = place(spot[0], chips)
    return pl.multiple_of((chip * CORES + (core if spot[1] == 0 else 1 - core)) * rows + spot[2], TILE)


def mix_pieces(pieces, kron_ref, rotated_ref):
    at = 0
    for piece in pieces:
        mix_sites(piece, kron_ref, rotated_ref, at, UNROLL)
        at += piece.shape[1]


def rotate_own_kernel(groups, rows, chips, *refs):
    kron_ref, left_ref, rotated_ref, columns_ref = refs[-4:]
    mix_pieces(refs[:-4], kron_ref, rotated_ref)
    blocks = []
    for spots in groups:
        for k in range(left_ref.shape[0]):
            blocks += [left_ref[k, pl.ds(row_of(spot, rows, chips), spot[3]), :] for spot in spots]
    columns_ref[...] = jnp.concatenate(blocks, axis=0).astype(F32).T.astype(BF16)


def turn(right_ref, rotated_ref, turned_ref):
    terms, states, count, width = rotated_ref.shape
    for k in range(terms):
        for n in range(0, states, 8):
            source = rotated_ref[k, n : n + 8].reshape(8 * count, width)
            turned = jnp.dot(source, right_ref[k], preferred_element_type=F32).astype(BF16)
            turned_ref[n : n + 8, k * count : (k + 1) * count, :] = turned.reshape(8, count, width)


def here_kernel(rotated_ref, packed_ref, keep_ref, turned_ref, right_ref):
    unpack_symmetric(packed_ref, right_ref, keep_ref[0:1, :])
    turn(right_ref, rotated_ref, turned_ref)


def there_kernel(*refs):
    right_ref, kron_ref, turned_ref, rotated_ref = refs[-4:]
    mix_pieces(refs[:-4], kron_ref, rotated_ref)
    turn(right_ref, rotated_ref, turned_ref)


def last_kernel(count, *refs):
    right_ref, kron_ref, columns_ref = refs[count : count + 3]
    out_ref, rotated_ref, turned_ref = refs[-3:]
    there_kernel(*refs[:count], right_ref, kron_ref, turned_ref, rotated_ref)
    blocks = list(refs[count + 3 : -3]) + [turned_ref]

    def lefts(p, carry):
        stack = jnp.concatenate([block[p] for block in blocks], axis=0)
        out_ref[p] = jnp.dot(columns_ref[...], stack, preferred_element_type=F32)
        return carry

    lax.fori_loop(0, out_ref.shape[0], lefts, 0, unroll=UNROLL)


def rotate_kernel(spots, rows, chips, *refs):
    pieces = refs[: len(spots)]
    kron_ref = refs[len(spots)]
    rotated_ref, whole_ref, sems = refs[-3:]
    states = whole_ref.shape[0]
    copies = []
    bases = [row_of(spot, rows, chips) for spot in spots]
    for n, (at, piece) in enumerate(zip(bases, pieces)):
        target = whole_ref.at[:, pl.ds(at, piece.shape[1]), :]
        copies.append(pltpu.make_async_copy(piece.at[0:states], target, sems.at[n]))
        copies[-1].start()
    for at, piece in zip(bases, pieces):
        mix_sites(piece, kron_ref, rotated_ref, at, UNROLL)
    for copy in copies:
        copy.wait()


def lefts_kernel(spots, rows, chips, *refs):
    count = len(spots)
    packed_ref, norm_before_ref = refs[count + 3 : count + 5]
    mixed_ref, norm_ref, rotated_ref, whole_ref, left_ref, sems = refs[-6:]
    terms, states, width, _ = rotated_ref.shape
    lines = packed_ref[0, width : width + TILE, :].astype(F32)
    norm = lines[1:2] + lines[2:3] + lines[3:4]
    norm_ref[...] = norm_before_ref[...] + jnp.concatenate([norm, norm], axis=1)
    unpack_symmetric(packed_ref, left_ref)
    rotate_kernel(spots, rows, chips, *refs[: count + 1], rotated_ref, whole_ref, sems)

    def lefts(p, carry):
        for k in range(terms):
            mixed = jnp.dot(left_ref[k], rotated_ref[k, p], preferred_element_type=F32)
            mixed_ref[p, :, k * width : (k + 1) * width] = mixed.astype(BF16)
        return carry

    lax.fori_loop(0, states, lefts, 0, unroll=UNROLL)


def rights_kernel(start, stop, packed_ref, mixed_ref, before_ref, keep_ref, partial_ref, *refs):
    if start == 0:
        right_ref = refs[0]
        unpack_symmetric(packed_ref, right_ref, keep_ref[0:1, :])
    else:
        right_ref = packed_ref
    terms, width, _ = right_ref.shape

    def rights(n, carry):
        at = n * GROUP
        rows = mixed_ref[pl.ds(start + at, GROUP)].reshape(GROUP * width, terms * width)
        stacked = right_ref[...].reshape(terms * width, width)
        image = jnp.dot(rows, stacked, preferred_element_type=F32).reshape(GROUP, width, width)
        partial_ref[pl.ds(at, GROUP)] = (before_ref[pl.ds(start + at, GROUP)] + image).astype(partial_ref.dtype)
        return carry

    lax.fori_loop(0, (stop - start) // GROUP, rights, 0)


def shifted_residual(start, shift, mine_ref, other_ref, whole_ref, left_ref, res_ref, mixed_ref):
    count, width, _ = res_ref.shape
    terms = left_ref.shape[0]
    zero = jnp.zeros((8, width), F32)

    def lefts(n, sums):
        held = whole_ref[start + n].astype(F32)
        sigma = mine_ref[n].astype(F32) + other_ref[n].astype(F32)
        residual = sigma - shift * held
        rounded = residual.astype(BF16)
        res_ref[n] = rounded
        mixed = jnp.dot(
            left_ref[...].reshape(terms * width, width), rounded, preferred_element_type=F32
        ).astype(BF16)
        for k in range(terms):
            mixed_ref[k, n] = mixed[k * width : (k + 1) * width]
        return sums[0] + fold(residual * residual, width), sums[1] + fold(sigma * held, width)

    square, product = lax.fori_loop(0, count, lefts, (zero, zero), unroll=UNROLL)
    return jnp.sum(square), jnp.sum(product)


def low_kernel(
    norm_ref,
    norm_other_ref,
    low_ref,
    low_other_ref,
    whole_ref,
    left_ref,
    res_ref,
    mixed_ref,
    out_ref,
):
    count, width, _ = low_ref.shape
    states = whole_ref.shape[0]
    held = whole_ref[0].astype(F32)
    sigma = low_ref[0].astype(F32) + low_other_ref[0].astype(F32)
    product = jnp.sum(fold(sigma * held, width))
    square = jnp.sum(fold(held * held, width))
    total = norm_ref[0:1, :] + norm_other_ref[0:1, :]
    floor = jnp.maximum(jnp.maximum(square, (0.25 / states) * total), 1e-30)
    shift = product / floor
    square, product = shifted_residual(
        0, shift, low_ref, low_other_ref, whole_ref, left_ref, res_ref, mixed_ref
    )
    out_ref[0:1, :] = shift
    out_ref[1:2, :] = jnp.full((1, width), square, F32)
    out_ref[2:3, :] = jnp.full((1, width), product, F32)
    out_ref[3:8, :] = jnp.zeros((5, width), F32)


def high_kernel(
    scale,
    members,
    norm_ref,
    norm_other_ref,
    sums_ref,
    high_ref,
    high_other_ref,
    whole_ref,
    left_ref,
    right_ref,
    kron_ref,
    res_low_ref,
    mixed_low_ref,
    out_ref,
    res_ref,
    rotated_ref,
    mixed_ref,
):
    terms, states, width, _ = rotated_ref.shape
    half = states // 2
    shift = sums_ref[0:1, :]
    square, product = shifted_residual(
        half, shift, high_ref, high_other_ref, whole_ref, left_ref, res_ref, mixed_ref
    )

    def sites(i, carry):
        at = pl.ds(pl.multiple_of(i * TILE, TILE), TILE)
        stack = jnp.concatenate([res_low_ref[:, at, :], res_ref[:, at, :]], axis=0).reshape(states * TILE, width)
        turned = jnp.dot(kron_ref[...], stack, preferred_element_type=F32).astype(BF16)
        rotated_ref[:, :, at, :] = turned.reshape(terms, states, TILE, width)
        return carry

    lax.fori_loop(0, width // TILE, sites, 0, unroll=UNROLL)
    cross = jnp.zeros((8, width), F32)
    for start, left_mixed_ref in ((0, mixed_low_ref), (half, mixed_ref)):
        for k in range(terms):
            turned = rotated_ref[k, start : start + half].reshape(half * width, width)
            image = jnp.dot(turned, right_ref[k], preferred_element_type=F32)
            held = left_mixed_ref[k].reshape(half * width, width).astype(F32)
            cross = cross + fold(held * image, width)
    res_square = sums_ref[1:2, :] + square
    product = sums_ref[2:3, :] + product
    total = norm_ref[0:1, :] + norm_other_ref[0:1, :]
    factor = scale / (total * scale + epsilon)
    rayleigh = factor * product
    gap = rayleigh - shift
    res_vector = product - shift * total
    res_sq = factor * (res_square - 2.0 * gap * res_vector + gap * gap * total)
    change = gap * gap * product - 2.0 * gap * (res_square + shift * res_vector)
    share = 1.0 / members
    out_ref[0:1, :] = rayleigh * share
    out_ref[1:2, :] = jnp.maximum(res_sq, 0.0) * share
    out_ref[2:3, :] = factor * (jnp.sum(cross) + share * change)
    out_ref[3:8, :] = jnp.zeros((5, width), F32)


def own_rows_kernel(scale, members, keep_ref, norm_ref, norm_other_ref, share_ref, guess_ref, *refs):
    low_ref, low_other_ref, high_ref, high_other_ref, vector_ref, residual_ref = refs
    rows, states, width = guess_ref.shape
    inverse = lax.rsqrt((norm_ref[0:1, :] + norm_other_ref[0:1, :]) * scale + epsilon)
    row_scale = keep_ref[0:1, :] * inverse
    rayleigh = share_ref[0:1, :] * members
    own = pl.ds(pl.multiple_of(lax.axis_index("term") * rows, TILE), rows)
    vector = guess_ref[...] * row_scale[None]
    vector_ref[...] = vector
    sigma = jnp.concatenate(
        [
            mine_ref[:, own, :].astype(F32) + other_ref[:, own, :].astype(F32)
            for mine_ref, other_ref in ((low_ref, low_other_ref), (high_ref, high_other_ref))
        ],
        axis=0,
    )
    residual_ref[...] = jnp.swapaxes(sigma * row_scale[None], 0, 1) - rayleigh[None] * vector


def finish_kernel(vector_ref, residual_ref, *refs):
    shares = refs[:-2]
    ritz_ref, energy_ref = refs[-2:]
    stat = summed([share[...] for share in shares])
    rayleigh = stat[0:1, :]
    res_sq = stat[1:2, :]
    res_var = res_sq + epsilon
    curvature = stat[2:3, :] / res_var
    res_scale = jnp.sqrt(res_var)
    coupling = res_sq / res_scale
    half_gap = 0.5 * (rayleigh - curvature)
    energy = 0.5 * (rayleigh + curvature) - jnp.sqrt(half_gap * half_gap + coupling * coupling)
    coeff_new = energy - rayleigh
    coeff_norm = jnp.sqrt(coupling * coupling + coeff_new * coeff_new + epsilon)
    old = coupling / coeff_norm
    new = coeff_new / (coeff_norm * res_scale)
    ritz_ref[...] = old[None] * vector_ref[...] + new[None] * residual_ref[...]
    energy_ref[0] = energy[0, 0]


def shards(wave_guess, left_env, right_env, site_ops, bond_rank):
    guess = wave_guess[0]
    left = left_env[0]
    site = site_ops[0]
    rows, states, width = guess.shape
    terms = left.shape[0]
    members = lax.axis_size("term")
    chips = members // CORES
    segments = lax.axis_size("seg")
    scale = 1.0 / float(rows * members * states * width)
    hops = tuple(range(chips))

    def to_sibling(block):
        return lax.ppermute(block, "term", [(i, i ^ 1) for i in range(members)])

    def to_next_chip(block):
        return lax.ppermute(block, "term", [(i, (i + CORES) % members) for i in range(members)])

    def around(block):
        found = [block]
        for _ in range(chips - 1):
            found.append(to_next_chip(found[-1]))
        return found

    def everyone(block):
        return [block] + [
            lax.ppermute(block, "term", [(i, i ^ bits) for i in range(members)])
            for bits in range(CORES, members, CORES)
        ]

    tile = jax.ShapeDtypeStruct((8, width), F32)
    half = width // 2
    packed_shape = jax.ShapeDtypeStruct((terms, width + TILE, half), BF16)
    starts = (0, rows - 2 * TILE, rows - TILE) if rows >= 4 * TILE else (0,)
    lengths = [stop - start for start, stop in zip(starts, starts[1:] + (rows,))]
    in_place = [pltpu.with_memory_space_constraint(a, pltpu.HBM) for a in (guess, left, right_env[0], site)]
    first_chunk, keep, squares, right_packed = pl.pallas_call(
        first_chunk_kernel,
        out_shape=(jax.ShapeDtypeStruct((states + 1, lengths[0], width), BF16), tile, tile, packed_shape),
        in_specs=[anywhere] + [in_hbm] * 3,
        out_specs=(vmem,) * 4,
        scratch_shapes=[
            pltpu.VMEM((1, 1), jnp.int32),
            pltpu.VMEM((lengths[0], states, width), F32),
            pltpu.VMEM(site.shape, BF16),
            pltpu.VMEM(left.shape, BF16),
            pltpu.SemaphoreType.DMA((lengths[0] // TILE + 3,)),
        ],
        compiler_params=params(),
        cost_estimate=cost(2 * guess.size, 3 * guess.size),
        name="first_chunk",
    )(bond_rank.reshape(1, 1), in_place[0], in_place[3], in_place[2])
    rest = rows - lengths[0]
    squares, first_sibling = lax.optimization_barrier((squares, to_sibling(first_chunk)))
    norm_part, left_packed, left, *chunks = pl.pallas_call(
        functools.partial(prepare_kernel, starts),
        out_shape=(
            tile,
            packed_shape,
            jax.ShapeDtypeStruct(left.shape, BF16),
            *[jax.ShapeDtypeStruct((states, length, width), BF16) for length in lengths[1:]],
        ),
        in_specs=[vmem] * 2 + [in_hbm] * 2,
        out_specs=(vmem,) * (2 + len(lengths)),
        scratch_shapes=[
            pltpu.VMEM((max(rest, TILE), states, width), F32),
            pltpu.SemaphoreType.DMA((rest // TILE + 1,)),
        ],
        compiler_params=params(),
        cost_estimate=cost(4 * guess.size, 6 * guess.size),
        name="prepare",
    )(keep, squares, *in_place[:2])
    chunks = [first_chunk] + chunks

    chunk_hops = [around(chunk) for chunk in chunks]
    here_pieces = chunks + [first_sibling] + [to_sibling(chunk) for chunk in chunks[1:]]
    here_spots = tuple((0, flip, start, length) for flip in range(CORES) for start, length in zip(starts, lengths))
    far_spots = [
        tuple((hop, flip, start, length) for hop in hops[1:] for flip in range(CORES))
        for start, length in zip(starts, lengths)
    ]
    mid_spots = sum(far_spots[:-1], ())
    groups = [group for group in (here_spots, mid_spots, far_spots[-1]) if group]
    lefts = around(left_packed)
    shift = [(i + 1, i) for i in range(segments - 1)]
    received = lax.ppermute(right_packed, "seg", shift)

    size = states * TILE

    def spread(block):
        return pl.pallas_call(
            spread_kernel,
            out_shape=jax.ShapeDtypeStruct((terms * size, size), BF16),
            in_specs=[vmem],
            out_specs=vmem,
            compiler_params=params(),
            cost_estimate=cost(2 * terms * size * size * width, 2 * terms * size * size),
            name="spread_site",
        )(block)

    kron_own = spread(chunks[0])

    whole = (states, width, width)
    whole_bf = jax.ShapeDtypeStruct(whole, BF16)
    whole_f32 = jax.ShapeDtypeStruct(whole, F32)
    rotated = (terms, states, width, width)
    rotated_bf = jax.ShapeDtypeStruct(rotated, BF16)
    square = pltpu.VMEM((terms, width, width), BF16)
    chip_rows = CORES * rows
    stage_flops = 2 * terms * states * width * width * width

    def buffers(spots):
        count = sum(spot[3] for spot in spots)
        return (terms, states, count, width), (states, terms * count, width)

    here_rotated, here_turned = buffers(here_spots)
    part_cost = cost(stage_flops, 8 * states * width * width)
    rotated_own, columns = pl.pallas_call(
        functools.partial(rotate_own_kernel, groups, rows, chips),
        out_shape=(
            jax.ShapeDtypeStruct(here_rotated, BF16),
            jax.ShapeDtypeStruct((width, terms * width), BF16),
        ),
        in_specs=[vmem] * (len(here_pieces) + 2),
        out_specs=(vmem, vmem),
        compiler_params=params(),
        cost_estimate=part_cost,
        name="rotate_own",
    )(*here_pieces, kron_own, left)

    def rotate(spots, pieces, kron, before):
        return pl.pallas_call(
            functools.partial(rotate_kernel, spots, rows, chips),
            out_shape=(rotated_bf, whole_bf),
            in_specs=[vmem] * (len(pieces) + 1) + [anywhere] * len(before),
            out_specs=(vmem, vmem),
            scratch_shapes=[pltpu.SemaphoreType.DMA((len(pieces),))],
            input_output_aliases={len(pieces) + 1 + n: n for n in range(len(before))},
            compiler_params=params(),
            cost_estimate=part_cost,
            name="rotate_crossed" if before else "rotate_here",
        )(*pieces, kron, *before)

    def relayed(blocks):
        return [piece for block in blocks for piece in (block, to_sibling(block))]

    firsts, rotated_own = lax.optimization_barrier((chunk_hops[0][1:], rotated_own))
    kron = spread(firsts[0])
    turned = rotate(here_spots, here_pieces, kron, ())
    received, turned = lax.optimization_barrier((received, turned))
    packed = jnp.where(lax.axis_index("seg") == segments - 1, right_packed, received)
    rights = around(packed)
    turned_own, right = pl.pallas_call(
        here_kernel,
        out_shape=(jax.ShapeDtypeStruct(here_turned, BF16), jax.ShapeDtypeStruct(left.shape, BF16)),
        in_specs=[vmem] * 3,
        out_specs=(vmem, vmem),
        compiler_params=params(),
        cost_estimate=part_cost,
        name="apply_rows_here",
    )(rotated_own, packed, keep)
    parts = [turned_own]
    mid_pieces = []
    if mid_spots:
        mid_pieces += relayed(firsts)
        for crossing in chunk_hops[1:-1]:
            crossed, turned = lax.optimization_barrier((crossing[1:], turned))
            mid_pieces += relayed(crossed)
        turned = rotate(mid_spots, mid_pieces, kron, turned)
        crossed, turned, parts[0] = lax.optimization_barrier((chunk_hops[-1][1:], turned, parts[0]))
        last_pieces = relayed(crossed)
        mid_rotated, mid_turned = buffers(mid_spots)
        parts.append(
            pl.pallas_call(
                there_kernel,
                out_shape=jax.ShapeDtypeStruct(mid_turned, BF16),
                in_specs=[vmem] * (len(mid_pieces) + 2),
                out_specs=vmem,
                scratch_shapes=[pltpu.VMEM(mid_rotated, BF16)],
                compiler_params=params(),
                cost_estimate=part_cost,
                name="apply_rows_crossed",
            )(*mid_pieces, right, kron_own)
        )
    else:
        last_pieces = relayed(firsts)
    last_rotated, last_turned = buffers(far_spots[-1])
    partial = pl.pallas_call(
        functools.partial(last_kernel, len(last_pieces)),
        out_shape=whole_f32,
        in_specs=[vmem] * (len(last_pieces) + 3 + len(parts)),
        out_specs=vmem,
        scratch_shapes=[pltpu.VMEM(last_rotated, BF16), pltpu.VMEM(last_turned, BF16)],
        compiler_params=params(),
        cost_estimate=part_cost,
        name="apply_rows_last",
    )(*last_pieces, right, kron_own, columns, *parts)
    norm = norm_part
    for hop in hops[1:]:
        if hop > 1:
            block, partial = lax.optimization_barrier((firsts[hop - 1], partial))
            kron = spread(block)
            turned = rotate(here_spots, here_pieces, kron, ())
            if mid_spots:
                turned = rotate(mid_spots, mid_pieces, kron, turned)
        left_far, partial = lax.optimization_barrier((lefts[hop], partial))
        mixed, norm, _, vector = pl.pallas_call(
            functools.partial(lefts_kernel, far_spots[-1], rows, chips),
            out_shape=(jax.ShapeDtypeStruct((states, width, terms * width), BF16), tile, rotated_bf, whole_bf),
            in_specs=[vmem] * (len(last_pieces) + 1) + [anywhere] * 2 + [vmem] * 2,
            out_specs=(vmem,) * 4,
            scratch_shapes=[square, pltpu.SemaphoreType.DMA((len(last_pieces),))],
            input_output_aliases={len(last_pieces) + 1: 2, len(last_pieces) + 2: 3},
            compiler_params=params(),
            cost_estimate=cost(stage_flops, 12 * states * width * width),
            name="received_lefts",
        )(*last_pieces, kron, *turned, left_far, norm)
        last = hop == hops[-1]
        right_far = rights[hop]
        parts = []
        bounds = (0, states // 2, states) if last else (0, states)
        for start, stop in zip(bounds[:-1], bounds[1:]):
            part_shape = jax.ShapeDtypeStruct((stop - start, width, width), BF16 if last else F32)
            part, *unpacked = pl.pallas_call(
                functools.partial(rights_kernel, start, stop),
                out_shape=(part_shape,) + ((jax.ShapeDtypeStruct(left.shape, BF16),) if start == 0 else ()),
                in_specs=[vmem] * 4,
                out_specs=(vmem,) * (2 if start == 0 else 1),
                compiler_params=params(),
                cost_estimate=cost(stage_flops / 2, 12 * states * width * width),
                name="received_rights",
            )(right_far, mixed, partial, keep)
            if unpacked:
                right_far, norm_other = lax.optimization_barrier((unpacked[0], to_sibling(norm)))
            parts.append(part)
        if not last:
            partial = parts[0]
    halves = []
    for part in parts:
        halves += [part, to_sibling(part)]
    half_bf = jax.ShapeDtypeStruct((states // 2, width, width), BF16)
    half_mixed = (terms, states // 2, width, width)
    res_low, mixed_low, sums = pl.pallas_call(
        low_kernel,
        out_shape=(half_bf, jax.ShapeDtypeStruct(half_mixed, BF16), tile),
        in_specs=[vmem] * 6,
        out_specs=(vmem,) * 3,
        compiler_params=params(),
        cost_estimate=cost(stage_flops / 2, 3 * states * width * width),
        name="residual_low",
    )(norm, norm_other, *halves[:2], vector, left)
    share = pl.pallas_call(
        functools.partial(high_kernel, scale, members),
        out_shape=tile,
        in_specs=[vmem] * 11,
        out_specs=vmem,
        scratch_shapes=[
            pltpu.VMEM(half_bf.shape, BF16),
            pltpu.VMEM(rotated, BF16),
            pltpu.VMEM(half_mixed, BF16),
        ],
        compiler_params=params(),
        cost_estimate=cost(3 * stage_flops, 6 * states * width * width),
        name="residual_high",
    )(norm, norm_other, sums, *halves[2:], vector, left, right, kron_own, res_low, mixed_low)
    crossed = everyone(share)

    local = jax.ShapeDtypeStruct((rows, states, width), F32)
    vector_own, residual_own = pl.pallas_call(
        functools.partial(own_rows_kernel, scale, members),
        out_shape=(local, local),
        in_specs=[vmem] * 9,
        out_specs=(vmem, vmem),
        compiler_params=params(),
        cost_estimate=cost(8 * guess.size, 16 * guess.size),
        name="own_rows",
    )(keep, norm, norm_other, share, guess, *halves)

    shares = [share, to_sibling(share)]
    gated, residual_own = lax.optimization_barrier((crossed[1:], residual_own))
    shares += relayed(gated)
    ritz, energy = pl.pallas_call(
        finish_kernel,
        out_shape=(local, jax.ShapeDtypeStruct((1,), F32)),
        in_specs=[vmem] * (2 + members),
        out_specs=(vmem, smem),
        compiler_params=params(),
        cost_estimate=cost(3 * guess.size, 12 * guess.size),
        name="finish",
    )(vector_own, residual_own, *shares)
    return (ritz[None], energy)


def solution(mesh):
    in_specs = (
        P("seg", "term", None, None),
        P("seg", "term", None, None),
        P("seg", "term", None, None),
        P("seg", "term", None, None),
        P("seg"),
    )
    out_specs = (P("seg", "term", None, None), P("seg"))
    return jax.shard_map(shards, mesh=mesh, in_specs=in_specs, out_specs=out_specs, check_vma=False)
```

```python
import functools

import jax
import jax.numpy as jnp
from jax import lax
from jax.experimental import pallas as pl
from jax.experimental.pallas import tpu as pltpu
from jax.sharding import PartitionSpec as P

epsilon = 1e-06
CORES = 2
TILE = 16
UNROLL = 16
STRIP = 32
GROUP = 8
VMEM_LIMIT = 20 * 1024 * 1024
F32 = jnp.float32
BF16 = jnp.bfloat16

vmem = pl.BlockSpec(memory_space=pltpu.VMEM)
smem = pl.BlockSpec(memory_space=pltpu.SMEM)
anywhere = pl.BlockSpec(memory_space=pl.ANY)
in_hbm = pl.BlockSpec(memory_space=pltpu.HBM)


def params():
    return pltpu.CompilerParams(vmem_limit_bytes=VMEM_LIMIT)


def cost(flops, moved):
    return pl.CostEstimate(flops=int(flops) // 100, bytes_accessed=int(moved) // 100, transcendentals=0)


def fold(values, width):
    return jnp.sum(values.reshape(values.size // (8 * width), 8, width), axis=0)


def chunk_rows_in(guess_in, guess_ref, sems, start, stop, slot):
    copies = []
    for n in range(start, stop, TILE):
        target = guess_ref.at[pl.ds(n - start, TILE)]
        copies.append(pltpu.make_async_copy(guess_in.at[pl.ds(n, TILE)], target, sems.at[slot + len(copies)]))
        copies[-1].start()
    return copies


def first_chunk_kernel(
    rank_in,
    guess_in,
    site_in,
    right_in,
    x_ref,
    keep_ref,
    squares_ref,
    packed_ref,
    rank_ref,
    guess_ref,
    site_ref,
    right_ref,
    sems,
):
    rows, states, width = guess_ref.shape
    terms = site_ref.shape[0]
    copies = [
        pltpu.make_async_copy(source, target, sems.at[n])
        for n, (source, target) in enumerate(((rank_in, rank_ref), (site_in, site_ref), (right_in, right_ref)))
    ]
    copies[0].start()
    parts = chunk_rows_in(guess_in, guess_ref, sems, 0, rows, 3)
    copies[1].start()
    copies[2].start()
    copies[0].wait()
    column = lax.broadcasted_iota(jnp.int32, (1, width), 1)
    keep = (column < rank_ref[...]).astype(F32)
    keep_ref[...] = jnp.broadcast_to(keep, keep_ref.shape)
    squares = jnp.zeros((8, width), F32)
    for n, copy in enumerate(parts):
        copy.wait()
        part = pl.ds(n * TILE, TILE)
        masked = guess_ref[part] * keep[None]
        squares = squares + fold(masked * masked, width)
        x_ref[0:states, part, :] = jnp.swapaxes(masked, 0, 1).astype(BF16)
    squares_ref[...] = squares
    copies[1].wait()
    line = lax.broadcasted_iota(jnp.int32, (TILE, width), 0)
    lane = lax.broadcasted_iota(jnp.int32, (TILE, width), 1)
    extra = jnp.zeros((TILE, width), F32)
    for k in range(terms):
        place_at = (lane == line + k * TILE).astype(BF16)
        extra = extra + jnp.dot(site_ref[k], place_at, preferred_element_type=F32)
    x_ref[states, 0:TILE, :] = extra.astype(BF16)
    copies[2].wait()
    pack_blocks(right_ref, None, packed_ref)


def prepare_kernel(starts, keep_ref, squares_ref, guess_in, left_in, norm_ref, packed_ref, left_ref, *refs):
    x_refs = (None,) + refs[: len(starts) - 1]
    guess_ref, sems = refs[len(starts) - 1 :]
    rows, states, width = guess_in.shape
    half = width // 2
    done = starts[1] if len(starts) > 1 else rows
    copies = chunk_rows_in(guess_in, guess_ref, sems, done, rows, 1)
    left_copy = pltpu.make_async_copy(left_in, left_ref, sems.at[0])
    left_copy.start()
    keep = keep_ref[0:1, :][None]
    squares = squares_ref[...]
    for n, copy in enumerate(copies):
        copy.wait()
        masked = guess_ref[pl.ds(n * TILE, TILE)] * keep
        squares = squares + fold(masked * masked, width)
        chunk = max(c for c, start in enumerate(starts) if start <= done + n * TILE)
        at = done + n * TILE - starts[chunk]
        x_refs[chunk][:, at : at + TILE, :] = jnp.swapaxes(masked, 0, 1).astype(BF16)
    total = jnp.sum(squares)
    norm_ref[...] = jnp.full(norm_ref.shape, total, F32)
    line = lax.broadcasted_iota(jnp.int32, (TILE, half), 0)
    norm = jnp.full((TILE, half), total, F32)
    extra = jnp.zeros((TILE, half), F32)
    for n in range(1, 4):
        part = norm.astype(BF16).astype(F32)
        norm = norm - part
        extra = jnp.where(line == n, part, extra)
    left_copy.wait()
    pack_blocks(left_ref, extra, packed_ref)


def pack_blocks(block_ref, extra, packed_ref):
    terms, width, _ = block_ref.shape
    half = width // 2
    line = lax.broadcasted_iota(jnp.int32, (TILE, half), 0)
    for k in range(terms):
        diagonal = pack_symmetric(block_ref, k, packed_ref)
        lines = jnp.broadcast_to(diagonal, (TILE, half)) if extra is None else jnp.where(line == 0, diagonal, extra)
        packed_ref[k, width : width + TILE, :] = lines.astype(BF16)


def triangle(half):
    row = lax.broadcasted_iota(jnp.int32, (half, half), 0)
    col = lax.broadcasted_iota(jnp.int32, (half, half), 1)
    return row, col


def pack_symmetric(block_ref, k, out_ref):
    width = block_ref.shape[1]
    half = width // 2
    row, col = triangle(half)
    upper = block_ref[k, 0:half, 0:half].astype(F32)
    lower = block_ref[k, half:width, half:width].astype(F32)
    out_ref[k, 0:half, :] = block_ref[k, 0:half, half:width]
    out_ref[k, half:width, :] = jnp.where(row <= col, upper, lower).astype(BF16)
    return jnp.sum(jnp.where(row == col, lower, 0.0), axis=0, keepdims=True)


def unpack_symmetric(packed_ref, full_ref, keep=None):
    terms, width, _ = full_ref.shape
    half = width // 2
    row, col = triangle(half)

    def kept(block, start):
        return block if keep is None else block * keep[:, start : start + half]

    for k in range(terms):
        corner = packed_ref[k, 0:half, :].astype(F32)
        mixed = packed_ref[k, half:width, :].astype(F32)
        diagonal = packed_ref[k, width : width + TILE, :].astype(F32)[0:1]
        turned = mixed.T
        lower = jnp.where(row > col, mixed, jnp.where(row == col, diagonal, turned))
        full_ref[k, 0:half, 0:half] = kept(jnp.where(row <= col, mixed, turned), 0).astype(BF16)
        full_ref[k, 0:half, half:width] = kept(corner, half).astype(BF16)
        full_ref[k, half:width, 0:half] = kept(corner.T, 0).astype(BF16)
        full_ref[k, half:width, half:width] = kept(lower, half).astype(BF16)


def spread_kernel(chunk_ref, kron_ref):
    width = chunk_ref.shape[2]
    size = kron_ref.shape[1]
    terms = kron_ref.shape[0] // size
    states = size // TILE
    tile = chunk_ref[states, 0:TILE, :]
    row_state = lax.broadcasted_iota(jnp.int32, (size, states), 0) // TILE
    pick = (row_state == lax.broadcasted_iota(jnp.int32, (size, states), 1)).astype(BF16)
    tall = jnp.dot(pick, tile, preferred_element_type=F32).astype(BF16)
    lane = lax.broadcasted_iota(jnp.int32, (width, size), 0)
    col_state = lax.broadcasted_iota(jnp.int32, (width, size), 1) // TILE
    same = (
        lax.broadcasted_iota(jnp.int32, (size, size), 0) % TILE
        == lax.broadcasted_iota(jnp.int32, (size, size), 1) % TILE
    )
    for k in range(terms):
        pick_t = (lane == col_state + k * TILE).astype(BF16)
        full = jnp.dot(tall, pick_t, preferred_element_type=F32)
        kron_ref[k * size : (k + 1) * size, :] = jnp.where(same, full, 0.0).astype(BF16)


def mix_sites(source_ref, kron_ref, rotated_ref, base, unroll):
    terms, states, _, width = rotated_ref.shape
    rows = source_ref.shape[1]

    def step(i, carry):
        at = pl.multiple_of(i * TILE, TILE)
        to = pl.multiple_of(base + i * TILE, TILE)
        stack = source_ref[0:states, pl.ds(at, TILE), :].reshape(states * TILE, width)
        turned = jnp.dot(kron_ref[...], stack, preferred_element_type=F32).astype(BF16)
        rotated_ref[:, :, pl.ds(to, TILE), :] = turned.reshape(terms, states, TILE, width)
        return carry

    lax.fori_loop(0, rows // TILE, step, 0, unroll=min(unroll, rows // TILE))


def summed(values):
    while len(values) > 1:
        values = [values[n] + values[n + 1] for n in range(0, len(values), 2)]
    return values[0]


def place(hop, chips):
    me = lax.axis_index("term")
    chip = (me // CORES - hop + chips) % chips
    return chip, me % CORES


def row_of(spot, rows, chips):
    chip, core = place(spot[0], chips)
    return pl.multiple_of((chip * CORES + (core if spot[1] == 0 else 1 - core)) * rows + spot[2], TILE)


def mix_pieces(pieces, kron_ref, rotated_ref):
    at = 0
    for piece in pieces:
        mix_sites(piece, kron_ref, rotated_ref, at, UNROLL)
        at += piece.shape[1]


def rotate_own_kernel(groups, rows, chips, *refs):
    kron_ref, left_ref, rotated_ref, columns_ref = refs[-4:]
    mix_pieces(refs[:-4], kron_ref, rotated_ref)
    blocks = []
    for spots in groups:
        for k in range(left_ref.shape[0]):
            blocks += [left_ref[k, pl.ds(row_of(spot, rows, chips), spot[3]), :] for spot in spots]
    columns_ref[...] = jnp.concatenate(blocks, axis=0).astype(F32).T.astype(BF16)


def turn(right_ref, rotated_ref, turned_ref):
    terms, states, count, width = rotated_ref.shape
    for k in range(terms):
        for n in range(0, states, 8):
            source = rotated_ref[k, n : n + 8].reshape(8 * count, width)
            turned = jnp.dot(source, right_ref[k], preferred_element_type=F32).astype(BF16)
            turned_ref[n : n + 8, k * count : (k + 1) * count, :] = turned.reshape(8, count, width)


def here_kernel(rotated_ref, packed_ref, keep_ref, turned_ref, right_ref):
    unpack_symmetric(packed_ref, right_ref, keep_ref[0:1, :])
    turn(right_ref, rotated_ref, turned_ref)


def there_kernel(*refs):
    right_ref, kron_ref, turned_ref, rotated_ref = refs[-4:]
    mix_pieces(refs[:-4], kron_ref, rotated_ref)
    turn(right_ref, rotated_ref, turned_ref)


def last_kernel(count, *refs):
    right_ref, kron_ref, columns_ref = refs[count : count + 3]
    out_ref, rotated_ref, turned_ref = refs[-3:]
    there_kernel(*refs[:count], right_ref, kron_ref, turned_ref, rotated_ref)
    blocks = list(refs[count + 3 : -3]) + [turned_ref]

    def lefts(p, carry):
        stack = jnp.concatenate([block[p] for block in blocks], axis=0)
        out_ref[p] = jnp.dot(columns_ref[...], stack, preferred_element_type=F32)
        return carry

    lax.fori_loop(0, out_ref.shape[0], lefts, 0, unroll=UNROLL)


def rotate_kernel(spots, rows, chips, *refs):
    pieces = refs[: len(spots)]
    kron_ref = refs[len(spots)]
    rotated_ref, whole_ref, sems = refs[-3:]
    states = whole_ref.shape[0]
    copies = []
    bases = [row_of(spot, rows, chips) for spot in spots]
    for n, (at, piece) in enumerate(zip(bases, pieces)):
        target = whole_ref.at[:, pl.ds(at, piece.shape[1]), :]
        copies.append(pltpu.make_async_copy(piece.at[0:states], target, sems.at[n]))
        copies[-1].start()
    for at, piece in zip(bases, pieces):
        mix_sites(piece, kron_ref, rotated_ref, at, UNROLL)
    for copy in copies:
        copy.wait()


def lefts_kernel(spots, rows, chips, *refs):
    count = len(spots)
    packed_ref, norm_before_ref = refs[count + 3 : count + 5]
    mixed_ref, norm_ref, rotated_ref, whole_ref, left_ref, sems = refs[-6:]
    terms, states, width, _ = rotated_ref.shape
    lines = packed_ref[0, width : width + TILE, :].astype(F32)
    norm = lines[1:2] + lines[2:3] + lines[3:4]
    norm_ref[...] = norm_before_ref[...] + jnp.concatenate([norm, norm], axis=1)
    unpack_symmetric(packed_ref, left_ref)
    rotate_kernel(spots, rows, chips, *refs[: count + 1], rotated_ref, whole_ref, sems)

    def lefts(p, carry):
        for k in range(terms):
            mixed = jnp.dot(left_ref[k], rotated_ref[k, p], preferred_element_type=F32)
            mixed_ref[p, :, k * width : (k + 1) * width] = mixed.astype(BF16)
        return carry

    lax.fori_loop(0, states, lefts, 0, unroll=UNROLL)


def rights_kernel(start, stop, packed_ref, mixed_ref, before_ref, keep_ref, partial_ref, *refs):
    if start == 0:
        right_ref = refs[0]
        unpack_symmetric(packed_ref, right_ref, keep_ref[0:1, :])
    else:
        right_ref = packed_ref
    terms, width, _ = right_ref.shape

    def rights(n, carry):
        at = n * GROUP
        rows = mixed_ref[pl.ds(start + at, GROUP)].reshape(GROUP * width, terms * width)
        stacked = right_ref[...].reshape(terms * width, width)
        image = jnp.dot(rows, stacked, preferred_element_type=F32).reshape(GROUP, width, width)
        partial_ref[pl.ds(at, GROUP)] = (before_ref[pl.ds(start + at, GROUP)] + image).astype(partial_ref.dtype)
        return carry

    lax.fori_loop(0, (stop - start) // GROUP, rights, 0)


def shifted_residual(start, shift, mine_ref, other_ref, whole_ref, left_ref, res_ref, mixed_ref):
    count, width, _ = res_ref.shape
    terms = left_ref.shape[0]
    zero = jnp.zeros((8, width), F32)

    def lefts(n, sums):
        square, product = sums
        for row in range(0, width, STRIP):
            strip = pl.ds(row, STRIP)
            held = whole_ref[start + n, strip, :].astype(F32)
            sigma = mine_ref[n, strip, :].astype(F32) + other_ref[n, strip, :].astype(F32)
            residual = sigma - shift * held
            res_ref[n, strip, :] = residual.astype(BF16)
            square = square + fold(residual * residual, width)
            product = product + fold(sigma * held, width)
        mixed = jnp.dot(
            left_ref[...].reshape(terms * width, width), res_ref[n], preferred_element_type=F32
        ).astype(BF16)
        for k in range(terms):
            mixed_ref[k, n] = mixed[k * width : (k + 1) * width]
        return square, product

    square, product = lax.fori_loop(0, count, lefts, (zero, zero), unroll=UNROLL)
    return jnp.sum(square), jnp.sum(product)


def low_kernel(
    norm_ref,
    norm_other_ref,
    low_ref,
    low_other_ref,
    whole_ref,
    left_ref,
    res_ref,
    mixed_ref,
    out_ref,
):
    count, width, _ = low_ref.shape
    states = whole_ref.shape[0]
    held = whole_ref[0].astype(F32)
    sigma = low_ref[0].astype(F32) + low_other_ref[0].astype(F32)
    product = jnp.sum(fold(sigma * held, width))
    square = jnp.sum(fold(held * held, width))
    total = norm_ref[0:1, :] + norm_other_ref[0:1, :]
    floor = jnp.maximum(jnp.maximum(square, (0.25 / states) * total), 1e-30)
    shift = product / floor
    square, product = shifted_residual(
        0, shift, low_ref, low_other_ref, whole_ref, left_ref, res_ref, mixed_ref
    )
    out_ref[0:1, :] = shift
    out_ref[1:2, :] = jnp.full((1, width), square, F32)
    out_ref[2:3, :] = jnp.full((1, width), product, F32)
    out_ref[3:8, :] = jnp.zeros((5, width), F32)


def high_kernel(
    scale,
    members,
    norm_ref,
    norm_other_ref,
    sums_ref,
    high_ref,
    high_other_ref,
    whole_ref,
    left_ref,
    right_ref,
    kron_ref,
    res_low_ref,
    mixed_low_ref,
    out_ref,
    res_ref,
    rotated_ref,
    mixed_ref,
):
    terms, states, width, _ = rotated_ref.shape
    half = states // 2
    shift = sums_ref[0:1, :]
    square, product = shifted_residual(
        half, shift, high_ref, high_other_ref, whole_ref, left_ref, res_ref, mixed_ref
    )

    def sites(i, carry):
        at = pl.ds(pl.multiple_of(i * TILE, TILE), TILE)
        stack = jnp.concatenate([res_low_ref[:, at, :], res_ref[:, at, :]], axis=0).reshape(states * TILE, width)
        turned = jnp.dot(kron_ref[...], stack, preferred_element_type=F32).astype(BF16)
        rotated_ref[:, :, at, :] = turned.reshape(terms, states, TILE, width)
        return carry

    lax.fori_loop(0, width // TILE, sites, 0, unroll=UNROLL)
    cross = jnp.zeros((8, width), F32)
    for start, left_mixed_ref in ((0, mixed_low_ref), (half, mixed_ref)):
        for k in range(terms):
            for n in range(half):
                image = jnp.dot(rotated_ref[k, start + n], right_ref[k], preferred_element_type=F32)
                cross = cross + fold(left_mixed_ref[k, n].astype(F32) * image, width)
    res_square = sums_ref[1:2, :] + square
    product = sums_ref[2:3, :] + product
    total = norm_ref[0:1, :] + norm_other_ref[0:1, :]
    factor = scale / (total * scale + epsilon)
    rayleigh = factor * product
    gap = rayleigh - shift
    res_vector = product - shift * total
    res_sq = factor * (res_square - 2.0 * gap * res_vector + gap * gap * total)
    change = gap * gap * product - 2.0 * gap * (res_square + shift * res_vector)
    share = 1.0 / members
    out_ref[0:1, :] = rayleigh * share
    out_ref[1:2, :] = jnp.maximum(res_sq, 0.0) * share
    out_ref[2:3, :] = factor * (jnp.sum(cross) + share * change)
    out_ref[3:8, :] = jnp.zeros((5, width), F32)


def own_rows_kernel(scale, members, keep_ref, norm_ref, norm_other_ref, share_ref, guess_ref, *refs):
    low_ref, low_other_ref, high_ref, high_other_ref, vector_ref, residual_ref = refs
    rows, states, width = guess_ref.shape
    inverse = lax.rsqrt((norm_ref[0:1, :] + norm_other_ref[0:1, :]) * scale + epsilon)
    row_scale = keep_ref[0:1, :] * inverse
    rayleigh = share_ref[0:1, :] * members
    own = pl.ds(pl.multiple_of(lax.axis_index("term") * rows, TILE), rows)
    vector = guess_ref[...] * row_scale[None]
    vector_ref[...] = vector
    sigma = jnp.concatenate(
        [
            mine_ref[:, own, :].astype(F32) + other_ref[:, own, :].astype(F32)
            for mine_ref, other_ref in ((low_ref, low_other_ref), (high_ref, high_other_ref))
        ],
        axis=0,
    )
    residual_ref[...] = jnp.swapaxes(sigma * row_scale[None], 0, 1) - rayleigh[None] * vector


def finish_kernel(vector_ref, residual_ref, *refs):
    shares = refs[:-2]
    ritz_ref, energy_ref = refs[-2:]
    stat = summed([share[...] for share in shares])
    rayleigh = stat[0:1, :]
    res_sq = stat[1:2, :]
    res_var = res_sq + epsilon
    curvature = stat[2:3, :] / res_var
    res_scale = jnp.sqrt(res_var)
    coupling = res_sq / res_scale
    half_gap = 0.5 * (rayleigh - curvature)
    energy = 0.5 * (rayleigh + curvature) - jnp.sqrt(half_gap * half_gap + coupling * coupling)
    coeff_new = energy - rayleigh
    coeff_norm = jnp.sqrt(coupling * coupling + coeff_new * coeff_new + epsilon)
    old = coupling / coeff_norm
    new = coeff_new / (coeff_norm * res_scale)
    ritz_ref[...] = old[None] * vector_ref[...] + new[None] * residual_ref[...]
    energy_ref[0] = energy[0, 0]


def shards(wave_guess, left_env, right_env, site_ops, bond_rank):
    guess = wave_guess[0]
    left = left_env[0]
    site = site_ops[0]
    rows, states, width = guess.shape
    terms = left.shape[0]
    members = lax.axis_size("term")
    chips = members // CORES
    segments = lax.axis_size("seg")
    scale = 1.0 / float(rows * members * states * width)
    hops = tuple(range(chips))

    def to_sibling(block):
        return lax.ppermute(block, "term", [(i, i ^ 1) for i in range(members)])

    def to_next_chip(block):
        return lax.ppermute(block, "term", [(i, (i + CORES) % members) for i in range(members)])

    def around(block):
        found = [block]
        for _ in range(chips - 1):
            found.append(to_next_chip(found[-1]))
        return found

    def everyone(block):
        return [block] + [
            lax.ppermute(block, "term", [(i, i ^ bits) for i in range(members)])
            for bits in range(CORES, members, CORES)
        ]

    tile = jax.ShapeDtypeStruct((8, width), F32)
    half = width // 2
    packed_shape = jax.ShapeDtypeStruct((terms, width + TILE, half), BF16)
    starts = (0, rows - 2 * TILE, rows - TILE) if rows >= 4 * TILE else (0,)
    lengths = [stop - start for start, stop in zip(starts, starts[1:] + (rows,))]
    in_place = [pltpu.with_memory_space_constraint(a, pltpu.HBM) for a in (guess, left, right_env[0], site)]
    first_chunk, keep, squares, right_packed = pl.pallas_call(
        first_chunk_kernel,
        out_shape=(jax.ShapeDtypeStruct((states + 1, lengths[0], width), BF16), tile, tile, packed_shape),
        in_specs=[anywhere] + [in_hbm] * 3,
        out_specs=(vmem,) * 4,
        scratch_shapes=[
            pltpu.VMEM((1, 1), jnp.int32),
            pltpu.VMEM((lengths[0], states, width), F32),
            pltpu.VMEM(site.shape, BF16),
            pltpu.VMEM(left.shape, BF16),
            pltpu.SemaphoreType.DMA((lengths[0] // TILE + 3,)),
        ],
        compiler_params=params(),
        cost_estimate=cost(2 * guess.size, 3 * guess.size),
        name="first_chunk",
    )(bond_rank.reshape(1, 1), in_place[0], in_place[3], in_place[2])
    rest = rows - lengths[0]
    squares, first_sibling = lax.optimization_barrier((squares, to_sibling(first_chunk)))
    norm_part, left_packed, left, *chunks = pl.pallas_call(
        functools.partial(prepare_kernel, starts),
        out_shape=(
            tile,
            packed_shape,
            jax.ShapeDtypeStruct(left.shape, BF16),
            *[jax.ShapeDtypeStruct((states, length, width), BF16) for length in lengths[1:]],
        ),
        in_specs=[vmem] * 2 + [in_hbm] * 2,
        out_specs=(vmem,) * (2 + len(lengths)),
        scratch_shapes=[
            pltpu.VMEM((max(rest, TILE), states, width), F32),
            pltpu.SemaphoreType.DMA((rest // TILE + 1,)),
        ],
        compiler_params=params(),
        cost_estimate=cost(4 * guess.size, 6 * guess.size),
        name="prepare",
    )(keep, squares, *in_place[:2])
    chunks = [first_chunk] + chunks

    chunk_hops = [around(chunk) for chunk in chunks]
    here_pieces = chunks + [first_sibling] + [to_sibling(chunk) for chunk in chunks[1:]]
    here_spots = tuple((0, flip, start, length) for flip in range(CORES) for start, length in zip(starts, lengths))
    far_spots = [
        tuple((hop, flip, start, length) for hop in hops[1:] for flip in range(CORES))
        for start, length in zip(starts, lengths)
    ]
    mid_spots = sum(far_spots[:-1], ())
    groups = [group for group in (here_spots, mid_spots, far_spots[-1]) if group]
    lefts = around(left_packed)
    shift = [(i + 1, i) for i in range(segments - 1)]
    received = lax.ppermute(right_packed, "seg", shift)

    size = states * TILE

    def spread(block):
        return pl.pallas_call(
            spread_kernel,
            out_shape=jax.ShapeDtypeStruct((terms * size, size), BF16),
            in_specs=[vmem],
            out_specs=vmem,
            compiler_params=params(),
            cost_estimate=cost(2 * terms * size * size * width, 2 * terms * size * size),
            name="spread_site",
        )(block)

    kron_own = spread(chunks[0])

    whole = (states, width, width)
    whole_bf = jax.ShapeDtypeStruct(whole, BF16)
    whole_f32 = jax.ShapeDtypeStruct(whole, F32)
    rotated = (terms, states, width, width)
    rotated_bf = jax.ShapeDtypeStruct(rotated, BF16)
    square = pltpu.VMEM((terms, width, width), BF16)
    chip_rows = CORES * rows
    stage_flops = 2 * terms * states * width * width * width

    def buffers(spots):
        count = sum(spot[3] for spot in spots)
        return (terms, states, count, width), (states, terms * count, width)

    here_rotated, here_turned = buffers(here_spots)
    part_cost = cost(stage_flops, 8 * states * width * width)
    rotated_own, columns = pl.pallas_call(
        functools.partial(rotate_own_kernel, groups, rows, chips),
        out_shape=(
            jax.ShapeDtypeStruct(here_rotated, BF16),
            jax.ShapeDtypeStruct((width, terms * width), BF16),
        ),
        in_specs=[vmem] * (len(here_pieces) + 2),
        out_specs=(vmem, vmem),
        compiler_params=params(),
        cost_estimate=part_cost,
        name="rotate_own",
    )(*here_pieces, kron_own, left)

    def rotate(spots, pieces, kron, before):
        return pl.pallas_call(
            functools.partial(rotate_kernel, spots, rows, chips),
            out_shape=(rotated_bf, whole_bf),
            in_specs=[vmem] * (len(pieces) + 1) + [anywhere] * len(before),
            out_specs=(vmem, vmem),
            scratch_shapes=[pltpu.SemaphoreType.DMA((len(pieces),))],
            input_output_aliases={len(pieces) + 1 + n: n for n in range(len(before))},
            compiler_params=params(),
            cost_estimate=part_cost,
            name="rotate_crossed" if before else "rotate_here",
        )(*pieces, kron, *before)

    def relayed(blocks):
        return [piece for block in blocks for piece in (block, to_sibling(block))]

    firsts, rotated_own = lax.optimization_barrier((chunk_hops[0][1:], rotated_own))
    kron = spread(firsts[0])
    turned = rotate(here_spots, here_pieces, kron, ())
    received, turned = lax.optimization_barrier((received, turned))
    packed = jnp.where(lax.axis_index("seg") == segments - 1, right_packed, received)
    rights = around(packed)
    turned_own, right = pl.pallas_call(
        here_kernel,
        out_shape=(jax.ShapeDtypeStruct(here_turned, BF16), jax.ShapeDtypeStruct(left.shape, BF16)),
        in_specs=[vmem] * 3,
        out_specs=(vmem, vmem),
        compiler_params=params(),
        cost_estimate=part_cost,
        name="apply_rows_here",
    )(rotated_own, packed, keep)
    parts = [turned_own]
    mid_pieces = []
    if mid_spots:
        mid_pieces += relayed(firsts)
        for crossing in chunk_hops[1:-1]:
            crossed, turned = lax.optimization_barrier((crossing[1:], turned))
            mid_pieces += relayed(crossed)
        turned = rotate(mid_spots, mid_pieces, kron, turned)
        crossed, turned, parts[0] = lax.optimization_barrier((chunk_hops[-1][1:], turned, parts[0]))
        last_pieces = relayed(crossed)
        mid_rotated, mid_turned = buffers(mid_spots)
        parts.append(
            pl.pallas_call(
                there_kernel,
                out_shape=jax.ShapeDtypeStruct(mid_turned, BF16),
                in_specs=[vmem] * (len(mid_pieces) + 2),
                out_specs=vmem,
                scratch_shapes=[pltpu.VMEM(mid_rotated, BF16)],
                compiler_params=params(),
                cost_estimate=part_cost,
                name="apply_rows_crossed",
            )(*mid_pieces, right, kron_own)
        )
    else:
        last_pieces = relayed(firsts)
    last_rotated, last_turned = buffers(far_spots[-1])
    partial = pl.pallas_call(
        functools.partial(last_kernel, len(last_pieces)),
        out_shape=whole_f32,
        in_specs=[vmem] * (len(last_pieces) + 3 + len(parts)),
        out_specs=vmem,
        scratch_shapes=[pltpu.VMEM(last_rotated, BF16), pltpu.VMEM(last_turned, BF16)],
        compiler_params=params(),
        cost_estimate=part_cost,
        name="apply_rows_last",
    )(*last_pieces, right, kron_own, columns, *parts)
    norm = norm_part
    for hop in hops[1:]:
        if hop > 1:
            block, partial = lax.optimization_barrier((firsts[hop - 1], partial))
            kron = spread(block)
            turned = rotate(here_spots, here_pieces, kron, ())
            if mid_spots:
                turned = rotate(mid_spots, mid_pieces, kron, turned)
        left_far, partial = lax.optimization_barrier((lefts[hop], partial))
        mixed, norm, _, vector = pl.pallas_call(
            functools.partial(lefts_kernel, far_spots[-1], rows, chips),
            out_shape=(jax.ShapeDtypeStruct((states, width, terms * width), BF16), tile, rotated_bf, whole_bf),
            in_specs=[vmem] * (len(last_pieces) + 1) + [anywhere] * 2 + [vmem] * 2,
            out_specs=(vmem,) * 4,
            scratch_shapes=[square, pltpu.SemaphoreType.DMA((len(last_pieces),))],
            input_output_aliases={len(last_pieces) + 1: 2, len(last_pieces) + 2: 3},
            compiler_params=params(),
            cost_estimate=cost(stage_flops, 12 * states * width * width),
            name="received_lefts",
        )(*last_pieces, kron, *turned, left_far, norm)
        last = hop == hops[-1]
        right_far = rights[hop]
        parts = []
        bounds = (0, states // 2, states) if last else (0, states)
        for start, stop in zip(bounds[:-1], bounds[1:]):
            part_shape = jax.ShapeDtypeStruct((stop - start, width, width), BF16 if last else F32)
            part, *unpacked = pl.pallas_call(
                functools.partial(rights_kernel, start, stop),
                out_shape=(part_shape,) + ((jax.ShapeDtypeStruct(left.shape, BF16),) if start == 0 else ()),
                in_specs=[vmem] * 4,
                out_specs=(vmem,) * (2 if start == 0 else 1),
                compiler_params=params(),
                cost_estimate=cost(stage_flops / 2, 12 * states * width * width),
                name="received_rights",
            )(right_far, mixed, partial, keep)
            if unpacked:
                right_far, norm_other = lax.optimization_barrier((unpacked[0], to_sibling(norm)))
            parts.append(part)
        if not last:
            partial = parts[0]
    halves = []
    for part in parts:
        halves += [part, to_sibling(part)]
    half_bf = jax.ShapeDtypeStruct((states // 2, width, width), BF16)
    half_mixed = (terms, states // 2, width, width)
    res_low, mixed_low, sums = pl.pallas_call(
        low_kernel,
        out_shape=(half_bf, jax.ShapeDtypeStruct(half_mixed, BF16), tile),
        in_specs=[vmem] * 6,
        out_specs=(vmem,) * 3,
        compiler_params=params(),
        cost_estimate=cost(stage_flops / 2, 3 * states * width * width),
        name="residual_low",
    )(norm, norm_other, *halves[:2], vector, left)
    share = pl.pallas_call(
        functools.partial(high_kernel, scale, members),
        out_shape=tile,
        in_specs=[vmem] * 11,
        out_specs=vmem,
        scratch_shapes=[
            pltpu.VMEM(half_bf.shape, BF16),
            pltpu.VMEM(rotated, BF16),
            pltpu.VMEM(half_mixed, BF16),
        ],
        compiler_params=params(),
        cost_estimate=cost(3 * stage_flops, 6 * states * width * width),
        name="residual_high",
    )(norm, norm_other, sums, *halves[2:], vector, left, right, kron_own, res_low, mixed_low)
    crossed = everyone(share)

    local = jax.ShapeDtypeStruct((rows, states, width), F32)
    vector_own, residual_own = pl.pallas_call(
        functools.partial(own_rows_kernel, scale, members),
        out_shape=(local, local),
        in_specs=[vmem] * 9,
        out_specs=(vmem, vmem),
        compiler_params=params(),
        cost_estimate=cost(8 * guess.size, 16 * guess.size),
        name="own_rows",
    )(keep, norm, norm_other, share, guess, *halves)

    shares = [share, to_sibling(share)]
    gated, residual_own = lax.optimization_barrier((crossed[1:], residual_own))
    shares += relayed(gated)
    ritz, energy = pl.pallas_call(
        finish_kernel,
        out_shape=(local, jax.ShapeDtypeStruct((1,), F32)),
        in_specs=[vmem] * (2 + members),
        out_specs=(vmem, smem),
        compiler_params=params(),
        cost_estimate=cost(3 * guess.size, 12 * guess.size),
        name="finish",
    )(vector_own, residual_own, *shares)
    return (ritz[None], energy)


def solution(mesh):
    in_specs = (
        P("seg", "term", None, None),
        P("seg", "term", None, None),
        P("seg", "term", None, None),
        P("seg", "term", None, None),
        P("seg"),
    )
    out_specs = (P("seg", "term", None, None), P("seg"))
    return jax.shard_map(shards, mesh=mesh, in_specs=in_specs, out_specs=out_specs, check_vma=False)
```

```python
import functools

import jax
import jax.numpy as jnp
from jax import lax
from jax.experimental import pallas as pl
from jax.experimental.pallas import tpu as pltpu
from jax.sharding import PartitionSpec as P

epsilon = 1e-06
CORES = 2
TILE = 16
UNROLL = 16
STRIP = 32
GROUP = 8
VMEM_LIMIT = 20 * 1024 * 1024
F32 = jnp.float32
BF16 = jnp.bfloat16

vmem = pl.BlockSpec(memory_space=pltpu.VMEM)
smem = pl.BlockSpec(memory_space=pltpu.SMEM)
anywhere = pl.BlockSpec(memory_space=pl.ANY)
in_hbm = pl.BlockSpec(memory_space=pltpu.HBM)


def params():
    return pltpu.CompilerParams(vmem_limit_bytes=VMEM_LIMIT)


def cost(flops, moved):
    return pl.CostEstimate(flops=int(flops) // 100, bytes_accessed=int(moved) // 100, transcendentals=0)


def fold(values, width):
    return jnp.sum(values.reshape(values.size // (8 * width), 8, width), axis=0)


def chunk_rows_in(guess_in, guess_ref, sems, start, stop, slot):
    copies = []
    for n in range(start, stop, TILE):
        target = guess_ref.at[pl.ds(n - start, TILE)]
        copies.append(pltpu.make_async_copy(guess_in.at[pl.ds(n, TILE)], target, sems.at[slot + len(copies)]))
        copies[-1].start()
    return copies


def first_chunk_kernel(
    rank_in,
    guess_in,
    site_in,
    right_in,
    x_ref,
    keep_ref,
    squares_ref,
    packed_ref,
    rank_ref,
    guess_ref,
    site_ref,
    right_ref,
    sems,
):
    rows, states, width = guess_ref.shape
    terms = site_ref.shape[0]
    copies = [
        pltpu.make_async_copy(source, target, sems.at[n])
        for n, (source, target) in enumerate(((rank_in, rank_ref), (site_in, site_ref), (right_in, right_ref)))
    ]
    copies[0].start()
    parts = chunk_rows_in(guess_in, guess_ref, sems, 0, rows, 3)
    copies[1].start()
    copies[2].start()
    copies[0].wait()
    column = lax.broadcasted_iota(jnp.int32, (1, width), 1)
    keep = (column < rank_ref[...]).astype(F32)
    keep_ref[...] = jnp.broadcast_to(keep, keep_ref.shape)
    squares = jnp.zeros((8, width), F32)
    for n, copy in enumerate(parts):
        copy.wait()
        part = pl.ds(n * TILE, TILE)
        masked = guess_ref[part] * keep[None]
        squares = squares + fold(masked * masked, width)
        x_ref[0:states, part, :] = jnp.swapaxes(masked, 0, 1).astype(BF16)
    squares_ref[...] = squares
    copies[1].wait()
    line = lax.broadcasted_iota(jnp.int32, (TILE, width), 0)
    lane = lax.broadcasted_iota(jnp.int32, (TILE, width), 1)
    extra = jnp.zeros((TILE, width), F32)
    for k in range(terms):
        place_at = (lane == line + k * TILE).astype(BF16)
        extra = extra + jnp.dot(site_ref[k], place_at, preferred_element_type=F32)
    x_ref[states, 0:TILE, :] = extra.astype(BF16)
    copies[2].wait()
    pack_blocks(right_ref, None, packed_ref)


def prepare_kernel(starts, keep_ref, squares_ref, guess_in, left_in, norm_ref, packed_ref, left_ref, *refs):
    x_refs = (None,) + refs[: len(starts) - 1]
    guess_ref, sems = refs[len(starts) - 1 :]
    rows, states, width = guess_in.shape
    half = width // 2
    done = starts[1] if len(starts) > 1 else rows
    copies = chunk_rows_in(guess_in, guess_ref, sems, done, rows, 1)
    left_copy = pltpu.make_async_copy(left_in, left_ref, sems.at[0])
    left_copy.start()
    keep = keep_ref[0:1, :][None]
    squares = squares_ref[...]
    for n, copy in enumerate(copies):
        copy.wait()
        masked = guess_ref[pl.ds(n * TILE, TILE)] * keep
        squares = squares + fold(masked * masked, width)
        chunk = max(c for c, start in enumerate(starts) if start <= done + n * TILE)
        at = done + n * TILE - starts[chunk]
        x_refs[chunk][:, at : at + TILE, :] = jnp.swapaxes(masked, 0, 1).astype(BF16)
    total = jnp.sum(squares)
    norm_ref[...] = jnp.full(norm_ref.shape, total, F32)
    line = lax.broadcasted_iota(jnp.int32, (TILE, half), 0)
    norm = jnp.full((TILE, half), total, F32)
    extra = jnp.zeros((TILE, half), F32)
    for n in range(1, 4):
        part = norm.astype(BF16).astype(F32)
        norm = norm - part
        extra = jnp.where(line == n, part, extra)
    left_copy.wait()
    pack_blocks(left_ref, extra, packed_ref)


def pack_blocks(block_ref, extra, packed_ref):
    terms, width, _ = block_ref.shape
    half = width // 2
    line = lax.broadcasted_iota(jnp.int32, (TILE, half), 0)
    for k in range(terms):
        diagonal = pack_symmetric(block_ref, k, packed_ref)
        lines = jnp.broadcast_to(diagonal, (TILE, half)) if extra is None else jnp.where(line == 0, diagonal, extra)
        packed_ref[k, width : width + TILE, :] = lines.astype(BF16)


def triangle(half):
    row = lax.broadcasted_iota(jnp.int32, (half, half), 0)
    col = lax.broadcasted_iota(jnp.int32, (half, half), 1)
    return row, col


def pack_symmetric(block_ref, k, out_ref):
    width = block_ref.shape[1]
    half = width // 2
    row, col = triangle(half)
    upper = block_ref[k, 0:half, 0:half].astype(F32)
    lower = block_ref[k, half:width, half:width].astype(F32)
    out_ref[k, 0:half, :] = block_ref[k, 0:half, half:width]
    out_ref[k, half:width, :] = jnp.where(row <= col, upper, lower).astype(BF16)
    return jnp.sum(jnp.where(row == col, lower, 0.0), axis=0, keepdims=True)


def unpack_symmetric(packed_ref, full_ref, keep=None):
    terms, width, _ = full_ref.shape
    half = width // 2
    row, col = triangle(half)

    def kept(block, start):
        return block if keep is None else block * keep[:, start : start + half]

    for k in range(terms):
        corner = packed_ref[k, 0:half, :].astype(F32)
        mixed = packed_ref[k, half:width, :].astype(F32)
        diagonal = packed_ref[k, width : width + TILE, :].astype(F32)[0:1]
        turned = mixed.T
        lower = jnp.where(row > col, mixed, jnp.where(row == col, diagonal, turned))
        full_ref[k, 0:half, 0:half] = kept(jnp.where(row <= col, mixed, turned), 0).astype(BF16)
        full_ref[k, 0:half, half:width] = kept(corner, half).astype(BF16)
        full_ref[k, half:width, 0:half] = kept(corner.T, 0).astype(BF16)
        full_ref[k, half:width, half:width] = kept(lower, half).astype(BF16)


def spread_kernel(chunk_ref, kron_ref):
    width = chunk_ref.shape[2]
    size = kron_ref.shape[1]
    terms = kron_ref.shape[0] // size
    states = size // TILE
    tile = chunk_ref[states, 0:TILE, :]
    row_state = lax.broadcasted_iota(jnp.int32, (size, states), 0) // TILE
    pick = (row_state == lax.broadcasted_iota(jnp.int32, (size, states), 1)).astype(BF16)
    tall = jnp.dot(pick, tile, preferred_element_type=F32).astype(BF16)
    lane = lax.broadcasted_iota(jnp.int32, (width, size), 0)
    col_state = lax.broadcasted_iota(jnp.int32, (width, size), 1) // TILE
    same = (
        lax.broadcasted_iota(jnp.int32, (size, size), 0) % TILE
        == lax.broadcasted_iota(jnp.int32, (size, size), 1) % TILE
    )
    for k in range(terms):
        pick_t = (lane == col_state + k * TILE).astype(BF16)
        full = jnp.dot(tall, pick_t, preferred_element_type=F32)
        kron_ref[k * size : (k + 1) * size, :] = jnp.where(same, full, 0.0).astype(BF16)


def mix_sites(source_ref, kron_ref, rotated_ref, base, unroll):
    terms, states, _, width = rotated_ref.shape
    rows = source_ref.shape[1]

    def step(i, carry):
        at = pl.multiple_of(i * TILE, TILE)
        to = pl.multiple_of(base + i * TILE, TILE)
        stack = source_ref[0:states, pl.ds(at, TILE), :].reshape(states * TILE, width)
        turned = jnp.dot(kron_ref[...], stack, preferred_element_type=F32).astype(BF16)
        rotated_ref[:, :, pl.ds(to, TILE), :] = turned.reshape(terms, states, TILE, width)
        return carry

    lax.fori_loop(0, rows // TILE, step, 0, unroll=min(unroll, rows // TILE))


def summed(values):
    while len(values) > 1:
        values = [values[n] + values[n + 1] for n in range(0, len(values), 2)]
    return values[0]


def place(hop, chips):
    me = lax.axis_index("term")
    chip = (me // CORES - hop + chips) % chips
    return chip, me % CORES


def row_of(spot, rows, chips):
    chip, core = place(spot[0], chips)
    return pl.multiple_of((chip * CORES + (core if spot[1] == 0 else 1 - core)) * rows + spot[2], TILE)


def mix_pieces(pieces, kron_ref, rotated_ref):
    at = 0
    for piece in pieces:
        mix_sites(piece, kron_ref, rotated_ref, at, UNROLL)
        at += piece.shape[1]


def rotate_own_kernel(groups, rows, chips, *refs):
    kron_ref, left_ref, rotated_ref, columns_ref = refs[-4:]
    mix_pieces(refs[:-4], kron_ref, rotated_ref)
    blocks = []
    for spots in groups:
        for k in range(left_ref.shape[0]):
            blocks += [left_ref[k, pl.ds(row_of(spot, rows, chips), spot[3]), :] for spot in spots]
    columns_ref[...] = jnp.concatenate(blocks, axis=0).astype(F32).T.astype(BF16)


def turn(right_ref, rotated_ref, turned_ref):
    terms, states, count, width = rotated_ref.shape
    for k in range(terms):
        for n in range(0, states, 8):
            source = rotated_ref[k, n : n + 8].reshape(8 * count, width)
            turned = jnp.dot(source, right_ref[k], preferred_element_type=F32).astype(BF16)
            turned_ref[n : n + 8, k * count : (k + 1) * count, :] = turned.reshape(8, count, width)


def here_kernel(rotated_ref, packed_ref, keep_ref, turned_ref, right_ref):
    unpack_symmetric(packed_ref, right_ref, keep_ref[0:1, :])
    turn(right_ref, rotated_ref, turned_ref)


def there_kernel(*refs):
    right_ref, kron_ref, turned_ref, rotated_ref = refs[-4:]
    mix_pieces(refs[:-4], kron_ref, rotated_ref)
    turn(right_ref, rotated_ref, turned_ref)


def last_kernel(count, *refs):
    right_ref, kron_ref, columns_ref = refs[count : count + 3]
    out_ref, rotated_ref, turned_ref = refs[-3:]
    there_kernel(*refs[:count], right_ref, kron_ref, turned_ref, rotated_ref)
    blocks = list(refs[count + 3 : -3]) + [turned_ref]

    def lefts(p, carry):
        stack = jnp.concatenate([block[p] for block in blocks], axis=0)
        out_ref[p] = jnp.dot(columns_ref[...], stack, preferred_element_type=F32)
        return carry

    lax.fori_loop(0, out_ref.shape[0], lefts, 0, unroll=out_ref.shape[0])


def rotate_kernel(spots, rows, chips, *refs):
    pieces = refs[: len(spots)]
    kron_ref = refs[len(spots)]
    rotated_ref, whole_ref, sems = refs[-3:]
    states = whole_ref.shape[0]
    copies = []
    bases = [row_of(spot, rows, chips) for spot in spots]
    for n, (at, piece) in enumerate(zip(bases, pieces)):
        target = whole_ref.at[:, pl.ds(at, piece.shape[1]), :]
        copies.append(pltpu.make_async_copy(piece.at[0:states], target, sems.at[n]))
        copies[-1].start()
    for at, piece in zip(bases, pieces):
        mix_sites(piece, kron_ref, rotated_ref, at, UNROLL)
    for copy in copies:
        copy.wait()


def lefts_kernel(spots, rows, chips, *refs):
    count = len(spots)
    packed_ref, norm_before_ref = refs[count + 3 : count + 5]
    mixed_ref, norm_ref, rotated_ref, whole_ref, left_ref, sems = refs[-6:]
    terms, states, width, _ = rotated_ref.shape
    lines = packed_ref[0, width : width + TILE, :].astype(F32)
    norm = lines[1:2] + lines[2:3] + lines[3:4]
    norm_ref[...] = norm_before_ref[...] + jnp.concatenate([norm, norm], axis=1)
    unpack_symmetric(packed_ref, left_ref)
    rotate_kernel(spots, rows, chips, *refs[: count + 1], rotated_ref, whole_ref, sems)

    def lefts(p, carry):
        for k in range(terms):
            mixed = jnp.dot(left_ref[k], rotated_ref[k, p], preferred_element_type=F32)
            mixed_ref[p, :, k * width : (k + 1) * width] = mixed.astype(BF16)
        return carry

    lax.fori_loop(0, states, lefts, 0, unroll=states)


def rights_kernel(start, stop, packed_ref, mixed_ref, before_ref, keep_ref, partial_ref, *refs):
    if start == 0:
        right_ref = refs[0]
        unpack_symmetric(packed_ref, right_ref, keep_ref[0:1, :])
    else:
        right_ref = packed_ref
    terms, width, _ = right_ref.shape

    def rights(n, carry):
        at = n * GROUP
        rows = mixed_ref[pl.ds(start + at, GROUP)].reshape(GROUP * width, terms * width)
        stacked = right_ref[...].reshape(terms * width, width)
        image = jnp.dot(rows, stacked, preferred_element_type=F32).reshape(GROUP, width, width)
        partial_ref[pl.ds(at, GROUP)] = (before_ref[pl.ds(start + at, GROUP)] + image).astype(partial_ref.dtype)
        return carry

    lax.fori_loop(0, (stop - start) // GROUP, rights, 0)


def shifted_residual(start, shift, mine_ref, other_ref, whole_ref, left_ref, res_ref, mixed_ref):
    count, width, _ = res_ref.shape
    terms = left_ref.shape[0]
    zero = jnp.zeros((8, width), F32)

    def lefts(n, sums):
        square, product = sums
        for row in range(0, width, STRIP):
            strip = pl.ds(row, STRIP)
            held = whole_ref[start + n, strip, :].astype(F32)
            sigma = mine_ref[n, strip, :].astype(F32) + other_ref[n, strip, :].astype(F32)
            residual = sigma - shift * held
            res_ref[n, strip, :] = residual.astype(BF16)
            square = square + fold(residual * residual, width)
            product = product + fold(sigma * held, width)
        mixed = jnp.dot(
            left_ref[...].reshape(terms * width, width), res_ref[n], preferred_element_type=F32
        ).astype(BF16)
        for k in range(terms):
            mixed_ref[k, n] = mixed[k * width : (k + 1) * width]
        return square, product

    square, product = lax.fori_loop(0, count, lefts, (zero, zero), unroll=count)
    return jnp.sum(square), jnp.sum(product)


def low_kernel(
    norm_ref,
    norm_other_ref,
    low_ref,
    low_other_ref,
    whole_ref,
    left_ref,
    res_ref,
    mixed_ref,
    out_ref,
):
    count, width, _ = low_ref.shape
    states = whole_ref.shape[0]
    held = whole_ref[0].astype(F32)
    sigma = low_ref[0].astype(F32) + low_other_ref[0].astype(F32)
    product = jnp.sum(fold(sigma * held, width))
    square = jnp.sum(fold(held * held, width))
    total = norm_ref[0:1, :] + norm_other_ref[0:1, :]
    floor = jnp.maximum(jnp.maximum(square, (0.25 / states) * total), 1e-30)
    shift = product / floor
    square, product = shifted_residual(
        0, shift, low_ref, low_other_ref, whole_ref, left_ref, res_ref, mixed_ref
    )
    out_ref[0:1, :] = shift
    out_ref[1:2, :] = jnp.full((1, width), square, F32)
    out_ref[2:3, :] = jnp.full((1, width), product, F32)
    out_ref[3:8, :] = jnp.zeros((5, width), F32)


def high_kernel(
    scale,
    members,
    norm_ref,
    norm_other_ref,
    sums_ref,
    high_ref,
    high_other_ref,
    whole_ref,
    left_ref,
    right_ref,
    kron_ref,
    res_low_ref,
    mixed_low_ref,
    out_ref,
    res_ref,
    rotated_ref,
    mixed_ref,
):
    terms, states, width, _ = rotated_ref.shape
    half = states // 2
    shift = sums_ref[0:1, :]
    square, product = shifted_residual(
        half, shift, high_ref, high_other_ref, whole_ref, left_ref, res_ref, mixed_ref
    )

    def sites(i, carry):
        at = pl.ds(pl.multiple_of(i * TILE, TILE), TILE)
        stack = jnp.concatenate([res_low_ref[:, at, :], res_ref[:, at, :]], axis=0).reshape(states * TILE, width)
        turned = jnp.dot(kron_ref[...], stack, preferred_element_type=F32).astype(BF16)
        rotated_ref[:, :, at, :] = turned.reshape(terms, states, TILE, width)
        return carry

    lax.fori_loop(0, width // TILE, sites, 0, unroll=width // TILE)
    cross = jnp.zeros((8, width), F32)
    for start, left_mixed_ref in ((0, mixed_low_ref), (half, mixed_ref)):
        for k in range(terms):
            turned = rotated_ref[k, start : start + half].reshape(half * width, width)
            image = jnp.dot(turned, right_ref[k], preferred_element_type=F32)
            held = left_mixed_ref[k].reshape(half * width, width).astype(F32)
            cross = cross + fold(held * image, width)
    res_square = sums_ref[1:2, :] + square
    product = sums_ref[2:3, :] + product
    total = norm_ref[0:1, :] + norm_other_ref[0:1, :]
    factor = scale / (total * scale + epsilon)
    rayleigh = factor * product
    gap = rayleigh - shift
    res_vector = product - shift * total
    res_sq = factor * (res_square - 2.0 * gap * res_vector + gap * gap * total)
    change = gap * gap * product - 2.0 * gap * (res_square + shift * res_vector)
    share = 1.0 / members
    out_ref[0:1, :] = rayleigh * share
    out_ref[1:2, :] = jnp.maximum(res_sq, 0.0) * share
    out_ref[2:3, :] = factor * (jnp.sum(cross) + share * change)
    out_ref[3:8, :] = jnp.zeros((5, width), F32)


def own_rows_kernel(scale, members, keep_ref, norm_ref, norm_other_ref, share_ref, guess_ref, *refs):
    low_ref, low_other_ref, high_ref, high_other_ref, vector_ref, residual_ref = refs
    rows, states, width = guess_ref.shape
    inverse = lax.rsqrt((norm_ref[0:1, :] + norm_other_ref[0:1, :]) * scale + epsilon)
    row_scale = keep_ref[0:1, :] * inverse
    rayleigh = share_ref[0:1, :] * members
    own = pl.ds(pl.multiple_of(lax.axis_index("term") * rows, TILE), rows)
    vector = guess_ref[...] * row_scale[None]
    vector_ref[...] = vector
    sigma = jnp.concatenate(
        [
            mine_ref[:, own, :].astype(F32) + other_ref[:, own, :].astype(F32)
            for mine_ref, other_ref in ((low_ref, low_other_ref), (high_ref, high_other_ref))
        ],
        axis=0,
    )
    residual_ref[...] = jnp.swapaxes(sigma * row_scale[None], 0, 1) - rayleigh[None] * vector


def finish_kernel(vector_ref, residual_ref, *refs):
    shares = refs[:-2]
    ritz_ref, energy_ref = refs[-2:]
    stat = summed([share[...] for share in shares])
    rayleigh = stat[0:1, :]
    res_sq = stat[1:2, :]
    res_var = res_sq + epsilon
    curvature = stat[2:3, :] / res_var
    res_scale = jnp.sqrt(res_var)
    coupling = res_sq / res_scale
    half_gap = 0.5 * (rayleigh - curvature)
    energy = 0.5 * (rayleigh + curvature) - jnp.sqrt(half_gap * half_gap + coupling * coupling)
    coeff_new = energy - rayleigh
    coeff_norm = jnp.sqrt(coupling * coupling + coeff_new * coeff_new + epsilon)
    old = coupling / coeff_norm
    new = coeff_new / (coeff_norm * res_scale)
    ritz_ref[...] = old[None] * vector_ref[...] + new[None] * residual_ref[...]
    energy_ref[0] = energy[0, 0]


def shards(wave_guess, left_env, right_env, site_ops, bond_rank):
    guess = wave_guess[0]
    left = left_env[0]
    site = site_ops[0]
    rows, states, width = guess.shape
    terms = left.shape[0]
    members = lax.axis_size("term")
    chips = members // CORES
    segments = lax.axis_size("seg")
    scale = 1.0 / float(rows * members * states * width)
    hops = tuple(range(chips))

    def to_sibling(block):
        return lax.ppermute(block, "term", [(i, i ^ 1) for i in range(members)])

    def to_next_chip(block):
        return lax.ppermute(block, "term", [(i, (i + CORES) % members) for i in range(members)])

    def around(block):
        found = [block]
        for _ in range(chips - 1):
            found.append(to_next_chip(found[-1]))
        return found

    def everyone(block):
        return [block] + [
            lax.ppermute(block, "term", [(i, i ^ bits) for i in range(members)])
            for bits in range(CORES, members, CORES)
        ]

    tile = jax.ShapeDtypeStruct((8, width), F32)
    half = width // 2
    packed_shape = jax.ShapeDtypeStruct((terms, width + TILE, half), BF16)
    starts = (0, rows - 2 * TILE, rows - TILE) if rows >= 4 * TILE else (0,)
    lengths = [stop - start for start, stop in zip(starts, starts[1:] + (rows,))]
    in_place = [pltpu.with_memory_space_constraint(a, pltpu.HBM) for a in (guess, left, right_env[0], site)]
    first_chunk, keep, squares, right_packed = pl.pallas_call(
        first_chunk_kernel,
        out_shape=(jax.ShapeDtypeStruct((states + 1, lengths[0], width), BF16), tile, tile, packed_shape),
        in_specs=[anywhere] + [in_hbm] * 3,
        out_specs=(vmem,) * 4,
        scratch_shapes=[
            pltpu.VMEM((1, 1), jnp.int32),
            pltpu.VMEM((lengths[0], states, width), F32),
            pltpu.VMEM(site.shape, BF16),
            pltpu.VMEM(left.shape, BF16),
            pltpu.SemaphoreType.DMA((lengths[0] // TILE + 3,)),
        ],
        compiler_params=params(),
        cost_estimate=cost(2 * guess.size, 3 * guess.size),
        name="first_chunk",
    )(bond_rank.reshape(1, 1), in_place[0], in_place[3], in_place[2])
    rest = rows - lengths[0]
    squares, first_sibling = lax.optimization_barrier((squares, to_sibling(first_chunk)))
    norm_part, left_packed, left, *chunks = pl.pallas_call(
        functools.partial(prepare_kernel, starts),
        out_shape=(
            tile,
            packed_shape,
            jax.ShapeDtypeStruct(left.shape, BF16),
            *[jax.ShapeDtypeStruct((states, length, width), BF16) for length in lengths[1:]],
        ),
        in_specs=[vmem] * 2 + [in_hbm] * 2,
        out_specs=(vmem,) * (2 + len(lengths)),
        scratch_shapes=[
            pltpu.VMEM((max(rest, TILE), states, width), F32),
            pltpu.SemaphoreType.DMA((rest // TILE + 1,)),
        ],
        compiler_params=params(),
        cost_estimate=cost(4 * guess.size, 6 * guess.size),
        name="prepare",
    )(keep, squares, *in_place[:2])
    chunks = [first_chunk] + chunks

    chunk_hops = [around(chunk) for chunk in chunks]
    here_pieces = chunks + [first_sibling] + [to_sibling(chunk) for chunk in chunks[1:]]
    here_spots = tuple((0, flip, start, length) for flip in range(CORES) for start, length in zip(starts, lengths))
    far_spots = [
        tuple((hop, flip, start, length) for hop in hops[1:] for flip in range(CORES))
        for start, length in zip(starts, lengths)
    ]
    mid_spots = sum(far_spots[:-1], ())
    groups = [group for group in (here_spots, mid_spots, far_spots[-1]) if group]
    lefts = around(left_packed)
    shift = [(i + 1, i) for i in range(segments - 1)]
    received = lax.ppermute(right_packed, "seg", shift)

    size = states * TILE

    def spread(block):
        return pl.pallas_call(
            spread_kernel,
            out_shape=jax.ShapeDtypeStruct((terms * size, size), BF16),
            in_specs=[vmem],
            out_specs=vmem,
            compiler_params=params(),
            cost_estimate=cost(2 * terms * size * size * width, 2 * terms * size * size),
            name="spread_site",
        )(block)

    kron_own = spread(chunks[0])

    whole = (states, width, width)
    whole_bf = jax.ShapeDtypeStruct(whole, BF16)
    whole_f32 = jax.ShapeDtypeStruct(whole, F32)
    rotated = (terms, states, width, width)
    rotated_bf = jax.ShapeDtypeStruct(rotated, BF16)
    square = pltpu.VMEM((terms, width, width), BF16)
    chip_rows = CORES * rows
    stage_flops = 2 * terms * states * width * width * width

    def buffers(spots):
        count = sum(spot[3] for spot in spots)
        return (terms, states, count, width), (states, terms * count, width)

    here_rotated, here_turned = buffers(here_spots)
    part_cost = cost(stage_flops, 8 * states * width * width)
    rotated_own, columns = pl.pallas_call(
        functools.partial(rotate_own_kernel, groups, rows, chips),
        out_shape=(
            jax.ShapeDtypeStruct(here_rotated, BF16),
            jax.ShapeDtypeStruct((width, terms * width), BF16),
        ),
        in_specs=[vmem] * (len(here_pieces) + 2),
        out_specs=(vmem, vmem),
        compiler_params=params(),
        cost_estimate=part_cost,
        name="rotate_own",
    )(*here_pieces, kron_own, left)

    def rotate(spots, pieces, kron, before):
        return pl.pallas_call(
            functools.partial(rotate_kernel, spots, rows, chips),
            out_shape=(rotated_bf, whole_bf),
            in_specs=[vmem] * (len(pieces) + 1) + [anywhere] * len(before),
            out_specs=(vmem, vmem),
            scratch_shapes=[pltpu.SemaphoreType.DMA((len(pieces),))],
            input_output_aliases={len(pieces) + 1 + n: n for n in range(len(before))},
            compiler_params=params(),
            cost_estimate=part_cost,
            name="rotate_crossed" if before else "rotate_here",
        )(*pieces, kron, *before)

    def relayed(blocks):
        return [piece for block in blocks for piece in (block, to_sibling(block))]

    firsts, rotated_own = lax.optimization_barrier((chunk_hops[0][1:], rotated_own))
    kron = spread(firsts[0])
    turned = rotate(here_spots, here_pieces, kron, ())
    received, turned = lax.optimization_barrier((received, turned))
    packed = jnp.where(lax.axis_index("seg") == segments - 1, right_packed, received)
    rights = around(packed)
    turned_own, right = pl.pallas_call(
        here_kernel,
        out_shape=(jax.ShapeDtypeStruct(here_turned, BF16), jax.ShapeDtypeStruct(left.shape, BF16)),
        in_specs=[vmem] * 3,
        out_specs=(vmem, vmem),
        compiler_params=params(),
        cost_estimate=part_cost,
        name="apply_rows_here",
    )(rotated_own, packed, keep)
    parts = [turned_own]
    mid_pieces = []
    if mid_spots:
        mid_pieces += relayed(firsts)
        for crossing in chunk_hops[1:-1]:
            crossed, turned = lax.optimization_barrier((crossing[1:], turned))
            mid_pieces += relayed(crossed)
        turned = rotate(mid_spots, mid_pieces, kron, turned)
        crossed, turned, parts[0] = lax.optimization_barrier((chunk_hops[-1][1:], turned, parts[0]))
        last_pieces = relayed(crossed)
        mid_rotated, mid_turned = buffers(mid_spots)
        parts.append(
            pl.pallas_call(
                there_kernel,
                out_shape=jax.ShapeDtypeStruct(mid_turned, BF16),
                in_specs=[vmem] * (len(mid_pieces) + 2),
                out_specs=vmem,
                scratch_shapes=[pltpu.VMEM(mid_rotated, BF16)],
                compiler_params=params(),
                cost_estimate=part_cost,
                name="apply_rows_crossed",
            )(*mid_pieces, right, kron_own)
        )
    else:
        last_pieces = relayed(firsts)
    last_rotated, last_turned = buffers(far_spots[-1])
    partial = pl.pallas_call(
        functools.partial(last_kernel, len(last_pieces)),
        out_shape=whole_f32,
        in_specs=[vmem] * (len(last_pieces) + 3 + len(parts)),
        out_specs=vmem,
        scratch_shapes=[pltpu.VMEM(last_rotated, BF16), pltpu.VMEM(last_turned, BF16)],
        compiler_params=params(),
        cost_estimate=part_cost,
        name="apply_rows_last",
    )(*last_pieces, right, kron_own, columns, *parts)
    norm = norm_part
    for hop in hops[1:]:
        if hop > 1:
            block, partial = lax.optimization_barrier((firsts[hop - 1], partial))
            kron = spread(block)
            turned = rotate(here_spots, here_pieces, kron, ())
            if mid_spots:
                turned = rotate(mid_spots, mid_pieces, kron, turned)
        left_far, partial = lax.optimization_barrier((lefts[hop], partial))
        mixed, norm, _, vector = pl.pallas_call(
            functools.partial(lefts_kernel, far_spots[-1], rows, chips),
            out_shape=(jax.ShapeDtypeStruct((states, width, terms * width), BF16), tile, rotated_bf, whole_bf),
            in_specs=[vmem] * (len(last_pieces) + 1) + [anywhere] * 2 + [vmem] * 2,
            out_specs=(vmem,) * 4,
            scratch_shapes=[square, pltpu.SemaphoreType.DMA((len(last_pieces),))],
            input_output_aliases={len(last_pieces) + 1: 2, len(last_pieces) + 2: 3},
            compiler_params=params(),
            cost_estimate=cost(stage_flops, 12 * states * width * width),
            name="received_lefts",
        )(*last_pieces, kron, *turned, left_far, norm)
        last = hop == hops[-1]
        right_far = rights[hop]
        parts = []
        bounds = (0, states // 2, states) if last else (0, states)
        for start, stop in zip(bounds[:-1], bounds[1:]):
            part_shape = jax.ShapeDtypeStruct((stop - start, width, width), BF16 if last else F32)
            part, *unpacked = pl.pallas_call(
                functools.partial(rights_kernel, start, stop),
                out_shape=(part_shape,) + ((jax.ShapeDtypeStruct(left.shape, BF16),) if start == 0 else ()),
                in_specs=[vmem] * 4,
                out_specs=(vmem,) * (2 if start == 0 else 1),
                compiler_params=params(),
                cost_estimate=cost(stage_flops / 2, 12 * states * width * width),
                name="received_rights",
            )(right_far, mixed, partial, keep)
            if unpacked:
                right_far, norm_other = lax.optimization_barrier((unpacked[0], to_sibling(norm)))
            parts.append(part)
        if not last:
            partial = parts[0]
    halves = []
    for part in parts:
        halves += [part, to_sibling(part)]
    half_bf = jax.ShapeDtypeStruct((states // 2, width, width), BF16)
    half_mixed = (terms, states // 2, width, width)
    res_low, mixed_low, sums = pl.pallas_call(
        low_kernel,
        out_shape=(half_bf, jax.ShapeDtypeStruct(half_mixed, BF16), tile),
        in_specs=[vmem] * 6,
        out_specs=(vmem,) * 3,
        compiler_params=params(),
        cost_estimate=cost(stage_flops / 2, 3 * states * width * width),
        name="residual_low",
    )(norm, norm_other, *halves[:2], vector, left)
    share = pl.pallas_call(
        functools.partial(high_kernel, scale, members),
        out_shape=tile,
        in_specs=[vmem] * 11,
        out_specs=vmem,
        scratch_shapes=[
            pltpu.VMEM(half_bf.shape, BF16),
            pltpu.VMEM(rotated, BF16),
            pltpu.VMEM(half_mixed, BF16),
        ],
        compiler_params=params(),
        cost_estimate=cost(3 * stage_flops, 6 * states * width * width),
        name="residual_high",
    )(norm, norm_other, sums, *halves[2:], vector, left, right, kron_own, res_low, mixed_low)
    crossed = everyone(share)

    local = jax.ShapeDtypeStruct((rows, states, width), F32)
    vector_own, residual_own = pl.pallas_call(
        functools.partial(own_rows_kernel, scale, members),
        out_shape=(local, local),
        in_specs=[vmem] * 9,
        out_specs=(vmem, vmem),
        compiler_params=params(),
        cost_estimate=cost(8 * guess.size, 16 * guess.size),
        name="own_rows",
    )(keep, norm, norm_other, share, guess, *halves)

    shares = [share, to_sibling(share)]
    gated, residual_own = lax.optimization_barrier((crossed[1:], residual_own))
    shares += relayed(gated)
    ritz, energy = pl.pallas_call(
        finish_kernel,
        out_shape=(local, jax.ShapeDtypeStruct((1,), F32)),
        in_specs=[vmem] * (2 + members),
        out_specs=(vmem, smem),
        compiler_params=params(),
        cost_estimate=cost(3 * guess.size, 12 * guess.size),
        name="finish",
    )(vector_own, residual_own, *shares)
    return (ritz[None], energy)


def solution(mesh):
    in_specs = (
        P("seg", "term", None, None),
        P("seg", "term", None, None),
        P("seg", "term", None, None),
        P("seg", "term", None, None),
        P("seg"),
    )
    out_specs = (P("seg", "term", None, None), P("seg"))
    return jax.shard_map(shards, mesh=mesh, in_specs=in_specs, out_specs=out_specs, check_vma=False)
```

```python
import functools

import jax
import jax.numpy as jnp
from jax import lax
from jax.experimental import pallas as pl
from jax.experimental.pallas import tpu as pltpu
from jax.sharding import PartitionSpec as P

epsilon = 1e-06
CORES = 2
TILE = 16
STRIP = 32
GROUP = 8
VMEM_LIMIT = 20 * 1024 * 1024
F32 = jnp.float32
BF16 = jnp.bfloat16

vmem = pl.BlockSpec(memory_space=pltpu.VMEM)
smem = pl.BlockSpec(memory_space=pltpu.SMEM)
anywhere = pl.BlockSpec(memory_space=pl.ANY)
in_hbm = pl.BlockSpec(memory_space=pltpu.HBM)


def params():
    return pltpu.CompilerParams(vmem_limit_bytes=VMEM_LIMIT)


def cost(flops, moved):
    return pl.CostEstimate(flops=int(flops) // 100, bytes_accessed=int(moved) // 100, transcendentals=0)


def fold(values, width):
    return jnp.sum(values.reshape(values.size // (8 * width), 8, width), axis=0)


def chunk_rows_in(guess_in, guess_ref, sems, start, stop, slot):
    copies = []
    for n in range(start, stop, TILE):
        target = guess_ref.at[pl.ds(n - start, TILE)]
        copies.append(pltpu.make_async_copy(guess_in.at[pl.ds(n, TILE)], target, sems.at[slot + len(copies)]))
        copies[-1].start()
    return copies


def first_chunk_kernel(
    rank_in,
    guess_in,
    site_in,
    right_in,
    x_ref,
    keep_ref,
    squares_ref,
    packed_ref,
    rank_ref,
    guess_ref,
    site_ref,
    right_ref,
    sems,
):
    rows, states, width = guess_ref.shape
    terms = site_ref.shape[0]
    blocks = rows // TILE
    copies = [
        pltpu.make_async_copy(source, target, sems.at[n])
        for n, (source, target) in enumerate(((rank_in, rank_ref), (site_in, site_ref), (right_in, right_ref)))
    ]
    copies[0].start()
    parts = chunk_rows_in(guess_in, guess_ref, sems, 0, rows, 3)
    copies[1].start()
    copies[2].start()
    copies[0].wait()
    column = lax.broadcasted_iota(jnp.int32, (1, width), 1)
    keep = (column < rank_ref[...]).astype(F32)
    keep_ref[...] = jnp.broadcast_to(keep, keep_ref.shape)
    squares = jnp.zeros((8, width), F32)
    for n, copy in enumerate(parts):
        copy.wait()
        masked = guess_ref[pl.ds(n * TILE, TILE)] * keep[None]
        squares = squares + fold(masked * masked, width)
        x_ref[n * states : (n + 1) * states] = jnp.swapaxes(masked, 0, 1).astype(BF16)
    squares_ref[...] = squares
    copies[1].wait()
    line = lax.broadcasted_iota(jnp.int32, (TILE, width), 0)
    lane = lax.broadcasted_iota(jnp.int32, (TILE, width), 1)
    extra = jnp.zeros((TILE, width), F32)
    for k in range(terms):
        place_at = (lane == line + k * TILE).astype(BF16)
        extra = extra + jnp.dot(site_ref[k], place_at, preferred_element_type=F32)
    x_ref[blocks * states] = extra.astype(BF16)
    copies[2].wait()
    pack_blocks(right_ref, None, packed_ref)


def prepare_kernel(starts, keep_ref, squares_ref, guess_in, left_in, norm_ref, packed_ref, left_ref, *refs):
    x_refs = (None,) + refs[: len(starts) - 1]
    guess_ref, sems = refs[len(starts) - 1 :]
    rows, states, width = guess_in.shape
    half = width // 2
    done = starts[1] if len(starts) > 1 else rows
    copies = chunk_rows_in(guess_in, guess_ref, sems, done, rows, 1)
    left_copy = pltpu.make_async_copy(left_in, left_ref, sems.at[0])
    left_copy.start()
    keep = keep_ref[0:1, :][None]
    squares = squares_ref[...]
    for n, copy in enumerate(copies):
        copy.wait()
        masked = guess_ref[pl.ds(n * TILE, TILE)] * keep
        squares = squares + fold(masked * masked, width)
        chunk = max(c for c, start in enumerate(starts) if start <= done + n * TILE)
        at = done + n * TILE - starts[chunk]
        block = at // TILE
        x_refs[chunk][block * states : (block + 1) * states] = jnp.swapaxes(masked, 0, 1).astype(BF16)
    total = jnp.sum(squares)
    norm_ref[...] = jnp.full(norm_ref.shape, total, F32)
    line = lax.broadcasted_iota(jnp.int32, (TILE, half), 0)
    norm = jnp.full((TILE, half), total, F32)
    extra = jnp.zeros((TILE, half), F32)
    for n in range(3):
        part = norm.astype(BF16).astype(F32)
        norm = norm - part
        extra = jnp.where(line == left_ref.shape[0] + n, part, extra)
    left_copy.wait()
    pack_blocks(left_ref, extra, packed_ref)


def pack_blocks(block_ref, extra, packed_ref):
    terms, width, _ = block_ref.shape
    half = width // 2
    line = lax.broadcasted_iota(jnp.int32, (TILE, half), 0)
    row, col = triangle(half)
    lines = jnp.zeros((TILE, half), F32) if extra is None else extra
    for k in range(terms):
        upper = block_ref[k, 0:half, 0:half].astype(F32)
        lower = block_ref[k, half:width, half:width].astype(F32)
        diagonal = jnp.sum(jnp.where(row == col, lower, 0.0), axis=0, keepdims=True)
        lines = jnp.where(line == k, diagonal, lines)
        base = k * width
        packed_ref[base : base + half, :] = block_ref[k, 0:half, half:width]
        packed_ref[base + half : base + width, :] = jnp.where(row <= col, upper, lower).astype(BF16)
    packed_ref[terms * width : terms * width + TILE, :] = lines.astype(BF16)


def triangle(half):
    row = lax.broadcasted_iota(jnp.int32, (half, half), 0)
    col = lax.broadcasted_iota(jnp.int32, (half, half), 1)
    return row, col


def unpack_symmetric(packed_ref, full_ref, keep=None):
    terms, width, _ = full_ref.shape
    half = width // 2
    row, col = triangle(half)

    def kept(block, start):
        return block if keep is None else block * keep[:, start : start + half]

    diagonals = packed_ref[terms * width : terms * width + TILE, :].astype(F32)
    for k in range(terms):
        base = k * width
        corner = packed_ref[base : base + half, :].astype(F32)
        mixed = packed_ref[base + half : base + width, :].astype(F32)
        diagonal = diagonals[k : k + 1]
        turned = mixed.T
        lower = jnp.where(row > col, mixed, jnp.where(row == col, diagonal, turned))
        full_ref[k, 0:half, 0:half] = kept(jnp.where(row <= col, mixed, turned), 0).astype(BF16)
        full_ref[k, 0:half, half:width] = kept(corner, half).astype(BF16)
        full_ref[k, half:width, 0:half] = kept(corner.T, 0).astype(BF16)
        full_ref[k, half:width, half:width] = kept(lower, half).astype(BF16)


def spread_kernel(chunk_ref, kron_ref):
    width = chunk_ref.shape[2]
    size = kron_ref.shape[1]
    terms = kron_ref.shape[0] // size
    states = size // TILE
    tile = chunk_ref[chunk_ref.shape[0] - 1]
    row_state = lax.broadcasted_iota(jnp.int32, (size, states), 0) // TILE
    pick = (row_state == lax.broadcasted_iota(jnp.int32, (size, states), 1)).astype(BF16)
    tall = jnp.dot(pick, tile, preferred_element_type=F32).astype(BF16)
    lane = lax.broadcasted_iota(jnp.int32, (width, size), 0)
    col_state = lax.broadcasted_iota(jnp.int32, (width, size), 1) // TILE
    same = (
        lax.broadcasted_iota(jnp.int32, (size, size), 0) % TILE
        == lax.broadcasted_iota(jnp.int32, (size, size), 1) % TILE
    )
    for k in range(terms):
        pick_t = (lane == col_state + k * TILE).astype(BF16)
        full = jnp.dot(tall, pick_t, preferred_element_type=F32)
        kron_ref[k * size : (k + 1) * size, :] = jnp.where(same, full, 0.0).astype(BF16)


def mix_sites(source_ref, kron_ref, rotated_ref, base):
    terms, states, _, width = rotated_ref.shape
    for i in range(source_ref.shape[0] // states):
        to = pl.ds(pl.multiple_of(base + i * TILE, TILE), TILE)
        stack = source_ref[i * states : (i + 1) * states].reshape(states * TILE, width)
        turned = jnp.dot(kron_ref[...], stack, preferred_element_type=F32).astype(BF16)
        rotated_ref[:, :, to, :] = turned.reshape(terms, states, TILE, width)


def summed(values):
    while len(values) > 1:
        values = [values[n] + values[n + 1] for n in range(0, len(values), 2)]
    return values[0]


def place(hop, chips):
    me = lax.axis_index("term")
    chip = (me // CORES - hop + chips) % chips
    return chip, me % CORES


def row_of(spot, rows, chips):
    chip, core = place(spot[0], chips)
    return pl.multiple_of((chip * CORES + (core if spot[1] == 0 else 1 - core)) * rows + spot[2], TILE)


def mix_pieces(pieces, kron_ref, rotated_ref):
    at = 0
    for piece in pieces:
        mix_sites(piece, kron_ref, rotated_ref, at)
        at += piece.shape[0] // rotated_ref.shape[1] * TILE


def rotate_own_kernel(groups, rows, chips, *refs):
    kron_ref, left_ref, rotated_ref, columns_ref = refs[-4:]
    mix_pieces(refs[:-4], kron_ref, rotated_ref)
    blocks = []
    for spots in groups:
        for k in range(left_ref.shape[0]):
            blocks += [left_ref[k, pl.ds(row_of(spot, rows, chips), spot[3]), :] for spot in spots]
    columns_ref[...] = jnp.concatenate(blocks, axis=0).astype(F32).T.astype(BF16)


def turn(right_ref, rotated_ref, turned_ref):
    terms, states, count, width = rotated_ref.shape
    for k in range(terms):
        for n in range(0, states, 8):
            source = rotated_ref[k, n : n + 8].reshape(8 * count, width)
            turned = jnp.dot(source, right_ref[k], preferred_element_type=F32).astype(BF16)
            turned_ref[n : n + 8, k * count : (k + 1) * count, :] = turned.reshape(8, count, width)


def here_kernel(rotated_ref, packed_ref, keep_ref, turned_ref, right_ref):
    unpack_symmetric(packed_ref, right_ref, keep_ref[0:1, :])
    turn(right_ref, rotated_ref, turned_ref)


def there_kernel(*refs):
    right_ref, kron_ref, turned_ref, rotated_ref = refs[-4:]
    mix_pieces(refs[:-4], kron_ref, rotated_ref)
    turn(right_ref, rotated_ref, turned_ref)


def last_kernel(count, *refs):
    right_ref, kron_ref, columns_ref = refs[count : count + 3]
    out_ref, rotated_ref, turned_ref = refs[-3:]
    there_kernel(*refs[:count], right_ref, kron_ref, turned_ref, rotated_ref)
    blocks = list(refs[count + 3 : -3]) + [turned_ref]

    def lefts(p, carry):
        stack = jnp.concatenate([block[p] for block in blocks], axis=0)
        out_ref[p] = jnp.dot(columns_ref[...], stack, preferred_element_type=F32)
        return carry

    lax.fori_loop(0, out_ref.shape[0], lefts, 0, unroll=out_ref.shape[0])


def rotate_kernel(spots, rows, chips, *refs):
    pieces = refs[: len(spots)]
    kron_ref = refs[len(spots)]
    rotated_ref, whole_ref, sems = refs[-3:]
    states = whole_ref.shape[0]
    copies = []
    bases = [row_of(spot, rows, chips) for spot in spots]
    for at, piece in zip(bases, pieces):
        for i in range(piece.shape[0] // states):
            target = whole_ref.at[:, pl.ds(pl.multiple_of(at + i * TILE, TILE), TILE), :]
            source = piece.at[i * states : (i + 1) * states]
            copies.append(pltpu.make_async_copy(source, target, sems.at[len(copies)]))
            copies[-1].start()
    for at, piece in zip(bases, pieces):
        mix_sites(piece, kron_ref, rotated_ref, at)
    for copy in copies:
        copy.wait()


def lefts_kernel(spots, rows, chips, *refs):
    count = len(spots)
    packed_ref, norm_before_ref = refs[count + 3 : count + 5]
    mixed_ref, norm_ref, rotated_ref, whole_ref, left_ref, sems = refs[-6:]
    terms, states, width, _ = rotated_ref.shape
    lines = packed_ref[terms * width : terms * width + TILE, :].astype(F32)
    norm = lines[terms : terms + 1] + lines[terms + 1 : terms + 2] + lines[terms + 2 : terms + 3]
    norm_ref[...] = norm_before_ref[...] + jnp.concatenate([norm, norm], axis=1)
    unpack_symmetric(packed_ref, left_ref)
    rotate_kernel(spots, rows, chips, *refs[: count + 1], rotated_ref, whole_ref, sems)

    def lefts(p, carry):
        for k in range(terms):
            mixed = jnp.dot(left_ref[k], rotated_ref[k, p], preferred_element_type=F32)
            mixed_ref[p, :, k * width : (k + 1) * width] = mixed.astype(BF16)
        return carry

    lax.fori_loop(0, states, lefts, 0, unroll=states)


def rights_kernel(start, stop, packed_ref, mixed_ref, before_ref, keep_ref, partial_ref, *refs):
    if start == 0:
        right_ref = refs[0]
        unpack_symmetric(packed_ref, right_ref, keep_ref[0:1, :])
    else:
        right_ref = packed_ref
    terms, width, _ = right_ref.shape

    def rights(n, carry):
        at = n * GROUP
        rows = mixed_ref[pl.ds(start + at, GROUP)].reshape(GROUP * width, terms * width)
        stacked = right_ref[...].reshape(terms * width, width)
        image = jnp.dot(rows, stacked, preferred_element_type=F32).reshape(GROUP, width, width)
        partial_ref[pl.ds(at, GROUP)] = (before_ref[pl.ds(start + at, GROUP)] + image).astype(partial_ref.dtype)
        return carry

    lax.fori_loop(0, (stop - start) // GROUP, rights, 0)


def shifted_residual(start, shift, mine_ref, other_ref, whole_ref, left_ref, res_ref, mixed_ref):
    count, width, _ = res_ref.shape
    terms = left_ref.shape[0]
    zero = jnp.zeros((8, width), F32)

    def lefts(n, sums):
        square, product = sums
        for row in range(0, width, STRIP):
            strip = pl.ds(row, STRIP)
            held = whole_ref[start + n, strip, :].astype(F32)
            sigma = mine_ref[n, strip, :].astype(F32) + other_ref[n, strip, :].astype(F32)
            residual = sigma - shift * held
            res_ref[n, strip, :] = residual.astype(BF16)
            square = square + fold(residual * residual, width)
            product = product + fold(sigma * held, width)
        mixed = jnp.dot(
            left_ref[...].reshape(terms * width, width), res_ref[n], preferred_element_type=F32
        ).astype(BF16)
        for k in range(terms):
            mixed_ref[k, n] = mixed[k * width : (k + 1) * width]
        return square, product

    square, product = lax.fori_loop(0, count, lefts, (zero, zero), unroll=count)
    return jnp.sum(square), jnp.sum(product)


def low_kernel(
    norm_ref,
    norm_other_ref,
    low_ref,
    low_other_ref,
    whole_ref,
    left_ref,
    res_ref,
    mixed_ref,
    out_ref,
):
    count, width, _ = low_ref.shape
    states = whole_ref.shape[0]
    held = whole_ref[0].astype(F32)
    sigma = low_ref[0].astype(F32) + low_other_ref[0].astype(F32)
    product = jnp.sum(fold(sigma * held, width))
    square = jnp.sum(fold(held * held, width))
    total = norm_ref[0:1, :] + norm_other_ref[0:1, :]
    floor = jnp.maximum(jnp.maximum(square, (0.25 / states) * total), 1e-30)
    shift = product / floor
    square, product = shifted_residual(
        0, shift, low_ref, low_other_ref, whole_ref, left_ref, res_ref, mixed_ref
    )
    out_ref[0:1, :] = shift
    out_ref[1:2, :] = jnp.full((1, width), square, F32)
    out_ref[2:3, :] = jnp.full((1, width), product, F32)
    out_ref[3:8, :] = jnp.zeros((5, width), F32)


def high_kernel(
    scale,
    members,
    norm_ref,
    norm_other_ref,
    sums_ref,
    high_ref,
    high_other_ref,
    whole_ref,
    left_ref,
    right_ref,
    kron_ref,
    res_low_ref,
    mixed_low_ref,
    out_ref,
    res_ref,
    rotated_ref,
    mixed_ref,
):
    terms, states, width, _ = rotated_ref.shape
    half = states // 2
    shift = sums_ref[0:1, :]
    square, product = shifted_residual(
        half, shift, high_ref, high_other_ref, whole_ref, left_ref, res_ref, mixed_ref
    )

    def sites(i, carry):
        at = pl.ds(pl.multiple_of(i * TILE, TILE), TILE)
        stack = jnp.concatenate([res_low_ref[:, at, :], res_ref[:, at, :]], axis=0).reshape(states * TILE, width)
        turned = jnp.dot(kron_ref[...], stack, preferred_element_type=F32).astype(BF16)
        rotated_ref[:, :, at, :] = turned.reshape(terms, states, TILE, width)
        return carry

    lax.fori_loop(0, width // TILE, sites, 0, unroll=width // TILE)
    cross = jnp.zeros((8, width), F32)
    for start, left_mixed_ref in ((0, mixed_low_ref), (half, mixed_ref)):
        for k in range(terms):
            turned = rotated_ref[k, start : start + half].reshape(half * width, width)
            image = jnp.dot(turned, right_ref[k], preferred_element_type=F32)
            held = left_mixed_ref[k].reshape(half * width, width).astype(F32)
            cross = cross + fold(held * image, width)
    res_square = sums_ref[1:2, :] + square
    product = sums_ref[2:3, :] + product
    total = norm_ref[0:1, :] + norm_other_ref[0:1, :]
    factor = scale / (total * scale + epsilon)
    rayleigh = factor * product
    gap = rayleigh - shift
    res_vector = product - shift * total
    res_sq = factor * (res_square - 2.0 * gap * res_vector + gap * gap * total)
    change = gap * gap * product - 2.0 * gap * (res_square + shift * res_vector)
    share = 1.0 / members
    out_ref[0:1, :] = rayleigh * share
    out_ref[1:2, :] = jnp.maximum(res_sq, 0.0) * share
    out_ref[2:3, :] = factor * (jnp.sum(cross) + share * change)
    out_ref[3:8, :] = jnp.zeros((5, width), F32)


def own_rows_kernel(scale, members, keep_ref, norm_ref, norm_other_ref, share_ref, guess_ref, *refs):
    low_ref, low_other_ref, high_ref, high_other_ref, vector_ref, residual_ref = refs
    rows, states, width = guess_ref.shape
    inverse = lax.rsqrt((norm_ref[0:1, :] + norm_other_ref[0:1, :]) * scale + epsilon)
    row_scale = keep_ref[0:1, :] * inverse
    rayleigh = share_ref[0:1, :] * members
    own = pl.ds(pl.multiple_of(lax.axis_index("term") * rows, TILE), rows)
    vector = guess_ref[...] * row_scale[None]
    vector_ref[...] = vector
    sigma = jnp.concatenate(
        [
            mine_ref[:, own, :].astype(F32) + other_ref[:, own, :].astype(F32)
            for mine_ref, other_ref in ((low_ref, low_other_ref), (high_ref, high_other_ref))
        ],
        axis=0,
    )
    residual_ref[...] = jnp.swapaxes(sigma * row_scale[None], 0, 1) - rayleigh[None] * vector


def finish_kernel(vector_ref, residual_ref, *refs):
    shares = refs[:-2]
    ritz_ref, energy_ref = refs[-2:]
    stat = summed([share[...] for share in shares])
    rayleigh = stat[0:1, :]
    res_sq = stat[1:2, :]
    res_var = res_sq + epsilon
    curvature = stat[2:3, :] / res_var
    res_scale = jnp.sqrt(res_var)
    coupling = res_sq / res_scale
    half_gap = 0.5 * (rayleigh - curvature)
    energy = 0.5 * (rayleigh + curvature) - jnp.sqrt(half_gap * half_gap + coupling * coupling)
    coeff_new = energy - rayleigh
    coeff_norm = jnp.sqrt(coupling * coupling + coeff_new * coeff_new + epsilon)
    old = coupling / coeff_norm
    new = coeff_new / (coeff_norm * res_scale)
    ritz_ref[...] = old[None] * vector_ref[...] + new[None] * residual_ref[...]
    energy_ref[0] = energy[0, 0]


def shards(wave_guess, left_env, right_env, site_ops, bond_rank):
    guess = wave_guess[0]
    left = left_env[0]
    site = site_ops[0]
    rows, states, width = guess.shape
    terms = left.shape[0]
    members = lax.axis_size("term")
    chips = members // CORES
    segments = lax.axis_size("seg")
    scale = 1.0 / float(rows * members * states * width)
    hops = tuple(range(chips))

    def to_sibling(block):
        return lax.ppermute(block, "term", [(i, i ^ 1) for i in range(members)])

    def to_next_chip(block):
        return lax.ppermute(block, "term", [(i, (i + CORES) % members) for i in range(members)])

    def around(block):
        found = [block]
        for _ in range(chips - 1):
            found.append(to_next_chip(found[-1]))
        return found

    def everyone(block):
        return [block] + [
            lax.ppermute(block, "term", [(i, i ^ bits) for i in range(members)])
            for bits in range(CORES, members, CORES)
        ]

    tile = jax.ShapeDtypeStruct((8, width), F32)
    half = width // 2
    packed_shape = jax.ShapeDtypeStruct((terms * width + TILE, half), BF16)
    starts = (0, rows - 2 * TILE, rows - TILE) if rows >= 4 * TILE else (0,)
    lengths = [stop - start for start, stop in zip(starts, starts[1:] + (rows,))]
    in_place = [pltpu.with_memory_space_constraint(a, pltpu.HBM) for a in (guess, left, right_env[0], site)]
    first_chunk, keep, squares, right_packed = pl.pallas_call(
        first_chunk_kernel,
        out_shape=(jax.ShapeDtypeStruct((lengths[0] // TILE * states + 1, TILE, width), BF16), tile, tile, packed_shape),
        in_specs=[anywhere] + [in_hbm] * 3,
        out_specs=(vmem,) * 4,
        scratch_shapes=[
            pltpu.VMEM((1, 1), jnp.int32),
            pltpu.VMEM((lengths[0], states, width), F32),
            pltpu.VMEM(site.shape, BF16),
            pltpu.VMEM(left.shape, BF16),
            pltpu.SemaphoreType.DMA((lengths[0] // TILE + 3,)),
        ],
        compiler_params=params(),
        cost_estimate=cost(2 * guess.size, 3 * guess.size),
        name="first_chunk",
    )(bond_rank.reshape(1, 1), in_place[0], in_place[3], in_place[2])
    rest = rows - lengths[0]
    squares, first_sibling = lax.optimization_barrier((squares, to_sibling(first_chunk)))
    norm_part, left_packed, left, *chunks = pl.pallas_call(
        functools.partial(prepare_kernel, starts),
        out_shape=(
            tile,
            packed_shape,
            jax.ShapeDtypeStruct(left.shape, BF16),
            *[jax.ShapeDtypeStruct((length // TILE * states, TILE, width), BF16) for length in lengths[1:]],
        ),
        in_specs=[vmem] * 2 + [in_hbm] * 2,
        out_specs=(vmem,) * (2 + len(lengths)),
        scratch_shapes=[
            pltpu.VMEM((max(rest, TILE), states, width), F32),
            pltpu.SemaphoreType.DMA((rest // TILE + 1,)),
        ],
        compiler_params=params(),
        cost_estimate=cost(4 * guess.size, 6 * guess.size),
        name="prepare",
    )(keep, squares, *in_place[:2])
    chunks = [first_chunk] + chunks

    chunk_hops = [around(chunk) for chunk in chunks]
    here_pieces = chunks + [first_sibling] + [to_sibling(chunk) for chunk in chunks[1:]]
    here_spots = tuple((0, flip, start, length) for flip in range(CORES) for start, length in zip(starts, lengths))
    far_spots = [
        tuple((hop, flip, start, length) for hop in hops[1:] for flip in range(CORES))
        for start, length in zip(starts, lengths)
    ]
    mid_spots = sum(far_spots[:-1], ())
    groups = [group for group in (here_spots, mid_spots, far_spots[-1]) if group]
    lefts = around(left_packed)
    shift = [(i + 1, i) for i in range(segments - 1)]
    received = lax.ppermute(right_packed, "seg", shift)

    size = states * TILE

    def spread(block):
        return pl.pallas_call(
            spread_kernel,
            out_shape=jax.ShapeDtypeStruct((terms * size, size), BF16),
            in_specs=[vmem],
            out_specs=vmem,
            compiler_params=params(),
            cost_estimate=cost(2 * terms * size * size * width, 2 * terms * size * size),
            name="spread_site",
        )(block)

    kron_own = spread(chunks[0])

    whole = (states, width, width)
    whole_bf = jax.ShapeDtypeStruct(whole, BF16)
    whole_f32 = jax.ShapeDtypeStruct(whole, F32)
    rotated = (terms, states, width, width)
    rotated_bf = jax.ShapeDtypeStruct(rotated, BF16)
    square = pltpu.VMEM((terms, width, width), BF16)
    chip_rows = CORES * rows
    stage_flops = 2 * terms * states * width * width * width

    def buffers(spots):
        count = sum(spot[3] for spot in spots)
        return (terms, states, count, width), (states, terms * count, width)

    here_rotated, here_turned = buffers(here_spots)
    part_cost = cost(stage_flops, 8 * states * width * width)
    rotated_own, columns = pl.pallas_call(
        functools.partial(rotate_own_kernel, groups, rows, chips),
        out_shape=(
            jax.ShapeDtypeStruct(here_rotated, BF16),
            jax.ShapeDtypeStruct((width, terms * width), BF16),
        ),
        in_specs=[vmem] * (len(here_pieces) + 2),
        out_specs=(vmem, vmem),
        compiler_params=params(),
        cost_estimate=part_cost,
        name="rotate_own",
    )(*here_pieces, kron_own, left)

    def rotate(spots, pieces, kron, before):
        return pl.pallas_call(
            functools.partial(rotate_kernel, spots, rows, chips),
            out_shape=(rotated_bf, whole_bf),
            in_specs=[vmem] * (len(pieces) + 1) + [anywhere] * len(before),
            out_specs=(vmem, vmem),
            scratch_shapes=[pltpu.SemaphoreType.DMA((sum(spot[3] for spot in spots) // TILE,))],
            input_output_aliases={len(pieces) + 1 + n: n for n in range(len(before))},
            compiler_params=params(),
            cost_estimate=part_cost,
            name="rotate_crossed" if before else "rotate_here",
        )(*pieces, kron, *before)

    def relayed(blocks):
        return [piece for block in blocks for piece in (block, to_sibling(block))]

    firsts, rotated_own = lax.optimization_barrier((chunk_hops[0][1:], rotated_own))
    kron = spread(firsts[0])
    turned = rotate(here_spots, here_pieces, kron, ())
    received, turned = lax.optimization_barrier((received, turned))
    packed = jnp.where(lax.axis_index("seg") == segments - 1, right_packed, received)
    rights = around(packed)
    turned_own, right = pl.pallas_call(
        here_kernel,
        out_shape=(jax.ShapeDtypeStruct(here_turned, BF16), jax.ShapeDtypeStruct(left.shape, BF16)),
        in_specs=[vmem] * 3,
        out_specs=(vmem, vmem),
        compiler_params=params(),
        cost_estimate=part_cost,
        name="apply_rows_here",
    )(rotated_own, packed, keep)
    parts = [turned_own]
    mid_pieces = []
    if mid_spots:
        mid_pieces += relayed(firsts)
        for crossing in chunk_hops[1:-1]:
            crossed, turned = lax.optimization_barrier((crossing[1:], turned))
            mid_pieces += relayed(crossed)
        turned = rotate(mid_spots, mid_pieces, kron, turned)
        crossed, turned, parts[0] = lax.optimization_barrier((chunk_hops[-1][1:], turned, parts[0]))
        last_pieces = relayed(crossed)
        mid_rotated, mid_turned = buffers(mid_spots)
        parts.append(
            pl.pallas_call(
                there_kernel,
                out_shape=jax.ShapeDtypeStruct(mid_turned, BF16),
                in_specs=[vmem] * (len(mid_pieces) + 2),
                out_specs=vmem,
                scratch_shapes=[pltpu.VMEM(mid_rotated, BF16)],
                compiler_params=params(),
                cost_estimate=part_cost,
                name="apply_rows_crossed",
            )(*mid_pieces, right, kron_own)
        )
    else:
        last_pieces = relayed(firsts)
    last_rotated, last_turned = buffers(far_spots[-1])
    partial = pl.pallas_call(
        functools.partial(last_kernel, len(last_pieces)),
        out_shape=whole_f32,
        in_specs=[vmem] * (len(last_pieces) + 3 + len(parts)),
        out_specs=vmem,
        scratch_shapes=[pltpu.VMEM(last_rotated, BF16), pltpu.VMEM(last_turned, BF16)],
        compiler_params=params(),
        cost_estimate=part_cost,
        name="apply_rows_last",
    )(*last_pieces, right, kron_own, columns, *parts)
    norm = norm_part
    for hop in hops[1:]:
        if hop > 1:
            block, partial = lax.optimization_barrier((firsts[hop - 1], partial))
            kron = spread(block)
            turned = rotate(here_spots, here_pieces, kron, ())
            if mid_spots:
                turned = rotate(mid_spots, mid_pieces, kron, turned)
        left_far, partial = lax.optimization_barrier((lefts[hop], partial))
        mixed, norm, _, vector = pl.pallas_call(
            functools.partial(lefts_kernel, far_spots[-1], rows, chips),
            out_shape=(jax.ShapeDtypeStruct((states, width, terms * width), BF16), tile, rotated_bf, whole_bf),
            in_specs=[vmem] * (len(last_pieces) + 1) + [anywhere] * 2 + [vmem] * 2,
            out_specs=(vmem,) * 4,
            scratch_shapes=[
                square,
                pltpu.SemaphoreType.DMA((sum(spot[3] for spot in far_spots[-1]) // TILE,)),
            ],
            input_output_aliases={len(last_pieces) + 1: 2, len(last_pieces) + 2: 3},
            compiler_params=params(),
            cost_estimate=cost(stage_flops, 12 * states * width * width),
            name="received_lefts",
        )(*last_pieces, kron, *turned, left_far, norm)
        last = hop == hops[-1]
        right_far = rights[hop]
        parts = []
        bounds = (0, states // 2, states) if last else (0, states)
        for start, stop in zip(bounds[:-1], bounds[1:]):
            part_shape = jax.ShapeDtypeStruct((stop - start, width, width), BF16 if last else F32)
            part, *unpacked = pl.pallas_call(
                functools.partial(rights_kernel, start, stop),
                out_shape=(part_shape,) + ((jax.ShapeDtypeStruct(left.shape, BF16),) if start == 0 else ()),
                in_specs=[vmem] * 4,
                out_specs=(vmem,) * (2 if start == 0 else 1),
                compiler_params=params(),
                cost_estimate=cost(stage_flops / 2, 12 * states * width * width),
                name="received_rights",
            )(right_far, mixed, partial, keep)
            if unpacked:
                right_far, norm_other = lax.optimization_barrier((unpacked[0], to_sibling(norm)))
            parts.append(part)
        if not last:
            partial = parts[0]
    halves = []
    for part in parts:
        halves += [part, to_sibling(part)]
    half_bf = jax.ShapeDtypeStruct((states // 2, width, width), BF16)
    half_mixed = (terms, states // 2, width, width)
    res_low, mixed_low, sums = pl.pallas_call(
        low_kernel,
        out_shape=(half_bf, jax.ShapeDtypeStruct(half_mixed, BF16), tile),
        in_specs=[vmem] * 6,
        out_specs=(vmem,) * 3,
        compiler_params=params(),
        cost_estimate=cost(stage_flops / 2, 3 * states * width * width),
        name="residual_low",
    )(norm, norm_other, *halves[:2], vector, left)
    share = pl.pallas_call(
        functools.partial(high_kernel, scale, members),
        out_shape=tile,
        in_specs=[vmem] * 11,
        out_specs=vmem,
        scratch_shapes=[
            pltpu.VMEM(half_bf.shape, BF16),
            pltpu.VMEM(rotated, BF16),
            pltpu.VMEM(half_mixed, BF16),
        ],
        compiler_params=params(),
        cost_estimate=cost(3 * stage_flops, 6 * states * width * width),
        name="residual_high",
    )(norm, norm_other, sums, *halves[2:], vector, left, right, kron_own, res_low, mixed_low)
    crossed = everyone(share)

    local = jax.ShapeDtypeStruct((rows, states, width), F32)
    vector_own, residual_own = pl.pallas_call(
        functools.partial(own_rows_kernel, scale, members),
        out_shape=(local, local),
        in_specs=[vmem] * 9,
        out_specs=(vmem, vmem),
        compiler_params=params(),
        cost_estimate=cost(8 * guess.size, 16 * guess.size),
        name="own_rows",
    )(keep, norm, norm_other, share, guess, *halves)

    shares = [share, to_sibling(share)]
    gated, residual_own = lax.optimization_barrier((crossed[1:], residual_own))
    shares += relayed(gated)
    ritz, energy = pl.pallas_call(
        finish_kernel,
        out_shape=(local, jax.ShapeDtypeStruct((1,), F32)),
        in_specs=[vmem] * (2 + members),
        out_specs=(vmem, smem),
        compiler_params=params(),
        cost_estimate=cost(3 * guess.size, 12 * guess.size),
        name="finish",
    )(vector_own, residual_own, *shares)
    return (ritz[None], energy)


def solution(mesh):
    in_specs = (
        P("seg", "term", None, None),
        P("seg", "term", None, None),
        P("seg", "term", None, None),
        P("seg", "term", None, None),
        P("seg"),
    )
    out_specs = (P("seg", "term", None, None), P("seg"))
    return jax.shard_map(shards, mesh=mesh, in_specs=in_specs, out_specs=out_specs, check_vma=False)
```

```python
import functools

import jax
import jax.numpy as jnp
from jax import lax
from jax.experimental import pallas as pl
from jax.experimental.pallas import tpu as pltpu
from jax.sharding import PartitionSpec as P

epsilon = 1e-06
CORES = 2
TILE = 16
STRIP = 32
GROUP = 8
VMEM_LIMIT = 20 * 1024 * 1024
F32 = jnp.float32
BF16 = jnp.bfloat16

vmem = pl.BlockSpec(memory_space=pltpu.VMEM)
smem = pl.BlockSpec(memory_space=pltpu.SMEM)
anywhere = pl.BlockSpec(memory_space=pl.ANY)
in_hbm = pl.BlockSpec(memory_space=pltpu.HBM)


def params():
    return pltpu.CompilerParams(vmem_limit_bytes=VMEM_LIMIT)


def cost(flops, moved):
    return pl.CostEstimate(flops=int(flops) // 100, bytes_accessed=int(moved) // 100, transcendentals=0)


def fold(values, width):
    return jnp.sum(values.reshape(values.size // (8 * width), 8, width), axis=0)


def chunk_rows_in(guess_in, guess_ref, sems, start, stop, slot):
    copies = []
    for n in range(start, stop, TILE):
        target = guess_ref.at[pl.ds(n - start, TILE)]
        copies.append(pltpu.make_async_copy(guess_in.at[pl.ds(n, TILE)], target, sems.at[slot + len(copies)]))
        copies[-1].start()
    return copies


def first_chunk_kernel(
    guess_in,
    site_in,
    right_in,
    x_ref,
    squares_ref,
    packed_ref,
    guess_ref,
    site_ref,
    right_ref,
    sems,
):
    rows, states, width = guess_ref.shape
    terms = site_ref.shape[0]
    blocks = rows // TILE
    copies = [
        pltpu.make_async_copy(source, target, sems.at[n])
        for n, (source, target) in enumerate(((site_in, site_ref), (right_in, right_ref)))
    ]
    parts = chunk_rows_in(guess_in, guess_ref, sems, 0, rows, 2)
    copies[0].start()
    copies[1].start()
    squares = jnp.zeros((8, width), F32)
    for n, copy in enumerate(parts):
        copy.wait()
        whole = guess_ref[pl.ds(n * TILE, TILE)]
        squares = squares + fold(whole * whole, width)
        x_ref[n * states : (n + 1) * states] = jnp.swapaxes(whole, 0, 1).astype(BF16)
    squares_ref[...] = squares
    copies[0].wait()
    line = lax.broadcasted_iota(jnp.int32, (TILE, width), 0)
    lane = lax.broadcasted_iota(jnp.int32, (TILE, width), 1)
    extra = jnp.zeros((TILE, width), F32)
    for k in range(terms):
        place_at = (lane == line + k * TILE).astype(BF16)
        extra = extra + jnp.dot(site_ref[k], place_at, preferred_element_type=F32)
    x_ref[blocks * states] = extra.astype(BF16)
    copies[1].wait()
    pack_blocks(right_ref, None, packed_ref)


def prepare_kernel(
    starts, rank_ref, squares_ref, guess_in, left_in, norm_ref, keep_ref, packed_ref, left_ref, *refs
):
    x_refs = (None,) + refs[: len(starts) - 1]
    guess_ref, sems = refs[len(starts) - 1 :]
    rows, states, width = guess_in.shape
    half = width // 2
    done = starts[1] if len(starts) > 1 else rows
    copies = chunk_rows_in(guess_in, guess_ref, sems, done, rows, 1)
    left_copy = pltpu.make_async_copy(left_in, left_ref, sems.at[0])
    left_copy.start()
    column = lax.broadcasted_iota(jnp.int32, (1, width), 1)
    keep = (column < rank_ref[...]).astype(F32)
    keep_ref[...] = jnp.broadcast_to(keep, keep_ref.shape)
    squares = squares_ref[...] * keep
    keep = keep[None]
    for n, copy in enumerate(copies):
        copy.wait()
        masked = guess_ref[pl.ds(n * TILE, TILE)] * keep
        squares = squares + fold(masked * masked, width)
        chunk = max(c for c, start in enumerate(starts) if start <= done + n * TILE)
        at = done + n * TILE - starts[chunk]
        block = at // TILE
        x_refs[chunk][block * states : (block + 1) * states] = jnp.swapaxes(masked, 0, 1).astype(BF16)
    total = jnp.sum(squares)
    norm_ref[...] = jnp.full(norm_ref.shape, total, F32)
    line = lax.broadcasted_iota(jnp.int32, (TILE, half), 0)
    norm = jnp.full((TILE, half), total, F32)
    extra = jnp.zeros((TILE, half), F32)
    for n in range(3):
        part = norm.astype(BF16).astype(F32)
        norm = norm - part
        extra = jnp.where(line == left_ref.shape[0] + n, part, extra)
    left_copy.wait()
    pack_blocks(left_ref, extra, packed_ref)


def pack_blocks(block_ref, extra, packed_ref):
    terms, width, _ = block_ref.shape
    half = width // 2
    line = lax.broadcasted_iota(jnp.int32, (TILE, half), 0)
    row, col = triangle(half)
    lines = jnp.zeros((TILE, half), F32) if extra is None else extra
    for k in range(terms):
        upper = block_ref[k, 0:half, 0:half].astype(F32)
        lower = block_ref[k, half:width, half:width].astype(F32)
        diagonal = jnp.sum(jnp.where(row == col, lower, 0.0), axis=0, keepdims=True)
        lines = jnp.where(line == k, diagonal, lines)
        base = k * width
        packed_ref[base : base + half, :] = block_ref[k, 0:half, half:width]
        packed_ref[base + half : base + width, :] = jnp.where(row <= col, upper, lower).astype(BF16)
    packed_ref[terms * width : terms * width + TILE, :] = lines.astype(BF16)


def triangle(half):
    row = lax.broadcasted_iota(jnp.int32, (half, half), 0)
    col = lax.broadcasted_iota(jnp.int32, (half, half), 1)
    return row, col


def unpack_symmetric(packed_ref, full_ref, keep=None):
    terms, width, _ = full_ref.shape
    half = width // 2
    row, col = triangle(half)

    rank = width if keep is None else jnp.sum(keep)
    row_index = row.astype(F32)

    def kept(block, top, start):
        if keep is None:
            return block
        return jnp.where(row_index < rank - top, block * keep[:, start : start + half], 0.0)

    diagonals = packed_ref[terms * width : terms * width + TILE, :].astype(F32)
    for k in range(terms):
        base = k * width
        corner = packed_ref[base : base + half, :].astype(F32)
        mixed = packed_ref[base + half : base + width, :].astype(F32)
        diagonal = diagonals[k : k + 1]
        turned = mixed.T
        lower = jnp.where(row > col, mixed, jnp.where(row == col, diagonal, turned))
        full_ref[k, 0:half, 0:half] = kept(jnp.where(row <= col, mixed, turned), 0, 0).astype(BF16)
        full_ref[k, 0:half, half:width] = kept(corner, 0, half).astype(BF16)
        full_ref[k, half:width, 0:half] = kept(corner.T, half, 0).astype(BF16)
        full_ref[k, half:width, half:width] = kept(lower, half, half).astype(BF16)


def spread_kernel(chunk_ref, kron_ref):
    width = chunk_ref.shape[2]
    size = kron_ref.shape[1]
    terms = kron_ref.shape[0] // size
    states = size // TILE
    tile = chunk_ref[chunk_ref.shape[0] - 1]
    row_state = lax.broadcasted_iota(jnp.int32, (size, states), 0) // TILE
    pick = (row_state == lax.broadcasted_iota(jnp.int32, (size, states), 1)).astype(BF16)
    tall = jnp.dot(pick, tile, preferred_element_type=F32).astype(BF16)
    lane = lax.broadcasted_iota(jnp.int32, (width, size), 0)
    col_state = lax.broadcasted_iota(jnp.int32, (width, size), 1) // TILE
    same = (
        lax.broadcasted_iota(jnp.int32, (size, size), 0) % TILE
        == lax.broadcasted_iota(jnp.int32, (size, size), 1) % TILE
    )
    for k in range(terms):
        pick_t = (lane == col_state + k * TILE).astype(BF16)
        full = jnp.dot(tall, pick_t, preferred_element_type=F32)
        kron_ref[k * size : (k + 1) * size, :] = jnp.where(same, full, 0.0).astype(BF16)


def mix_sites(source_ref, kron_ref, rotated_ref, base):
    terms, states, _, width = rotated_ref.shape
    for i in range(source_ref.shape[0] // states):
        to = pl.ds(pl.multiple_of(base + i * TILE, TILE), TILE)
        stack = source_ref[i * states : (i + 1) * states].reshape(states * TILE, width)
        turned = jnp.dot(kron_ref[...], stack, preferred_element_type=F32).astype(BF16)
        rotated_ref[:, :, to, :] = turned.reshape(terms, states, TILE, width)


def summed(values):
    while len(values) > 1:
        values = [values[n] + values[n + 1] for n in range(0, len(values), 2)]
    return values[0]


def place(hop, chips):
    me = lax.axis_index("term")
    chip = (me // CORES - hop + chips) % chips
    return chip, me % CORES


def row_of(spot, rows, chips):
    chip, core = place(spot[0], chips)
    return pl.multiple_of((chip * CORES + (core if spot[1] == 0 else 1 - core)) * rows + spot[2], TILE)


def mix_pieces(pieces, kron_ref, rotated_ref):
    at = 0
    for piece in pieces:
        mix_sites(piece, kron_ref, rotated_ref, at)
        at += piece.shape[0] // rotated_ref.shape[1] * TILE


def rotate_own_kernel(groups, rows, chips, *refs):
    kron_ref, left_ref, rotated_ref, columns_ref = refs[-4:]
    mix_pieces(refs[:-4], kron_ref, rotated_ref)
    blocks = []
    for spots in groups:
        for k in range(left_ref.shape[0]):
            blocks += [left_ref[k, pl.ds(row_of(spot, rows, chips), spot[3]), :] for spot in spots]
    columns_ref[...] = jnp.concatenate(blocks, axis=0).astype(F32).T.astype(BF16)


def turn(right_ref, rotated_ref, turned_ref):
    terms, states, count, width = rotated_ref.shape
    for k in range(terms):
        for n in range(0, states, 8):
            source = rotated_ref[k, n : n + 8].reshape(8 * count, width)
            turned = jnp.dot(source, right_ref[k], preferred_element_type=F32).astype(BF16)
            turned_ref[n : n + 8, k * count : (k + 1) * count, :] = turned.reshape(8, count, width)


def here_kernel(rotated_ref, packed_ref, keep_ref, turned_ref, right_ref):
    unpack_symmetric(packed_ref, right_ref, keep_ref[0:1, :])
    turn(right_ref, rotated_ref, turned_ref)


def there_kernel(*refs):
    right_ref, kron_ref, turned_ref, rotated_ref = refs[-4:]
    mix_pieces(refs[:-4], kron_ref, rotated_ref)
    turn(right_ref, rotated_ref, turned_ref)


def last_kernel(count, *refs):
    right_ref, kron_ref, columns_ref = refs[count : count + 3]
    out_ref, rotated_ref, turned_ref = refs[-3:]
    there_kernel(*refs[:count], right_ref, kron_ref, turned_ref, rotated_ref)
    blocks = list(refs[count + 3 : -3]) + [turned_ref]

    def lefts(p, carry):
        stack = jnp.concatenate([block[p] for block in blocks], axis=0)
        out_ref[p] = jnp.dot(columns_ref[...], stack, preferred_element_type=F32)
        return carry

    lax.fori_loop(0, out_ref.shape[0], lefts, 0, unroll=out_ref.shape[0])


def rotate_kernel(spots, rows, chips, *refs):
    pieces = refs[: len(spots)]
    kron_ref = refs[len(spots)]
    rotated_ref, whole_ref, sems = refs[-3:]
    states = whole_ref.shape[0]
    copies = []
    bases = [row_of(spot, rows, chips) for spot in spots]
    for at, piece in zip(bases, pieces):
        for i in range(piece.shape[0] // states):
            target = whole_ref.at[:, pl.ds(pl.multiple_of(at + i * TILE, TILE), TILE), :]
            source = piece.at[i * states : (i + 1) * states]
            copies.append(pltpu.make_async_copy(source, target, sems.at[len(copies)]))
            copies[-1].start()
    for at, piece in zip(bases, pieces):
        mix_sites(piece, kron_ref, rotated_ref, at)
    for copy in copies:
        copy.wait()


def lefts_kernel(spots, rows, chips, *refs):
    count = len(spots)
    packed_ref, norm_before_ref = refs[count + 3 : count + 5]
    mixed_ref, norm_ref, rotated_ref, whole_ref, left_ref, sems = refs[-6:]
    terms, states, width, _ = rotated_ref.shape
    lines = packed_ref[terms * width : terms * width + TILE, :].astype(F32)
    norm = lines[terms : terms + 1] + lines[terms + 1 : terms + 2] + lines[terms + 2 : terms + 3]
    norm_ref[...] = norm_before_ref[...] + jnp.concatenate([norm, norm], axis=1)
    unpack_symmetric(packed_ref, left_ref)
    rotate_kernel(spots, rows, chips, *refs[: count + 1], rotated_ref, whole_ref, sems)

    def lefts(p, carry):
        for k in range(terms):
            mixed = jnp.dot(left_ref[k], rotated_ref[k, p], preferred_element_type=F32)
            mixed_ref[p, :, k * width : (k + 1) * width] = mixed.astype(BF16)
        return carry

    lax.fori_loop(0, states, lefts, 0, unroll=states)


def rights_kernel(start, stop, packed_ref, mixed_ref, before_ref, keep_ref, partial_ref, *refs):
    if start == 0:
        right_ref = refs[0]
        unpack_symmetric(packed_ref, right_ref, keep_ref[0:1, :])
    else:
        right_ref = packed_ref
    terms, width, _ = right_ref.shape

    def rights(n, carry):
        at = n * GROUP
        rows = mixed_ref[pl.ds(start + at, GROUP)].reshape(GROUP * width, terms * width)
        stacked = right_ref[...].reshape(terms * width, width)
        image = jnp.dot(rows, stacked, preferred_element_type=F32).reshape(GROUP, width, width)
        partial_ref[pl.ds(at, GROUP)] = (before_ref[pl.ds(start + at, GROUP)] + image).astype(partial_ref.dtype)
        return carry

    lax.fori_loop(0, (stop - start) // GROUP, rights, 0)


def shifted_residual(start, shift, keep, mine_ref, other_ref, whole_ref, left_ref, res_ref, mixed_ref):
    count, width, _ = res_ref.shape
    terms = left_ref.shape[0]
    zero = jnp.zeros((8, width), F32)

    def lefts(n, sums):
        square, product = sums
        for row in range(0, width, STRIP):
            strip = pl.ds(row, STRIP)
            held = whole_ref[start + n, strip, :].astype(F32) * keep
            sigma = mine_ref[n, strip, :].astype(F32) + other_ref[n, strip, :].astype(F32)
            residual = sigma - shift * held
            res_ref[n, strip, :] = residual.astype(BF16)
            square = square + fold(residual * residual, width)
            product = product + fold(sigma * held, width)
        mixed = jnp.dot(
            left_ref[...].reshape(terms * width, width), res_ref[n], preferred_element_type=F32
        ).astype(BF16)
        for k in range(terms):
            mixed_ref[k, n] = mixed[k * width : (k + 1) * width]
        return square, product

    square, product = lax.fori_loop(0, count, lefts, (zero, zero), unroll=count)
    return jnp.sum(square), jnp.sum(product)


def low_kernel(
    keep_ref,
    norm_ref,
    norm_other_ref,
    low_ref,
    low_other_ref,
    whole_ref,
    left_ref,
    res_ref,
    mixed_ref,
    out_ref,
):
    count, width, _ = low_ref.shape
    states = whole_ref.shape[0]
    keep = keep_ref[0:1, :]
    held = whole_ref[0].astype(F32) * keep
    sigma = low_ref[0].astype(F32) + low_other_ref[0].astype(F32)
    product = jnp.sum(fold(sigma * held, width))
    square = jnp.sum(fold(held * held, width))
    total = norm_ref[0:1, :] + norm_other_ref[0:1, :]
    floor = jnp.maximum(jnp.maximum(square, (0.25 / states) * total), 1e-30)
    shift = product / floor
    square, product = shifted_residual(
        0, shift, keep, low_ref, low_other_ref, whole_ref, left_ref, res_ref, mixed_ref
    )
    out_ref[0:1, :] = shift
    out_ref[1:2, :] = jnp.full((1, width), square, F32)
    out_ref[2:3, :] = jnp.full((1, width), product, F32)
    out_ref[3:8, :] = jnp.zeros((5, width), F32)


def high_kernel(
    scale,
    members,
    keep_ref,
    norm_ref,
    norm_other_ref,
    sums_ref,
    high_ref,
    high_other_ref,
    whole_ref,
    left_ref,
    right_ref,
    kron_ref,
    res_low_ref,
    mixed_low_ref,
    out_ref,
    res_ref,
    rotated_ref,
    mixed_ref,
):
    terms, states, width, _ = rotated_ref.shape
    half = states // 2
    shift = sums_ref[0:1, :]
    square, product = shifted_residual(
        half, shift, keep_ref[0:1, :], high_ref, high_other_ref, whole_ref, left_ref, res_ref, mixed_ref
    )

    def sites(i, carry):
        at = pl.ds(pl.multiple_of(i * TILE, TILE), TILE)
        stack = jnp.concatenate([res_low_ref[:, at, :], res_ref[:, at, :]], axis=0).reshape(states * TILE, width)
        turned = jnp.dot(kron_ref[...], stack, preferred_element_type=F32).astype(BF16)
        rotated_ref[:, :, at, :] = turned.reshape(terms, states, TILE, width)
        return carry

    lax.fori_loop(0, width // TILE, sites, 0, unroll=width // TILE)
    cross = jnp.zeros((8, width), F32)
    for start, left_mixed_ref in ((0, mixed_low_ref), (half, mixed_ref)):
        for k in range(terms):
            turned = rotated_ref[k, start : start + half].reshape(half * width, width)
            image = jnp.dot(turned, right_ref[k], preferred_element_type=F32)
            held = left_mixed_ref[k].reshape(half * width, width).astype(F32)
            cross = cross + fold(held * image, width)
    res_square = sums_ref[1:2, :] + square
    product = sums_ref[2:3, :] + product
    total = norm_ref[0:1, :] + norm_other_ref[0:1, :]
    factor = scale / (total * scale + epsilon)
    rayleigh = factor * product
    gap = rayleigh - shift
    res_vector = product - shift * total
    res_sq = factor * (res_square - 2.0 * gap * res_vector + gap * gap * total)
    change = gap * gap * product - 2.0 * gap * (res_square + shift * res_vector)
    share = 1.0 / members
    out_ref[0:1, :] = rayleigh * share
    out_ref[1:2, :] = jnp.maximum(res_sq, 0.0) * share
    out_ref[2:3, :] = factor * (jnp.sum(cross) + share * change)
    out_ref[3:8, :] = jnp.zeros((5, width), F32)


def own_rows_kernel(scale, members, keep_ref, norm_ref, norm_other_ref, share_ref, guess_ref, *refs):
    low_ref, low_other_ref, high_ref, high_other_ref, vector_ref, residual_ref = refs
    rows, states, width = guess_ref.shape
    inverse = lax.rsqrt((norm_ref[0:1, :] + norm_other_ref[0:1, :]) * scale + epsilon)
    row_scale = keep_ref[0:1, :] * inverse
    rayleigh = share_ref[0:1, :] * members
    own = pl.ds(pl.multiple_of(lax.axis_index("term") * rows, TILE), rows)
    vector = guess_ref[...] * row_scale[None]
    vector_ref[...] = vector
    sigma = jnp.concatenate(
        [
            mine_ref[:, own, :].astype(F32) + other_ref[:, own, :].astype(F32)
            for mine_ref, other_ref in ((low_ref, low_other_ref), (high_ref, high_other_ref))
        ],
        axis=0,
    )
    residual_ref[...] = jnp.swapaxes(sigma * row_scale[None], 0, 1) - rayleigh[None] * vector


def finish_kernel(vector_ref, residual_ref, *refs):
    shares = refs[:-2]
    ritz_ref, energy_ref = refs[-2:]
    stat = summed([share[...] for share in shares])
    rayleigh = stat[0:1, :]
    res_sq = stat[1:2, :]
    res_var = res_sq + epsilon
    curvature = stat[2:3, :] / res_var
    res_scale = jnp.sqrt(res_var)
    coupling = res_sq / res_scale
    half_gap = 0.5 * (rayleigh - curvature)
    energy = 0.5 * (rayleigh + curvature) - jnp.sqrt(half_gap * half_gap + coupling * coupling)
    coeff_new = energy - rayleigh
    coeff_norm = jnp.sqrt(coupling * coupling + coeff_new * coeff_new + epsilon)
    old = coupling / coeff_norm
    new = coeff_new / (coeff_norm * res_scale)
    ritz_ref[...] = old[None] * vector_ref[...] + new[None] * residual_ref[...]
    energy_ref[0] = energy[0, 0]


def shards(wave_guess, left_env, right_env, site_ops, bond_rank):
    guess = wave_guess[0]
    left = left_env[0]
    site = site_ops[0]
    rows, states, width = guess.shape
    terms = left.shape[0]
    members = lax.axis_size("term")
    chips = members // CORES
    segments = lax.axis_size("seg")
    scale = 1.0 / float(rows * members * states * width)
    hops = tuple(range(chips))

    def to_sibling(block):
        return lax.ppermute(block, "term", [(i, i ^ 1) for i in range(members)])

    def to_next_chip(block):
        return lax.ppermute(block, "term", [(i, (i + CORES) % members) for i in range(members)])

    def around(block):
        found = [block]
        for _ in range(chips - 1):
            found.append(to_next_chip(found[-1]))
        return found

    def everyone(block):
        return [block] + [
            lax.ppermute(block, "term", [(i, i ^ bits) for i in range(members)])
            for bits in range(CORES, members, CORES)
        ]

    tile = jax.ShapeDtypeStruct((8, width), F32)
    half = width // 2
    packed_shape = jax.ShapeDtypeStruct((terms * width + TILE, half), BF16)
    starts = (0, rows - 2 * TILE, rows - TILE) if rows >= 4 * TILE else (0,)
    lengths = [stop - start for start, stop in zip(starts, starts[1:] + (rows,))]
    in_place = [pltpu.with_memory_space_constraint(a, pltpu.HBM) for a in (guess, left, right_env[0], site)]
    first_chunk, squares, right_packed = pl.pallas_call(
        first_chunk_kernel,
        out_shape=(jax.ShapeDtypeStruct((lengths[0] // TILE * states + 1, TILE, width), BF16), tile, packed_shape),
        in_specs=[in_hbm] * 3,
        out_specs=(vmem,) * 3,
        scratch_shapes=[
            pltpu.VMEM((lengths[0], states, width), F32),
            pltpu.VMEM(site.shape, BF16),
            pltpu.VMEM(left.shape, BF16),
            pltpu.SemaphoreType.DMA((lengths[0] // TILE + 2,)),
        ],
        compiler_params=params(),
        cost_estimate=cost(2 * guess.size, 3 * guess.size),
        name="first_chunk",
    )(in_place[0], in_place[3], in_place[2])
    rest = rows - lengths[0]
    squares, first_sibling = lax.optimization_barrier((squares, to_sibling(first_chunk)))
    norm_part, keep, left_packed, left, *chunks = pl.pallas_call(
        functools.partial(prepare_kernel, starts),
        out_shape=(
            tile,
            tile,
            packed_shape,
            jax.ShapeDtypeStruct(left.shape, BF16),
            *[jax.ShapeDtypeStruct((length // TILE * states, TILE, width), BF16) for length in lengths[1:]],
        ),
        in_specs=[vmem] * 2 + [in_hbm] * 2,
        out_specs=(vmem,) * (3 + len(lengths)),
        scratch_shapes=[
            pltpu.VMEM((max(rest, TILE), states, width), F32),
            pltpu.SemaphoreType.DMA((rest // TILE + 1,)),
        ],
        compiler_params=params(),
        cost_estimate=cost(4 * guess.size, 6 * guess.size),
        name="prepare",
    )(bond_rank.reshape(1, 1), squares, *in_place[:2])
    chunks = [first_chunk] + chunks

    chunk_hops = [around(chunk) for chunk in chunks]
    here_pieces = chunks + [first_sibling] + [to_sibling(chunk) for chunk in chunks[1:]]
    here_spots = tuple((0, flip, start, length) for flip in range(CORES) for start, length in zip(starts, lengths))
    far_spots = [
        tuple((hop, flip, start, length) for hop in hops[1:] for flip in range(CORES))
        for start, length in zip(starts, lengths)
    ]
    mid_spots = sum(far_spots[:-1], ())
    groups = [group for group in (here_spots, mid_spots, far_spots[-1]) if group]
    lefts = around(left_packed)
    shift = [(i + 1, i) for i in range(segments - 1)]
    received = lax.ppermute(right_packed, "seg", shift)

    size = states * TILE

    def spread(block):
        return pl.pallas_call(
            spread_kernel,
            out_shape=jax.ShapeDtypeStruct((terms * size, size), BF16),
            in_specs=[vmem],
            out_specs=vmem,
            compiler_params=params(),
            cost_estimate=cost(2 * terms * size * size * width, 2 * terms * size * size),
            name="spread_site",
        )(block)

    kron_own = spread(chunks[0])

    whole = (states, width, width)
    whole_bf = jax.ShapeDtypeStruct(whole, BF16)
    whole_f32 = jax.ShapeDtypeStruct(whole, F32)
    rotated = (terms, states, width, width)
    rotated_bf = jax.ShapeDtypeStruct(rotated, BF16)
    square = pltpu.VMEM((terms, width, width), BF16)
    chip_rows = CORES * rows
    stage_flops = 2 * terms * states * width * width * width

    def buffers(spots):
        count = sum(spot[3] for spot in spots)
        return (terms, states, count, width), (states, terms * count, width)

    here_rotated, here_turned = buffers(here_spots)
    part_cost = cost(stage_flops, 8 * states * width * width)
    rotated_own, columns = pl.pallas_call(
        functools.partial(rotate_own_kernel, groups, rows, chips),
        out_shape=(
            jax.ShapeDtypeStruct(here_rotated, BF16),
            jax.ShapeDtypeStruct((width, terms * width), BF16),
        ),
        in_specs=[vmem] * (len(here_pieces) + 2),
        out_specs=(vmem, vmem),
        compiler_params=params(),
        cost_estimate=part_cost,
        name="rotate_own",
    )(*here_pieces, kron_own, left)

    def rotate(spots, pieces, kron, before):
        return pl.pallas_call(
            functools.partial(rotate_kernel, spots, rows, chips),
            out_shape=(rotated_bf, whole_bf),
            in_specs=[vmem] * (len(pieces) + 1) + [anywhere] * len(before),
            out_specs=(vmem, vmem),
            scratch_shapes=[pltpu.SemaphoreType.DMA((sum(spot[3] for spot in spots) // TILE,))],
            input_output_aliases={len(pieces) + 1 + n: n for n in range(len(before))},
            compiler_params=params(),
            cost_estimate=part_cost,
            name="rotate_crossed" if before else "rotate_here",
        )(*pieces, kron, *before)

    def relayed(blocks):
        return [piece for block in blocks for piece in (block, to_sibling(block))]

    firsts, rotated_own = lax.optimization_barrier((chunk_hops[0][1:], rotated_own))
    kron = spread(firsts[0])
    turned = rotate(here_spots, here_pieces, kron, ())
    received, turned = lax.optimization_barrier((received, turned))
    packed = jnp.where(lax.axis_index("seg") == segments - 1, right_packed, received)
    rights = around(packed)
    turned_own, right = pl.pallas_call(
        here_kernel,
        out_shape=(jax.ShapeDtypeStruct(here_turned, BF16), jax.ShapeDtypeStruct(left.shape, BF16)),
        in_specs=[vmem] * 3,
        out_specs=(vmem, vmem),
        compiler_params=params(),
        cost_estimate=part_cost,
        name="apply_rows_here",
    )(rotated_own, packed, keep)
    parts = [turned_own]
    mid_pieces = []
    if mid_spots:
        mid_pieces += relayed(firsts)
        for crossing in chunk_hops[1:-1]:
            crossed, turned = lax.optimization_barrier((crossing[1:], turned))
            mid_pieces += relayed(crossed)
        turned = rotate(mid_spots, mid_pieces, kron, turned)
        crossed, turned, parts[0] = lax.optimization_barrier((chunk_hops[-1][1:], turned, parts[0]))
        last_pieces = relayed(crossed)
        mid_rotated, mid_turned = buffers(mid_spots)
        parts.append(
            pl.pallas_call(
                there_kernel,
                out_shape=jax.ShapeDtypeStruct(mid_turned, BF16),
                in_specs=[vmem] * (len(mid_pieces) + 2),
                out_specs=vmem,
                scratch_shapes=[pltpu.VMEM(mid_rotated, BF16)],
                compiler_params=params(),
                cost_estimate=part_cost,
                name="apply_rows_crossed",
            )(*mid_pieces, right, kron_own)
        )
    else:
        last_pieces = relayed(firsts)
    last_rotated, last_turned = buffers(far_spots[-1])
    partial = pl.pallas_call(
        functools.partial(last_kernel, len(last_pieces)),
        out_shape=whole_f32,
        in_specs=[vmem] * (len(last_pieces) + 3 + len(parts)),
        out_specs=vmem,
        scratch_shapes=[pltpu.VMEM(last_rotated, BF16), pltpu.VMEM(last_turned, BF16)],
        compiler_params=params(),
        cost_estimate=part_cost,
        name="apply_rows_last",
    )(*last_pieces, right, kron_own, columns, *parts)
    norm = norm_part
    for hop in hops[1:]:
        if hop > 1:
            block, partial = lax.optimization_barrier((firsts[hop - 1], partial))
            kron = spread(block)
            turned = rotate(here_spots, here_pieces, kron, ())
            if mid_spots:
                turned = rotate(mid_spots, mid_pieces, kron, turned)
        left_far, partial = lax.optimization_barrier((lefts[hop], partial))
        mixed, norm, _, vector = pl.pallas_call(
            functools.partial(lefts_kernel, far_spots[-1], rows, chips),
            out_shape=(jax.ShapeDtypeStruct((states, width, terms * width), BF16), tile, rotated_bf, whole_bf),
            in_specs=[vmem] * (len(last_pieces) + 1) + [anywhere] * 2 + [vmem] * 2,
            out_specs=(vmem,) * 4,
            scratch_shapes=[
                square,
                pltpu.SemaphoreType.DMA((sum(spot[3] for spot in far_spots[-1]) // TILE,)),
            ],
            input_output_aliases={len(last_pieces) + 1: 2, len(last_pieces) + 2: 3},
            compiler_params=params(),
            cost_estimate=cost(stage_flops, 12 * states * width * width),
            name="received_lefts",
        )(*last_pieces, kron, *turned, left_far, norm)
        last = hop == hops[-1]
        right_far = rights[hop]
        parts = []
        bounds = (0, states // 2, states) if last else (0, states)
        for start, stop in zip(bounds[:-1], bounds[1:]):
            part_shape = jax.ShapeDtypeStruct((stop - start, width, width), BF16 if last else F32)
            part, *unpacked = pl.pallas_call(
                functools.partial(rights_kernel, start, stop),
                out_shape=(part_shape,) + ((jax.ShapeDtypeStruct(left.shape, BF16),) if start == 0 else ()),
                in_specs=[vmem] * 4,
                out_specs=(vmem,) * (2 if start == 0 else 1),
                compiler_params=params(),
                cost_estimate=cost(stage_flops / 2, 12 * states * width * width),
                name="received_rights",
            )(right_far, mixed, partial, keep)
            if unpacked:
                right_far, norm_other = lax.optimization_barrier((unpacked[0], to_sibling(norm)))
            parts.append(part)
        if not last:
            partial = parts[0]
    halves = []
    for part in parts:
        halves += [part, to_sibling(part)]
    half_bf = jax.ShapeDtypeStruct((states // 2, width, width), BF16)
    half_mixed = (terms, states // 2, width, width)
    res_low, mixed_low, sums = pl.pallas_call(
        low_kernel,
        out_shape=(half_bf, jax.ShapeDtypeStruct(half_mixed, BF16), tile),
        in_specs=[vmem] * 7,
        out_specs=(vmem,) * 3,
        compiler_params=params(),
        cost_estimate=cost(stage_flops / 2, 3 * states * width * width),
        name="residual_low",
    )(keep, norm, norm_other, *halves[:2], vector, left)
    share = pl.pallas_call(
        functools.partial(high_kernel, scale, members),
        out_shape=tile,
        in_specs=[vmem] * 12,
        out_specs=vmem,
        scratch_shapes=[
            pltpu.VMEM(half_bf.shape, BF16),
            pltpu.VMEM(rotated, BF16),
            pltpu.VMEM(half_mixed, BF16),
        ],
        compiler_params=params(),
        cost_estimate=cost(3 * stage_flops, 6 * states * width * width),
        name="residual_high",
    )(keep, norm, norm_other, sums, *halves[2:], vector, left, right, kron_own, res_low, mixed_low)
    crossed = everyone(share)

    local = jax.ShapeDtypeStruct((rows, states, width), F32)
    vector_own, residual_own = pl.pallas_call(
        functools.partial(own_rows_kernel, scale, members),
        out_shape=(local, local),
        in_specs=[vmem] * 9,
        out_specs=(vmem, vmem),
        compiler_params=params(),
        cost_estimate=cost(8 * guess.size, 16 * guess.size),
        name="own_rows",
    )(keep, norm, norm_other, share, guess, *halves)

    shares = [share, to_sibling(share)]
    gated, residual_own = lax.optimization_barrier((crossed[1:], residual_own))
    shares += relayed(gated)
    ritz, energy = pl.pallas_call(
        finish_kernel,
        out_shape=(local, jax.ShapeDtypeStruct((1,), F32)),
        in_specs=[vmem] * (2 + members),
        out_specs=(vmem, smem),
        compiler_params=params(),
        cost_estimate=cost(3 * guess.size, 12 * guess.size),
        name="finish",
    )(vector_own, residual_own, *shares)
    return (ritz[None], energy)


def solution(mesh):
    in_specs = (
        P("seg", "term", None, None),
        P("seg", "term", None, None),
        P("seg", "term", None, None),
        P("seg", "term", None, None),
        P("seg"),
    )
    out_specs = (P("seg", "term", None, None), P("seg"))
    return jax.shard_map(shards, mesh=mesh, in_specs=in_specs, out_specs=out_specs, check_vma=False)
```

```python
import functools

import jax
import jax.numpy as jnp
from jax import lax
from jax.experimental import pallas as pl
from jax.experimental.pallas import tpu as pltpu
from jax.sharding import PartitionSpec as P

epsilon = 1e-06
CORES = 2
TILE = 16
STRIP = 32
GROUP = 8
VMEM_LIMIT = 20 * 1024 * 1024
F32 = jnp.float32
BF16 = jnp.bfloat16

vmem = pl.BlockSpec(memory_space=pltpu.VMEM)
smem = pl.BlockSpec(memory_space=pltpu.SMEM)
anywhere = pl.BlockSpec(memory_space=pl.ANY)
in_hbm = pl.BlockSpec(memory_space=pltpu.HBM)


def params():
    return pltpu.CompilerParams(vmem_limit_bytes=VMEM_LIMIT)


def cost(flops, moved):
    return pl.CostEstimate(flops=int(flops) // 100, bytes_accessed=int(moved) // 100, transcendentals=0)


def fold(values, width):
    return jnp.sum(values.reshape(values.size // (8 * width), 8, width), axis=0)


def chunk_rows_in(guess_in, guess_ref, sems, start, stop, slot):
    copies = []
    for n in range(start, stop, TILE):
        target = guess_ref.at[pl.ds(n - start, TILE)]
        copies.append(pltpu.make_async_copy(guess_in.at[pl.ds(n, TILE)], target, sems.at[slot + len(copies)]))
        copies[-1].start()
    return copies


def first_chunk_kernel(
    guess_in,
    site_in,
    right_in,
    x_ref,
    squares_ref,
    packed_ref,
    guess_ref,
    site_ref,
    right_ref,
    sems,
):
    rows, states, width = guess_ref.shape
    terms = site_ref.shape[0]
    blocks = rows // TILE
    copies = [
        pltpu.make_async_copy(source, target, sems.at[n])
        for n, (source, target) in enumerate(((site_in, site_ref), (right_in, right_ref)))
    ]
    parts = chunk_rows_in(guess_in, guess_ref, sems, 0, rows, 2)
    copies[0].start()
    copies[1].start()
    squares = jnp.zeros((8, width), F32)
    for n, copy in enumerate(parts):
        copy.wait()
        whole = guess_ref[pl.ds(n * TILE, TILE)]
        squares = squares + fold(whole * whole, width)
        x_ref[n * states : (n + 1) * states] = jnp.swapaxes(whole, 0, 1).astype(BF16)
    squares_ref[...] = squares
    copies[0].wait()
    line = lax.broadcasted_iota(jnp.int32, (TILE, width), 0)
    lane = lax.broadcasted_iota(jnp.int32, (TILE, width), 1)
    extra = jnp.zeros((TILE, width), F32)
    for k in range(terms):
        place_at = (lane == line + k * TILE).astype(BF16)
        extra = extra + jnp.dot(site_ref[k], place_at, preferred_element_type=F32)
    x_ref[blocks * states] = extra.astype(BF16)
    copies[1].wait()
    pack_blocks(right_ref, None, packed_ref)


def prepare_kernel(
    starts, rank_ref, squares_ref, guess_in, left_in, norm_ref, keep_ref, packed_ref, left_ref, *refs
):
    x_refs = (None,) + refs[: len(starts) - 1]
    guess_ref, sems = refs[len(starts) - 1 :]
    rows, states, width = guess_in.shape
    half = width // 2
    done = starts[1] if len(starts) > 1 else rows
    copies = chunk_rows_in(guess_in, guess_ref, sems, done, rows, 1)
    left_copy = pltpu.make_async_copy(left_in, left_ref, sems.at[0])
    left_copy.start()
    column = lax.broadcasted_iota(jnp.int32, (1, width), 1)
    keep = (column < rank_ref[...]).astype(F32)
    keep_ref[...] = jnp.broadcast_to(keep, keep_ref.shape)
    squares = squares_ref[...] * keep
    keep = keep[None]
    for n, copy in enumerate(copies):
        copy.wait()
        masked = guess_ref[pl.ds(n * TILE, TILE)] * keep
        squares = squares + fold(masked * masked, width)
        chunk = max(c for c, start in enumerate(starts) if start <= done + n * TILE)
        at = done + n * TILE - starts[chunk]
        block = at // TILE
        x_refs[chunk][block * states : (block + 1) * states] = jnp.swapaxes(masked, 0, 1).astype(BF16)
    total = jnp.sum(squares)
    norm_ref[...] = jnp.full(norm_ref.shape, total, F32)
    line = lax.broadcasted_iota(jnp.int32, (TILE, half), 0)
    norm = jnp.full((TILE, half), total, F32)
    extra = jnp.zeros((TILE, half), F32)
    for n in range(3):
        part = norm.astype(BF16).astype(F32)
        norm = norm - part
        extra = jnp.where(line == left_ref.shape[0] + n, part, extra)
    left_copy.wait()
    pack_blocks(left_ref, extra, packed_ref)


def pack_blocks(block_ref, extra, packed_ref):
    terms, width, _ = block_ref.shape
    half = width // 2
    line = lax.broadcasted_iota(jnp.int32, (TILE, half), 0)
    row, col = triangle(half)
    lines = jnp.zeros((TILE, half), F32) if extra is None else extra
    for k in range(terms):
        upper = block_ref[k, 0:half, 0:half].astype(F32)
        lower = block_ref[k, half:width, half:width].astype(F32)
        diagonal = jnp.sum(jnp.where(row == col, lower, 0.0), axis=0, keepdims=True)
        lines = jnp.where(line == k, diagonal, lines)
        base = k * width
        packed_ref[base : base + half, :] = block_ref[k, 0:half, half:width]
        packed_ref[base + half : base + width, :] = jnp.where(row <= col, upper, lower).astype(BF16)
    packed_ref[terms * width : terms * width + TILE, :] = lines.astype(BF16)


def triangle(half):
    row = lax.broadcasted_iota(jnp.int32, (half, half), 0)
    col = lax.broadcasted_iota(jnp.int32, (half, half), 1)
    return row, col


def unpack_symmetric(packed_ref, full_ref, keep=None):
    terms, width, _ = full_ref.shape
    half = width // 2
    row, col = triangle(half)

    rank = width if keep is None else jnp.sum(keep)
    row_index = row.astype(F32)

    def kept(block, top, start):
        if keep is None:
            return block
        return jnp.where(row_index < rank - top, block * keep[:, start : start + half], 0.0)

    diagonals = packed_ref[terms * width : terms * width + TILE, :].astype(F32)
    for k in range(terms):
        base = k * width
        corner = packed_ref[base : base + half, :].astype(F32)
        mixed = packed_ref[base + half : base + width, :].astype(F32)
        diagonal = diagonals[k : k + 1]
        turned = mixed.T
        lower = jnp.where(row > col, mixed, jnp.where(row == col, diagonal, turned))
        full_ref[k, 0:half, 0:half] = kept(jnp.where(row <= col, mixed, turned), 0, 0).astype(BF16)
        full_ref[k, 0:half, half:width] = kept(corner, 0, half).astype(BF16)
        full_ref[k, half:width, 0:half] = kept(corner.T, half, 0).astype(BF16)
        full_ref[k, half:width, half:width] = kept(lower, half, half).astype(BF16)


def spread_kernel(chunk_ref, kron_ref):
    width = chunk_ref.shape[2]
    size = kron_ref.shape[1]
    terms = kron_ref.shape[0] // size
    states = size // TILE
    tile = chunk_ref[chunk_ref.shape[0] - 1]
    row_state = lax.broadcasted_iota(jnp.int32, (size, states), 0) // TILE
    pick = (row_state == lax.broadcasted_iota(jnp.int32, (size, states), 1)).astype(BF16)
    tall = jnp.dot(pick, tile, preferred_element_type=F32).astype(BF16)
    lane = lax.broadcasted_iota(jnp.int32, (width, size), 0)
    col_state = lax.broadcasted_iota(jnp.int32, (width, size), 1) // TILE
    same = (
        lax.broadcasted_iota(jnp.int32, (size, size), 0) % TILE
        == lax.broadcasted_iota(jnp.int32, (size, size), 1) % TILE
    )
    for k in range(terms):
        pick_t = (lane == col_state + k * TILE).astype(BF16)
        full = jnp.dot(tall, pick_t, preferred_element_type=F32)
        kron_ref[k * size : (k + 1) * size, :] = jnp.where(same, full, 0.0).astype(BF16)


def mix_sites(source_ref, kron_ref, rotated_ref, base):
    terms, states, _, width = rotated_ref.shape
    for i in range(source_ref.shape[0] // states):
        to = pl.ds(pl.multiple_of(base + i * TILE, TILE), TILE)
        stack = source_ref[i * states : (i + 1) * states].reshape(states * TILE, width)
        turned = jnp.dot(kron_ref[...], stack, preferred_element_type=F32).astype(BF16)
        rotated_ref[:, :, to, :] = turned.reshape(terms, states, TILE, width)


def summed(values):
    while len(values) > 1:
        values = [values[n] + values[n + 1] for n in range(0, len(values), 2)]
    return values[0]


def place(hop, chips):
    me = lax.axis_index("term")
    chip = (me // CORES - hop + chips) % chips
    return chip, me % CORES


def row_of(spot, rows, chips):
    chip, core = place(spot[0], chips)
    return pl.multiple_of((chip * CORES + (core if spot[1] == 0 else 1 - core)) * rows + spot[2], TILE)


def mix_pieces(pieces, kron_ref, rotated_ref):
    at = 0
    for piece in pieces:
        mix_sites(piece, kron_ref, rotated_ref, at)
        at += piece.shape[0] // rotated_ref.shape[1] * TILE


def rotate_own_kernel(groups, rows, chips, *refs):
    kron_ref, left_ref, rotated_ref, columns_ref = refs[-4:]
    mix_pieces(refs[:-4], kron_ref, rotated_ref)
    blocks = []
    for spots in groups:
        for k in range(left_ref.shape[0]):
            blocks += [left_ref[k, pl.ds(row_of(spot, rows, chips), spot[3]), :] for spot in spots]
    columns_ref[...] = jnp.concatenate(blocks, axis=0).astype(F32).T.astype(BF16)


def turn(right_ref, rotated_ref, turned_ref):
    terms, states, count, width = rotated_ref.shape
    for k in range(terms):
        for n in range(0, states, 8):
            source = rotated_ref[k, n : n + 8].reshape(8 * count, width)
            turned = jnp.dot(source, right_ref[k], preferred_element_type=F32).astype(BF16)
            turned_ref[n : n + 8, k * count : (k + 1) * count, :] = turned.reshape(8, count, width)


def here_kernel(rotated_ref, packed_ref, keep_ref, turned_ref, right_ref):
    unpack_symmetric(packed_ref, right_ref, keep_ref[0:1, :])
    turn(right_ref, rotated_ref, turned_ref)


def there_kernel(*refs):
    right_ref, kron_ref, turned_ref, rotated_ref = refs[-4:]
    mix_pieces(refs[:-4], kron_ref, rotated_ref)
    turn(right_ref, rotated_ref, turned_ref)


def assemble(spots, rows, chips, pieces, whole_ref, sems):
    states = whole_ref.shape[0]
    copies = []
    for spot, piece in zip(spots, pieces):
        at = row_of(spot, rows, chips)
        for i in range(piece.shape[0] // states):
            target = whole_ref.at[:, pl.ds(pl.multiple_of(at + i * TILE, TILE), TILE), :]
            source = piece.at[i * states : (i + 1) * states]
            copies.append(pltpu.make_async_copy(source, target, sems.at[len(copies)]))
            copies[-1].start()
    return copies


def last_kernel(count, spots, rows, chips, *refs):
    far = refs[: len(spots)]
    right_ref, kron_ref, columns_ref = refs[len(spots) : len(spots) + 3]
    out_ref, whole_ref, rotated_ref, turned_ref, sems = refs[-5:]
    copies = assemble(spots, rows, chips, far, whole_ref, sems)
    there_kernel(*far[:count], right_ref, kron_ref, turned_ref, rotated_ref)
    blocks = list(refs[len(spots) + 3 : -5]) + [turned_ref]

    def lefts(p, carry):
        stack = jnp.concatenate([block[p] for block in blocks], axis=0)
        out_ref[p] = jnp.dot(columns_ref[...], stack, preferred_element_type=F32)
        return carry

    lax.fori_loop(0, out_ref.shape[0], lefts, 0, unroll=out_ref.shape[0])
    for copy in copies:
        copy.wait()


def rotate_kernel(spots, rows, chips, *refs):
    pieces = refs[: len(spots)]
    kron_ref, rotated_ref = refs[len(spots)], refs[-1]
    for spot, piece in zip(spots, pieces):
        mix_sites(piece, kron_ref, rotated_ref, row_of(spot, rows, chips))


def lefts_kernel(spots, here_spots, rows, chips, *refs):
    count = len(spots)
    packed_ref, norm_before_ref = refs[count + 3 : count + 5]
    here = refs[count + 5 : count + 5 + len(here_spots)]
    mixed_ref, norm_ref, rotated_ref, whole_ref, left_ref, sems = refs[-6:]
    terms, states, width, _ = rotated_ref.shape
    copies = assemble(here_spots, rows, chips, here, whole_ref, sems)
    lines = packed_ref[terms * width : terms * width + TILE, :].astype(F32)
    norm = lines[terms : terms + 1] + lines[terms + 1 : terms + 2] + lines[terms + 2 : terms + 3]
    norm_ref[...] = norm_before_ref[...] + jnp.concatenate([norm, norm], axis=1)
    unpack_symmetric(packed_ref, left_ref)
    rotate_kernel(spots, rows, chips, *refs[: count + 1], rotated_ref)

    def lefts(p, carry):
        for k in range(terms):
            mixed = jnp.dot(left_ref[k], rotated_ref[k, p], preferred_element_type=F32)
            mixed_ref[p, :, k * width : (k + 1) * width] = mixed.astype(BF16)
        return carry

    lax.fori_loop(0, states, lefts, 0, unroll=states)
    for copy in copies:
        copy.wait()


def rights_kernel(start, stop, packed_ref, mixed_ref, before_ref, keep_ref, partial_ref, *refs):
    if start == 0:
        right_ref = refs[0]
        unpack_symmetric(packed_ref, right_ref, keep_ref[0:1, :])
    else:
        right_ref = packed_ref
    terms, width, _ = right_ref.shape

    def rights(n, carry):
        at = n * GROUP
        rows = mixed_ref[pl.ds(start + at, GROUP)].reshape(GROUP * width, terms * width)
        stacked = right_ref[...].reshape(terms * width, width)
        image = jnp.dot(rows, stacked, preferred_element_type=F32).reshape(GROUP, width, width)
        partial_ref[pl.ds(at, GROUP)] = (before_ref[pl.ds(start + at, GROUP)] + image).astype(partial_ref.dtype)
        return carry

    lax.fori_loop(0, (stop - start) // GROUP, rights, 0)


def shifted_residual(start, shift, keep, mine_ref, other_ref, whole_ref, left_ref, res_ref, mixed_ref):
    count, width, _ = res_ref.shape
    terms = left_ref.shape[0]
    zero = jnp.zeros((8, width), F32)
    shift_keep = shift * keep

    def lefts(n, sums):
        square, product = sums
        for row in range(0, width, STRIP):
            strip = pl.ds(row, STRIP)
            held = whole_ref[start + n, strip, :].astype(F32)
            sigma = mine_ref[n, strip, :].astype(F32) + other_ref[n, strip, :].astype(F32)
            residual = sigma - shift_keep * held
            res_ref[n, strip, :] = residual.astype(BF16)
            square = square + fold(residual * residual, width)
            product = product + fold(sigma * held, width)
        mixed = jnp.dot(
            left_ref[...].reshape(terms * width, width), res_ref[n], preferred_element_type=F32
        ).astype(BF16)
        for k in range(terms):
            mixed_ref[k, n] = mixed[k * width : (k + 1) * width]
        return square, product

    square, product = lax.fori_loop(0, count, lefts, (zero, zero), unroll=count)
    return jnp.sum(square), jnp.sum(product)


def low_kernel(
    keep_ref,
    norm_ref,
    norm_other_ref,
    low_ref,
    low_other_ref,
    whole_ref,
    left_ref,
    res_ref,
    mixed_ref,
    out_ref,
):
    count, width, _ = low_ref.shape
    states = whole_ref.shape[0]
    keep = keep_ref[0:1, :]
    held = whole_ref[0].astype(F32) * keep
    sigma = low_ref[0].astype(F32) + low_other_ref[0].astype(F32)
    product = jnp.sum(fold(sigma * held, width))
    square = jnp.sum(fold(held * held, width))
    total = norm_ref[0:1, :] + norm_other_ref[0:1, :]
    floor = jnp.maximum(jnp.maximum(square, (0.25 / states) * total), 1e-30)
    shift = product / floor
    square, product = shifted_residual(
        0, shift, keep, low_ref, low_other_ref, whole_ref, left_ref, res_ref, mixed_ref
    )
    out_ref[0:1, :] = shift
    out_ref[1:2, :] = jnp.full((1, width), square, F32)
    out_ref[2:3, :] = jnp.full((1, width), product, F32)
    out_ref[3:8, :] = jnp.zeros((5, width), F32)


def high_kernel(
    scale,
    members,
    keep_ref,
    norm_ref,
    norm_other_ref,
    sums_ref,
    high_ref,
    high_other_ref,
    whole_ref,
    left_ref,
    right_ref,
    kron_ref,
    res_low_ref,
    mixed_low_ref,
    out_ref,
    res_ref,
    rotated_ref,
    mixed_ref,
):
    terms, states, width, _ = rotated_ref.shape
    half = states // 2
    shift = sums_ref[0:1, :]
    square, product = shifted_residual(
        half, shift, keep_ref[0:1, :], high_ref, high_other_ref, whole_ref, left_ref, res_ref, mixed_ref
    )

    def sites(i, carry):
        at = pl.ds(pl.multiple_of(i * TILE, TILE), TILE)
        stack = jnp.concatenate([res_low_ref[:, at, :], res_ref[:, at, :]], axis=0).reshape(states * TILE, width)
        turned = jnp.dot(kron_ref[...], stack, preferred_element_type=F32).astype(BF16)
        rotated_ref[:, :, at, :] = turned.reshape(terms, states, TILE, width)
        return carry

    lax.fori_loop(0, width // TILE, sites, 0, unroll=width // TILE)
    cross = jnp.zeros((8, width), F32)
    for start, left_mixed_ref in ((0, mixed_low_ref), (half, mixed_ref)):
        for k in range(terms):
            turned = rotated_ref[k, start : start + half].reshape(half * width, width)
            image = jnp.dot(turned, right_ref[k], preferred_element_type=F32)
            held = left_mixed_ref[k].reshape(half * width, width).astype(F32)
            cross = cross + fold(held * image, width)
    res_square = sums_ref[1:2, :] + square
    product = sums_ref[2:3, :] + product
    total = norm_ref[0:1, :] + norm_other_ref[0:1, :]
    factor = scale / (total * scale + epsilon)
    rayleigh = factor * product
    gap = rayleigh - shift
    res_vector = product - shift * total
    res_sq = factor * (res_square - 2.0 * gap * res_vector + gap * gap * total)
    change = gap * gap * product - 2.0 * gap * (res_square + shift * res_vector)
    share = 1.0 / members
    out_ref[0:1, :] = rayleigh * share
    out_ref[1:2, :] = jnp.maximum(res_sq, 0.0) * share
    out_ref[2:3, :] = factor * (jnp.sum(cross) + share * change)
    out_ref[3:8, :] = jnp.zeros((5, width), F32)


def own_rows_kernel(scale, members, keep_ref, norm_ref, norm_other_ref, share_ref, guess_ref, *refs):
    low_ref, low_other_ref, high_ref, high_other_ref, vector_ref, residual_ref = refs
    rows, states, width = guess_ref.shape
    inverse = lax.rsqrt((norm_ref[0:1, :] + norm_other_ref[0:1, :]) * scale + epsilon)
    row_scale = keep_ref[0:1, :] * inverse
    rayleigh = share_ref[0:1, :] * members
    own = pl.ds(pl.multiple_of(lax.axis_index("term") * rows, TILE), rows)
    vector = guess_ref[...] * row_scale[None]
    vector_ref[...] = vector
    sigma = jnp.concatenate(
        [
            mine_ref[:, own, :].astype(F32) + other_ref[:, own, :].astype(F32)
            for mine_ref, other_ref in ((low_ref, low_other_ref), (high_ref, high_other_ref))
        ],
        axis=0,
    )
    residual_ref[...] = jnp.swapaxes(sigma * row_scale[None], 0, 1) - rayleigh[None] * vector


def finish_kernel(vector_ref, residual_ref, *refs):
    shares = refs[:-2]
    ritz_ref, energy_ref = refs[-2:]
    stat = summed([share[...] for share in shares])
    rayleigh = stat[0:1, :]
    res_sq = stat[1:2, :]
    res_var = res_sq + epsilon
    curvature = stat[2:3, :] / res_var
    res_scale = jnp.sqrt(res_var)
    coupling = res_sq / res_scale
    half_gap = 0.5 * (rayleigh - curvature)
    energy = 0.5 * (rayleigh + curvature) - jnp.sqrt(half_gap * half_gap + coupling * coupling)
    coeff_new = energy - rayleigh
    coeff_norm = jnp.sqrt(coupling * coupling + coeff_new * coeff_new + epsilon)
    old = coupling / coeff_norm
    new = coeff_new / (coeff_norm * res_scale)
    ritz_ref[...] = old[None] * vector_ref[...] + new[None] * residual_ref[...]
    energy_ref[0] = energy[0, 0]


def shards(wave_guess, left_env, right_env, site_ops, bond_rank):
    guess = wave_guess[0]
    left = left_env[0]
    site = site_ops[0]
    rows, states, width = guess.shape
    terms = left.shape[0]
    members = lax.axis_size("term")
    chips = members // CORES
    segments = lax.axis_size("seg")
    scale = 1.0 / float(rows * members * states * width)
    hops = tuple(range(chips))

    def to_sibling(block):
        return lax.ppermute(block, "term", [(i, i ^ 1) for i in range(members)])

    def to_next_chip(block):
        return lax.ppermute(block, "term", [(i, (i + CORES) % members) for i in range(members)])

    def around(block):
        found = [block]
        for _ in range(chips - 1):
            found.append(to_next_chip(found[-1]))
        return found

    def everyone(block):
        return [block] + [
            lax.ppermute(block, "term", [(i, i ^ bits) for i in range(members)])
            for bits in range(CORES, members, CORES)
        ]

    tile = jax.ShapeDtypeStruct((8, width), F32)
    half = width // 2
    packed_shape = jax.ShapeDtypeStruct((terms * width + TILE, half), BF16)
    starts = (0, rows - 2 * TILE, rows - TILE) if rows >= 4 * TILE else (0,)
    lengths = [stop - start for start, stop in zip(starts, starts[1:] + (rows,))]
    in_place = [pltpu.with_memory_space_constraint(a, pltpu.HBM) for a in (guess, left, right_env[0], site)]
    first_chunk, squares, right_packed = pl.pallas_call(
        first_chunk_kernel,
        out_shape=(jax.ShapeDtypeStruct((lengths[0] // TILE * states + 1, TILE, width), BF16), tile, packed_shape),
        in_specs=[in_hbm] * 3,
        out_specs=(vmem,) * 3,
        scratch_shapes=[
            pltpu.VMEM((lengths[0], states, width), F32),
            pltpu.VMEM(site.shape, BF16),
            pltpu.VMEM(left.shape, BF16),
            pltpu.SemaphoreType.DMA((lengths[0] // TILE + 2,)),
        ],
        compiler_params=params(),
        cost_estimate=cost(2 * guess.size, 3 * guess.size),
        name="first_chunk",
    )(in_place[0], in_place[3], in_place[2])
    rest = rows - lengths[0]
    squares, first_sibling = lax.optimization_barrier((squares, to_sibling(first_chunk)))
    norm_part, keep, left_packed, left, *chunks = pl.pallas_call(
        functools.partial(prepare_kernel, starts),
        out_shape=(
            tile,
            tile,
            packed_shape,
            jax.ShapeDtypeStruct(left.shape, BF16),
            *[jax.ShapeDtypeStruct((length // TILE * states, TILE, width), BF16) for length in lengths[1:]],
        ),
        in_specs=[vmem] * 2 + [in_hbm] * 2,
        out_specs=(vmem,) * (3 + len(lengths)),
        scratch_shapes=[
            pltpu.VMEM((max(rest, TILE), states, width), F32),
            pltpu.SemaphoreType.DMA((rest // TILE + 1,)),
        ],
        compiler_params=params(),
        cost_estimate=cost(4 * guess.size, 6 * guess.size),
        name="prepare",
    )(bond_rank.reshape(1, 1), squares, *in_place[:2])
    chunks = [first_chunk] + chunks

    chunk_hops = [around(chunk) for chunk in chunks]
    here_pieces = chunks + [first_sibling] + [to_sibling(chunk) for chunk in chunks[1:]]
    here_spots = tuple((0, flip, start, length) for flip in range(CORES) for start, length in zip(starts, lengths))
    far_spots = [
        tuple((hop, flip, start, length) for hop in hops[1:] for flip in range(CORES))
        for start, length in zip(starts, lengths)
    ]
    mid_spots = sum(far_spots[:-1], ())
    groups = [group for group in (here_spots, mid_spots, far_spots[-1]) if group]
    lefts = around(left_packed)
    shift = [(i + 1, i) for i in range(segments - 1)]
    received = lax.ppermute(right_packed, "seg", shift)

    size = states * TILE

    def spread(block):
        return pl.pallas_call(
            spread_kernel,
            out_shape=jax.ShapeDtypeStruct((terms * size, size), BF16),
            in_specs=[vmem],
            out_specs=vmem,
            compiler_params=params(),
            cost_estimate=cost(2 * terms * size * size * width, 2 * terms * size * size),
            name="spread_site",
        )(block)

    kron_own = spread(chunks[0])

    whole = (states, width, width)
    whole_bf = jax.ShapeDtypeStruct(whole, BF16)
    whole_f32 = jax.ShapeDtypeStruct(whole, F32)
    rotated = (terms, states, width, width)
    rotated_bf = jax.ShapeDtypeStruct(rotated, BF16)
    square = pltpu.VMEM((terms, width, width), BF16)
    chip_rows = CORES * rows
    stage_flops = 2 * terms * states * width * width * width

    def buffers(spots):
        count = sum(spot[3] for spot in spots)
        return (terms, states, count, width), (states, terms * count, width)

    here_rotated, here_turned = buffers(here_spots)
    part_cost = cost(stage_flops, 8 * states * width * width)
    rotated_own, columns = pl.pallas_call(
        functools.partial(rotate_own_kernel, groups, rows, chips),
        out_shape=(
            jax.ShapeDtypeStruct(here_rotated, BF16),
            jax.ShapeDtypeStruct((width, terms * width), BF16),
        ),
        in_specs=[vmem] * (len(here_pieces) + 2),
        out_specs=(vmem, vmem),
        compiler_params=params(),
        cost_estimate=part_cost,
        name="rotate_own",
    )(*here_pieces, kron_own, left)

    def rotate(spots, pieces, kron, before):
        return pl.pallas_call(
            functools.partial(rotate_kernel, spots, rows, chips),
            out_shape=rotated_bf,
            in_specs=[vmem] * (len(pieces) + 1) + [anywhere] * len(before),
            out_specs=vmem,
            input_output_aliases={len(pieces) + 1 + n: n for n in range(len(before))},
            compiler_params=params(),
            cost_estimate=part_cost,
            name="rotate_crossed" if before else "rotate_here",
        )(*pieces, kron, *before)

    def tiles(spots):
        return pltpu.SemaphoreType.DMA((sum(spot[3] for spot in spots) // TILE,))

    def relayed(blocks):
        return [piece for block in blocks for piece in (block, to_sibling(block))]

    firsts, rotated_own = lax.optimization_barrier((chunk_hops[0][1:], rotated_own))
    kron = spread(firsts[0])
    turned = rotate(here_spots, here_pieces, kron, ())
    received, turned = lax.optimization_barrier((received, turned))
    packed = jnp.where(lax.axis_index("seg") == segments - 1, right_packed, received)
    rights = around(packed)
    turned_own, right = pl.pallas_call(
        here_kernel,
        out_shape=(jax.ShapeDtypeStruct(here_turned, BF16), jax.ShapeDtypeStruct(left.shape, BF16)),
        in_specs=[vmem] * 3,
        out_specs=(vmem, vmem),
        compiler_params=params(),
        cost_estimate=part_cost,
        name="apply_rows_here",
    )(rotated_own, packed, keep)
    parts = [turned_own]
    mid_pieces = []
    if mid_spots:
        mid_pieces += relayed(firsts)
        for crossing in chunk_hops[1:-1]:
            crossed, turned = lax.optimization_barrier((crossing[1:], turned))
            mid_pieces += relayed(crossed)
        turned = rotate(mid_spots, mid_pieces, kron, (turned,))
        crossed, turned, parts[0] = lax.optimization_barrier((chunk_hops[-1][1:], turned, parts[0]))
        last_pieces = relayed(crossed)
        mid_rotated, mid_turned = buffers(mid_spots)
        parts.append(
            pl.pallas_call(
                there_kernel,
                out_shape=jax.ShapeDtypeStruct(mid_turned, BF16),
                in_specs=[vmem] * (len(mid_pieces) + 2),
                out_specs=vmem,
                scratch_shapes=[pltpu.VMEM(mid_rotated, BF16)],
                compiler_params=params(),
                cost_estimate=part_cost,
                name="apply_rows_crossed",
            )(*mid_pieces, right, kron_own)
        )
    else:
        last_pieces = relayed(firsts)
    last_rotated, last_turned = buffers(far_spots[-1])
    all_spots = far_spots[-1] + mid_spots
    partial, vector = pl.pallas_call(
        functools.partial(last_kernel, len(last_pieces), all_spots, rows, chips),
        out_shape=(whole_f32, whole_bf),
        in_specs=[vmem] * (len(all_spots) + 3 + len(parts)),
        out_specs=(vmem, vmem),
        scratch_shapes=[pltpu.VMEM(last_rotated, BF16), pltpu.VMEM(last_turned, BF16), tiles(all_spots)],
        compiler_params=params(),
        cost_estimate=part_cost,
        name="apply_rows_last",
    )(*last_pieces, *mid_pieces, right, kron_own, columns, *parts)
    norm = norm_part
    for hop in hops[1:]:
        if hop > 1:
            block, partial = lax.optimization_barrier((firsts[hop - 1], partial))
            kron = spread(block)
            turned = rotate(here_spots, here_pieces, kron, ())
            if mid_spots:
                turned = rotate(mid_spots, mid_pieces, kron, (turned,))
        left_far, partial = lax.optimization_barrier((lefts[hop], partial))
        mixed, norm, _, vector = pl.pallas_call(
            functools.partial(lefts_kernel, far_spots[-1], here_spots, rows, chips),
            out_shape=(jax.ShapeDtypeStruct((states, width, terms * width), BF16), tile, rotated_bf, whole_bf),
            in_specs=[vmem] * (len(last_pieces) + 1) + [anywhere] * 2 + [vmem] * (2 + len(here_pieces)),
            out_specs=(vmem,) * 4,
            scratch_shapes=[square, tiles(here_spots)],
            input_output_aliases={len(last_pieces) + 1: 2, len(last_pieces) + 2: 3},
            compiler_params=params(),
            cost_estimate=cost(stage_flops, 12 * states * width * width),
            name="received_lefts",
        )(*last_pieces, kron, turned, vector, left_far, norm, *here_pieces)
        last = hop == hops[-1]
        right_far = rights[hop]
        parts = []
        bounds = (0, states // 2, states) if last else (0, states)
        for start, stop in zip(bounds[:-1], bounds[1:]):
            part_shape = jax.ShapeDtypeStruct((stop - start, width, width), BF16 if last else F32)
            part, *unpacked = pl.pallas_call(
                functools.partial(rights_kernel, start, stop),
                out_shape=(part_shape,) + ((jax.ShapeDtypeStruct(left.shape, BF16),) if start == 0 else ()),
                in_specs=[vmem] * 4,
                out_specs=(vmem,) * (2 if start == 0 else 1),
                compiler_params=params(),
                cost_estimate=cost(stage_flops / 2, 12 * states * width * width),
                name="received_rights",
            )(right_far, mixed, partial, keep)
            if unpacked:
                right_far, norm_other = lax.optimization_barrier((unpacked[0], to_sibling(norm)))
            parts.append(part)
        if not last:
            partial = parts[0]
    halves = []
    for part in parts:
        halves += [part, to_sibling(part)]
    half_bf = jax.ShapeDtypeStruct((states // 2, width, width), BF16)
    half_mixed = (terms, states // 2, width, width)
    res_low, mixed_low, sums = pl.pallas_call(
        low_kernel,
        out_shape=(half_bf, jax.ShapeDtypeStruct(half_mixed, BF16), tile),
        in_specs=[vmem] * 7,
        out_specs=(vmem,) * 3,
        compiler_params=params(),
        cost_estimate=cost(stage_flops / 2, 3 * states * width * width),
        name="residual_low",
    )(keep, norm, norm_other, *halves[:2], vector, left)
    share = pl.pallas_call(
        functools.partial(high_kernel, scale, members),
        out_shape=tile,
        in_specs=[vmem] * 12,
        out_specs=vmem,
        scratch_shapes=[
            pltpu.VMEM(half_bf.shape, BF16),
            pltpu.VMEM(rotated, BF16),
            pltpu.VMEM(half_mixed, BF16),
        ],
        compiler_params=params(),
        cost_estimate=cost(3 * stage_flops, 6 * states * width * width),
        name="residual_high",
    )(keep, norm, norm_other, sums, *halves[2:], vector, left, right, kron_own, res_low, mixed_low)
    crossed = everyone(share)

    local = jax.ShapeDtypeStruct((rows, states, width), F32)
    vector_own, residual_own = pl.pallas_call(
        functools.partial(own_rows_kernel, scale, members),
        out_shape=(local, local),
        in_specs=[vmem] * 9,
        out_specs=(vmem, vmem),
        compiler_params=params(),
        cost_estimate=cost(8 * guess.size, 16 * guess.size),
        name="own_rows",
    )(keep, norm, norm_other, share, guess, *halves)

    shares = [share, to_sibling(share)]
    gated, residual_own = lax.optimization_barrier((crossed[1:], residual_own))
    shares += relayed(gated)
    ritz, energy = pl.pallas_call(
        finish_kernel,
        out_shape=(local, jax.ShapeDtypeStruct((1,), F32)),
        in_specs=[vmem] * (2 + members),
        out_specs=(vmem, smem),
        compiler_params=params(),
        cost_estimate=cost(3 * guess.size, 12 * guess.size),
        name="finish",
    )(vector_own, residual_own, *shares)
    return (ritz[None], energy)


def solution(mesh):
    in_specs = (
        P("seg", "term", None, None),
        P("seg", "term", None, None),
        P("seg", "term", None, None),
        P("seg", "term", None, None),
        P("seg"),
    )
    out_specs = (P("seg", "term", None, None), P("seg"))
    return jax.shard_map(shards, mesh=mesh, in_specs=in_specs, out_specs=out_specs, check_vma=False)
```

```python
import functools

import jax
import jax.numpy as jnp
from jax import lax
from jax.experimental import pallas as pl
from jax.experimental.pallas import tpu as pltpu
from jax.sharding import PartitionSpec as P

epsilon = 1e-06
CORES = 2
TILE = 16
STRIP = 32
GROUP = 8
VMEM_LIMIT = 20 * 1024 * 1024
F32 = jnp.float32
BF16 = jnp.bfloat16

vmem = pl.BlockSpec(memory_space=pltpu.VMEM)
smem = pl.BlockSpec(memory_space=pltpu.SMEM)
anywhere = pl.BlockSpec(memory_space=pl.ANY)
in_hbm = pl.BlockSpec(memory_space=pltpu.HBM)


def params():
    return pltpu.CompilerParams(vmem_limit_bytes=VMEM_LIMIT)


def cost(flops, moved):
    return pl.CostEstimate(flops=int(flops) // 100, bytes_accessed=int(moved) // 100, transcendentals=0)


def fold(values, width):
    return jnp.sum(values.reshape(values.size // (8 * width), 8, width), axis=0)


def chunk_rows_in(guess_in, guess_ref, sems, start, stop, slot):
    copies = []
    for n in range(start, stop, TILE):
        target = guess_ref.at[pl.ds(n - start, TILE)]
        copies.append(pltpu.make_async_copy(guess_in.at[pl.ds(n, TILE)], target, sems.at[slot + len(copies)]))
        copies[-1].start()
    return copies


def first_chunk_kernel(
    rank_in,
    guess_in,
    site_in,
    right_in,
    x_ref,
    keep_ref,
    squares_ref,
    packed_ref,
    rank_ref,
    guess_ref,
    site_ref,
    right_ref,
    sems,
):
    rows, states, width = guess_ref.shape
    terms = site_ref.shape[0]
    blocks = rows // TILE
    copies = [
        pltpu.make_async_copy(source, target, sems.at[n])
        for n, (source, target) in enumerate(((rank_in, rank_ref), (site_in, site_ref), (right_in, right_ref)))
    ]
    copies[0].start()
    parts = chunk_rows_in(guess_in, guess_ref, sems, 0, rows, 3)
    copies[1].start()
    copies[2].start()
    copies[0].wait()
    column = lax.broadcasted_iota(jnp.int32, (1, width), 1)
    keep = (column < rank_ref[...]).astype(F32)
    keep_ref[...] = jnp.broadcast_to(keep, keep_ref.shape)
    squares = jnp.zeros((8, width), F32)
    for n, copy in enumerate(parts):
        copy.wait()
        masked = guess_ref[pl.ds(n * TILE, TILE)] * keep[None]
        squares = squares + fold(masked * masked, width)
        x_ref[n * states : (n + 1) * states] = jnp.swapaxes(masked, 0, 1).astype(BF16)
    squares_ref[...] = squares
    copies[1].wait()
    line = lax.broadcasted_iota(jnp.int32, (TILE, width), 0)
    lane = lax.broadcasted_iota(jnp.int32, (TILE, width), 1)
    extra = jnp.zeros((TILE, width), F32)
    for k in range(terms):
        place_at = (lane == line + k * TILE).astype(BF16)
        extra = extra + jnp.dot(site_ref[k], place_at, preferred_element_type=F32)
    x_ref[blocks * states] = extra.astype(BF16)
    copies[2].wait()
    pack_blocks(right_ref, None, packed_ref)


def prepare_kernel(starts, keep_ref, squares_ref, guess_in, left_in, norm_ref, packed_ref, left_ref, *refs):
    x_refs = (None,) + refs[: len(starts) - 1]
    guess_ref, sems = refs[len(starts) - 1 :]
    rows, states, width = guess_in.shape
    half = width // 2
    done = starts[1] if len(starts) > 1 else rows
    copies = chunk_rows_in(guess_in, guess_ref, sems, done, rows, 1)
    left_copy = pltpu.make_async_copy(left_in, left_ref, sems.at[0])
    left_copy.start()
    keep = keep_ref[0:1, :][None]
    squares = squares_ref[...]
    for n, copy in enumerate(copies):
        copy.wait()
        masked = guess_ref[pl.ds(n * TILE, TILE)] * keep
        squares = squares + fold(masked * masked, width)
        chunk = max(c for c, start in enumerate(starts) if start <= done + n * TILE)
        at = done + n * TILE - starts[chunk]
        block = at // TILE
        x_refs[chunk][block * states : (block + 1) * states] = jnp.swapaxes(masked, 0, 1).astype(BF16)
    total = jnp.sum(squares)
    norm_ref[...] = jnp.full(norm_ref.shape, total, F32)
    line = lax.broadcasted_iota(jnp.int32, (TILE, half), 0)
    norm = jnp.full((TILE, half), total, F32)
    extra = jnp.zeros((TILE, half), F32)
    for n in range(3):
        part = norm.astype(BF16).astype(F32)
        norm = norm - part
        extra = jnp.where(line == left_ref.shape[0] + n, part, extra)
    left_copy.wait()
    pack_blocks(left_ref, extra, packed_ref)


def pack_blocks(block_ref, extra, packed_ref):
    terms, width, _ = block_ref.shape
    half = width // 2
    line = lax.broadcasted_iota(jnp.int32, (TILE, half), 0)
    row, col = triangle(half)
    lines = jnp.zeros((TILE, half), F32) if extra is None else extra
    for k in range(terms):
        upper = block_ref[k, 0:half, 0:half].astype(F32)
        lower = block_ref[k, half:width, half:width].astype(F32)
        diagonal = jnp.sum(jnp.where(row == col, lower, 0.0), axis=0, keepdims=True)
        lines = jnp.where(line == k, diagonal, lines)
        base = k * width
        packed_ref[base : base + half, :] = block_ref[k, 0:half, half:width]
        packed_ref[base + half : base + width, :] = jnp.where(row <= col, upper, lower).astype(BF16)
    packed_ref[terms * width : terms * width + TILE, :] = lines.astype(BF16)


def triangle(half):
    row = lax.broadcasted_iota(jnp.int32, (half, half), 0)
    col = lax.broadcasted_iota(jnp.int32, (half, half), 1)
    return row, col


def unpack_symmetric(packed_ref, full_ref, keep=None):
    terms, width, _ = full_ref.shape
    half = width // 2
    row, col = triangle(half)

    def kept(block, start):
        return block if keep is None else block * keep[:, start : start + half]

    diagonals = packed_ref[terms * width : terms * width + TILE, :].astype(F32)
    for k in range(terms):
        base = k * width
        corner = packed_ref[base : base + half, :].astype(F32)
        mixed = packed_ref[base + half : base + width, :].astype(F32)
        diagonal = diagonals[k : k + 1]
        turned = mixed.T
        lower = jnp.where(row > col, mixed, jnp.where(row == col, diagonal, turned))
        full_ref[k, 0:half, 0:half] = kept(jnp.where(row <= col, mixed, turned), 0).astype(BF16)
        full_ref[k, 0:half, half:width] = kept(corner, half).astype(BF16)
        full_ref[k, half:width, 0:half] = kept(corner.T, 0).astype(BF16)
        full_ref[k, half:width, half:width] = kept(lower, half).astype(BF16)


def spread_kernel(chunk_ref, kron_ref):
    width = chunk_ref.shape[2]
    size = kron_ref.shape[1]
    terms = kron_ref.shape[0] // size
    states = size // TILE
    tile = chunk_ref[chunk_ref.shape[0] - 1]
    row_state = lax.broadcasted_iota(jnp.int32, (size, states), 0) // TILE
    pick = (row_state == lax.broadcasted_iota(jnp.int32, (size, states), 1)).astype(BF16)
    tall = jnp.dot(pick, tile, preferred_element_type=F32).astype(BF16)
    lane = lax.broadcasted_iota(jnp.int32, (width, size), 0)
    col_state = lax.broadcasted_iota(jnp.int32, (width, size), 1) // TILE
    same = (
        lax.broadcasted_iota(jnp.int32, (size, size), 0) % TILE
        == lax.broadcasted_iota(jnp.int32, (size, size), 1) % TILE
    )
    for k in range(terms):
        pick_t = (lane == col_state + k * TILE).astype(BF16)
        full = jnp.dot(tall, pick_t, preferred_element_type=F32)
        kron_ref[k * size : (k + 1) * size, :] = jnp.where(same, full, 0.0).astype(BF16)


def mix_sites(source_ref, kron_ref, rotated_ref, base):
    terms, states, _, width = rotated_ref.shape
    for i in range(source_ref.shape[0] // states):
        to = pl.ds(pl.multiple_of(base + i * TILE, TILE), TILE)
        stack = source_ref[i * states : (i + 1) * states].reshape(states * TILE, width)
        turned = jnp.dot(kron_ref[...], stack, preferred_element_type=F32).astype(BF16)
        rotated_ref[:, :, to, :] = turned.reshape(terms, states, TILE, width)


def summed(values):
    while len(values) > 1:
        values = [values[n] + values[n + 1] for n in range(0, len(values), 2)]
    return values[0]


def place(hop, chips):
    me = lax.axis_index("term")
    chip = (me // CORES - hop + chips) % chips
    return chip, me % CORES


def row_of(spot, rows, chips):
    chip, core = place(spot[0], chips)
    return pl.multiple_of((chip * CORES + (core if spot[1] == 0 else 1 - core)) * rows + spot[2], TILE)


def mix_pieces(pieces, kron_ref, rotated_ref):
    at = 0
    for piece in pieces:
        mix_sites(piece, kron_ref, rotated_ref, at)
        at += piece.shape[0] // rotated_ref.shape[1] * TILE


def rotate_own_kernel(groups, rows, chips, *refs):
    kron_ref, left_ref, rotated_ref, columns_ref = refs[-4:]
    mix_pieces(refs[:-4], kron_ref, rotated_ref)
    blocks = []
    for spots in groups:
        for k in range(left_ref.shape[0]):
            blocks += [left_ref[k, pl.ds(row_of(spot, rows, chips), spot[3]), :] for spot in spots]
    columns_ref[...] = jnp.concatenate(blocks, axis=0).astype(F32).T.astype(BF16)


def turn(right_ref, rotated_ref, turned_ref):
    terms, states, count, width = rotated_ref.shape
    for k in range(terms):
        source = rotated_ref[k].reshape(states * count, width)
        turned = jnp.dot(source, right_ref[k], preferred_element_type=F32).astype(BF16)
        turned_ref[:, k * count : (k + 1) * count, :] = turned.reshape(states, count, width)


def here_kernel(rotated_ref, packed_ref, keep_ref, turned_ref, right_ref):
    unpack_symmetric(packed_ref, right_ref, keep_ref[0:1, :])
    turn(right_ref, rotated_ref, turned_ref)


def there_kernel(*refs):
    right_ref, kron_ref, turned_ref, rotated_ref = refs[-4:]
    mix_pieces(refs[:-4], kron_ref, rotated_ref)
    turn(right_ref, rotated_ref, turned_ref)


def last_kernel(count, *refs):
    right_ref, kron_ref, columns_ref = refs[count : count + 3]
    out_ref, rotated_ref, turned_ref = refs[-3:]
    there_kernel(*refs[:count], right_ref, kron_ref, turned_ref, rotated_ref)
    blocks = list(refs[count + 3 : -3]) + [turned_ref]

    def lefts(p, carry):
        stack = jnp.concatenate([block[p] for block in blocks], axis=0)
        out_ref[p] = jnp.dot(columns_ref[...], stack, preferred_element_type=F32)
        return carry

    lax.fori_loop(0, out_ref.shape[0], lefts, 0, unroll=out_ref.shape[0])


def rotate_kernel(spots, rows, chips, *refs):
    pieces = refs[: len(spots)]
    kron_ref = refs[len(spots)]
    rotated_ref, whole_ref, sems = refs[-3:]
    states = whole_ref.shape[0]
    copies = []
    bases = [row_of(spot, rows, chips) for spot in spots]
    for at, piece in zip(bases, pieces):
        for i in range(piece.shape[0] // states):
            target = whole_ref.at[:, pl.ds(pl.multiple_of(at + i * TILE, TILE), TILE), :]
            source = piece.at[i * states : (i + 1) * states]
            copies.append(pltpu.make_async_copy(source, target, sems.at[len(copies)]))
            copies[-1].start()
    for at, piece in zip(bases, pieces):
        mix_sites(piece, kron_ref, rotated_ref, at)
    for copy in copies:
        copy.wait()


def lefts_kernel(spots, rows, chips, *refs):
    count = len(spots)
    packed_ref, norm_before_ref = refs[count + 3 : count + 5]
    mixed_ref, norm_ref, rotated_ref, whole_ref, left_ref, sems = refs[-6:]
    terms, states, width, _ = rotated_ref.shape
    lines = packed_ref[terms * width : terms * width + TILE, :].astype(F32)
    norm = lines[terms : terms + 1] + lines[terms + 1 : terms + 2] + lines[terms + 2 : terms + 3]
    norm_ref[...] = norm_before_ref[...] + jnp.concatenate([norm, norm], axis=1)
    unpack_symmetric(packed_ref, left_ref)
    rotate_kernel(spots, rows, chips, *refs[: count + 1], rotated_ref, whole_ref, sems)

    def lefts(p, carry):
        for k in range(terms):
            mixed = jnp.dot(left_ref[k], rotated_ref[k, p], preferred_element_type=F32)
            mixed_ref[p, :, k * width : (k + 1) * width] = mixed.astype(BF16)
        return carry

    lax.fori_loop(0, states, lefts, 0, unroll=states)


def rights_kernel(start, stop, packed_ref, mixed_ref, before_ref, keep_ref, partial_ref, *refs):
    if start == 0:
        right_ref = refs[0]
        unpack_symmetric(packed_ref, right_ref, keep_ref[0:1, :])
    else:
        right_ref = packed_ref
    terms, width, _ = right_ref.shape

    def rights(n, carry):
        at = n * GROUP
        rows = mixed_ref[pl.ds(start + at, GROUP)].reshape(GROUP * width, terms * width)
        stacked = right_ref[...].reshape(terms * width, width)
        image = jnp.dot(rows, stacked, preferred_element_type=F32).reshape(GROUP, width, width)
        partial_ref[pl.ds(at, GROUP)] = (before_ref[pl.ds(start + at, GROUP)] + image).astype(partial_ref.dtype)
        return carry

    lax.fori_loop(0, (stop - start) // GROUP, rights, 0)


def shifted_residual(start, shift, mine_ref, other_ref, whole_ref, left_ref, res_ref, mixed_ref):
    count, width, _ = res_ref.shape
    terms = left_ref.shape[0]
    zero = jnp.zeros((8, width), F32)

    def lefts(n, sums):
        square, product = sums
        for row in range(0, width, STRIP):
            strip = pl.ds(row, STRIP)
            held = whole_ref[start + n, strip, :].astype(F32)
            sigma = mine_ref[n, strip, :].astype(F32) + other_ref[n, strip, :].astype(F32)
            residual = sigma - shift * held
            res_ref[n, strip, :] = residual.astype(BF16)
            square = square + fold(residual * residual, width)
            product = product + fold(sigma * held, width)
        mixed = jnp.dot(
            left_ref[...].reshape(terms * width, width), res_ref[n], preferred_element_type=F32
        ).astype(BF16)
        for k in range(terms):
            mixed_ref[k, n] = mixed[k * width : (k + 1) * width]
        return square, product

    square, product = lax.fori_loop(0, count, lefts, (zero, zero), unroll=count)
    return jnp.sum(square), jnp.sum(product)


def low_kernel(
    norm_ref,
    norm_other_ref,
    low_ref,
    low_other_ref,
    whole_ref,
    left_ref,
    res_ref,
    mixed_ref,
    out_ref,
):
    count, width, _ = low_ref.shape
    states = whole_ref.shape[0]
    held = whole_ref[0].astype(F32)
    sigma = low_ref[0].astype(F32) + low_other_ref[0].astype(F32)
    product = jnp.sum(fold(sigma * held, width))
    square = jnp.sum(fold(held * held, width))
    total = norm_ref[0:1, :] + norm_other_ref[0:1, :]
    floor = jnp.maximum(jnp.maximum(square, (0.25 / states) * total), 1e-30)
    shift = product / floor
    square, product = shifted_residual(
        0, shift, low_ref, low_other_ref, whole_ref, left_ref, res_ref, mixed_ref
    )
    out_ref[0:1, :] = shift
    out_ref[1:2, :] = jnp.full((1, width), square, F32)
    out_ref[2:3, :] = jnp.full((1, width), product, F32)
    out_ref[3:8, :] = jnp.zeros((5, width), F32)


def high_kernel(
    scale,
    members,
    norm_ref,
    norm_other_ref,
    sums_ref,
    high_ref,
    high_other_ref,
    whole_ref,
    left_ref,
    right_ref,
    kron_ref,
    res_low_ref,
    mixed_low_ref,
    out_ref,
    res_ref,
    rotated_ref,
    mixed_ref,
):
    terms, states, width, _ = rotated_ref.shape
    half = states // 2
    shift = sums_ref[0:1, :]
    square, product = shifted_residual(
        half, shift, high_ref, high_other_ref, whole_ref, left_ref, res_ref, mixed_ref
    )

    def sites(i, carry):
        at = pl.ds(pl.multiple_of(i * TILE, TILE), TILE)
        stack = jnp.concatenate([res_low_ref[:, at, :], res_ref[:, at, :]], axis=0).reshape(states * TILE, width)
        turned = jnp.dot(kron_ref[...], stack, preferred_element_type=F32).astype(BF16)
        rotated_ref[:, :, at, :] = turned.reshape(terms, states, TILE, width)
        return carry

    lax.fori_loop(0, width // TILE, sites, 0, unroll=width // TILE)
    cross = jnp.zeros((8, width), F32)
    for start, left_mixed_ref in ((0, mixed_low_ref), (half, mixed_ref)):
        for k in range(terms):
            turned = rotated_ref[k, start : start + half].reshape(half * width, width)
            image = jnp.dot(turned, right_ref[k], preferred_element_type=F32)
            held = left_mixed_ref[k].reshape(half * width, width).astype(F32)
            cross = cross + fold(held * image, width)
    res_square = sums_ref[1:2, :] + square
    product = sums_ref[2:3, :] + product
    total = norm_ref[0:1, :] + norm_other_ref[0:1, :]
    factor = scale / (total * scale + epsilon)
    rayleigh = factor * product
    gap = rayleigh - shift
    res_vector = product - shift * total
    res_sq = factor * (res_square - 2.0 * gap * res_vector + gap * gap * total)
    change = gap * gap * product - 2.0 * gap * (res_square + shift * res_vector)
    share = 1.0 / members
    out_ref[0:1, :] = rayleigh * share
    out_ref[1:2, :] = jnp.maximum(res_sq, 0.0) * share
    out_ref[2:3, :] = factor * (jnp.sum(cross) + share * change)
    out_ref[3:8, :] = jnp.zeros((5, width), F32)


def own_rows_kernel(scale, members, keep_ref, norm_ref, norm_other_ref, share_ref, guess_ref, *refs):
    low_ref, low_other_ref, high_ref, high_other_ref, vector_ref, residual_ref = refs
    rows, states, width = guess_ref.shape
    inverse = lax.rsqrt((norm_ref[0:1, :] + norm_other_ref[0:1, :]) * scale + epsilon)
    row_scale = keep_ref[0:1, :] * inverse
    rayleigh = share_ref[0:1, :] * members
    own = pl.ds(pl.multiple_of(lax.axis_index("term") * rows, TILE), rows)
    vector = guess_ref[...] * row_scale[None]
    vector_ref[...] = vector
    sigma = jnp.concatenate(
        [
            mine_ref[:, own, :].astype(F32) + other_ref[:, own, :].astype(F32)
            for mine_ref, other_ref in ((low_ref, low_other_ref), (high_ref, high_other_ref))
        ],
        axis=0,
    )
    residual_ref[...] = jnp.swapaxes(sigma * row_scale[None], 0, 1) - rayleigh[None] * vector


def finish_kernel(vector_ref, residual_ref, *refs):
    shares = refs[:-2]
    ritz_ref, energy_ref = refs[-2:]
    stat = summed([share[...] for share in shares])
    rayleigh = stat[0:1, :]
    res_sq = stat[1:2, :]
    res_var = res_sq + epsilon
    curvature = stat[2:3, :] / res_var
    res_scale = jnp.sqrt(res_var)
    coupling = res_sq / res_scale
    half_gap = 0.5 * (rayleigh - curvature)
    energy = 0.5 * (rayleigh + curvature) - jnp.sqrt(half_gap * half_gap + coupling * coupling)
    coeff_new = energy - rayleigh
    coeff_norm = jnp.sqrt(coupling * coupling + coeff_new * coeff_new + epsilon)
    old = coupling / coeff_norm
    new = coeff_new / (coeff_norm * res_scale)
    ritz_ref[...] = old[None] * vector_ref[...] + new[None] * residual_ref[...]
    energy_ref[0] = energy[0, 0]


def shards(wave_guess, left_env, right_env, site_ops, bond_rank):
    guess = wave_guess[0]
    left = left_env[0]
    site = site_ops[0]
    rows, states, width = guess.shape
    terms = left.shape[0]
    members = lax.axis_size("term")
    chips = members // CORES
    segments = lax.axis_size("seg")
    scale = 1.0 / float(rows * members * states * width)
    hops = tuple(range(chips))

    def to_sibling(block):
        return lax.ppermute(block, "term", [(i, i ^ 1) for i in range(members)])

    def to_next_chip(block):
        return lax.ppermute(block, "term", [(i, (i + CORES) % members) for i in range(members)])

    def around(block):
        found = [block]
        for _ in range(chips - 1):
            found.append(to_next_chip(found[-1]))
        return found

    def everyone(block):
        return [block] + [
            lax.ppermute(block, "term", [(i, i ^ bits) for i in range(members)])
            for bits in range(CORES, members, CORES)
        ]

    tile = jax.ShapeDtypeStruct((8, width), F32)
    half = width // 2
    packed_shape = jax.ShapeDtypeStruct((terms * width + TILE, half), BF16)
    starts = (0, rows - 2 * TILE, rows - TILE) if rows >= 4 * TILE else (0,)
    lengths = [stop - start for start, stop in zip(starts, starts[1:] + (rows,))]
    in_place = [pltpu.with_memory_space_constraint(a, pltpu.HBM) for a in (guess, left, right_env[0], site)]
    first_chunk, keep, squares, right_packed = pl.pallas_call(
        first_chunk_kernel,
        out_shape=(jax.ShapeDtypeStruct((lengths[0] // TILE * states + 1, TILE, width), BF16), tile, tile, packed_shape),
        in_specs=[anywhere] + [in_hbm] * 3,
        out_specs=(vmem,) * 4,
        scratch_shapes=[
            pltpu.VMEM((1, 1), jnp.int32),
            pltpu.VMEM((lengths[0], states, width), F32),
            pltpu.VMEM(site.shape, BF16),
            pltpu.VMEM(left.shape, BF16),
            pltpu.SemaphoreType.DMA((lengths[0] // TILE + 3,)),
        ],
        compiler_params=params(),
        cost_estimate=cost(2 * guess.size, 3 * guess.size),
        name="first_chunk",
    )(bond_rank.reshape(1, 1), in_place[0], in_place[3], in_place[2])
    rest = rows - lengths[0]
    squares, first_sibling = lax.optimization_barrier((squares, to_sibling(first_chunk)))
    norm_part, left_packed, left, *chunks = pl.pallas_call(
        functools.partial(prepare_kernel, starts),
        out_shape=(
            tile,
            packed_shape,
            jax.ShapeDtypeStruct(left.shape, BF16),
            *[jax.ShapeDtypeStruct((length // TILE * states, TILE, width), BF16) for length in lengths[1:]],
        ),
        in_specs=[vmem] * 2 + [in_hbm] * 2,
        out_specs=(vmem,) * (2 + len(lengths)),
        scratch_shapes=[
            pltpu.VMEM((max(rest, TILE), states, width), F32),
            pltpu.SemaphoreType.DMA((rest // TILE + 1,)),
        ],
        compiler_params=params(),
        cost_estimate=cost(4 * guess.size, 6 * guess.size),
        name="prepare",
    )(keep, squares, *in_place[:2])
    chunks = [first_chunk] + chunks

    chunk_hops = [around(chunk) for chunk in chunks]
    here_pieces = chunks + [first_sibling] + [to_sibling(chunk) for chunk in chunks[1:]]
    here_spots = tuple((0, flip, start, length) for flip in range(CORES) for start, length in zip(starts, lengths))
    far_spots = [
        tuple((hop, flip, start, length) for hop in hops[1:] for flip in range(CORES))
        for start, length in zip(starts, lengths)
    ]
    mid_spots = sum(far_spots[:-1], ())
    groups = [group for group in (here_spots, mid_spots, far_spots[-1]) if group]
    lefts = around(left_packed)
    shift = [(i + 1, i) for i in range(segments - 1)]
    received = lax.ppermute(right_packed, "seg", shift)

    size = states * TILE

    def spread(block):
        return pl.pallas_call(
            spread_kernel,
            out_shape=jax.ShapeDtypeStruct((terms * size, size), BF16),
            in_specs=[vmem],
            out_specs=vmem,
            compiler_params=params(),
            cost_estimate=cost(2 * terms * size * size * width, 2 * terms * size * size),
            name="spread_site",
        )(block)

    kron_own = spread(chunks[0])

    whole = (states, width, width)
    whole_bf = jax.ShapeDtypeStruct(whole, BF16)
    whole_f32 = jax.ShapeDtypeStruct(whole, F32)
    rotated = (terms, states, width, width)
    rotated_bf = jax.ShapeDtypeStruct(rotated, BF16)
    square = pltpu.VMEM((terms, width, width), BF16)
    chip_rows = CORES * rows
    stage_flops = 2 * terms * states * width * width * width

    def buffers(spots):
        count = sum(spot[3] for spot in spots)
        return (terms, states, count, width), (states, terms * count, width)

    here_rotated, here_turned = buffers(here_spots)
    part_cost = cost(stage_flops, 8 * states * width * width)
    rotated_own, columns = pl.pallas_call(
        functools.partial(rotate_own_kernel, groups, rows, chips),
        out_shape=(
            jax.ShapeDtypeStruct(here_rotated, BF16),
            jax.ShapeDtypeStruct((width, terms * width), BF16),
        ),
        in_specs=[vmem] * (len(here_pieces) + 2),
        out_specs=(vmem, vmem),
        compiler_params=params(),
        cost_estimate=part_cost,
        name="rotate_own",
    )(*here_pieces, kron_own, left)

    def rotate(spots, pieces, kron, before):
        return pl.pallas_call(
            functools.partial(rotate_kernel, spots, rows, chips),
            out_shape=(rotated_bf, whole_bf),
            in_specs=[vmem] * (len(pieces) + 1) + [anywhere] * len(before),
            out_specs=(vmem, vmem),
            scratch_shapes=[pltpu.SemaphoreType.DMA((sum(spot[3] for spot in spots) // TILE,))],
            input_output_aliases={len(pieces) + 1 + n: n for n in range(len(before))},
            compiler_params=params(),
            cost_estimate=part_cost,
            name="rotate_crossed" if before else "rotate_here",
        )(*pieces, kron, *before)

    def relayed(blocks):
        return [piece for block in blocks for piece in (block, to_sibling(block))]

    firsts, rotated_own = lax.optimization_barrier((chunk_hops[0][1:], rotated_own))
    kron = spread(firsts[0])
    turned = rotate(here_spots, here_pieces, kron, ())
    received, turned = lax.optimization_barrier((received, turned))
    packed = jnp.where(lax.axis_index("seg") == segments - 1, right_packed, received)
    rights = around(packed)
    turned_own, right = pl.pallas_call(
        here_kernel,
        out_shape=(jax.ShapeDtypeStruct(here_turned, BF16), jax.ShapeDtypeStruct(left.shape, BF16)),
        in_specs=[vmem] * 3,
        out_specs=(vmem, vmem),
        compiler_params=params(),
        cost_estimate=part_cost,
        name="apply_rows_here",
    )(rotated_own, packed, keep)
    parts = [turned_own]
    mid_pieces = []
    if mid_spots:
        mid_pieces += relayed(firsts)
        for crossing in chunk_hops[1:-1]:
            crossed, turned = lax.optimization_barrier((crossing[1:], turned))
            mid_pieces += relayed(crossed)
        turned = rotate(mid_spots, mid_pieces, kron, turned)
        crossed, turned, parts[0] = lax.optimization_barrier((chunk_hops[-1][1:], turned, parts[0]))
        last_pieces = relayed(crossed)
        mid_rotated, mid_turned = buffers(mid_spots)
        parts.append(
            pl.pallas_call(
                there_kernel,
                out_shape=jax.ShapeDtypeStruct(mid_turned, BF16),
                in_specs=[vmem] * (len(mid_pieces) + 2),
                out_specs=vmem,
                scratch_shapes=[pltpu.VMEM(mid_rotated, BF16)],
                compiler_params=params(),
                cost_estimate=part_cost,
                name="apply_rows_crossed",
            )(*mid_pieces, right, kron_own)
        )
    else:
        last_pieces = relayed(firsts)
    last_rotated, last_turned = buffers(far_spots[-1])
    partial = pl.pallas_call(
        functools.partial(last_kernel, len(last_pieces)),
        out_shape=whole_f32,
        in_specs=[vmem] * (len(last_pieces) + 3 + len(parts)),
        out_specs=vmem,
        scratch_shapes=[pltpu.VMEM(last_rotated, BF16), pltpu.VMEM(last_turned, BF16)],
        compiler_params=params(),
        cost_estimate=part_cost,
        name="apply_rows_last",
    )(*last_pieces, right, kron_own, columns, *parts)
    norm = norm_part
    for hop in hops[1:]:
        if hop > 1:
            block, partial = lax.optimization_barrier((firsts[hop - 1], partial))
            kron = spread(block)
            turned = rotate(here_spots, here_pieces, kron, ())
            if mid_spots:
                turned = rotate(mid_spots, mid_pieces, kron, turned)
        left_far, partial = lax.optimization_barrier((lefts[hop], partial))
        mixed, norm, _, vector = pl.pallas_call(
            functools.partial(lefts_kernel, far_spots[-1], rows, chips),
            out_shape=(jax.ShapeDtypeStruct((states, width, terms * width), BF16), tile, rotated_bf, whole_bf),
            in_specs=[vmem] * (len(last_pieces) + 1) + [anywhere] * 2 + [vmem] * 2,
            out_specs=(vmem,) * 4,
            scratch_shapes=[
                square,
                pltpu.SemaphoreType.DMA((sum(spot[3] for spot in far_spots[-1]) // TILE,)),
            ],
            input_output_aliases={len(last_pieces) + 1: 2, len(last_pieces) + 2: 3},
            compiler_params=params(),
            cost_estimate=cost(stage_flops, 12 * states * width * width),
            name="received_lefts",
        )(*last_pieces, kron, *turned, left_far, norm)
        last = hop == hops[-1]
        right_far = rights[hop]
        parts = []
        bounds = (0, states // 2, states) if last else (0, states)
        for start, stop in zip(bounds[:-1], bounds[1:]):
            part_shape = jax.ShapeDtypeStruct((stop - start, width, width), BF16 if last else F32)
            part, *unpacked = pl.pallas_call(
                functools.partial(rights_kernel, start, stop),
                out_shape=(part_shape,) + ((jax.ShapeDtypeStruct(left.shape, BF16),) if start == 0 else ()),
                in_specs=[vmem] * 4,
                out_specs=(vmem,) * (2 if start == 0 else 1),
                compiler_params=params(),
                cost_estimate=cost(stage_flops / 2, 12 * states * width * width),
                name="received_rights",
            )(right_far, mixed, partial, keep)
            if unpacked:
                right_far, norm_other = lax.optimization_barrier((unpacked[0], to_sibling(norm)))
            parts.append(part)
        if not last:
            partial = parts[0]
    halves = []
    for part in parts:
        halves += [part, to_sibling(part)]
    half_bf = jax.ShapeDtypeStruct((states // 2, width, width), BF16)
    half_mixed = (terms, states // 2, width, width)
    res_low, mixed_low, sums = pl.pallas_call(
        low_kernel,
        out_shape=(half_bf, jax.ShapeDtypeStruct(half_mixed, BF16), tile),
        in_specs=[vmem] * 6,
        out_specs=(vmem,) * 3,
        compiler_params=params(),
        cost_estimate=cost(stage_flops / 2, 3 * states * width * width),
        name="residual_low",
    )(norm, norm_other, *halves[:2], vector, left)
    share = pl.pallas_call(
        functools.partial(high_kernel, scale, members),
        out_shape=tile,
        in_specs=[vmem] * 11,
        out_specs=vmem,
        scratch_shapes=[
            pltpu.VMEM(half_bf.shape, BF16),
            pltpu.VMEM(rotated, BF16),
            pltpu.VMEM(half_mixed, BF16),
        ],
        compiler_params=params(),
        cost_estimate=cost(3 * stage_flops, 6 * states * width * width),
        name="residual_high",
    )(norm, norm_other, sums, *halves[2:], vector, left, right, kron_own, res_low, mixed_low)
    crossed = everyone(share)

    local = jax.ShapeDtypeStruct((rows, states, width), F32)
    vector_own, residual_own = pl.pallas_call(
        functools.partial(own_rows_kernel, scale, members),
        out_shape=(local, local),
        in_specs=[vmem] * 9,
        out_specs=(vmem, vmem),
        compiler_params=params(),
        cost_estimate=cost(8 * guess.size, 16 * guess.size),
        name="own_rows",
    )(keep, norm, norm_other, share, guess, *halves)

    shares = [share, to_sibling(share)]
    gated, residual_own = lax.optimization_barrier((crossed[1:], residual_own))
    shares += relayed(gated)
    ritz, energy = pl.pallas_call(
        finish_kernel,
        out_shape=(local, jax.ShapeDtypeStruct((1,), F32)),
        in_specs=[vmem] * (2 + members),
        out_specs=(vmem, smem),
        compiler_params=params(),
        cost_estimate=cost(3 * guess.size, 12 * guess.size),
        name="finish",
    )(vector_own, residual_own, *shares)
    return (ritz[None], energy)


def solution(mesh):
    in_specs = (
        P("seg", "term", None, None),
        P("seg", "term", None, None),
        P("seg", "term", None, None),
        P("seg", "term", None, None),
        P("seg"),
    )
    out_specs = (P("seg", "term", None, None), P("seg"))
    return jax.shard_map(shards, mesh=mesh, in_specs=in_specs, out_specs=out_specs, check_vma=False)
```

```python
import functools

import jax
import jax.numpy as jnp
from jax import lax
from jax.experimental import pallas as pl
from jax.experimental.pallas import tpu as pltpu
from jax.sharding import PartitionSpec as P

epsilon = 1e-06
CORES = 2
TILE = 16
STRIP = 16
GROUP = 8
VMEM_LIMIT = 20 * 1024 * 1024
F32 = jnp.float32
BF16 = jnp.bfloat16

vmem = pl.BlockSpec(memory_space=pltpu.VMEM)
smem = pl.BlockSpec(memory_space=pltpu.SMEM)
anywhere = pl.BlockSpec(memory_space=pl.ANY)
in_hbm = pl.BlockSpec(memory_space=pltpu.HBM)


def params():
    return pltpu.CompilerParams(vmem_limit_bytes=VMEM_LIMIT)


def cost(flops, moved):
    return pl.CostEstimate(flops=int(flops) // 100, bytes_accessed=int(moved) // 100, transcendentals=0)


def fold(values, width):
    return jnp.sum(values.reshape(values.size // (8 * width), 8, width), axis=0)


def chunk_rows_in(guess_in, guess_ref, sems, start, stop, slot):
    copies = []
    for n in range(start, stop, TILE):
        target = guess_ref.at[pl.ds(n - start, TILE)]
        copies.append(pltpu.make_async_copy(guess_in.at[pl.ds(n, TILE)], target, sems.at[slot + len(copies)]))
        copies[-1].start()
    return copies


def first_chunk_kernel(
    rank_in,
    guess_in,
    site_in,
    right_in,
    x_ref,
    keep_ref,
    squares_ref,
    packed_ref,
    rank_ref,
    guess_ref,
    site_ref,
    right_ref,
    sems,
):
    rows, states, width = guess_ref.shape
    terms = site_ref.shape[0]
    blocks = rows // TILE
    copies = [
        pltpu.make_async_copy(source, target, sems.at[n])
        for n, (source, target) in enumerate(((rank_in, rank_ref), (site_in, site_ref), (right_in, right_ref)))
    ]
    copies[0].start()
    parts = chunk_rows_in(guess_in, guess_ref, sems, 0, rows, 3)
    copies[1].start()
    copies[2].start()
    copies[0].wait()
    column = lax.broadcasted_iota(jnp.int32, (1, width), 1)
    keep = (column < rank_ref[...]).astype(F32)
    keep_ref[...] = jnp.broadcast_to(keep, keep_ref.shape)
    squares = jnp.zeros((8, width), F32)
    for n, copy in enumerate(parts):
        copy.wait()
        masked = guess_ref[pl.ds(n * TILE, TILE)] * keep[None]
        squares = squares + fold(masked * masked, width)
        x_ref[n * states : (n + 1) * states] = jnp.swapaxes(masked, 0, 1).astype(BF16)
    squares_ref[...] = squares
    copies[1].wait()
    line = lax.broadcasted_iota(jnp.int32, (TILE, width), 0)
    lane = lax.broadcasted_iota(jnp.int32, (TILE, width), 1)
    extra = jnp.zeros((TILE, width), F32)
    for k in range(terms):
        place_at = (lane == line + k * TILE).astype(BF16)
        extra = extra + jnp.dot(site_ref[k], place_at, preferred_element_type=F32)
    x_ref[blocks * states] = extra.astype(BF16)
    copies[2].wait()
    pack_blocks(right_ref, None, packed_ref)


def prepare_kernel(starts, keep_ref, squares_ref, guess_in, left_in, norm_ref, packed_ref, left_ref, *refs):
    x_refs = (None,) + refs[: len(starts) - 1]
    guess_ref, sems = refs[len(starts) - 1 :]
    rows, states, width = guess_in.shape
    half = width // 2
    done = starts[1] if len(starts) > 1 else rows
    copies = chunk_rows_in(guess_in, guess_ref, sems, done, rows, 1)
    left_copy = pltpu.make_async_copy(left_in, left_ref, sems.at[0])
    left_copy.start()
    keep = keep_ref[0:1, :][None]
    squares = squares_ref[...]
    for n, copy in enumerate(copies):
        copy.wait()
        masked = guess_ref[pl.ds(n * TILE, TILE)] * keep
        squares = squares + fold(masked * masked, width)
        chunk = max(c for c, start in enumerate(starts) if start <= done + n * TILE)
        at = done + n * TILE - starts[chunk]
        block = at // TILE
        x_refs[chunk][block * states : (block + 1) * states] = jnp.swapaxes(masked, 0, 1).astype(BF16)
    total = jnp.sum(squares)
    norm_ref[...] = jnp.full(norm_ref.shape, total, F32)
    line = lax.broadcasted_iota(jnp.int32, (TILE, half), 0)
    norm = jnp.full((TILE, half), total, F32)
    extra = jnp.zeros((TILE, half), F32)
    for n in range(3):
        part = norm.astype(BF16).astype(F32)
        norm = norm - part
        extra = jnp.where(line == left_ref.shape[0] + n, part, extra)
    left_copy.wait()
    pack_blocks(left_ref, extra, packed_ref)


def pack_blocks(block_ref, extra, packed_ref):
    terms, width, _ = block_ref.shape
    half = width // 2
    line = lax.broadcasted_iota(jnp.int32, (TILE, half), 0)
    row, col = triangle(half)
    lines = jnp.zeros((TILE, half), F32) if extra is None else extra
    for k in range(terms):
        upper = block_ref[k, 0:half, 0:half].astype(F32)
        lower = block_ref[k, half:width, half:width].astype(F32)
        diagonal = jnp.sum(jnp.where(row == col, lower, 0.0), axis=0, keepdims=True)
        lines = jnp.where(line == k, diagonal, lines)
        base = k * width
        packed_ref[base : base + half, :] = block_ref[k, 0:half, half:width]
        packed_ref[base + half : base + width, :] = jnp.where(row <= col, upper, lower).astype(BF16)
    packed_ref[terms * width : terms * width + TILE, :] = lines.astype(BF16)


def triangle(half):
    row = lax.broadcasted_iota(jnp.int32, (half, half), 0)
    col = lax.broadcasted_iota(jnp.int32, (half, half), 1)
    return row, col


def unpack_symmetric(packed_ref, full_ref, keep=None):
    terms, width, _ = full_ref.shape
    half = width // 2
    row, col = triangle(half)

    def kept(block, start):
        return block if keep is None else block * keep[:, start : start + half]

    diagonals = packed_ref[terms * width : terms * width + TILE, :].astype(F32)
    for k in range(terms):
        base = k * width
        corner = packed_ref[base : base + half, :].astype(F32)
        mixed = packed_ref[base + half : base + width, :].astype(F32)
        diagonal = diagonals[k : k + 1]
        turned = mixed.T
        lower = jnp.where(row > col, mixed, jnp.where(row == col, diagonal, turned))
        full_ref[k, 0:half, 0:half] = kept(jnp.where(row <= col, mixed, turned), 0).astype(BF16)
        full_ref[k, 0:half, half:width] = kept(corner, half).astype(BF16)
        full_ref[k, half:width, 0:half] = kept(corner.T, 0).astype(BF16)
        full_ref[k, half:width, half:width] = kept(lower, half).astype(BF16)


def spread_kernel(chunk_ref, kron_ref):
    width = chunk_ref.shape[2]
    size = kron_ref.shape[1]
    terms = kron_ref.shape[0] // size
    states = size // TILE
    tile = chunk_ref[chunk_ref.shape[0] - 1]
    row_state = lax.broadcasted_iota(jnp.int32, (size, states), 0) // TILE
    pick = (row_state == lax.broadcasted_iota(jnp.int32, (size, states), 1)).astype(BF16)
    tall = jnp.dot(pick, tile, preferred_element_type=F32).astype(BF16)
    lane = lax.broadcasted_iota(jnp.int32, (width, size), 0)
    col_state = lax.broadcasted_iota(jnp.int32, (width, size), 1) // TILE
    same = (
        lax.broadcasted_iota(jnp.int32, (size, size), 0) % TILE
        == lax.broadcasted_iota(jnp.int32, (size, size), 1) % TILE
    )
    for k in range(terms):
        pick_t = (lane == col_state + k * TILE).astype(BF16)
        full = jnp.dot(tall, pick_t, preferred_element_type=F32)
        kron_ref[k * size : (k + 1) * size, :] = jnp.where(same, full, 0.0).astype(BF16)


def mix_sites(source_ref, kron_ref, rotated_ref, base):
    terms, states, _, width = rotated_ref.shape
    for i in range(source_ref.shape[0] // states):
        to = pl.ds(pl.multiple_of(base + i * TILE, TILE), TILE)
        stack = source_ref[i * states : (i + 1) * states].reshape(states * TILE, width)
        turned = jnp.dot(kron_ref[...], stack, preferred_element_type=F32).astype(BF16)
        rotated_ref[:, :, to, :] = turned.reshape(terms, states, TILE, width)


def summed(values):
    while len(values) > 1:
        values = [values[n] + values[n + 1] for n in range(0, len(values), 2)]
    return values[0]


def place(hop, chips):
    me = lax.axis_index("term")
    chip = (me // CORES - hop + chips) % chips
    return chip, me % CORES


def row_of(spot, rows, chips):
    chip, core = place(spot[0], chips)
    return pl.multiple_of((chip * CORES + (core if spot[1] == 0 else 1 - core)) * rows + spot[2], TILE)


def mix_pieces(pieces, kron_ref, rotated_ref):
    at = 0
    for piece in pieces:
        mix_sites(piece, kron_ref, rotated_ref, at)
        at += piece.shape[0] // rotated_ref.shape[1] * TILE


def rotate_own_kernel(groups, rows, chips, *refs):
    kron_ref, left_ref, rotated_ref, columns_ref = refs[-4:]
    mix_pieces(refs[:-4], kron_ref, rotated_ref)
    blocks = []
    for spots in groups:
        for k in range(left_ref.shape[0]):
            blocks += [left_ref[k, pl.ds(row_of(spot, rows, chips), spot[3]), :] for spot in spots]
    columns_ref[...] = jnp.concatenate(blocks, axis=0).astype(F32).T.astype(BF16)


def turn(right_ref, rotated_ref, turned_ref):
    terms, states, count, width = rotated_ref.shape
    for k in range(terms):
        for n in range(0, states, 8):
            source = rotated_ref[k, n : n + 8].reshape(8 * count, width)
            turned = jnp.dot(source, right_ref[k], preferred_element_type=F32).astype(BF16)
            turned_ref[n : n + 8, k * count : (k + 1) * count, :] = turned.reshape(8, count, width)


def here_kernel(rotated_ref, packed_ref, keep_ref, turned_ref, right_ref):
    unpack_symmetric(packed_ref, right_ref, keep_ref[0:1, :])
    turn(right_ref, rotated_ref, turned_ref)


def there_kernel(*refs):
    right_ref, kron_ref, turned_ref, rotated_ref = refs[-4:]
    mix_pieces(refs[:-4], kron_ref, rotated_ref)
    turn(right_ref, rotated_ref, turned_ref)


def last_kernel(count, *refs):
    right_ref, kron_ref, columns_ref = refs[count : count + 3]
    out_ref, rotated_ref, turned_ref = refs[-3:]
    there_kernel(*refs[:count], right_ref, kron_ref, turned_ref, rotated_ref)
    blocks = list(refs[count + 3 : -3]) + [turned_ref]

    def lefts(p, carry):
        stack = jnp.concatenate([block[p] for block in blocks], axis=0)
        out_ref[p] = jnp.dot(columns_ref[...], stack, preferred_element_type=F32)
        return carry

    lax.fori_loop(0, out_ref.shape[0], lefts, 0, unroll=out_ref.shape[0])


def rotate_kernel(spots, rows, chips, *refs):
    pieces = refs[: len(spots)]
    kron_ref = refs[len(spots)]
    rotated_ref, whole_ref, sems = refs[-3:]
    states = whole_ref.shape[0]
    copies = []
    bases = [row_of(spot, rows, chips) for spot in spots]
    for at, piece in zip(bases, pieces):
        for i in range(piece.shape[0] // states):
            target = whole_ref.at[:, pl.ds(pl.multiple_of(at + i * TILE, TILE), TILE), :]
            source = piece.at[i * states : (i + 1) * states]
            copies.append(pltpu.make_async_copy(source, target, sems.at[len(copies)]))
            copies[-1].start()
    for at, piece in zip(bases, pieces):
        mix_sites(piece, kron_ref, rotated_ref, at)
    for copy in copies:
        copy.wait()


def lefts_kernel(spots, rows, chips, *refs):
    count = len(spots)
    packed_ref, norm_before_ref = refs[count + 3 : count + 5]
    mixed_ref, norm_ref, rotated_ref, whole_ref, left_ref, sems = refs[-6:]
    terms, states, width, _ = rotated_ref.shape
    lines = packed_ref[terms * width : terms * width + TILE, :].astype(F32)
    norm = lines[terms : terms + 1] + lines[terms + 1 : terms + 2] + lines[terms + 2 : terms + 3]
    norm_ref[...] = norm_before_ref[...] + jnp.concatenate([norm, norm], axis=1)
    unpack_symmetric(packed_ref, left_ref)
    rotate_kernel(spots, rows, chips, *refs[: count + 1], rotated_ref, whole_ref, sems)

    def lefts(p, carry):
        for k in range(terms):
            mixed = jnp.dot(left_ref[k], rotated_ref[k, p], preferred_element_type=F32)
            mixed_ref[p, :, k * width : (k + 1) * width] = mixed.astype(BF16)
        return carry

    lax.fori_loop(0, states, lefts, 0, unroll=states)


def rights_kernel(start, stop, packed_ref, mixed_ref, before_ref, keep_ref, partial_ref, *refs):
    if start == 0:
        right_ref = refs[0]
        unpack_symmetric(packed_ref, right_ref, keep_ref[0:1, :])
    else:
        right_ref = packed_ref
    terms, width, _ = right_ref.shape

    def rights(n, carry):
        at = n * GROUP
        rows = mixed_ref[pl.ds(start + at, GROUP)].reshape(GROUP * width, terms * width)
        stacked = right_ref[...].reshape(terms * width, width)
        image = jnp.dot(rows, stacked, preferred_element_type=F32).reshape(GROUP, width, width)
        partial_ref[pl.ds(at, GROUP)] = (before_ref[pl.ds(start + at, GROUP)] + image).astype(partial_ref.dtype)
        return carry

    lax.fori_loop(0, (stop - start) // GROUP, rights, 0)


def shifted_residual(start, shift, mine_ref, other_ref, whole_ref, left_ref, res_ref, mixed_ref):
    count, width, _ = res_ref.shape
    terms = left_ref.shape[0]
    zero = jnp.zeros((8, width), F32)

    def lefts(n, sums):
        square, product = sums
        for row in range(0, width, STRIP):
            strip = pl.ds(row, STRIP)
            held = whole_ref[start + n, strip, :].astype(F32)
            sigma = mine_ref[n, strip, :].astype(F32) + other_ref[n, strip, :].astype(F32)
            residual = sigma - shift * held
            res_ref[n, strip, :] = residual.astype(BF16)
            square = square + fold(residual * residual, width)
            product = product + fold(sigma * held, width)
        mixed = jnp.dot(
            left_ref[...].reshape(terms * width, width), res_ref[n], preferred_element_type=F32
        ).astype(BF16)
        for k in range(terms):
            mixed_ref[k, n] = mixed[k * width : (k + 1) * width]
        return square, product

    square, product = lax.fori_loop(0, count, lefts, (zero, zero), unroll=count)
    return jnp.sum(square), jnp.sum(product)


def low_kernel(
    norm_ref,
    norm_other_ref,
    low_ref,
    low_other_ref,
    whole_ref,
    left_ref,
    res_ref,
    mixed_ref,
    out_ref,
):
    count, width, _ = low_ref.shape
    states = whole_ref.shape[0]
    held = whole_ref[0].astype(F32)
    sigma = low_ref[0].astype(F32) + low_other_ref[0].astype(F32)
    product = jnp.sum(fold(sigma * held, width))
    square = jnp.sum(fold(held * held, width))
    total = norm_ref[0:1, :] + norm_other_ref[0:1, :]
    floor = jnp.maximum(jnp.maximum(square, (0.25 / states) * total), 1e-30)
    shift = product / floor
    square, product = shifted_residual(
        0, shift, low_ref, low_other_ref, whole_ref, left_ref, res_ref, mixed_ref
    )
    out_ref[0:1, :] = shift
    out_ref[1:2, :] = jnp.full((1, width), square, F32)
    out_ref[2:3, :] = jnp.full((1, width), product, F32)
    out_ref[3:8, :] = jnp.zeros((5, width), F32)


def high_kernel(
    scale,
    members,
    norm_ref,
    norm_other_ref,
    sums_ref,
    high_ref,
    high_other_ref,
    whole_ref,
    left_ref,
    right_ref,
    kron_ref,
    res_low_ref,
    mixed_low_ref,
    out_ref,
    res_ref,
    rotated_ref,
    mixed_ref,
):
    terms, states, width, _ = rotated_ref.shape
    half = states // 2
    shift = sums_ref[0:1, :]
    square, product = shifted_residual(
        half, shift, high_ref, high_other_ref, whole_ref, left_ref, res_ref, mixed_ref
    )

    def sites(i, carry):
        at = pl.ds(pl.multiple_of(i * TILE, TILE), TILE)
        stack = jnp.concatenate([res_low_ref[:, at, :], res_ref[:, at, :]], axis=0).reshape(states * TILE, width)
        turned = jnp.dot(kron_ref[...], stack, preferred_element_type=F32).astype(BF16)
        rotated_ref[:, :, at, :] = turned.reshape(terms, states, TILE, width)
        return carry

    lax.fori_loop(0, width // TILE, sites, 0, unroll=width // TILE)
    cross = jnp.zeros((8, width), F32)
    for start, left_mixed_ref in ((0, mixed_low_ref), (half, mixed_ref)):
        for k in range(terms):
            turned = rotated_ref[k, start : start + half].reshape(half * width, width)
            image = jnp.dot(turned, right_ref[k], preferred_element_type=F32)
            held = left_mixed_ref[k].reshape(half * width, width).astype(F32)
            cross = cross + fold(held * image, width)
    res_square = sums_ref[1:2, :] + square
    product = sums_ref[2:3, :] + product
    total = norm_ref[0:1, :] + norm_other_ref[0:1, :]
    factor = scale / (total * scale + epsilon)
    rayleigh = factor * product
    gap = rayleigh - shift
    res_vector = product - shift * total
    res_sq = factor * (res_square - 2.0 * gap * res_vector + gap * gap * total)
    change = gap * gap * product - 2.0 * gap * (res_square + shift * res_vector)
    share = 1.0 / members
    out_ref[0:1, :] = rayleigh * share
    out_ref[1:2, :] = jnp.maximum(res_sq, 0.0) * share
    out_ref[2:3, :] = factor * (jnp.sum(cross) + share * change)
    out_ref[3:8, :] = jnp.zeros((5, width), F32)


def own_rows_kernel(scale, members, keep_ref, norm_ref, norm_other_ref, share_ref, guess_ref, *refs):
    low_ref, low_other_ref, high_ref, high_other_ref, vector_ref, residual_ref = refs
    rows, states, width = guess_ref.shape
    inverse = lax.rsqrt((norm_ref[0:1, :] + norm_other_ref[0:1, :]) * scale + epsilon)
    row_scale = keep_ref[0:1, :] * inverse
    rayleigh = share_ref[0:1, :] * members
    own = pl.ds(pl.multiple_of(lax.axis_index("term") * rows, TILE), rows)
    vector = guess_ref[...] * row_scale[None]
    vector_ref[...] = vector
    sigma = jnp.concatenate(
        [
            mine_ref[:, own, :].astype(F32) + other_ref[:, own, :].astype(F32)
            for mine_ref, other_ref in ((low_ref, low_other_ref), (high_ref, high_other_ref))
        ],
        axis=0,
    )
    residual_ref[...] = jnp.swapaxes(sigma * row_scale[None], 0, 1) - rayleigh[None] * vector


def finish_kernel(vector_ref, residual_ref, *refs):
    shares = refs[:-2]
    ritz_ref, energy_ref = refs[-2:]
    stat = summed([share[...] for share in shares])
    rayleigh = stat[0:1, :]
    res_sq = stat[1:2, :]
    res_var = res_sq + epsilon
    curvature = stat[2:3, :] / res_var
    res_scale = jnp.sqrt(res_var)
    coupling = res_sq / res_scale
    half_gap = 0.5 * (rayleigh - curvature)
    energy = 0.5 * (rayleigh + curvature) - jnp.sqrt(half_gap * half_gap + coupling * coupling)
    coeff_new = energy - rayleigh
    coeff_norm = jnp.sqrt(coupling * coupling + coeff_new * coeff_new + epsilon)
    old = coupling / coeff_norm
    new = coeff_new / (coeff_norm * res_scale)
    ritz_ref[...] = old[None] * vector_ref[...] + new[None] * residual_ref[...]
    energy_ref[0] = energy[0, 0]


def shards(wave_guess, left_env, right_env, site_ops, bond_rank):
    guess = wave_guess[0]
    left = left_env[0]
    site = site_ops[0]
    rows, states, width = guess.shape
    terms = left.shape[0]
    members = lax.axis_size("term")
    chips = members // CORES
    segments = lax.axis_size("seg")
    scale = 1.0 / float(rows * members * states * width)
    hops = tuple(range(chips))

    def to_sibling(block):
        return lax.ppermute(block, "term", [(i, i ^ 1) for i in range(members)])

    def to_next_chip(block):
        return lax.ppermute(block, "term", [(i, (i + CORES) % members) for i in range(members)])

    def around(block):
        found = [block]
        for _ in range(chips - 1):
            found.append(to_next_chip(found[-1]))
        return found

    def everyone(block):
        return [block] + [
            lax.ppermute(block, "term", [(i, i ^ bits) for i in range(members)])
            for bits in range(CORES, members, CORES)
        ]

    tile = jax.ShapeDtypeStruct((8, width), F32)
    half = width // 2
    packed_shape = jax.ShapeDtypeStruct((terms * width + TILE, half), BF16)
    starts = (0, rows - 2 * TILE, rows - TILE) if rows >= 4 * TILE else (0,)
    lengths = [stop - start for start, stop in zip(starts, starts[1:] + (rows,))]
    in_place = [pltpu.with_memory_space_constraint(a, pltpu.HBM) for a in (guess, left, right_env[0], site)]
    first_chunk, keep, squares, right_packed = pl.pallas_call(
        first_chunk_kernel,
        out_shape=(jax.ShapeDtypeStruct((lengths[0] // TILE * states + 1, TILE, width), BF16), tile, tile, packed_shape),
        in_specs=[anywhere] + [in_hbm] * 3,
        out_specs=(vmem,) * 4,
        scratch_shapes=[
            pltpu.VMEM((1, 1), jnp.int32),
            pltpu.VMEM((lengths[0], states, width), F32),
            pltpu.VMEM(site.shape, BF16),
            pltpu.VMEM(left.shape, BF16),
            pltpu.SemaphoreType.DMA((lengths[0] // TILE + 3,)),
        ],
        compiler_params=params(),
        cost_estimate=cost(2 * guess.size, 3 * guess.size),
        name="first_chunk",
    )(bond_rank.reshape(1, 1), in_place[0], in_place[3], in_place[2])
    rest = rows - lengths[0]
    squares, first_sibling = lax.optimization_barrier((squares, to_sibling(first_chunk)))
    norm_part, left_packed, left, *chunks = pl.pallas_call(
        functools.partial(prepare_kernel, starts),
        out_shape=(
            tile,
            packed_shape,
            jax.ShapeDtypeStruct(left.shape, BF16),
            *[jax.ShapeDtypeStruct((length // TILE * states, TILE, width), BF16) for length in lengths[1:]],
        ),
        in_specs=[vmem] * 2 + [in_hbm] * 2,
        out_specs=(vmem,) * (2 + len(lengths)),
        scratch_shapes=[
            pltpu.VMEM((max(rest, TILE), states, width), F32),
            pltpu.SemaphoreType.DMA((rest // TILE + 1,)),
        ],
        compiler_params=params(),
        cost_estimate=cost(4 * guess.size, 6 * guess.size),
        name="prepare",
    )(keep, squares, *in_place[:2])
    chunks = [first_chunk] + chunks

    chunk_hops = [around(chunk) for chunk in chunks]
    here_pieces = chunks + [first_sibling] + [to_sibling(chunk) for chunk in chunks[1:]]
    here_spots = tuple((0, flip, start, length) for flip in range(CORES) for start, length in zip(starts, lengths))
    far_spots = [
        tuple((hop, flip, start, length) for hop in hops[1:] for flip in range(CORES))
        for start, length in zip(starts, lengths)
    ]
    mid_spots = sum(far_spots[:-1], ())
    groups = [group for group in (here_spots, mid_spots, far_spots[-1]) if group]
    lefts = around(left_packed)
    shift = [(i + 1, i) for i in range(segments - 1)]
    received = lax.ppermute(right_packed, "seg", shift)

    size = states * TILE

    def spread(block):
        return pl.pallas_call(
            spread_kernel,
            out_shape=jax.ShapeDtypeStruct((terms * size, size), BF16),
            in_specs=[vmem],
            out_specs=vmem,
            compiler_params=params(),
            cost_estimate=cost(2 * terms * size * size * width, 2 * terms * size * size),
            name="spread_site",
        )(block)

    kron_own = spread(chunks[0])

    whole = (states, width, width)
    whole_bf = jax.ShapeDtypeStruct(whole, BF16)
    whole_f32 = jax.ShapeDtypeStruct(whole, F32)
    rotated = (terms, states, width, width)
    rotated_bf = jax.ShapeDtypeStruct(rotated, BF16)
    square = pltpu.VMEM((terms, width, width), BF16)
    chip_rows = CORES * rows
    stage_flops = 2 * terms * states * width * width * width

    def buffers(spots):
        count = sum(spot[3] for spot in spots)
        return (terms, states, count, width), (states, terms * count, width)

    here_rotated, here_turned = buffers(here_spots)
    part_cost = cost(stage_flops, 8 * states * width * width)
    rotated_own, columns = pl.pallas_call(
        functools.partial(rotate_own_kernel, groups, rows, chips),
        out_shape=(
            jax.ShapeDtypeStruct(here_rotated, BF16),
            jax.ShapeDtypeStruct((width, terms * width), BF16),
        ),
        in_specs=[vmem] * (len(here_pieces) + 2),
        out_specs=(vmem, vmem),
        compiler_params=params(),
        cost_estimate=part_cost,
        name="rotate_own",
    )(*here_pieces, kron_own, left)

    def rotate(spots, pieces, kron, before):
        return pl.pallas_call(
            functools.partial(rotate_kernel, spots, rows, chips),
            out_shape=(rotated_bf, whole_bf),
            in_specs=[vmem] * (len(pieces) + 1) + [anywhere] * len(before),
            out_specs=(vmem, vmem),
            scratch_shapes=[pltpu.SemaphoreType.DMA((sum(spot[3] for spot in spots) // TILE,))],
            input_output_aliases={len(pieces) + 1 + n: n for n in range(len(before))},
            compiler_params=params(),
            cost_estimate=part_cost,
            name="rotate_crossed" if before else "rotate_here",
        )(*pieces, kron, *before)

    def relayed(blocks):
        return [piece for block in blocks for piece in (block, to_sibling(block))]

    firsts, rotated_own = lax.optimization_barrier((chunk_hops[0][1:], rotated_own))
    kron = spread(firsts[0])
    turned = rotate(here_spots, here_pieces, kron, ())
    received, turned = lax.optimization_barrier((received, turned))
    packed = jnp.where(lax.axis_index("seg") == segments - 1, right_packed, received)
    rights = around(packed)
    turned_own, right = pl.pallas_call(
        here_kernel,
        out_shape=(jax.ShapeDtypeStruct(here_turned, BF16), jax.ShapeDtypeStruct(left.shape, BF16)),
        in_specs=[vmem] * 3,
        out_specs=(vmem, vmem),
        compiler_params=params(),
        cost_estimate=part_cost,
        name="apply_rows_here",
    )(rotated_own, packed, keep)
    parts = [turned_own]
    mid_pieces = []
    if mid_spots:
        mid_pieces += relayed(firsts)
        for crossing in chunk_hops[1:-1]:
            crossed, turned = lax.optimization_barrier((crossing[1:], turned))
            mid_pieces += relayed(crossed)
        turned = rotate(mid_spots, mid_pieces, kron, turned)
        crossed, turned, parts[0] = lax.optimization_barrier((chunk_hops[-1][1:], turned, parts[0]))
        last_pieces = relayed(crossed)
        mid_rotated, mid_turned = buffers(mid_spots)
        parts.append(
            pl.pallas_call(
                there_kernel,
                out_shape=jax.ShapeDtypeStruct(mid_turned, BF16),
                in_specs=[vmem] * (len(mid_pieces) + 2),
                out_specs=vmem,
                scratch_shapes=[pltpu.VMEM(mid_rotated, BF16)],
                compiler_params=params(),
                cost_estimate=part_cost,
                name="apply_rows_crossed",
            )(*mid_pieces, right, kron_own)
        )
    else:
        last_pieces = relayed(firsts)
    last_rotated, last_turned = buffers(far_spots[-1])
    partial = pl.pallas_call(
        functools.partial(last_kernel, len(last_pieces)),
        out_shape=whole_f32,
        in_specs=[vmem] * (len(last_pieces) + 3 + len(parts)),
        out_specs=vmem,
        scratch_shapes=[pltpu.VMEM(last_rotated, BF16), pltpu.VMEM(last_turned, BF16)],
        compiler_params=params(),
        cost_estimate=part_cost,
        name="apply_rows_last",
    )(*last_pieces, right, kron_own, columns, *parts)
    norm = norm_part
    for hop in hops[1:]:
        if hop > 1:
            block, partial = lax.optimization_barrier((firsts[hop - 1], partial))
            kron = spread(block)
            turned = rotate(here_spots, here_pieces, kron, ())
            if mid_spots:
                turned = rotate(mid_spots, mid_pieces, kron, turned)
        left_far, partial = lax.optimization_barrier((lefts[hop], partial))
        mixed, norm, _, vector = pl.pallas_call(
            functools.partial(lefts_kernel, far_spots[-1], rows, chips),
            out_shape=(jax.ShapeDtypeStruct((states, width, terms * width), BF16), tile, rotated_bf, whole_bf),
            in_specs=[vmem] * (len(last_pieces) + 1) + [anywhere] * 2 + [vmem] * 2,
            out_specs=(vmem,) * 4,
            scratch_shapes=[
                square,
                pltpu.SemaphoreType.DMA((sum(spot[3] for spot in far_spots[-1]) // TILE,)),
            ],
            input_output_aliases={len(last_pieces) + 1: 2, len(last_pieces) + 2: 3},
            compiler_params=params(),
            cost_estimate=cost(stage_flops, 12 * states * width * width),
            name="received_lefts",
        )(*last_pieces, kron, *turned, left_far, norm)
        last = hop == hops[-1]
        right_far = rights[hop]
        parts = []
        bounds = (0, states // 2, states) if last else (0, states)
        for start, stop in zip(bounds[:-1], bounds[1:]):
            part_shape = jax.ShapeDtypeStruct((stop - start, width, width), BF16 if last else F32)
            part, *unpacked = pl.pallas_call(
                functools.partial(rights_kernel, start, stop),
                out_shape=(part_shape,) + ((jax.ShapeDtypeStruct(left.shape, BF16),) if start == 0 else ()),
                in_specs=[vmem] * 4,
                out_specs=(vmem,) * (2 if start == 0 else 1),
                compiler_params=params(),
                cost_estimate=cost(stage_flops / 2, 12 * states * width * width),
                name="received_rights",
            )(right_far, mixed, partial, keep)
            if unpacked:
                right_far, norm_other = lax.optimization_barrier((unpacked[0], to_sibling(norm)))
            parts.append(part)
        if not last:
            partial = parts[0]
    halves = []
    for part in parts:
        halves += [part, to_sibling(part)]
    half_bf = jax.ShapeDtypeStruct((states // 2, width, width), BF16)
    half_mixed = (terms, states // 2, width, width)
    res_low, mixed_low, sums = pl.pallas_call(
        low_kernel,
        out_shape=(half_bf, jax.ShapeDtypeStruct(half_mixed, BF16), tile),
        in_specs=[vmem] * 6,
        out_specs=(vmem,) * 3,
        compiler_params=params(),
        cost_estimate=cost(stage_flops / 2, 3 * states * width * width),
        name="residual_low",
    )(norm, norm_other, *halves[:2], vector, left)
    share = pl.pallas_call(
        functools.partial(high_kernel, scale, members),
        out_shape=tile,
        in_specs=[vmem] * 11,
        out_specs=vmem,
        scratch_shapes=[
            pltpu.VMEM(half_bf.shape, BF16),
            pltpu.VMEM(rotated, BF16),
            pltpu.VMEM(half_mixed, BF16),
        ],
        compiler_params=params(),
        cost_estimate=cost(3 * stage_flops, 6 * states * width * width),
        name="residual_high",
    )(norm, norm_other, sums, *halves[2:], vector, left, right, kron_own, res_low, mixed_low)
    crossed = everyone(share)

    local = jax.ShapeDtypeStruct((rows, states, width), F32)
    vector_own, residual_own = pl.pallas_call(
        functools.partial(own_rows_kernel, scale, members),
        out_shape=(local, local),
        in_specs=[vmem] * 9,
        out_specs=(vmem, vmem),
        compiler_params=params(),
        cost_estimate=cost(8 * guess.size, 16 * guess.size),
        name="own_rows",
    )(keep, norm, norm_other, share, guess, *halves)

    shares = [share, to_sibling(share)]
    gated, residual_own = lax.optimization_barrier((crossed[1:], residual_own))
    shares += relayed(gated)
    ritz, energy = pl.pallas_call(
        finish_kernel,
        out_shape=(local, jax.ShapeDtypeStruct((1,), F32)),
        in_specs=[vmem] * (2 + members),
        out_specs=(vmem, smem),
        compiler_params=params(),
        cost_estimate=cost(3 * guess.size, 12 * guess.size),
        name="finish",
    )(vector_own, residual_own, *shares)
    return (ritz[None], energy)


def solution(mesh):
    in_specs = (
        P("seg", "term", None, None),
        P("seg", "term", None, None),
        P("seg", "term", None, None),
        P("seg", "term", None, None),
        P("seg"),
    )
    out_specs = (P("seg", "term", None, None), P("seg"))
    return jax.shard_map(shards, mesh=mesh, in_specs=in_specs, out_specs=out_specs, check_vma=False)
```
